32 devices in a mesh: blk: 8 (over z, x), head: 4 (over y, core).
Axes of the slice: x: 2, y: 2, z: 4, core: 2. Of those that a mesh axis runs over, the one named last changes fastest.
Arguments:
- hidden_in: bfloat16 [2, 2048, 2048], P(None, ('blk', 'head')), may hold values from -6 to 6
- lengths: int32 [2, 9], replicated, may hold values from 1 to 1920, as said below
- query_weight: bfloat16 [2048, 2048], P('blk', 'head'), may hold values from -0.125 to 0.125
- key_matrix: bfloat16 [2048, 1024], P('blk', 'head'), may hold values from -0.125 to 0.125
- value_matrix: bfloat16 [2048, 1024], P('blk', 'head'), may hold values from -0.125 to 0.125
- out_weight: bfloat16 [2048, 2048], P('blk', 'head'), may hold values from -1 to 1
- gate_weight: bfloat16 [2048, 6144], P('blk', 'head'), may hold values from -0.125 to 0.125
- up_weight: bfloat16 [2048, 6144], P('blk', 'head'), may hold values from -0.125 to 0.125
- down_weight: bfloat16 [2048, 6144], P('blk', 'head'), may hold values from -0.078125 to 0.078125
- attn_gain: bfloat16 [2048], replicated, may hold values from 0.25 to 1.75
- query_gain: bfloat16 [128], replicated, may hold values from 0.25 to 1.75
- key_gain: bfloat16 [128], replicated, may hold values from 0.25 to 1.75
- mlp_gain: bfloat16 [2048], replicated, may hold values from 0.25 to 1.75
- cotangent: bfloat16 [2, 2048, 2048], P(None, ('blk', 'head')), may hold values from -6 to 6
Outputs:
- mixed: bfloat16 [2, 2048, 2048], P(None, ('blk', 'head'))
- input_grad: float32 [2, 2048, 2048], P(None, ('blk', 'head'))
- query_weight_grad: float32 [2048, 2048], P('blk', 'head')
- key_weight_grad: float32 [2048, 1024], P('blk', 'head')
- value_weight_grad: float32 [2048, 1024], P('blk', 'head')
- out_weight_grad: float32 [2048, 2048], P('blk', 'head')
- gate_weight_grad: float32 [2048, 6144], P('blk', 'head')
- up_weight_grad: float32 [2048, 6144], P('blk', 'head')
- down_weight_grad: float32 [2048, 6144], P('blk', 'head')
- attn_gain_grad: float32 [2048], replicated
- query_gain_grad: float32 [128], replicated
- key_gain_grad: float32 [128], replicated
- mlp_gain_grad: float32 [2048], replicated
The draws below stay inside these ranges and needn't reach their ends.
Inputs may be any that keep to these rules, and one draw needn't show every extreme that they name: In each micro-batch the lengths sum to 2048; one document, at a place drawn from the seed, has exactly 1920 tokens, and the others together have 128.
All inputs are finite; a program needn't handle non-finite values.
Results may differ from the reference program's by a relative error of at most 0.023.
Values may be sent and summed in bfloat16 or wider, within the bound.
A program may use at most 448 MiB of HBM per device.

```python
import jax
import jax.numpy as jnp
from jax import lax

MODEL_WIDTH = 2048
QUERY_HEADS = 16
KEY_VALUE_HEADS = 8
HEAD_WIDTH = 128
FF = 6144
MB = 2
DOCS = 9
SEQ = 2048
REST = 128


def draw_lengths(key, part):
    key = jax.random.fold_in(key, 11)
    rows_out = []
    for micro_idx in range(MB):
        sub_key = jax.random.fold_in(key, micro_idx)
        cut_key, spot_key = jax.random.split(sub_key)
        chosen = jax.random.permutation(cut_key, REST - 1)[:DOCS - 2] + 1
        chosen = jnp.sort(chosen).astype(jnp.int32)
        edges = jnp.concatenate([jnp.zeros((1,), jnp.int32), chosen, jnp.full((1,), REST, jnp.int32)])
        shorter = edges[1:] - edges[:-1]
        spot_at = jax.random.randint(spot_key, (), 0, DOCS)
        slots = jnp.arange(DOCS, dtype=jnp.int32)
        source = jnp.clip(jnp.where(slots < spot_at, slots, slots - 1), 0, DOCS - 2)
        rows_out.append(jnp.where(slots == spot_at, SEQ - REST, shorter[source]).astype(jnp.int32))
    return jnp.stack(rows_out)


def shard_levels(key, dims, cuts, least, largest):
    loudness, own = 1.0, jax.random.fold_in(key, 6)
    for dim, blocks in cuts:
        draws = jnp.exp(jax.random.uniform(jax.random.fold_in(own, dim), (blocks,), jnp.float32, least / len(cuts), largest / len(cuts)))
        loudness = loudness * jnp.repeat(draws, dims[dim] // blocks).reshape([-1 if axis == dim else 1 for axis in range(len(dims))])
    return loudness


def centred(rng, extent, deviation, reach, pieces=(), kind=jnp.bfloat16):
    loudness = shard_levels(rng, extent, pieces, -0.22, 0.18) if pieces else 1.0
    entries = jax.random.normal(rng, extent, jnp.float32) * deviation * loudness
    return jnp.minimum(jnp.maximum(entries, -reach), reach).astype(kind)


def setup_inputs(seed: int = 0) -> dict:
    splits = jax.random.split(jax.random.key(seed), 15)
    return {
        "hidden_in": centred(splits[0], (MB, SEQ, MODEL_WIDTH), 1.0, 6.0, ((1, 32),)),
        "lengths": draw_lengths(jax.random.fold_in(splits[14], 71), 0),
        "query_weight": centred(splits[2], (MODEL_WIDTH, QUERY_HEADS * HEAD_WIDTH), MODEL_WIDTH ** -0.5, 0.125, ((0, 8), (1, 4))),
        "key_matrix": centred(splits[3], (MODEL_WIDTH, KEY_VALUE_HEADS * HEAD_WIDTH), MODEL_WIDTH ** -0.5, 0.125, ((0, 8), (1, 4))),
        "value_matrix": centred(splits[4], (MODEL_WIDTH, KEY_VALUE_HEADS * HEAD_WIDTH), MODEL_WIDTH ** -0.5, 0.125, ((0, 8), (1, 4))),
        "out_weight": centred(splits[5], (MODEL_WIDTH, QUERY_HEADS * HEAD_WIDTH), (QUERY_HEADS * HEAD_WIDTH // 64) ** -0.5, 1.0, ((0, 8), (1, 4))),
        "gate_weight": centred(splits[6], (MODEL_WIDTH, FF), MODEL_WIDTH ** -0.5, 0.125, ((0, 8), (1, 4))),
        "up_weight": centred(splits[7], (MODEL_WIDTH, FF), MODEL_WIDTH ** -0.5, 0.125, ((0, 8), (1, 4))),
        "down_weight": centred(splits[8], (MODEL_WIDTH, FF), FF ** -0.5, 0.078125, ((0, 8), (1, 4))),
        "attn_gain": jnp.clip(1.0 + 0.15 * jax.random.normal(splits[9], (MODEL_WIDTH,), jnp.float32), 0.25, 1.75).astype(jnp.bfloat16),
        "query_gain": jnp.clip(1.0 + 0.15 * jax.random.normal(splits[10], (HEAD_WIDTH,), jnp.float32), 0.25, 1.75).astype(jnp.bfloat16),
        "key_gain": jnp.clip(1.0 + 0.15 * jax.random.normal(splits[11], (HEAD_WIDTH,), jnp.float32), 0.25, 1.75).astype(jnp.bfloat16),
        "mlp_gain": jnp.clip(1.0 + 0.15 * jax.random.normal(splits[12], (MODEL_WIDTH,), jnp.float32), 0.25, 1.75).astype(jnp.bfloat16),
        "cotangent": centred(splits[13], (MB, SEQ, MODEL_WIDTH), 1.0, 6.0, ((1, 32),)),
    }


EPS = 1e-06
THETA = 1000000.0
NEG = -1e+30

@jax.custom_vjp
def reduced_precision(v):
    return lax.optimization_barrier(v.astype(jnp.bfloat16)).astype(jnp.float32)

@jax.custom_vjp
def reduced_precision_back(v):
    return v

def low_keep(v):
    return (reduced_precision(v), None)

def low_pass(kept, grad):
    return (grad,)

def back_keep(v):
    return (v, None)

def back_low(kept, grad):
    return (reduced_precision(grad),)
reduced_precision.defvjp(low_keep, low_pass)
reduced_precision_back.defvjp(back_keep, back_low)

def doc_layout(length_row, offset, token_count):
    doc_ends = jnp.cumsum(length_row).astype(jnp.int32)
    token_index = offset + jnp.arange(token_count, dtype=jnp.int32)
    passed = doc_ends[None, :] <= token_index[:, None]
    segment = lax.optimization_barrier(jnp.sum(passed.astype(jnp.int32), axis=1))
    doc_start = lax.optimization_barrier(jnp.max(jnp.where(passed, doc_ends[None, :], 0), axis=1))
    return (segment, token_index - doc_start)

def rms_scale(values, weight):
    return values * lax.rsqrt(lax.optimization_barrier(jnp.mean(values * values, axis=-1, keepdims=True)) + EPS) * weight

def rotary(values, position):
    half_dim = values.shape[-1] // 2
    inverse = THETA ** (-jnp.arange(half_dim, dtype=jnp.float32) / half_dim)
    angles = position.astype(jnp.float32)[:, None] * inverse[None, :]
    cosine = jnp.cos(angles)[:, None, :]
    sine_of = jnp.sin(angles)[:, None, :]
    leading = values[..., :half_dim]
    trailing = values[..., half_dim:]
    return jnp.concatenate([leading * cosine - trailing * sine_of, trailing * cosine + leading * sine_of], axis=-1)

def matrix_product(first_op, second_op):
    return jnp.dot(first_op, second_op, precision=lax.Precision.HIGHEST, preferred_element_type=jnp.float32)

def product_t(first_op, second_op):
    return lax.dot_general(first_op, second_op, (((1,), (1,)), ((), ())), precision=lax.Precision.HIGHEST, preferred_element_type=jnp.float32)

def attend(queries, keys_rot, value_matrix_rows, segment):
    token_count = queries.shape[0]
    repeat_factor = QUERY_HEADS // KEY_VALUE_HEADS
    key_rep = jnp.repeat(keys_rot, repeat_factor, axis=1)
    value_rep = jnp.repeat(value_matrix_rows, repeat_factor, axis=1)
    token_index = jnp.arange(token_count, dtype=jnp.int32)
    rows_each = min(512, token_count)
    block_count = token_count // rows_each

    def one_block(packed):
        query_blk, segment_blk, index_blk = packed
        scores = reduced_precision_back(jnp.einsum('qhd,khd->hqk', query_blk, key_rep, precision=lax.Precision.HIGHEST) * HEAD_WIDTH ** (-0.5))
        allowed = (segment_blk[:, None] == segment[None, :]) & (index_blk[:, None] >= token_index[None, :])
        masked = jnp.where(allowed[None], scores, NEG)
        highest = lax.optimization_barrier(jnp.max(masked, axis=-1, keepdims=True))
        weights = jnp.where(allowed[None], jnp.exp(masked - highest), 0.0)
        totals = lax.optimization_barrier(jnp.sum(weights, axis=-1, keepdims=True))
        mixed_out = jnp.einsum('hqk,khd->hqd', reduced_precision(weights), value_rep, precision=lax.Precision.HIGHEST) / totals
        return jnp.transpose(mixed_out, (1, 0, 2))
    packed = (queries.reshape(block_count, rows_each, QUERY_HEADS, HEAD_WIDTH), segment.reshape(block_count, rows_each), token_index.reshape(block_count, rows_each))
    out_blocks = lax.map(jax.checkpoint(one_block), packed)
    return out_blocks.reshape(token_count, QUERY_HEADS, HEAD_WIDTH)

def layer(rows_in, query_weight, key_matrix, value_matrix, out_weight, gate_weight, up_weight, down_weight, attn_gain, query_gain, key_gain, mlp_gain, segment, position):
    token_count = rows_in.shape[0]
    normalized_attention_input = reduced_precision(rms_scale(rows_in, attn_gain))
    query_raw = reduced_precision_back(matrix_product(normalized_attention_input, query_weight)).reshape(token_count, QUERY_HEADS, HEAD_WIDTH)
    key_unrotated = reduced_precision_back(matrix_product(normalized_attention_input, key_matrix)).reshape(token_count, KEY_VALUE_HEADS, HEAD_WIDTH)
    value_matrix_rows = reduced_precision(reduced_precision_back(matrix_product(normalized_attention_input, value_matrix))).reshape(token_count, KEY_VALUE_HEADS, HEAD_WIDTH)
    queries = reduced_precision(rotary(rms_scale(query_raw, query_gain), position))
    keys_rot = reduced_precision(rotary(rms_scale(key_unrotated, key_gain), position))
    attended = attend(queries, keys_rot, value_matrix_rows, segment).reshape(token_count, QUERY_HEADS * HEAD_WIDTH)
    attn_rows = reduced_precision(reduced_precision_back(attended))
    middle = rows_in + reduced_precision_back(product_t(attn_rows, out_weight))
    normed_m = reduced_precision(rms_scale(middle, mlp_gain))
    gate_rows = reduced_precision_back(matrix_product(normed_m, gate_weight))
    up_rows = reduced_precision_back(matrix_product(normed_m, up_weight))
    active = reduced_precision(jax.nn.silu(gate_rows) * up_rows)
    return middle + reduced_precision_back(product_t(active, down_weight))

def reference(hidden_in, lengths, query_weight, key_matrix, value_matrix, out_weight, gate_weight, up_weight, down_weight, attn_gain, query_gain, key_gain, mlp_gain, cotangent):
    weights_f = tuple((weight_arr.astype(jnp.float32) for weight_arr in (query_weight, key_matrix, value_matrix, out_weight, gate_weight, up_weight, down_weight, attn_gain, query_gain, key_gain, mlp_gain)))
    outputs = []
    input_grads = []
    totals = None
    for micro_idx in range(MB):
        segment, position = doc_layout(lengths[micro_idx], 0, SEQ)

        def forward(rows_in, *params):
            return layer(rows_in, *params, segment, position)
        result, pullback = jax.vjp(forward, hidden_in[micro_idx].astype(jnp.float32), *weights_f)
        gradients = pullback(cotangent[micro_idx].astype(jnp.float32))
        outputs.append(result.astype(jnp.bfloat16))
        input_grads.append(gradients[0])
        if totals is None:
            totals = gradients[1:]
        else:
            totals = tuple((first_op + second_op for first_op, second_op in zip(totals, gradients[1:])))
    return (jnp.stack(outputs), jnp.stack(input_grads), totals[0], totals[1], totals[2], totals[3], totals[4], totals[5], totals[6], totals[7], totals[8], totals[9], totals[10])
```

```python
import functools

import jax
import jax.numpy as jnp
from jax import lax
from jax.experimental import pallas as pl
from jax.experimental.pallas import tpu as pltpu
from jax.sharding import PartitionSpec as P

EPS = 1e-06
THETA = 1000000.0
LOG2E = 1.4426950408889634
F32 = jnp.float32
BF16 = jnp.bfloat16

TENSOR_BIT = 1


def nt(a, b):
    return lax.dot_general(a, b, (((1,), (1,)), ((), ())), preferred_element_type=F32)


def tn(a, b):
    return lax.dot_general(a, b, (((0,), (0,)), ((), ())), preferred_element_type=F32)


def nn(a, b):
    return jnp.dot(a, b, preferred_element_type=F32)


def bit_of(value, bit):
    return (value >> bit) & 1


def over_blk(value, bit):
    count = lax.axis_size("blk")
    return lax.ppermute(value, "blk", [(i, i ^ (1 << bit)) for i in range(count)])


def over_head(value, bit):
    count = lax.axis_size("head")
    return lax.ppermute(value, "head", [(i, i ^ (1 << bit)) for i in range(count)])


def in_order(flag, own, other, axis):
    return jnp.where(
        flag == 0,
        jnp.concatenate([own, other], axis=axis),
        jnp.concatenate([other, own], axis=axis),
    )


def token_offset(head_place, index, sub):
    core, upper, inner = index // (2 * sub), (index // sub) % 2, index % sub
    return (head_place ^ (upper * 2) ^ core) * sub + inner


def allowed_mask(meta_ref, start_row, q_block, k_block, rows, half, q_lanes):
    sub = half // 2
    head_place = meta_ref[0]
    k_index = lax.broadcasted_iota(jnp.int32, (2 * half, 1), 0)
    k_token = token_offset(head_place, k_index, sub) + k_block * (2 * half)
    q_index = lax.broadcasted_iota(jnp.int32, (1, q_lanes), 1) % (2 * half)
    q_token = token_offset(head_place, q_index, sub) + q_block * (2 * half)
    return (k_token <= q_token) & (k_token >= start_row)


def stacked(ref, heads, width):
    return jnp.concatenate(
        [ref[c, 0, :, h * width : (h + 1) * width] for h in range(heads) for c in range(2)], axis=0
    )


def key_rows(ref, part, block):
    return jnp.concatenate([ref[part, 0, block], ref[part, 1, block]], axis=0)


def attend_kernel(meta_ref, q_ref, k_ref, v_ref, start_ref, o_ref, ot_ref, l_ref, vt_ref, acc_ref, sum_ref, *, factor, heads):
    q_pos = pl.program_id(0)
    parts, _, blocks, half, width = k_ref.shape
    lanes = heads * 2 * half

    @pl.when(q_pos == 0)
    def _():
        for part in range(parts):
            for block in range(blocks):
                vt_ref[part * blocks + block] = key_rows(v_ref, part, block).T

    q_rows = stacked(q_ref, heads, width)
    acc_ref[...] = jnp.zeros_like(acc_ref)
    sum_ref[...] = jnp.zeros_like(sum_ref)
    start_row = start_ref[0]
    q_block = meta_ref[1 + q_pos]
    total = parts * blocks

    def add(kb, masked):
        e = jnp.exp2(nt(key_rows(k_ref, kb // blocks, kb % blocks), q_rows) * factor)
        if masked:
            k_block = meta_ref[1 + blocks + kb]
            e = jnp.where(allowed_mask(meta_ref, start_row, q_block, k_block, None, half, lanes), e, 0.0)
        sum_ref[...] += jnp.sum(e, axis=0, keepdims=True)
        acc_ref[...] += nn(vt_ref[kb], e.astype(BF16))

    def step(kb, carry):
        flag = meta_ref[1 + blocks + total + q_pos * total + kb]

        @pl.when(flag == 1)
        def _():
            add(kb, False)

        @pl.when(flag == 2)
        def _():
            add(kb, True)

        return carry

    lax.fori_loop(0, total, step, 0)
    out = acc_ref[...] / sum_ref[...]
    ot_ref[0] = out
    l_ref[0] = sum_ref[...]
    rows = out.T
    for h in range(heads):
        for c in range(2):
            at = (h * 2 + c) * half
            o_ref[c, 0, :, h * width : (h + 1) * width] = rows[at : at + half].astype(BF16)


def attend_back_kernel(
    meta_ref, q_ref, do_ref, k_ref, v_ref, start_ref, ot_ref, l_ref, dq_ref, dk_ref, dv_ref, kt_ref, acc_ref, *, factor, scaling, heads
):
    q_pos = pl.program_id(0)
    parts, _, blocks, half, width = k_ref.shape
    lanes = heads * 2 * half

    @pl.when(q_pos == 0)
    def _():
        dk_ref[...] = jnp.zeros_like(dk_ref)
        dv_ref[...] = jnp.zeros_like(dv_ref)
        for part in range(parts):
            for block in range(blocks):
                kt_ref[part * blocks + block] = key_rows(k_ref, part, block).T

    q_rows = stacked(q_ref, heads, width)
    do_rows = stacked(do_ref, heads, width)
    delta = jnp.sum(do_rows.astype(F32).T * ot_ref[0], axis=0, keepdims=True)
    inverse = 1.0 / l_ref[0]
    acc_ref[...] = jnp.zeros_like(acc_ref)
    start_row = start_ref[0]
    q_block = meta_ref[1 + q_pos]
    total = parts * blocks

    def add(kb, masked):
        part, block = kb // blocks, kb % blocks
        e = jnp.exp2(nt(key_rows(k_ref, part, block), q_rows) * factor)
        if masked:
            k_block = meta_ref[1 + blocks + kb]
            e = jnp.where(allowed_mask(meta_ref, start_row, q_block, k_block, None, half, lanes), e, 0.0)
        p = e * inverse
        dp = nt(key_rows(v_ref, part, block), do_rows)
        ds = (p * (dp - delta)).astype(BF16)
        dv = nn(p.astype(BF16), do_rows)
        dk = nn(ds, q_rows) * scaling
        for c in range(2):
            dv_ref[part, c, block] += dv[c * half : (c + 1) * half]
            dk_ref[part, c, block] += dk[c * half : (c + 1) * half]
        acc_ref[...] += nn(kt_ref[kb], ds)

    def step(kb, carry):
        flag = meta_ref[1 + blocks + total + q_pos * total + kb]

        @pl.when(flag == 1)
        def _():
            add(kb, False)

        @pl.when(flag == 2)
        def _():
            add(kb, True)

        return carry

    lax.fori_loop(0, total, step, 0)
    rows = acc_ref[...].T * scaling
    for h in range(heads):
        for c in range(2):
            at = (h * 2 + c) * half
            dq_ref[c, 0, :, h * width : (h + 1) * width] = rows[at : at + half]


def attend(meta, q, k, v, start, scaling):
    _, blocks, half, columns = q.shape
    parts, width = k.shape[0], k.shape[-1]
    heads = columns // width
    lanes = heads * 2 * half
    total = parts * blocks
    row_spec = pl.BlockSpec((2, 1, half, columns), lambda i: (0, i, 0, 0))
    key_spec = pl.BlockSpec(k.shape, lambda i: (0, 0, 0, 0, 0))
    lane_spec = pl.BlockSpec((1, 1, lanes), lambda i: (i, 0, 0))
    return pl.pallas_call(
        functools.partial(attend_kernel, factor=scaling * LOG2E, heads=heads),
        grid=(blocks,),
        in_specs=[pl.BlockSpec(memory_space=pltpu.SMEM), row_spec, key_spec, key_spec, lane_spec],
        out_specs=[row_spec, pl.BlockSpec((1, width, lanes), lambda i: (i, 0, 0)), lane_spec],
        out_shape=[
            jax.ShapeDtypeStruct(q.shape, BF16),
            jax.ShapeDtypeStruct((blocks, width, lanes), F32),
            jax.ShapeDtypeStruct((blocks, 1, lanes), F32),
        ],
        scratch_shapes=[
            pltpu.VMEM((total, width, 2 * half), BF16),
            pltpu.VMEM((width, lanes), F32),
            pltpu.VMEM((1, lanes), F32),
        ],
        compiler_params=pltpu.CompilerParams(vmem_limit_bytes=40 * 1024 * 1024),
        cost_estimate=pl.CostEstimate(
            flops=2 * 2 * lanes * 2 * half * width * blocks * total,
            bytes_accessed=8 * q.size + 8 * k.size,
            transcendentals=lanes * 2 * half * blocks * total,
        ),
    )(meta, q, k, v, start)


def attend_back(meta, q, do, k, v, start, out_t, total_e, scaling):
    _, blocks, half, columns = q.shape
    parts, width = k.shape[0], k.shape[-1]
    heads = columns // width
    lanes = heads * 2 * half
    total = parts * blocks
    row_spec = pl.BlockSpec((2, 1, half, columns), lambda i: (0, i, 0, 0))
    key_spec = pl.BlockSpec(k.shape, lambda i: (0, 0, 0, 0, 0))
    lane_spec = pl.BlockSpec((1, 1, lanes), lambda i: (i, 0, 0))
    return pl.pallas_call(
        functools.partial(attend_back_kernel, factor=scaling * LOG2E, scaling=scaling, heads=heads),
        grid=(blocks,),
        in_specs=[
            pl.BlockSpec(memory_space=pltpu.SMEM),
            row_spec,
            row_spec,
            key_spec,
            key_spec,
            lane_spec,
            pl.BlockSpec((1, width, lanes), lambda i: (i, 0, 0)),
            lane_spec,
        ],
        out_specs=[row_spec, key_spec, key_spec],
        out_shape=[
            jax.ShapeDtypeStruct(q.shape, F32),
            jax.ShapeDtypeStruct(k.shape, F32),
            jax.ShapeDtypeStruct(k.shape, F32),
        ],
        scratch_shapes=[
            pltpu.VMEM((total, width, 2 * half), BF16),
            pltpu.VMEM((width, lanes), F32),
        ],
        compiler_params=pltpu.CompilerParams(vmem_limit_bytes=48 * 1024 * 1024),
        cost_estimate=pl.CostEstimate(
            flops=5 * 2 * lanes * 2 * half * width * blocks * total,
            bytes_accessed=12 * q.size + 16 * k.size,
            transcendentals=lanes * 2 * half * blocks * total,
        ),
    )(meta, q, do, k, v, start, out_t, total_e)


def local(
    hidden_in,
    lengths,
    query_weight,
    key_matrix,
    value_matrix,
    out_weight,
    gate_weight,
    up_weight,
    down_weight,
    attn_gain,
    query_gain,
    key_gain,
    mlp_gain,
    cotangent,
):
    ring = lax.axis_size("blk")
    bits = ring.bit_length() - 1
    batch_bit = bits - 1
    seq_bits = [i for i in range(bits) if i not in (TENSOR_BIT, batch_bit)]
    data_bits = [batch_bit, *seq_bits]
    parts = 1 << len(seq_bits)
    blk, head = lax.axis_index("blk"), lax.axis_index("head")
    batch, tensor = bit_of(blk, batch_bit), bit_of(blk, TENSOR_BIT)

    local_rows, width = hidden_in.shape[1:]
    block_rows = local_rows * lax.axis_size("head")
    half = block_rows // 2
    row_features = width // ring
    head_size = query_gain.shape[0]
    scaling = head_size ** (-0.5)
    tokens = 16 * local_rows
    heads = query_weight.shape[1] // (2 * head_size)
    ff = gate_weight.shape[1] // 2

    axis_order = [*reversed(seq_bits), batch_bit, TENSOR_BIT]

    def to_group(values):
        lead = values.shape[:-1]
        n = len(lead)
        cut = values.reshape(*lead, *([2] * bits), row_features)
        for b in data_bits:
            cut = jnp.where(bit_of(blk, b) == 1, jnp.flip(cut, n + bits - 1 - b), cut)
        order = [*range(n), *[n + bits - 1 - b for b in axis_order], n + bits]
        return jnp.transpose(cut, order).reshape(*lead, width)

    def from_group(values):
        lead = values.shape[:-1]
        n = len(lead)
        cut = values.reshape(*lead, *([2] * bits), row_features)
        back = [axis_order.index(b) for b in range(bits - 1, -1, -1)]
        cut = jnp.transpose(cut, [*range(n), *[n + i for i in back], n + bits])
        for b in data_bits:
            cut = jnp.where(bit_of(blk, b) == 1, jnp.flip(cut, n + bits - 1 - b), cut)
        return cut.reshape(*lead, width)

    def cut_half(weight, which):
        return lax.dynamic_slice_in_dim(weight, which * (weight.shape[1] // 2), weight.shape[1] // 2, 1)

    def collect(weights):
        own = jnp.concatenate([cut_half(w, tensor) for w in weights], axis=1)
        other = over_blk(jnp.concatenate([cut_half(w, 1 - tensor) for w in weights], axis=1), TENSOR_BIT)
        chunks = [in_order(tensor, own, other, 0)]
        for b in data_bits:
            chunks = chunks + [over_blk(c, b) for c in chunks]
        return jnp.concatenate(chunks, axis=0)

    def settle(grad, column_widths):
        for b in reversed(data_bits):
            n = grad.shape[0] // 2
            grad = grad[:n] + over_blk(grad[n:].astype(BF16), b).astype(F32)
        own = lax.dynamic_slice_in_dim(grad, tensor * row_features, row_features, 0)
        other = over_blk(
            lax.dynamic_slice_in_dim(grad, (1 - tensor) * row_features, row_features, 0).astype(BF16), TENSOR_BIT
        ).astype(F32)
        results, at = [], 0
        for w in column_widths:
            results.append(in_order(tensor, own[:, at : at + w], other[:, at : at + w], 1))
            at += w
        return results

    def spread(rows):
        flat = rows.reshape(2 * local_rows, width)
        by_y = over_head(flat, 1)
        by_t = over_blk(flat, TENSOR_BIT)
        by_ty = over_head(by_t, 1)
        near = [flat, by_y, by_t, by_ty]
        far = [over_head(piece, 0) for piece in near]
        cut = [
            piece.reshape(2, local_rows, width)[m]
            for group in (near, far)
            for m in range(2)
            for piece in group
        ]
        return jnp.concatenate(cut, axis=0)

    def gather_sum(left, weight):
        n = tokens // 2
        away = over_head(nt(left[n:], weight).astype(BF16), 0)
        held = (nt(left[:n], weight) + away.astype(F32)).reshape(2, 2, 2, local_rows, width)
        from_y1 = over_head(held[:, 1, 1].astype(BF16), 1)
        from_y0 = over_head(held[:, 0, 1].astype(BF16), 1)
        from_t = over_blk((held[:, 1, 0] + from_y1.astype(F32)).astype(BF16), TENSOR_BIT)
        return held[:, 0, 0] + from_y0.astype(F32) + from_t.astype(F32)

    def take_batch(rows):
        mine = lax.dynamic_index_in_dim(rows, batch, 0, keepdims=False)
        theirs = lax.dynamic_index_in_dim(rows, 1 - batch, 0, keepdims=False)
        return to_group(jnp.stack([mine, over_blk(theirs, batch_bit)]))

    def give_batch(rows):
        rows = from_group(rows)
        back = over_blk(rows[1].astype(BF16), batch_bit).astype(rows.dtype)
        return in_order(batch, rows[0][None], back[None], 0)

    length_row = lax.dynamic_index_in_dim(lengths, batch, 0, keepdims=False)
    doc_ends = jnp.cumsum(length_row)
    batch_flip = jnp.arange(2, dtype=jnp.int32)[:, None] << batch_bit
    tensor_flip = jnp.arange(2, dtype=jnp.int32)[None, :] << TENSOR_BIT
    q_blocks = (blk ^ batch_flip ^ tensor_flip).reshape(4)
    index = jnp.arange(2 * half, dtype=jnp.int32)
    in_block = token_offset(head, index, local_rows).reshape(2, 1, half)
    token_index = q_blocks[None, :, None] * block_rows + in_block
    passed = doc_ends <= token_index[..., None]
    doc_start = jnp.max(jnp.where(passed, doc_ends, 0), axis=-1).astype(jnp.int32)
    position = (token_index - doc_start).reshape(tokens)
    start_lanes = jnp.tile(jnp.transpose(doc_start, (1, 0, 2)).reshape(4, 1, 2 * half), (1, 1, heads))
    k_blocks = q_blocks
    for b in seq_bits:
        k_blocks = jnp.concatenate([k_blocks, k_blocks ^ (1 << b)])
    least_start = jnp.min(doc_start, axis=(0, 2))[:, None]
    last_start = jnp.max(doc_start, axis=(0, 2))[:, None]
    k_first = (k_blocks * block_rows)[None, :]
    none = (k_blocks[None, :] > q_blocks[:, None]) | (k_first + block_rows <= least_start)
    whole = (k_blocks[None, :] < q_blocks[:, None]) & (k_first >= last_start)
    flags = jnp.where(none, 0, jnp.where(whole, 1, 2))
    meta = jnp.concatenate([head[None], q_blocks, k_blocks, flags.reshape(-1)]).astype(jnp.int32)

    inverse_freq = THETA ** (-jnp.arange(head_size // 2, dtype=F32) / (head_size // 2))
    angles = position.astype(F32)[:, None] * inverse_freq[None, :]
    cosine = jnp.cos(angles)[:, None, :]
    sine = jnp.sin(angles)[:, None, :]

    def rope(values):
        a, b = values[..., : head_size // 2], values[..., head_size // 2 :]
        return jnp.concatenate([a * cosine - b * sine, b * cosine + a * sine], axis=-1)

    def rope_back(values):
        a, b = values[..., : head_size // 2], values[..., head_size // 2 :]
        return jnp.concatenate([a * cosine + b * sine, b * cosine - a * sine], axis=-1)

    def rms(values):
        return lax.rsqrt(jnp.mean(values * values, axis=-1, keepdims=True) + EPS)

    def norm_back(grad, normed, inverse, gain):
        scaled = grad * gain
        return inverse * (scaled - normed * jnp.mean(scaled * normed, axis=-1, keepdims=True))

    gain_a = to_group(attn_gain.astype(F32))
    gain_m = to_group(mlp_gain.astype(F32))
    gain_q = query_gain.astype(F32)
    gain_k = key_gain.astype(F32)

    rows_in = take_batch(hidden_in).astype(F32)
    cot = take_batch(cotangent)
    w_qkv = collect((query_weight, key_matrix, value_matrix))
    inverse_a = rms(rows_in)
    normal_a = rows_in * inverse_a
    xa = spread((normal_a * gain_a).astype(BF16))
    w_out = collect((out_weight,))
    w_gu = collect((gate_weight, up_weight))
    w_down = collect((down_weight,))
    cot_all = spread(cot)

    qkv = nn(xa, w_qkv)
    q_columns, k_columns = heads * head_size, head_size
    q_raw = qkv[:, :q_columns].reshape(tokens, heads, head_size)
    k_raw = qkv[:, q_columns : q_columns + k_columns].reshape(tokens, 1, head_size)
    value = qkv[:, q_columns + k_columns :].astype(BF16)
    q_inverse, k_inverse = rms(q_raw), rms(k_raw)
    q_normal, k_normal = q_raw * q_inverse, k_raw * k_inverse
    query = rope(q_normal * gain_q).astype(BF16).reshape(2, 4, half, q_columns)
    key = rope(k_normal * gain_k).astype(BF16).reshape(tokens, head_size)
    key_value = [jnp.concatenate([key, value], axis=1)]
    for b in seq_bits:
        key_value = key_value + [over_blk(c, b) for c in key_value]
    key_value = jnp.stack(key_value)
    keys = key_value[..., :head_size].reshape(parts, 2, 4, half, head_size)
    values = key_value[..., head_size:].reshape(parts, 2, 4, half, head_size)
    attn, attn_t, total_e = attend(meta, query, keys, values, start_lanes, scaling)
    attn = attn.reshape(tokens, q_columns)
    middle = rows_in + gather_sum(attn, w_out)
    inverse_m = rms(middle)
    normal_m = middle * inverse_m
    xm = spread((normal_m * gain_m).astype(BF16))
    d_active = nn(cot_all, w_down)
    gate_up = nn(xm, w_gu)
    gate, up = gate_up[:, :ff], gate_up[:, ff:]
    sig = jax.nn.sigmoid(gate)
    silu = gate * sig
    active = (silu * up).astype(BF16)
    d_gate = (d_active * up * sig * (1.0 + gate * (1.0 - sig))).astype(BF16)
    d_up = (d_active * silu).astype(BF16)
    d_gu = jnp.concatenate([d_gate, d_up], axis=1)

    d_xm = gather_sum(d_gu, w_gu)
    mixed = give_batch((middle + gather_sum(active, w_down)).astype(BF16))
    g_gate, g_up = settle(tn(xm, d_gu), (ff, ff))
    (g_down,) = settle(tn(cot_all, active), (ff,))
    d_middle = cot.astype(F32) + norm_back(d_xm, normal_m, inverse_m, gain_m)
    d_mid_all = spread(d_middle.astype(BF16))
    d_attn = nn(d_mid_all, w_out).astype(BF16).reshape(2, 4, half, q_columns)
    d_query, d_key, d_value = attend_back(
        meta, query, d_attn, keys, values, start_lanes, attn_t, total_e, scaling
    )
    (g_out,) = settle(tn(d_mid_all, attn), (q_columns,))
    d_key_value = jnp.concatenate(
        [d_key.reshape(parts, tokens, head_size), d_value.reshape(parts, tokens, head_size)], axis=-1
    )
    for b in reversed(seq_bits):
        n = d_key_value.shape[0] // 2
        d_key_value = d_key_value[:n] + over_blk(d_key_value[n:].astype(BF16), b).astype(F32)
    d_key, d_value = d_key_value[0, :, :head_size], d_key_value[0, :, head_size:]
    dq_turned = rope_back(d_query.reshape(tokens, heads, head_size))
    dk_turned = rope_back(d_key.reshape(tokens, 1, head_size))
    gain_q_grad = jnp.sum(dq_turned * q_normal, axis=(0, 1))
    gain_k_grad = jnp.sum(dk_turned * k_normal, axis=(0, 1))
    dq_raw = norm_back(dq_turned, q_normal, q_inverse, gain_q).reshape(tokens, q_columns)
    dk_raw = norm_back(dk_turned, k_normal, k_inverse, gain_k).reshape(tokens, k_columns)
    d_qkv = jnp.concatenate([dq_raw, dk_raw, d_value], axis=1).astype(BF16)
    g_query, g_key, g_value = settle(tn(xa, d_qkv), (q_columns, k_columns, k_columns))
    d_xa = gather_sum(d_qkv, w_qkv)
    input_grad = give_batch(d_middle + norm_back(d_xa, normal_a, inverse_a, gain_a))
    gain_a_grad = from_group(jnp.sum(d_xa * normal_a, axis=(0, 1)))
    gain_m_grad = from_group(jnp.sum(d_xm * normal_m, axis=(0, 1)))
    gains = lax.psum((gain_a_grad, gain_q_grad, gain_k_grad, gain_m_grad), ("blk", "head"))
    return (
        mixed,
        input_grad,
        g_query,
        g_key,
        g_value,
        g_out,
        g_gate,
        g_up,
        g_down,
        *gains,
    )


def solution(mesh):
    rows = P(None, ("blk", "head"), None)
    weight = P("blk", "head")
    return jax.shard_map(
        local,
        mesh=mesh,
        in_specs=(rows, P(), *([weight] * 7), P(), P(), P(), P(), rows),
        out_specs=(rows, rows, *([weight] * 7), P(), P(), P(), P()),
        check_vma=False,
    )
```

```python
import functools

import jax
import jax.numpy as jnp
from jax import lax
from jax.experimental import pallas as pl
from jax.experimental.pallas import tpu as pltpu
from jax.sharding import PartitionSpec as P

EPS = 1e-06
THETA = 1000000.0
LOG2E = 1.4426950408889634
F32 = jnp.float32
BF16 = jnp.bfloat16

TENSOR_BIT = 1
SEQ_BIT = 0


def nt(a, b):
    return lax.dot_general(a, b, (((1,), (1,)), ((), ())), preferred_element_type=F32)


def tn(a, b):
    return lax.dot_general(a, b, (((0,), (0,)), ((), ())), preferred_element_type=F32)


def nn(a, b):
    return jnp.dot(a, b, preferred_element_type=F32)


def bit_of(value, bit):
    return (value >> bit) & 1


def over_blk(value, mask):
    count = lax.axis_size("blk")
    return lax.ppermute(value, "blk", [(i, i ^ mask) for i in range(count)])


def over_head(value, mask):
    count = lax.axis_size("head")
    return lax.ppermute(value, "head", [(i, i ^ mask) for i in range(count)])


def pin(values):
    return lax.optimization_barrier(values)


def in_order(flag, own, other, axis):
    return jnp.where(
        flag == 0,
        jnp.concatenate([own, other], axis=axis),
        jnp.concatenate([other, own], axis=axis),
    )


def token_offset(head_place, index, sub):
    core, upper, inner = index // (2 * sub), (index // sub) % 2, index % sub
    return (head_place ^ (upper * 2) ^ core) * sub + inner


def allowed_mask(meta_ref, start_row, q_block, k_block, rows, half, q_lanes):
    sub = half // 2
    head_place = meta_ref[0]
    k_index = lax.broadcasted_iota(jnp.int32, (2 * half, 1), 0)
    k_token = token_offset(head_place, k_index, sub) + k_block * (2 * half)
    q_index = lax.broadcasted_iota(jnp.int32, (1, q_lanes), 1) % (2 * half)
    q_token = token_offset(head_place, q_index, sub) + q_block * (2 * half)
    return (k_token <= q_token) & (k_token >= start_row)


def stacked(ref, heads, width):
    return jnp.concatenate(
        [ref[c, 0, :, h * width : (h + 1) * width] for h in range(heads) for c in range(2)], axis=0
    )


def key_rows(ref, part, block):
    return jnp.concatenate([ref[part, 0, block], ref[part, 1, block]], axis=0)


def attend_kernel(meta_ref, q_ref, k_ref, v_ref, start_ref, o_ref, ot_ref, l_ref, vt_ref, acc_ref, sum_ref, *, factor, heads):
    q_pos = pl.program_id(0)
    parts, _, blocks, half, width = k_ref.shape
    lanes = heads * 2 * half

    @pl.when(q_pos == 0)
    def _():
        for part in range(parts):
            for block in range(blocks):
                vt_ref[part * blocks + block] = key_rows(v_ref, part, block).T

    q_rows = stacked(q_ref, heads, width)
    acc_ref[...] = jnp.zeros_like(acc_ref)
    sum_ref[...] = jnp.zeros_like(sum_ref)
    start_row = start_ref[0]
    q_block = meta_ref[1 + q_pos]
    total = parts * blocks

    def add(kb, masked):
        e = jnp.exp2(nt(key_rows(k_ref, kb // blocks, kb % blocks), q_rows) * factor)
        if masked:
            k_block = meta_ref[1 + blocks + kb]
            e = jnp.where(allowed_mask(meta_ref, start_row, q_block, k_block, None, half, lanes), e, 0.0)
        sum_ref[...] += jnp.sum(e, axis=0, keepdims=True)
        acc_ref[...] += nn(vt_ref[kb], e.astype(BF16))

    def step(kb, carry):
        flag = meta_ref[1 + blocks + total + q_pos * total + kb]

        @pl.when(flag == 1)
        def _():
            add(kb, False)

        @pl.when(flag == 2)
        def _():
            add(kb, True)

        return carry

    lax.fori_loop(0, total, step, 0)
    out = acc_ref[...] / sum_ref[...]
    ot_ref[0] = out
    l_ref[0] = sum_ref[...]
    rows = out.T
    for h in range(heads):
        for c in range(2):
            at = (h * 2 + c) * half
            o_ref[c, 0, :, h * width : (h + 1) * width] = rows[at : at + half].astype(BF16)


def attend_back_kernel(
    meta_ref, q_ref, do_ref, k_ref, v_ref, start_ref, ot_ref, l_ref, dq_ref, dk_ref, dv_ref, kt_ref, acc_ref, *, factor, scaling, heads
):
    q_pos = pl.program_id(0)
    parts, _, blocks, half, width = k_ref.shape
    lanes = heads * 2 * half

    @pl.when(q_pos == 0)
    def _():
        dk_ref[...] = jnp.zeros_like(dk_ref)
        dv_ref[...] = jnp.zeros_like(dv_ref)
        for part in range(parts):
            for block in range(blocks):
                kt_ref[part * blocks + block] = key_rows(k_ref, part, block).T

    q_rows = stacked(q_ref, heads, width)
    do_rows = stacked(do_ref, heads, width)
    delta = jnp.sum(do_rows.astype(F32).T * ot_ref[0], axis=0, keepdims=True)
    inverse = 1.0 / l_ref[0]
    acc_ref[...] = jnp.zeros_like(acc_ref)
    start_row = start_ref[0]
    q_block = meta_ref[1 + q_pos]
    total = parts * blocks

    def add(kb, masked):
        part, block = kb // blocks, kb % blocks
        e = jnp.exp2(nt(key_rows(k_ref, part, block), q_rows) * factor)
        if masked:
            k_block = meta_ref[1 + blocks + kb]
            e = jnp.where(allowed_mask(meta_ref, start_row, q_block, k_block, None, half, lanes), e, 0.0)
        p = e * inverse
        dp = nt(key_rows(v_ref, part, block), do_rows)
        ds = (p * (dp - delta)).astype(BF16)
        dv = nn(p.astype(BF16), do_rows)
        dk = nn(ds, q_rows) * scaling
        for c in range(2):
            dv_ref[part, c, block] += dv[c * half : (c + 1) * half]
            dk_ref[part, c, block] += dk[c * half : (c + 1) * half]
        acc_ref[...] += nn(kt_ref[kb], ds)

    def step(kb, carry):
        flag = meta_ref[1 + blocks + total + q_pos * total + kb]

        @pl.when(flag == 1)
        def _():
            add(kb, False)

        @pl.when(flag == 2)
        def _():
            add(kb, True)

        return carry

    lax.fori_loop(0, total, step, 0)
    rows = acc_ref[...].T * scaling
    for h in range(heads):
        for c in range(2):
            at = (h * 2 + c) * half
            dq_ref[c, 0, :, h * width : (h + 1) * width] = rows[at : at + half]


def attend(meta, q, k, v, start, scaling):
    _, blocks, half, columns = q.shape
    parts, width = k.shape[0], k.shape[-1]
    heads = columns // width
    lanes = heads * 2 * half
    total = parts * blocks
    row_spec = pl.BlockSpec((2, 1, half, columns), lambda i: (0, i, 0, 0))
    key_spec = pl.BlockSpec(k.shape, lambda i: (0, 0, 0, 0, 0))
    lane_spec = pl.BlockSpec((1, 1, lanes), lambda i: (i, 0, 0))
    return pl.pallas_call(
        functools.partial(attend_kernel, factor=scaling * LOG2E, heads=heads),
        grid=(blocks,),
        in_specs=[pl.BlockSpec(memory_space=pltpu.SMEM), row_spec, key_spec, key_spec, lane_spec],
        out_specs=[row_spec, pl.BlockSpec((1, width, lanes), lambda i: (i, 0, 0)), lane_spec],
        out_shape=[
            jax.ShapeDtypeStruct(q.shape, BF16),
            jax.ShapeDtypeStruct((blocks, width, lanes), F32),
            jax.ShapeDtypeStruct((blocks, 1, lanes), F32),
        ],
        scratch_shapes=[
            pltpu.VMEM((total, width, 2 * half), BF16),
            pltpu.VMEM((width, lanes), F32),
            pltpu.VMEM((1, lanes), F32),
        ],
        compiler_params=pltpu.CompilerParams(vmem_limit_bytes=40 * 1024 * 1024),
        cost_estimate=pl.CostEstimate(
            flops=2 * 2 * lanes * 2 * half * width * blocks * total,
            bytes_accessed=8 * q.size + 8 * k.size,
            transcendentals=lanes * 2 * half * blocks * total,
        ),
    )(meta, q, k, v, start)


def attend_back(meta, q, do, k, v, start, out_t, total_e, scaling):
    _, blocks, half, columns = q.shape
    parts, width = k.shape[0], k.shape[-1]
    heads = columns // width
    lanes = heads * 2 * half
    total = parts * blocks
    row_spec = pl.BlockSpec((2, 1, half, columns), lambda i: (0, i, 0, 0))
    key_spec = pl.BlockSpec(k.shape, lambda i: (0, 0, 0, 0, 0))
    lane_spec = pl.BlockSpec((1, 1, lanes), lambda i: (i, 0, 0))
    return pl.pallas_call(
        functools.partial(attend_back_kernel, factor=scaling * LOG2E, scaling=scaling, heads=heads),
        grid=(blocks,),
        in_specs=[
            pl.BlockSpec(memory_space=pltpu.SMEM),
            row_spec,
            row_spec,
            key_spec,
            key_spec,
            lane_spec,
            pl.BlockSpec((1, width, lanes), lambda i: (i, 0, 0)),
            lane_spec,
        ],
        out_specs=[row_spec, key_spec, key_spec],
        out_shape=[
            jax.ShapeDtypeStruct(q.shape, F32),
            jax.ShapeDtypeStruct(k.shape, F32),
            jax.ShapeDtypeStruct(k.shape, F32),
        ],
        scratch_shapes=[
            pltpu.VMEM((total, width, 2 * half), BF16),
            pltpu.VMEM((width, lanes), F32),
        ],
        compiler_params=pltpu.CompilerParams(vmem_limit_bytes=48 * 1024 * 1024),
        cost_estimate=pl.CostEstimate(
            flops=5 * 2 * lanes * 2 * half * width * blocks * total,
            bytes_accessed=12 * q.size + 16 * k.size,
            transcendentals=lanes * 2 * half * blocks * total,
        ),
    )(meta, q, do, k, v, start, out_t, total_e)


TINY_COST = pl.CostEstimate(flops=0, bytes_accessed=0, transcendentals=0)


def remote(src, dst, send, recv, target):
    copy = pltpu.make_async_remote_copy(
        src_ref=src, dst_ref=dst, send_sem=send, recv_sem=recv, device_id=target, device_id_type=pl.DeviceIdType.MESH
    )
    copy.start()
    return copy


class Plan:
    def __init__(self):
        self.inputs, self.shapes, self.aliases, self.jobs = [], [], {}, []

    def read(self, array):
        self.inputs.append(array)
        return ("in", len(self.inputs) - 1)

    def fresh(self, shape, dtype):
        self.shapes.append(jax.ShapeDtypeStruct(shape, dtype))
        return ("out", len(self.shapes) - 1)

    def through(self, array):
        self.inputs.append(array)
        self.aliases[len(self.inputs) - 1] = len(self.shapes)
        return self.fresh(array.shape, array.dtype)

    def copy(self, src, dst, mask, after=None, point=0):
        self.jobs.append((src, dst, mask, after, point))
        return len(self.jobs) - 1


def run(plan, main, collective_id):
    inputs, in_specs, out_shapes, out_specs, scratch, body = main
    n_in, n_out = len(inputs), len(out_shapes)
    m_in, m_out = len(plan.inputs), len(plan.shapes)
    jobs = plan.jobs
    masks = sorted({job[2] for job in jobs if job[2]} - {1 << TENSOR_BIT})
    any_spec = pl.BlockSpec(memory_space=pl.ANY)

    def kernel(*refs):
        main_in, refs = refs[:n_in], refs[n_in:]
        plan_in, refs = refs[:m_in], refs[m_in:]
        main_out, refs = refs[:n_out], refs[n_out:]
        plan_out, refs = refs[:m_out], refs[m_out:]
        send, recv, *rest = refs
        blk, head = lax.axis_index("blk"), lax.axis_index("head")
        core, near, across = (blk, head ^ 1), (blk, head ^ 2), (blk ^ (1 << TENSOR_BIT), head)
        barrier = pltpu.get_barrier_semaphore()
        partners = [core, near, across, *[(blk ^ m, head) for m in masks]]
        for target in partners:
            pl.semaphore_signal(barrier, inc=1, device_id=target, device_id_type=pl.DeviceIdType.MESH)
        pl.semaphore_wait(barrier, len(partners))
        started, arrived = {}, set()

        def arrive(i):
            if i not in arrived:
                arrived.add(i)
                (started[i].wait_recv if jobs[i][2] else started[i].wait)()

        def part(side):
            (kind, index), cut = side
            return cut((plan_in if kind == "in" else plan_out)[index])

        def issue(point):
            for i, (src, dst, mask, after, at) in enumerate(jobs):
                if i in started or (at != point and point is not None):
                    continue
                if after is not None:
                    arrive(after)
                if mask:
                    started[i] = remote(part(src), part(dst), send.at[i], recv.at[i], (blk ^ mask, head))
                else:
                    started[i] = pltpu.make_async_copy(part(src), part(dst), recv.at[i])
                    started[i].start()

        point = 0
        for _ in body((core, near, across), main_in, main_out, rest):
            issue(point)
            point += 1
        issue(None)
        for i in range(len(jobs)):
            arrive(i)
            if jobs[i][2]:
                started[i].wait_send()

    results = pl.pallas_call(
        kernel,
        out_shape=[*out_shapes, *plan.shapes],
        in_specs=[*in_specs, *[any_spec] * m_in],
        out_specs=[*out_specs, *[any_spec] * m_out],
        scratch_shapes=[
            pltpu.SemaphoreType.DMA((max(1, len(jobs)),)),
            pltpu.SemaphoreType.DMA((max(1, len(jobs)),)),
            *scratch,
        ],
        input_output_aliases={n_in + i: n_out + o for i, o in plan.aliases.items()},
        compiler_params=pltpu.CompilerParams(
            collective_id=collective_id, has_side_effects=True, vmem_limit_bytes=32 * 1024 * 1024
        ),
        cost_estimate=TINY_COST,
    )(*inputs, *plan.inputs)
    return results[:n_out], results[n_out:]


def spread_main(flat, chunk):
    rows, width = flat.shape[0] // 2, flat.shape[1]
    pieces = width // chunk

    def body(partners, ins, outs, scratch):
        core, near, across = partners
        (s_ref,), (o_ref,), (local_sem, send, recv) = ins, outs, scratch
        first = remote(s_ref, o_ref.at[0, :, 0, 1], send.at[0], recv.at[0], near)
        second = [
            remote(
                s_ref.at[:, :, pl.ds(i * chunk, chunk)],
                o_ref.at[0, :, 1, 0, :, pl.ds((i ^ 1) * chunk, chunk)],
                send.at[6 + i],
                recv.at[6 + i],
                across,
            )
            for i in range(pieces)
        ]
        third = remote(s_ref, o_ref.at[1, :, 0, 0], send.at[1], recv.at[1], core)
        own = pltpu.make_async_copy(s_ref, o_ref.at[0, :, 0, 0], local_sem)
        own.start()
        yield
        for copy in second:
            copy.wait_recv()
        fourth = remote(o_ref.at[0, :, 1, 0], o_ref.at[0, :, 1, 1], send.at[2], recv.at[2], near)
        fifth = remote(o_ref.at[0, :, 1, 0], o_ref.at[1, :, 1, 0], send.at[3], recv.at[3], core)
        yield
        first.wait_recv()
        sixth = remote(o_ref.at[0, :, 0, 1], o_ref.at[1, :, 0, 1], send.at[4], recv.at[4], core)
        yield
        fourth.wait_recv()
        seventh = remote(o_ref.at[0, :, 1, 1], o_ref.at[1, :, 1, 1], send.at[5], recv.at[5], core)
        yield
        own.wait()
        for copy in (first, *second, third, fourth, fifth, sixth, seventh):
            copy.wait_send()
        for copy in (third, fifth, sixth, seventh):
            copy.wait_recv()

    any_spec = pl.BlockSpec(memory_space=pl.ANY)
    return (
        [flat.reshape(2, rows, width)],
        [any_spec],
        [jax.ShapeDtypeStruct((2, 2, 2, 2, rows, width), flat.dtype)],
        [any_spec],
        [
            pltpu.SemaphoreType.DMA,
            pltpu.SemaphoreType.DMA((6 + pieces,)),
            pltpu.SemaphoreType.DMA((6 + pieces,)),
        ],
        body,
    )


def gather_main(partial, chunk):
    rows, width = partial.shape[0] // 16, partial.shape[1]
    share = (2, rows, width)
    pieces = width // chunk

    def body(partners, ins, outs, scratch):
        core, near, across = partners
        (p_ref,), (o_ref,) = ins, outs
        core_in, out_y, in_y, out_t, in_t, hold, send, recv = scratch
        order = ((1, 1), (0, 1), (1, 0), (0, 0))
        from_core = [
            remote(p_ref.at[1, :, t, y], core_in.at[i], send.at[i], recv.at[i], core) for i, (t, y) in enumerate(order)
        ]
        from_y = []
        for i in range(2):
            t, y = order[i]
            from_core[i].wait_recv()
            out_y[i] = (p_ref[0, :, t, y].astype(F32) + core_in[i].astype(F32)).astype(BF16)
            from_y.append(remote(out_y.at[i], in_y.at[i], send.at[4 + i], recv.at[4 + i], near))
        yield
        from_core[2].wait_recv()
        hold[...] = p_ref[0, :, 1, 0].astype(F32) + core_in[2].astype(F32)
        from_y[0].wait_recv()
        for i in range(pieces):
            a, b = slice(i * chunk, (i + 1) * chunk), slice((i ^ 1) * chunk, ((i ^ 1) + 1) * chunk)
            out_t[:, :, b] = (hold[:, :, a] + in_y[0, :, :, a].astype(F32)).astype(BF16)
        from_t = remote(out_t, in_t, send.at[6], recv.at[6], across)
        yield
        from_core[3].wait_recv()
        hold[...] = p_ref[0, :, 0, 0].astype(F32) + core_in[3].astype(F32)
        from_y[1].wait_recv()
        hold[...] += in_y[1].astype(F32)
        yield
        from_t.wait_recv()
        o_ref[...] = hold[...] + in_t[...].astype(F32)
        for copy in (*from_core, *from_y, from_t):
            copy.wait_send()

    vmem_spec = pl.BlockSpec(memory_space=pltpu.VMEM)
    return (
        [partial.reshape(2, 2, 2, 2, rows, width)],
        [vmem_spec],
        [jax.ShapeDtypeStruct(share, F32)],
        [vmem_spec],
        [
            pltpu.VMEM((4, *share), BF16),
            pltpu.VMEM((2, *share), BF16),
            pltpu.VMEM((2, *share), BF16),
            pltpu.VMEM(share, BF16),
            pltpu.VMEM(share, BF16),
            pltpu.VMEM(share, F32),
            pltpu.SemaphoreType.DMA((7,)),
            pltpu.SemaphoreType.DMA((7,)),
        ],
        body,
    )


def local(
    hidden_in,
    lengths,
    query_weight,
    key_matrix,
    value_matrix,
    out_weight,
    gate_weight,
    up_weight,
    down_weight,
    attn_gain,
    query_gain,
    key_gain,
    mlp_gain,
    cotangent,
):
    ring = lax.axis_size("blk")
    bits = ring.bit_length() - 1
    batch_bit = bits - 1
    extra_bits = [i for i in range(bits) if i not in (TENSOR_BIT, SEQ_BIT, batch_bit)]
    seq_bits = [SEQ_BIT, *extra_bits]
    parts = 1 << len(seq_bits)
    bit_order = [batch_bit, TENSOR_BIT, SEQ_BIT, *extra_bits]
    b_mask, t_mask, x_mask = 1 << batch_bit, 1 << TENSOR_BIT, 1 << SEQ_BIT
    blk, head = lax.axis_index("blk"), lax.axis_index("head")
    batch, tensor = bit_of(blk, batch_bit), bit_of(blk, TENSOR_BIT)

    local_rows, width = hidden_in.shape[1:]
    block_rows = local_rows * lax.axis_size("head")
    half = block_rows // 2
    row_features = width // ring
    head_size = query_gain.shape[0]
    scaling = head_size ** (-0.5)
    tokens = 16 * local_rows
    heads = query_weight.shape[1] // (2 * head_size)
    ff = gate_weight.shape[1] // 2

    def moved(values, place_of):
        axis = values.ndim - 1
        return jnp.concatenate(
            [
                lax.dynamic_slice_in_dim(values, place_of(i) * row_features, row_features, axis)
                for i in range(ring)
            ],
            axis=axis,
        )

    def regroup(values):
        return moved(values, lambda p: blk ^ sum(((p >> i) & 1) << b for i, b in enumerate(bit_order)))

    def ungroup(values):
        return moved(values, lambda n: sum(bit_of(blk ^ n, b) << i for i, b in enumerate(bit_order)))

    def rows_at(p):
        return lambda ref: ref.at[pl.ds(p * row_features, row_features), :]

    def put(plan, weights, buffer, near, far, onward_far=True, point=0):
        here = [plan.read(w) for w in weights]
        at, columns = 0, []
        for w in weights:
            columns.append((at, w.shape[1] // 2))
            at += w.shape[1] // 2

        def half_of(k, other):
            n = columns[k][1]

            def cut(ref):
                place = bit_of(lax.axis_index("blk"), TENSOR_BIT)
                place = 1 - place if other else place
                return ref.at[:, pl.ds(pl.multiple_of(place * n, n), n)]

            return cut

        def into(k, p):
            start, n = columns[k]
            return lambda ref: ref.at[pl.ds(p * row_features, row_features), pl.ds(start, n)]

        def from_here(p, mask):
            ids = [
                plan.copy((here[k], half_of(k, mask & t_mask)), (buffer, into(k, p)), mask, point=point)
                for k in range(len(weights))
            ]
            return ids

        if near:
            by_t = from_here(2, t_mask)
            from_here(4, x_mask)
            from_here(0, 0)
        if far:
            by_b = from_here(1, b_mask)
            by_tb = from_here(3, b_mask | t_mask)
        if near:
            for k, i in enumerate(by_t):
                plan.copy((buffer, into(k, 2)), (buffer, into(k, 6)), x_mask, after=i, point=point + 1)
        if far and onward_far:
            for p, ids in ((1, by_b), (3, by_tb)):
                for k, i in enumerate(ids):
                    plan.copy((buffer, into(k, p)), (buffer, into(k, p + 4)), x_mask, after=i, point=point + 3)

    def put_onward(plan, buffer):
        for p in (1, 3):
            plan.copy((buffer, rows_at(p)), (buffer, rows_at(p + 4)), x_mask)

    def buffer_shape(weights):
        return (8 * row_features, sum(w.shape[1] for w in weights) // 2)

    def whole_weight(buffer):
        pieces = [buffer]
        for b in extra_bits:
            pieces = pieces + [over_blk(c, 1 << b) for c in pieces]
        return jnp.concatenate(pieces, axis=0) if extra_bits else buffer

    def split_grad(grad):
        for b in reversed(extra_bits):
            n = grad.shape[0] // 2
            grad = grad[:n] + over_blk(grad[n:].astype(BF16), 1 << b).astype(F32)
        n = grad.shape[0] // 2
        return grad[:n], grad[n:].astype(BF16)

    def everything(ref):
        return ref

    def fold(plan, away):
        out = plan.fresh(away.shape, away.dtype)
        plan.copy((plan.read(away), everything), (out, everything), x_mask)

    def to_settle(keep, got):
        total = keep + got.astype(F32)
        return total[:row_features], total[row_features:].astype(BF16)

    def settle(plan, away):
        out, here = plan.fresh(away.shape, away.dtype), plan.read(away)
        for i, mask in enumerate((b_mask, t_mask, b_mask | t_mask)):
            plan.copy((here, rows_at(i)), (out, rows_at(i)), mask)

    def settle_apart(away):
        cut = [away[i * row_features : (i + 1) * row_features] for i in range(3)]
        return jnp.concatenate(
            [over_blk(c, mask) for c, mask in zip(cut, (b_mask, t_mask, b_mask | t_mask))], axis=0
        )

    def settled(own, got, column_widths):
        f = row_features
        own = own + got[:f].astype(F32)
        other = got[f : 2 * f].astype(F32) + got[2 * f :].astype(F32)
        results, at = [], 0
        for w in column_widths:
            results.append(in_order(tensor, own[:, at : at + w], other[:, at : at + w], 1))
            at += w
        return results

    chunk = 2 * row_features
    ids = iter(range(100))

    def spread(flat, plan):
        (out,), rest = run(plan, spread_main(flat, chunk), next(ids))
        return out.reshape(tokens, width), rest

    def gather_sum(partial, plan):
        (out,), rest = run(plan, gather_main(partial, chunk), next(ids))
        return out.reshape(2 * local_rows, width), rest

    def partial_sum(left, weight):
        return nt(left, weight).astype(BF16)

    def take_batch(rows):
        mine = lax.dynamic_index_in_dim(rows, batch, 0, keepdims=False)
        theirs = lax.dynamic_index_in_dim(rows, 1 - batch, 0, keepdims=False)
        return regroup(jnp.concatenate([mine, over_blk(theirs, b_mask)], axis=0))

    def give_batch(rows):
        rows = ungroup(rows)
        back = over_blk(rows[local_rows:].astype(BF16), b_mask).astype(rows.dtype)
        return in_order(batch, rows[None, :local_rows], back[None], 0)

    length_row = lax.dynamic_index_in_dim(lengths, batch, 0, keepdims=False)
    doc_ends = jnp.cumsum(length_row)
    batch_flip = jnp.arange(2, dtype=jnp.int32)[:, None] << batch_bit
    tensor_flip = jnp.arange(2, dtype=jnp.int32)[None, :] << TENSOR_BIT
    q_blocks = (blk ^ batch_flip ^ tensor_flip).reshape(4)
    index = jnp.arange(2 * half, dtype=jnp.int32)
    in_block = token_offset(head, index, local_rows).reshape(2, 1, half)
    token_index = q_blocks[None, :, None] * block_rows + in_block
    passed = doc_ends <= token_index[..., None]
    doc_start = jnp.max(jnp.where(passed, doc_ends, 0), axis=-1).astype(jnp.int32)
    position = (token_index - doc_start).reshape(tokens)
    start_lanes = jnp.tile(jnp.transpose(doc_start, (1, 0, 2)).reshape(4, 1, 2 * half), (1, 1, heads))
    k_blocks = q_blocks
    for b in seq_bits:
        k_blocks = jnp.concatenate([k_blocks, k_blocks ^ (1 << b)])
    least_start = jnp.min(doc_start, axis=(0, 2))[:, None]
    last_start = jnp.max(doc_start, axis=(0, 2))[:, None]
    k_first = (k_blocks * block_rows)[None, :]
    none = (k_blocks[None, :] > q_blocks[:, None]) | (k_first + block_rows <= least_start)
    whole = (k_blocks[None, :] < q_blocks[:, None]) & (k_first >= last_start)
    flags = jnp.where(none, 0, jnp.where(whole, 1, 2))
    meta = jnp.concatenate([head[None], q_blocks, k_blocks, flags.reshape(-1)]).astype(jnp.int32)

    inverse_freq = THETA ** (-jnp.arange(head_size // 2, dtype=F32) / (head_size // 2))
    angles = position.astype(F32)[:, None] * inverse_freq[None, :]
    cosine = jnp.cos(angles)[:, None, :]
    sine = jnp.sin(angles)[:, None, :]

    def rope(values):
        a, b = values[..., : head_size // 2], values[..., head_size // 2 :]
        return jnp.concatenate([a * cosine - b * sine, b * cosine + a * sine], axis=-1)

    def rope_back(values):
        a, b = values[..., : head_size // 2], values[..., head_size // 2 :]
        return jnp.concatenate([a * cosine + b * sine, b * cosine - a * sine], axis=-1)

    def rms(values):
        return lax.rsqrt(jnp.mean(values * values, axis=-1, keepdims=True) + EPS)

    def norm_back(grad, normed, inverse, gain):
        scaled = grad * gain
        return inverse * (scaled - normed * jnp.mean(scaled * normed, axis=-1, keepdims=True))

    gain_a = regroup(attn_gain.astype(F32))
    gain_m = regroup(mlp_gain.astype(F32))
    gain_q = query_gain.astype(F32)
    gain_k = key_gain.astype(F32)

    a_weights, o_weights = (query_weight, key_matrix, value_matrix), (out_weight,)
    x_low = take_batch(hidden_in)
    rows_in = x_low.astype(F32)
    inverse_a = rms(rows_in)
    normal_a = rows_in * inverse_a

    plan = Plan()
    a_buffer = plan.fresh(buffer_shape(a_weights), BF16)
    put(plan, a_weights, a_buffer, True, True)
    here, cot_out = plan.read(cotangent), plan.fresh((2, local_rows, width), BF16)
    plan.copy((here, lambda ref: ref.at[bit_of(lax.axis_index("blk"), batch_bit)]), (cot_out, lambda ref: ref.at[0]), 0)
    plan.copy(
        (here, lambda ref: ref.at[1 - bit_of(lax.axis_index("blk"), batch_bit)]), (cot_out, lambda ref: ref.at[1]), b_mask
    )
    put(plan, (down_weight,), plan.fresh(buffer_shape((down_weight,)), BF16), True, False)
    xa, (w_qkv, cot, w_down) = spread((normal_a * gain_a).astype(BF16), plan)
    w_qkv = whole_weight(w_qkv)
    cot = regroup(cot.reshape(2 * local_rows, width))

    (xa, up_in) = pin((xa, up_weight))
    up_half = lax.dynamic_slice_in_dim(up_in, tensor * ff, ff, 1)
    up_other = lax.dynamic_slice_in_dim(up_in, (1 - tensor) * ff, ff, 1)
    up_b, up_tb = over_blk(up_half, b_mask), over_blk(up_other, b_mask | t_mask)

    qkv = nn(xa, w_qkv)
    q_columns, k_columns = heads * head_size, head_size
    q_raw = qkv[:, :q_columns].reshape(tokens, heads, head_size)
    k_raw = qkv[:, q_columns : q_columns + k_columns].reshape(tokens, 1, head_size)
    value = qkv[:, q_columns + k_columns :].astype(BF16)
    q_inverse, k_inverse = rms(q_raw), rms(k_raw)
    q_normal, k_normal = q_raw * q_inverse, k_raw * k_inverse
    query = rope(q_normal * gain_q).astype(BF16).reshape(2, 4, half, q_columns)
    key = rope(k_normal * gain_k).astype(BF16).reshape(tokens, head_size)
    key_value = jnp.concatenate([key, value], axis=1)

    plan = Plan()
    put(plan, o_weights, plan.fresh(buffer_shape(o_weights), BF16), True, True)
    kv_out = plan.fresh(key_value.shape, BF16)
    plan.copy((plan.read(key_value), everything), (kv_out, everything), x_mask)
    put(plan, (down_weight,), plan.through(w_down), False, True, onward_far=False)
    put(plan, (gate_weight,), plan.fresh(buffer_shape((gate_weight,)), BF16), True, False)
    cot_all, (w_out, kv_x, w_down, w_gate) = spread(cot, plan)
    w_out = whole_weight(w_out)
    key_value = [key_value, kv_x]
    for b in extra_bits:
        key_value = key_value + [over_blk(c, 1 << b) for c in key_value]
    key_value = jnp.stack(key_value)
    keys = key_value[..., :head_size].reshape(parts, 2, 4, half, head_size)
    values = key_value[..., head_size:].reshape(parts, 2, 4, half, head_size)
    attn, attn_t, total_e = attend(meta, query, keys, values, start_lanes, scaling)
    attn = attn.reshape(tokens, q_columns)

    plan = Plan()
    put_onward(plan, plan.through(w_down))
    put(plan, (gate_weight,), plan.through(w_gate), False, True, onward_far=False)
    put(plan, (up_weight,), plan.fresh(buffer_shape((up_weight,)), BF16), True, False)
    out_sum, (w_down, w_gate, w_up) = gather_sum(partial_sum(attn, w_out), plan)
    w_down = whole_weight(w_down)
    middle = x_low.astype(F32) + out_sum
    inverse_m = rms(middle)
    normal_m = middle * inverse_m

    plan = Plan()
    put_onward(plan, plan.through(w_gate))
    u_buffer = plan.through(w_up)
    for p, got in ((1, up_b), (3, up_tb)):
        here = plan.read(got)
        plan.copy((here, everything), (u_buffer, rows_at(p + 4)), x_mask)
        plan.copy((here, everything), (u_buffer, rows_at(p)), 0)
    xm, (w_gate, w_up) = spread((normal_m * gain_m).astype(BF16), plan)
    w_gate, w_up = whole_weight(w_gate), whole_weight(w_up)
    d_active = nn(cot_all, w_down)
    gate = nn(xm, w_gate)
    up = nn(xm, w_up)
    sig = jax.nn.sigmoid(gate)
    silu = gate * sig
    active = (silu * up).astype(BF16)
    d_gate = (d_active * up * sig * (1.0 + gate * (1.0 - sig))).astype(BF16)
    d_up = (d_active * silu).astype(BF16)

    keep_down, away_down = split_grad(tn(cot_all, active))
    plan = Plan()
    fold(plan, away_down)
    d_xm, (got,) = gather_sum((nt(d_gate, w_gate) + nt(d_up, w_up)).astype(BF16), plan)
    own_down, away_down = to_settle(keep_down, got)
    keep_gate, away_gate = split_grad(tn(xm, d_gate))
    d_middle = cot.astype(F32) + norm_back(d_xm, normal_m, inverse_m, gain_m)

    plan = Plan()
    settle(plan, away_down)
    fold(plan, away_gate)
    d_mid_all, (got_down, got) = spread(d_middle.astype(BF16), plan)
    (g_down,) = settled(own_down, got_down, (ff,))
    own_gate, away_gate = to_settle(keep_gate, got)
    keep_up, away_up = split_grad(tn(xm, d_up))
    keep_out, away_out = split_grad(tn(d_mid_all, attn))
    d_attn = nn(d_mid_all, w_out).astype(BF16).reshape(2, 4, half, q_columns)
    d_query, d_key, d_value = attend_back(
        meta, query, d_attn, keys, values, start_lanes, attn_t, total_e, scaling
    )
    d_key_value = jnp.concatenate(
        [d_key.reshape(parts, tokens, head_size), d_value.reshape(parts, tokens, head_size)], axis=-1
    )
    for b in reversed(extra_bits):
        n = d_key_value.shape[0] // 2
        d_key_value = d_key_value[:n] + over_blk(d_key_value[n:].astype(BF16), 1 << b).astype(F32)

    plan = Plan()
    fold(plan, d_key_value[1].astype(BF16))
    fold(plan, away_up)
    settle(plan, away_gate)
    mixed_sum, (got_kv, got, got_gate) = gather_sum(partial_sum(active, w_down), plan)
    (g_gate,) = settled(own_gate, got_gate, (ff,))
    own_up, away_up = to_settle(keep_up, got)
    mixed = give_batch((middle + mixed_sum).astype(BF16))
    d_key_value = d_key_value[0] + got_kv.astype(F32)
    d_key, d_value = d_key_value[:, :head_size], d_key_value[:, head_size:]
    dq_turned = rope_back(d_query.reshape(tokens, heads, head_size))
    dk_turned = rope_back(d_key.reshape(tokens, 1, head_size))
    gain_q_grad = jnp.sum(dq_turned * q_normal, axis=(0, 1))
    gain_k_grad = jnp.sum(dk_turned * k_normal, axis=(0, 1))
    dq_raw = norm_back(dq_turned, q_normal, q_inverse, gain_q).reshape(tokens, q_columns)
    dk_raw = norm_back(dk_turned, k_normal, k_inverse, gain_k).reshape(tokens, k_columns)
    d_qkv = jnp.concatenate([dq_raw, dk_raw, d_value], axis=1).astype(BF16)
    keep_qkv, away_qkv = split_grad(tn(xa, d_qkv))

    plan = Plan()
    settle(plan, away_up)
    fold(plan, away_qkv)
    fold(plan, away_out)
    d_xa, (got_up, got, got_o) = gather_sum(partial_sum(d_qkv, w_qkv), plan)
    (g_up,) = settled(own_up, got_up, (ff,))
    own_qkv, away_qkv = to_settle(keep_qkv, got)
    own_out, away_out = to_settle(keep_out, got_o)
    got = settle_apart(jnp.concatenate([away_qkv, away_out], axis=1))
    own = jnp.concatenate([own_qkv, own_out], axis=1)
    g_query, g_key, g_value, g_out = settled(own, got, (q_columns, k_columns, k_columns, q_columns))
    input_grad = give_batch(d_middle + norm_back(d_xa, normal_a, inverse_a, gain_a))
    sums = jnp.concatenate(
        [
            ungroup(jnp.sum(d_xa * normal_a, axis=0)),
            gain_q_grad,
            gain_k_grad,
            ungroup(jnp.sum(d_xm * normal_m, axis=0)),
        ]
    )
    for b in range(2):
        sums = sums + over_head(sums, 1 << b)
    for b in range(bits):
        sums = sums + over_blk(sums, 1 << b)
    at = [width, width + head_size, width + 2 * head_size]
    gains = jnp.split(sums, at)
    return (
        mixed,
        input_grad,
        g_query,
        g_key,
        g_value,
        g_out,
        g_gate,
        g_up,
        g_down,
        *gains,
    )


def solution(mesh):
    rows = P(None, ("blk", "head"), None)
    weight = P("blk", "head")
    return jax.shard_map(
        local,
        mesh=mesh,
        in_specs=(rows, P(), *([weight] * 7), P(), P(), P(), P(), rows),
        out_specs=(rows, rows, *([weight] * 7), P(), P(), P(), P()),
        check_vma=False,
    )
```

```python
import functools

import jax
import jax.numpy as jnp
from jax import lax
from jax.experimental import pallas as pl
from jax.experimental.pallas import tpu as pltpu
from jax.sharding import PartitionSpec as P

EPS = 1e-06
THETA = 1000000.0
LOG2E = 1.4426950408889634
F32 = jnp.float32
BF16 = jnp.bfloat16

MIB = 1024 * 1024
TINY_COST = pl.CostEstimate(flops=0, bytes_accessed=0, transcendentals=0)
VMEM_LIMIT = 32 * MIB
TENSOR_BIT = 1
SEQ_BIT = 0


def nt(a, b):
    return lax.dot_general(a, b, (((1,), (1,)), ((), ())), preferred_element_type=F32)


def tn(a, b):
    return lax.dot_general(a, b, (((0,), (0,)), ((), ())), preferred_element_type=F32)


def nn(a, b):
    return jnp.dot(a, b, preferred_element_type=F32)


def bit_of(value, bit):
    return (value >> bit) & 1


def over_blk(value, mask):
    count = lax.axis_size("blk")
    return lax.ppermute(value, "blk", [(i, i ^ mask) for i in range(count)])


def over_head(value, mask):
    count = lax.axis_size("head")
    return lax.ppermute(value, "head", [(i, i ^ mask) for i in range(count)])


def pin(values):
    return lax.optimization_barrier(values)


def in_order(flag, own, other, axis):
    return jnp.where(
        flag == 0,
        jnp.concatenate([own, other], axis=axis),
        jnp.concatenate([other, own], axis=axis),
    )


def token_offset(head_place, index, sub):
    core, upper, inner = index // (2 * sub), (index // sub) % 2, index % sub
    return (head_place ^ (upper * 2) ^ core) * sub + inner


def allowed_mask(meta_ref, start_row, q_block, k_block, rows, half, q_lanes):
    sub = half // 2
    head_place = meta_ref[0]
    k_index = lax.broadcasted_iota(jnp.int32, (2 * half, 1), 0)
    k_token = token_offset(head_place, k_index, sub) + k_block * (2 * half)
    q_index = lax.broadcasted_iota(jnp.int32, (1, q_lanes), 1) % (2 * half)
    q_token = token_offset(head_place, q_index, sub) + q_block * (2 * half)
    return (k_token <= q_token) & (k_token >= start_row)


def stacked(ref, heads, width):
    return jnp.concatenate(
        [ref[c, 0, :, h * width : (h + 1) * width] for h in range(heads) for c in range(2)], axis=0
    )


def key_rows(ref, part, block):
    return jnp.concatenate([ref[part, 0, block], ref[part, 1, block]], axis=0)


def attend_kernel(meta_ref, q_ref, k_ref, v_ref, start_ref, o_ref, ot_ref, l_ref, vt_ref, acc_ref, sum_ref, *, factor, heads):
    q_pos = pl.program_id(0)
    parts, _, blocks, half, width = k_ref.shape
    lanes = heads * 2 * half

    @pl.when(q_pos == 0)
    def _():
        for part in range(parts):
            for block in range(blocks):
                vt_ref[part * blocks + block] = key_rows(v_ref, part, block).T

    q_rows = stacked(q_ref, heads, width)
    acc_ref[...] = jnp.zeros_like(acc_ref)
    sum_ref[...] = jnp.zeros_like(sum_ref)
    start_row = start_ref[0]
    q_block = meta_ref[1 + q_pos]
    total = parts * blocks

    def add(kb, masked):
        e = jnp.exp2(nt(key_rows(k_ref, kb // blocks, kb % blocks), q_rows) * factor)
        if masked:
            k_block = meta_ref[1 + blocks + kb]
            e = jnp.where(allowed_mask(meta_ref, start_row, q_block, k_block, None, half, lanes), e, 0.0)
        sum_ref[...] += jnp.sum(e, axis=0, keepdims=True)
        acc_ref[...] += nn(vt_ref[kb], e.astype(BF16))

    def step(kb, carry):
        flag = meta_ref[1 + blocks + total + q_pos * total + kb]

        @pl.when(flag == 1)
        def _():
            add(kb, False)

        @pl.when(flag == 2)
        def _():
            add(kb, True)

        return carry

    lax.fori_loop(0, total, step, 0)
    out = acc_ref[...] / sum_ref[...]
    ot_ref[0] = out
    l_ref[0] = sum_ref[...]
    rows = out.T
    for h in range(heads):
        for c in range(2):
            at = (h * 2 + c) * half
            o_ref[c, 0, :, h * width : (h + 1) * width] = rows[at : at + half].astype(BF16)


def attend_back_kernel(
    meta_ref, q_ref, do_ref, k_ref, v_ref, start_ref, ot_ref, l_ref, dq_ref, dk_ref, dv_ref, kt_ref, acc_ref, *, factor, scaling, heads
):
    q_pos = pl.program_id(0)
    parts, _, blocks, half, width = k_ref.shape
    lanes = heads * 2 * half

    @pl.when(q_pos == 0)
    def _():
        dk_ref[...] = jnp.zeros_like(dk_ref)
        dv_ref[...] = jnp.zeros_like(dv_ref)
        for part in range(parts):
            for block in range(blocks):
                kt_ref[part * blocks + block] = key_rows(k_ref, part, block).T

    q_rows = stacked(q_ref, heads, width)
    do_rows = stacked(do_ref, heads, width)
    delta = jnp.sum(do_rows.astype(F32).T * ot_ref[0], axis=0, keepdims=True)
    inverse = 1.0 / l_ref[0]
    acc_ref[...] = jnp.zeros_like(acc_ref)
    start_row = start_ref[0]
    q_block = meta_ref[1 + q_pos]
    total = parts * blocks

    def add(kb, masked):
        part, block = kb // blocks, kb % blocks
        e = jnp.exp2(nt(key_rows(k_ref, part, block), q_rows) * factor)
        if masked:
            k_block = meta_ref[1 + blocks + kb]
            e = jnp.where(allowed_mask(meta_ref, start_row, q_block, k_block, None, half, lanes), e, 0.0)
        p = e * inverse
        dp = nt(key_rows(v_ref, part, block), do_rows)
        ds = (p * (dp - delta)).astype(BF16)
        dv = nn(p.astype(BF16), do_rows)
        dk = nn(ds, q_rows) * scaling
        for c in range(2):
            dv_ref[part, c, block] += dv[c * half : (c + 1) * half]
            dk_ref[part, c, block] += dk[c * half : (c + 1) * half]
        acc_ref[...] += nn(kt_ref[kb], ds)

    def step(kb, carry):
        flag = meta_ref[1 + blocks + total + q_pos * total + kb]

        @pl.when(flag == 1)
        def _():
            add(kb, False)

        @pl.when(flag == 2)
        def _():
            add(kb, True)

        return carry

    lax.fori_loop(0, total, step, 0)
    rows = acc_ref[...].T * scaling
    for h in range(heads):
        for c in range(2):
            at = (h * 2 + c) * half
            dq_ref[c, 0, :, h * width : (h + 1) * width] = rows[at : at + half]


def attend(meta, q, k, v, start, scaling):
    _, blocks, half, columns = q.shape
    parts, width = k.shape[0], k.shape[-1]
    heads = columns // width
    lanes = heads * 2 * half
    total = parts * blocks
    row_spec = pl.BlockSpec((2, 1, half, columns), lambda i: (0, i, 0, 0))
    key_spec = pl.BlockSpec(k.shape, lambda i: (0, 0, 0, 0, 0))
    lane_spec = pl.BlockSpec((1, 1, lanes), lambda i: (i, 0, 0))
    return pl.pallas_call(
        functools.partial(attend_kernel, factor=scaling * LOG2E, heads=heads),
        grid=(blocks,),
        in_specs=[pl.BlockSpec(memory_space=pltpu.SMEM), row_spec, key_spec, key_spec, lane_spec],
        out_specs=[row_spec, pl.BlockSpec((1, width, lanes), lambda i: (i, 0, 0)), lane_spec],
        out_shape=[
            jax.ShapeDtypeStruct(q.shape, BF16),
            jax.ShapeDtypeStruct((blocks, width, lanes), F32),
            jax.ShapeDtypeStruct((blocks, 1, lanes), F32),
        ],
        scratch_shapes=[
            pltpu.VMEM((total, width, 2 * half), BF16),
            pltpu.VMEM((width, lanes), F32),
            pltpu.VMEM((1, lanes), F32),
        ],
        compiler_params=pltpu.CompilerParams(vmem_limit_bytes=VMEM_LIMIT),
        cost_estimate=pl.CostEstimate(
            flops=2 * 2 * lanes * 2 * half * width * blocks * total,
            bytes_accessed=8 * q.size + 8 * k.size,
            transcendentals=lanes * 2 * half * blocks * total,
        ),
    )(meta, q, k, v, start)


def attend_back(meta, q, do, k, v, start, out_t, total_e, scaling):
    _, blocks, half, columns = q.shape
    parts, width = k.shape[0], k.shape[-1]
    heads = columns // width
    lanes = heads * 2 * half
    total = parts * blocks
    row_spec = pl.BlockSpec((2, 1, half, columns), lambda i: (0, i, 0, 0))
    key_spec = pl.BlockSpec(k.shape, lambda i: (0, 0, 0, 0, 0))
    lane_spec = pl.BlockSpec((1, 1, lanes), lambda i: (i, 0, 0))
    return pl.pallas_call(
        functools.partial(attend_back_kernel, factor=scaling * LOG2E, scaling=scaling, heads=heads),
        grid=(blocks,),
        in_specs=[
            pl.BlockSpec(memory_space=pltpu.SMEM),
            row_spec,
            row_spec,
            key_spec,
            key_spec,
            lane_spec,
            pl.BlockSpec((1, width, lanes), lambda i: (i, 0, 0)),
            lane_spec,
        ],
        out_specs=[row_spec, key_spec, key_spec],
        out_shape=[
            jax.ShapeDtypeStruct(q.shape, F32),
            jax.ShapeDtypeStruct(k.shape, F32),
            jax.ShapeDtypeStruct(k.shape, F32),
        ],
        scratch_shapes=[
            pltpu.VMEM((total, width, 2 * half), BF16),
            pltpu.VMEM((width, lanes), F32),
        ],
        compiler_params=pltpu.CompilerParams(vmem_limit_bytes=VMEM_LIMIT),
        cost_estimate=pl.CostEstimate(
            flops=5 * 2 * lanes * 2 * half * width * blocks * total,
            bytes_accessed=12 * q.size + 16 * k.size,
            transcendentals=lanes * 2 * half * blocks * total,
        ),
    )(meta, q, do, k, v, start, out_t, total_e)


def prepare_kernel(x_ref, w_ref, cos_ref, sin_ref, gq_ref, gk_ref, q_ref, kv_ref, raw_ref, *, heads, width):
    acc = jnp.dot(x_ref[...], w_ref[...], preferred_element_type=F32)
    raw_ref[...] = acc[:, : (heads + 1) * width]
    for h in range(heads + 1):
        part = acc[:, h * width : (h + 1) * width]
        normed = part * lax.rsqrt(jnp.mean(part * part, axis=-1, keepdims=True) + EPS)
        scaled = normed * (gq_ref if h < heads else gk_ref)[...]
        turned = (scaled * cos_ref[...] + pltpu.roll(scaled, width // 2, 1) * sin_ref[...]).astype(BF16)
        if h < heads:
            q_ref[:, h * width : (h + 1) * width] = turned
        else:
            kv_ref[:, :width] = turned
    kv_ref[:, width:] = acc[:, (heads + 1) * width :].astype(BF16)


def prepare(x, w, cos, sin, gain_q, gain_k, heads):
    tokens, depth = x.shape
    width, tile = gain_q.shape[1], 256
    row = lambda n: pl.BlockSpec((tile, n), lambda i: (i, 0))
    fixed = lambda a: pl.BlockSpec(a.shape, lambda i: (0, 0))
    return pl.pallas_call(
        functools.partial(prepare_kernel, heads=heads, width=width),
        grid=(tokens // tile,),
        in_specs=[row(depth), fixed(w), row(width), row(width), fixed(gain_q), fixed(gain_k)],
        out_specs=[row(heads * width), row(2 * width), row((heads + 1) * width)],
        out_shape=[
            jax.ShapeDtypeStruct((tokens, heads * width), BF16),
            jax.ShapeDtypeStruct((tokens, 2 * width), BF16),
            jax.ShapeDtypeStruct((tokens, (heads + 1) * width), F32),
        ],
        compiler_params=pltpu.CompilerParams(vmem_limit_bytes=VMEM_LIMIT),
        cost_estimate=TINY_COST,
    )(x, w, cos, sin, gain_q, gain_k)


def prepare_back_kernel(
    dq_ref, dk_ref, dv_ref, got_ref, raw_ref, cos_ref, sin_ref, gq_ref, gk_ref, w_ref, d_ref, p_ref, g_ref, *, heads, width
):
    @pl.when(pl.program_id(0) == 0)
    def _():
        g_ref[...] = jnp.zeros_like(g_ref)

    got = got_ref[...].astype(F32)
    for h in range(heads + 1):
        at = slice(h * width, (h + 1) * width)
        grad = dq_ref[:, at] if h < heads else dk_ref[0] + got[:, :width]
        gain = (gq_ref if h < heads else gk_ref)[...]
        raw = raw_ref[:, at]
        inverse = lax.rsqrt(jnp.mean(raw * raw, axis=-1, keepdims=True) + EPS)
        normed = raw * inverse
        turned = grad * cos_ref[...] - pltpu.roll(grad, width // 2, 1) * sin_ref[...]
        row = 0 if h < heads else 1
        g_ref[row : row + 1, :] += jnp.sum(turned * normed, axis=0, keepdims=True)
        scaled = turned * gain
        d_ref[:, at] = (inverse * (scaled - normed * jnp.mean(scaled * normed, axis=-1, keepdims=True))).astype(BF16)
    d_ref[:, (heads + 1) * width :] = (dv_ref[0] + got[:, width:]).astype(BF16)
    p_ref[...] = nt(d_ref[...], w_ref[...]).astype(BF16)


def prepare_back(dq, dk, dv, got, raw, cos, sin, gain_q, gain_k, w, heads):
    tokens, width, tile = dq.shape[0], gain_q.shape[1], 256
    row = lambda n: pl.BlockSpec((tile, n), lambda i: (i, 0))
    part = pl.BlockSpec((1, tile, width), lambda i: (0, i, 0))
    fixed = lambda a: pl.BlockSpec(a.shape, lambda i: (0, 0))
    return pl.pallas_call(
        functools.partial(prepare_back_kernel, heads=heads, width=width),
        grid=(tokens // tile,),
        in_specs=[
            row(heads * width),
            part,
            part,
            row(2 * width),
            row((heads + 1) * width),
            row(width),
            row(width),
            fixed(gain_q),
            fixed(gain_k),
            fixed(w),
        ],
        out_specs=[row(w.shape[1]), row(w.shape[0]), pl.BlockSpec((8, width), lambda i: (0, 0))],
        out_shape=[
            jax.ShapeDtypeStruct((tokens, w.shape[1]), BF16),
            jax.ShapeDtypeStruct((tokens, w.shape[0]), BF16),
            jax.ShapeDtypeStruct((8, width), F32),
        ],
        compiler_params=pltpu.CompilerParams(vmem_limit_bytes=VMEM_LIMIT),
        cost_estimate=TINY_COST,
    )(dq, dk, dv, got, raw, cos, sin, gain_q, gain_k, w)


def place_of_block(blk, bit_order, p):
    return blk ^ sum(((p >> i) & 1) << b for i, b in enumerate(bit_order))


def enter_kernel(blk_ref, *refs, bit_order, normed):
    if normed:
        mine_ref, other_ref, gain_ref, low_ref, out_ref, gains_ref = refs
    else:
        mine_ref, low_ref = refs
    rows, width = mine_ref.shape
    n = width >> len(bit_order)
    for p in range(1 << len(bit_order)):
        at = pl.ds(pl.multiple_of(place_of_block(blk_ref[0], bit_order, p) * n, n), n)
        low_ref[:rows, p * n : (p + 1) * n] = mine_ref[:, at]
        if normed:
            low_ref[rows:, p * n : (p + 1) * n] = other_ref[:, at]
            gains_ref[:, p * n : (p + 1) * n] = gain_ref[:, at]
    if normed:
        values = low_ref[...].astype(F32)
        inverse = lax.rsqrt(jnp.mean(values * values, axis=-1, keepdims=True) + EPS)
        out_ref[...] = (values * inverse * gains_ref[:1]).astype(BF16)


def enter(blk, bit_order, mine, other=None, gain=None):
    rows, width = mine.shape
    normed = gain is not None
    total = (2 * rows if normed else rows, width)
    vmem = pl.BlockSpec(memory_space=pltpu.VMEM)
    operands = [mine, other, gain] if normed else [mine]
    return pl.pallas_call(
        functools.partial(enter_kernel, bit_order=bit_order, normed=normed),
        in_specs=[pl.BlockSpec(memory_space=pltpu.SMEM), *[vmem] * len(operands)],
        out_specs=[vmem] * (3 if normed else 1),
        out_shape=[
            *[jax.ShapeDtypeStruct(total, BF16)] * (2 if normed else 1),
            *([jax.ShapeDtypeStruct(gain.shape, F32)] if normed else []),
        ],
        compiler_params=pltpu.CompilerParams(vmem_limit_bytes=VMEM_LIMIT),
        cost_estimate=TINY_COST,
    )(blk[None].astype(jnp.int32), *operands)


def assemble_kernel(place_ref, *refs, sources, widths):
    ins, outs = refs[: 2 * sources], refs[2 * sources :]
    place, k, at = place_ref[0], 0, 0
    for own_ref, got_ref in zip(ins[::2], ins[1::2]):
        f, at = own_ref.shape[0], 0
        while at < own_ref.shape[1]:
            w, cut = widths[k], slice(at, at + widths[k])
            mine = pl.ds(pl.multiple_of(place * w, w), w)
            theirs = pl.ds(pl.multiple_of((1 - place) * w, w), w)
            outs[k][:, mine] = own_ref[:, cut] + got_ref[:f, cut].astype(F32)
            outs[k][:, theirs] = got_ref[f : 2 * f, cut].astype(F32) + got_ref[2 * f :, cut].astype(F32)
            at += w
            k += 1


def assemble(place, sources, widths):
    vmem = pl.BlockSpec(memory_space=pltpu.VMEM)
    flat = [a for pair in sources for a in pair]
    return pl.pallas_call(
        functools.partial(assemble_kernel, sources=len(sources), widths=widths),
        in_specs=[pl.BlockSpec(memory_space=pltpu.SMEM), *[vmem] * len(flat)],
        out_specs=[vmem] * len(widths),
        out_shape=[jax.ShapeDtypeStruct((sources[0][0].shape[0], 2 * w), F32) for w in widths],
        compiler_params=pltpu.CompilerParams(vmem_limit_bytes=VMEM_LIMIT),
        cost_estimate=TINY_COST,
    )(place[None].astype(jnp.int32), *flat)


def back_kernel(*refs):
    *ins, out_ref = refs
    n = len(ins) // 2
    out_ref[...] = sum(nt(d[...], w[...]) for d, w in zip(ins[:n], ins[n:])).astype(BF16)


def back_through(grads, weights):
    tokens, depth, tile = grads[0].shape[0], weights[0].shape[0], 256
    return pl.pallas_call(
        back_kernel,
        grid=(depth // tile,),
        in_specs=[
            *[pl.BlockSpec(g.shape, lambda i: (0, 0)) for g in grads],
            *[pl.BlockSpec((tile, w.shape[1]), lambda i: (i, 0)) for w in weights],
        ],
        out_specs=pl.BlockSpec((tokens, tile), lambda i: (0, i)),
        out_shape=jax.ShapeDtypeStruct((tokens, depth), BF16),
        compiler_params=pltpu.CompilerParams(vmem_limit_bytes=VMEM_LIMIT),
        cost_estimate=TINY_COST,
    )(*grads, *weights)


def weight_grad_kernel(a_ref, b_ref, keep_ref, away_ref):
    product = tn(a_ref[...], b_ref[...])
    first = pl.program_id(0) < pl.num_programs(0) // 2

    @pl.when(first)
    def _():
        keep_ref[...] = product

    @pl.when(jnp.logical_not(first))
    def _():
        away_ref[...] = product.astype(BF16)


def weight_grad(a, b):
    tokens, depth = a.shape
    n, tile = b.shape[1], 256
    steps = depth // tile
    return pl.pallas_call(
        weight_grad_kernel,
        grid=(steps,),
        in_specs=[
            pl.BlockSpec((tokens, tile), lambda i: (0, i)),
            pl.BlockSpec((tokens, n), lambda i: (0, 0)),
        ],
        out_specs=[
            pl.BlockSpec((tile, n), lambda i: (jnp.minimum(i, steps // 2 - 1), 0)),
            pl.BlockSpec((tile, n), lambda i: (jnp.maximum(i - steps // 2, 0), 0)),
        ],
        out_shape=[
            jax.ShapeDtypeStruct((depth // 2, n), F32),
            jax.ShapeDtypeStruct((depth // 2, n), BF16),
        ],
        compiler_params=pltpu.CompilerParams(vmem_limit_bytes=VMEM_LIMIT),
        cost_estimate=TINY_COST,
    )(a, b)


def remote(src, dst, send, recv, target):
    copy = pltpu.make_async_remote_copy(
        src_ref=src, dst_ref=dst, send_sem=send, recv_sem=recv, device_id=target, device_id_type=pl.DeviceIdType.MESH
    )
    copy.start()
    return copy


class Plan:
    def __init__(self):
        self.inputs, self.shapes, self.aliases, self.jobs = [], [], {}, []

    def read(self, array):
        self.inputs.append(array)
        return ("in", len(self.inputs) - 1)

    def fresh(self, shape, dtype):
        self.shapes.append(jax.ShapeDtypeStruct(shape, dtype))
        return ("out", len(self.shapes) - 1)

    def through(self, array):
        self.inputs.append(array)
        self.aliases[len(self.inputs) - 1] = len(self.shapes)
        return self.fresh(array.shape, array.dtype)

    def copy(self, src, dst, mask, after=None, point=0):
        self.jobs.append((src, dst, mask, after, point, None))
        return len(self.jobs) - 1

    def local(self, src, dst, shape, point=0):
        self.jobs.append((src, dst, 0, None, point, shape))
        return len(self.jobs) - 1


def run(plan, main, collective_id, greeted=()):
    inputs, in_specs, out_shapes, out_specs, scratch, body, limit = main
    n_in, n_out = len(inputs), len(out_shapes)
    m_in, m_out = len(plan.inputs), len(plan.shapes)
    jobs = plan.jobs
    local_jobs = [i for i, job in enumerate(jobs) if not job[2]]
    masks = sorted({*greeted, *[job[2] for job in jobs if job[2]]} - {1 << TENSOR_BIT})
    any_spec = pl.BlockSpec(memory_space=pltpu.HBM)

    def kernel(*refs):
        main_in, refs = refs[:n_in], refs[n_in:]
        plan_in, refs = refs[:m_in], refs[m_in:]
        main_out, refs = refs[:n_out], refs[n_out:]
        plan_out, refs = refs[:m_out], refs[m_out:]
        send, recv, *rest = refs
        bounce = dict(zip(local_jobs, rest))
        rest = rest[len(local_jobs) :]
        blk, head = lax.axis_index("blk"), lax.axis_index("head")
        core, near, across = (blk, head ^ 1), (blk, head ^ 2), (blk ^ (1 << TENSOR_BIT), head)
        barrier = pltpu.get_barrier_semaphore()
        partners = [core, near, across, *[(blk ^ m, head) for m in masks]]
        for target in partners:
            pl.semaphore_signal(barrier, inc=1, device_id=target, device_id_type=pl.DeviceIdType.MESH)
        pl.semaphore_wait(barrier, len(partners))
        started, arrived, halfway = {}, set(), []

        def arrive(i):
            if i not in arrived:
                arrived.add(i)
                (started[i].wait_recv if jobs[i][2] else started[i].wait)()

        def part(side):
            (kind, index), cut = side
            return cut((plan_in if kind == "in" else plan_out)[index])

        def issue(point):
            for i in list(halfway):
                started[i].wait()
                started[i] = pltpu.make_async_copy(bounce[i], part(jobs[i][1]), recv.at[i])
                started[i].start()
                halfway.remove(i)
            for i, (src, dst, mask, after, at, shape) in enumerate(jobs):
                if i in started or (at != point and point is not None):
                    continue
                if after is not None:
                    arrive(after)
                if mask:
                    started[i] = remote(part(src), part(dst), send.at[i], recv.at[i], (blk ^ mask, head))
                else:
                    started[i] = pltpu.make_async_copy(part(src), bounce[i], send.at[i])
                    started[i].start()
                    halfway.append(i)

        point = 0
        for _ in body((core, near, across), main_in, main_out, rest):
            issue(point)
            point += 1
        issue(None)
        issue(None)
        for i in range(len(jobs)):
            arrive(i)
            if jobs[i][2]:
                started[i].wait_send()

    results = pl.pallas_call(
        kernel,
        out_shape=[*out_shapes, *plan.shapes],
        in_specs=[*in_specs, *[any_spec] * m_in],
        out_specs=[*out_specs, *[any_spec] * m_out],
        scratch_shapes=[
            pltpu.SemaphoreType.DMA((max(1, len(jobs)),)),
            pltpu.SemaphoreType.DMA((max(1, len(jobs)),)),
            *[pltpu.VMEM(jobs[i][5], BF16) for i in local_jobs],
            *scratch,
        ],
        input_output_aliases={n_in + i: n_out + o for i, o in plan.aliases.items()},
        compiler_params=pltpu.CompilerParams(
            collective_id=collective_id, has_side_effects=True, vmem_limit_bytes=limit
        ),
        cost_estimate=TINY_COST,
    )(*inputs, *plan.inputs)
    return results[:n_out], results[n_out:]


def spread_main(flat, chunk):
    rows, width = flat.shape[0] // 2, flat.shape[1]
    pieces = width // chunk

    def body(partners, ins, outs, scratch):
        core, near, across = partners
        (s_ref,), (o_ref,), (hold, local_sem, send, recv) = ins, outs, scratch
        first = remote(s_ref, o_ref.at[0, :, 0, 1], send.at[0], recv.at[0], near)
        second = [
            remote(
                s_ref.at[:, :, pl.ds(i * chunk, chunk)],
                o_ref.at[0, :, 1, 0, :, pl.ds((i ^ 1) * chunk, chunk)],
                send.at[6 + i],
                recv.at[6 + i],
                across,
            )
            for i in range(pieces)
        ]
        third = remote(s_ref, o_ref.at[1, :, 0, 0], send.at[1], recv.at[1], core)
        held = pltpu.make_async_copy(s_ref, hold, local_sem.at[0])
        held.start()
        yield
        held.wait()
        own = pltpu.make_async_copy(hold, o_ref.at[0, :, 0, 0], local_sem.at[1])
        own.start()
        for copy in second:
            copy.wait_recv()
        fourth = remote(o_ref.at[0, :, 1, 0], o_ref.at[0, :, 1, 1], send.at[2], recv.at[2], near)
        fifth = remote(o_ref.at[0, :, 1, 0], o_ref.at[1, :, 1, 0], send.at[3], recv.at[3], core)
        yield
        first.wait_recv()
        sixth = remote(o_ref.at[0, :, 0, 1], o_ref.at[1, :, 0, 1], send.at[4], recv.at[4], core)
        yield
        fourth.wait_recv()
        seventh = remote(o_ref.at[0, :, 1, 1], o_ref.at[1, :, 1, 1], send.at[5], recv.at[5], core)
        yield
        own.wait()
        for copy in (first, *second, third, fourth, fifth, sixth, seventh):
            copy.wait_send()
        for copy in (third, fifth, sixth, seventh):
            copy.wait_recv()

    any_spec = pl.BlockSpec(memory_space=pltpu.HBM)
    return (
        [flat.reshape(2, rows, width)],
        [any_spec],
        [jax.ShapeDtypeStruct((2, 2, 2, 2, rows, width), flat.dtype)],
        [any_spec],
        [
            pltpu.VMEM((2, rows, width), flat.dtype),
            pltpu.SemaphoreType.DMA((2,)),
            pltpu.SemaphoreType.DMA((6 + pieces,)),
            pltpu.SemaphoreType.DMA((6 + pieces,)),
        ],
        body,
        8 * MIB,
    )


def gather_main(partial, chunk, extra, outs_like, finish):
    rows, width = partial.shape[0] // 16, partial.shape[1]
    share = (2, rows, width)
    pieces = width // chunk

    def body(partners, ins, outs, scratch):
        core, near, across = partners
        p_ref, *extra_refs = ins
        core_in, out_y, in_y, out_t, in_t, hold, send, recv = scratch
        order = ((1, 1), (0, 1), (1, 0), (0, 0))
        from_core = [
            remote(p_ref.at[1, :, t, y], core_in.at[i], send.at[i], recv.at[i], core) for i, (t, y) in enumerate(order)
        ]
        from_y = []
        for i in range(2):
            t, y = order[i]
            from_core[i].wait_recv()
            out_y[i] = (p_ref[0, :, t, y].astype(F32) + core_in[i].astype(F32)).astype(BF16)
            from_y.append(remote(out_y.at[i], in_y.at[i], send.at[4 + i], recv.at[4 + i], near))
        yield
        from_core[2].wait_recv()
        hold[...] = p_ref[0, :, 1, 0].astype(F32) + core_in[2].astype(F32)
        from_y[0].wait_recv()
        for i in range(pieces):
            a, b = slice(i * chunk, (i + 1) * chunk), slice((i ^ 1) * chunk, ((i ^ 1) + 1) * chunk)
            out_t[:, :, b] = (hold[:, :, a] + in_y[0, :, :, a].astype(F32)).astype(BF16)
        from_t = remote(out_t, in_t, send.at[6], recv.at[6], across)
        yield
        from_core[3].wait_recv()
        hold[...] = p_ref[0, :, 0, 0].astype(F32) + core_in[3].astype(F32)
        from_y[1].wait_recv()
        hold[...] += in_y[1].astype(F32)
        yield
        from_t.wait_recv()
        hold[...] += in_t[...].astype(F32)
        finish(hold, extra_refs, outs)
        for copy in (*from_core, *from_y, from_t):
            copy.wait_send()

    vmem_spec = pl.BlockSpec(memory_space=pltpu.VMEM)
    return (
        [partial.reshape(2, 2, 2, 2, rows, width), *extra],
        [vmem_spec] * (1 + len(extra)),
        outs_like,
        [vmem_spec] * len(outs_like),
        [
            pltpu.VMEM((4, *share), BF16),
            pltpu.VMEM((2, *share), BF16),
            pltpu.VMEM((2, *share), BF16),
            pltpu.VMEM(share, BF16),
            pltpu.VMEM(share, BF16),
            pltpu.VMEM(share, F32),
            pltpu.SemaphoreType.DMA((7,)),
            pltpu.SemaphoreType.DMA((7,)),
        ],
        body,
        24 * MIB,
    )


def inverse_rms(values):
    return lax.rsqrt(jnp.mean(values * values, axis=-1, keepdims=True) + EPS)


def finish_middle(total, extra, outs):
    (low_ref, gain_ref), (middle_ref, normed_ref) = extra, outs
    for m in range(2):
        middle = low_ref[m].astype(F32) + total[m]
        middle_ref[m] = middle
        normed_ref[m] = (middle * inverse_rms(middle) * gain_ref[...]).astype(BF16)


def norm_grad(total, values, gain, gain_grad_ref, m):
    inverse = inverse_rms(values)
    normal = values * inverse
    part = jnp.sum(total * normal, axis=0, keepdims=True)
    gain_grad_ref[...] = part if m == 0 else gain_grad_ref[...] + part
    scaled = total * gain
    return inverse * (scaled - normal * jnp.mean(scaled * normal, axis=-1, keepdims=True))


def finish_mlp_norm(total, extra, outs):
    (cot_ref, middle_ref, gain_ref), (grad_ref, low_ref, gain_grad_ref) = extra, outs
    for m in range(2):
        grad = cot_ref[m].astype(F32) + norm_grad(total[m], middle_ref[m], gain_ref[...], gain_grad_ref, m)
        grad_ref[m] = grad
        low_ref[m] = grad.astype(BF16)


def store_ungrouped(value, ref, blk, bit_order, lead=()):
    n = value.shape[-1] >> len(bit_order)
    for p in range(1 << len(bit_order)):
        block = value[:, p * n : (p + 1) * n]
        if bit_order and n % 128 == 0:
            at = pl.ds(pl.multiple_of(place_of_block(blk, bit_order, p) * n, n), n)
        else:
            at = pl.ds(p * n, n)
        ref[(*lead, slice(None), at)] = block.astype(ref.dtype)


def finish_mixed(total, extra, outs, *, bit_order):
    (middle_ref,), (mixed_ref,) = extra, outs
    blk = lax.axis_index("blk")
    for m in range(2):
        store_ungrouped(middle_ref[m] + total[m], mixed_ref, blk, bit_order, (m,))


def finish_input(total, extra, outs, *, bit_order):
    (low_ref, mid_ref, gain_ref), (own_ref, away_ref, gain_grad_ref) = extra, outs
    blk = lax.axis_index("blk")
    for m in range(2):
        grad = mid_ref[m] + norm_grad(total[m], low_ref[m].astype(F32), gain_ref[...], gain_grad_ref, m)
        store_ungrouped(grad, own_ref if m == 0 else away_ref, blk, bit_order)


def total_main(values):
    rows, width = values.shape
    rounds = 2 + lax.axis_size("blk").bit_length() - 1

    def body(partners, ins, outs, scratch):
        (v_ref,), (o_ref,) = ins, outs
        out_buf, in_buf, send, recv = scratch
        blk, head = lax.axis_index("blk"), lax.axis_index("head")
        o_ref[...] = v_ref[...]
        yield
        for i in range(rounds):
            target = (blk, head ^ (1 << i)) if i < 2 else (blk ^ (1 << (i - 2)), head)
            out_buf[i] = o_ref[...]
            copy = remote(out_buf.at[i], in_buf.at[i], send.at[i], recv.at[i], target)
            copy.wait_recv()
            o_ref[...] += in_buf[i]
            copy.wait_send()
        yield

    vmem_spec = pl.BlockSpec(memory_space=pltpu.VMEM)
    return (
        [values],
        [vmem_spec],
        [jax.ShapeDtypeStruct(values.shape, F32)],
        [vmem_spec],
        [
            pltpu.VMEM((rounds, rows, width), F32),
            pltpu.VMEM((rounds, rows, width), F32),
            pltpu.SemaphoreType.DMA((rounds,)),
            pltpu.SemaphoreType.DMA((rounds,)),
        ],
        body,
        8 * MIB,
    )


def local(
    hidden_in,
    lengths,
    query_weight,
    key_matrix,
    value_matrix,
    out_weight,
    gate_weight,
    up_weight,
    down_weight,
    attn_gain,
    query_gain,
    key_gain,
    mlp_gain,
    cotangent,
):
    ring = lax.axis_size("blk")
    bits = ring.bit_length() - 1
    batch_bit = bits - 1
    extra_bits = [i for i in range(bits) if i not in (TENSOR_BIT, SEQ_BIT, batch_bit)]
    seq_bits = [SEQ_BIT, *extra_bits]
    parts = 1 << len(seq_bits)
    bit_order = [batch_bit, TENSOR_BIT, SEQ_BIT, *extra_bits]
    b_mask, t_mask, x_mask = 1 << batch_bit, 1 << TENSOR_BIT, 1 << SEQ_BIT
    blk, head = lax.axis_index("blk"), lax.axis_index("head")
    batch, tensor = bit_of(blk, batch_bit), bit_of(blk, TENSOR_BIT)

    local_rows, width = hidden_in.shape[1:]
    block_rows = local_rows * lax.axis_size("head")
    half = block_rows // 2
    row_features = width // ring
    head_size = query_gain.shape[0]
    scaling = head_size ** (-0.5)
    tokens = 16 * local_rows
    heads = query_weight.shape[1] // (2 * head_size)
    ff = gate_weight.shape[1] // 2

    def moved(values, place_of):
        axis = values.ndim - 1
        return jnp.concatenate(
            [
                lax.dynamic_slice_in_dim(values, place_of(i) * row_features, row_features, axis)
                for i in range(ring)
            ],
            axis=axis,
        )

    def regroup(values):
        return moved(values, lambda p: blk ^ sum(((p >> i) & 1) << b for i, b in enumerate(bit_order)))

    def ungroup(values):
        return moved(values, lambda n: sum(bit_of(blk ^ n, b) << i for i, b in enumerate(bit_order)))

    def everything(ref):
        return ref

    def mask_of(p):
        return sum(((p >> i) & 1) << b for i, b in enumerate(bit_order))

    def rows_at(p):
        return lambda ref: ref.at[pl.ds(p * row_features, row_features), :]

    def half_cut(n, other):
        def cut(ref):
            place = bit_of(lax.axis_index("blk"), TENSOR_BIT)
            place = 1 - place if other else place
            return ref.at[:, pl.ds(pl.multiple_of(place * n, n), n)]

        return cut

    def send_over(plan, weight, buffer, p, point):
        mask, n = mask_of(p), weight.shape[1] // 2
        plan.copy((plan.read(weight), half_cut(n, mask & t_mask)), (buffer, rows_at(p)), mask, point=point)

    def keep_own(plan, weight, buffer, point, onward=True):
        here, n = plan.read(weight), weight.shape[1] // 2
        if onward:
            plan.copy((here, half_cut(n, 0)), (buffer, rows_at(4)), x_mask, point=point)
        plan.local((here, half_cut(n, 0)), (buffer, rows_at(0)), (row_features, n), point=point)

    def send_on(plan, buffer, places, point, after=None):
        for p in places:
            plan.copy((buffer, rows_at(p)), (buffer, rows_at(p + 4)), x_mask, after=after, point=point)

    def lay(plan, array, buffer, p, point=0, columns=None, onward=False):
        here = plan.read(array)
        cut = (lambda ref: ref.at[:, pl.ds(*columns)]) if columns else everything
        if onward:
            plan.copy((here, cut), (buffer, rows_at(p + 4)), x_mask, point=point)
        plan.local((here, cut), (buffer, rows_at(p)), (row_features, columns[1] if columns else array.shape[1]), point)

    def fresh_for(plan, weights):
        return plan.fresh(buffer_shape(weights), BF16)

    def buffer_shape(weights):
        return (8 * row_features, sum(w.shape[1] for w in weights) // 2)

    def whole_weight(buffer):
        pieces = [buffer]
        for b in extra_bits:
            pieces = pieces + [over_blk(c, 1 << b) for c in pieces]
        return jnp.concatenate(pieces, axis=0) if extra_bits else buffer

    def split_grad(grad):
        for b in reversed(extra_bits):
            n = grad.shape[0] // 2
            grad = grad[:n] + over_blk(grad[n:].astype(BF16), 1 << b).astype(F32)
        n = grad.shape[0] // 2
        return grad[:n], grad[n:].astype(BF16)

    def weight_sum(a, b):
        return split_grad(tn(a, b)) if extra_bits else weight_grad(a, b)

    def fold(plan, away):
        out = plan.fresh(away.shape, away.dtype)
        plan.copy((plan.read(away), everything), (out, everything), x_mask)

    def fold_part(plan, away, buffer, start, n):
        def part(ref):
            return ref.at[:, pl.ds(start, n)]

        plan.copy((plan.read(away), part), (buffer, part), x_mask)

    def to_settle(keep, got):
        total = keep + got.astype(F32)
        return total[:row_features], total[row_features:].astype(BF16)

    def settle(plan, away, t_point=0):
        out, here = plan.fresh(away.shape, away.dtype), plan.read(away)
        for i, mask in ((0, b_mask), (2, b_mask | t_mask), (1, t_mask)):
            plan.copy((here, rows_at(i)), (out, rows_at(i)), mask, point=t_point if mask == t_mask else 0)

    def settled(sources, column_widths):
        if all(w % 128 == 0 for w in column_widths):
            return assemble(tensor, sources, column_widths)
        f, results = row_features, []
        widths = iter(column_widths)
        for own, got in sources:
            own = own + got[:f].astype(F32)
            other = got[f : 2 * f].astype(F32) + got[2 * f :].astype(F32)
            at = 0
            while at < own.shape[1]:
                w = next(widths)
                results.append(in_order(tensor, own[:, at : at + w], other[:, at : at + w], 1))
                at += w
        return results

    chunk = 2 * row_features
    ids = iter(range(100))

    def spread(flat, plan):
        (out,), rest = run(plan, spread_main(flat, chunk), next(ids))
        return out.reshape(tokens, width), rest

    share = (2, local_rows, width)

    def gather_sum(partial, plan, extra, outs_like, finish):
        return run(plan, gather_main(partial, chunk, extra, outs_like, finish), next(ids))

    def like(shape, dtype):
        return jax.ShapeDtypeStruct(shape, dtype)

    aligned = row_features % 128 == 0
    local_order = bit_order if aligned else []

    def split_batch(rows):
        mine = lax.dynamic_index_in_dim(rows, batch, 0, keepdims=False)
        theirs = lax.dynamic_index_in_dim(rows, 1 - batch, 0, keepdims=False)
        return mine, theirs

    def natural(rows):
        return rows if aligned else ungroup(rows)

    length_row = lax.dynamic_index_in_dim(lengths, batch, 0, keepdims=False)
    doc_ends = jnp.cumsum(length_row)
    batch_flip = jnp.arange(2, dtype=jnp.int32)[:, None] << batch_bit
    tensor_flip = jnp.arange(2, dtype=jnp.int32)[None, :] << TENSOR_BIT
    q_blocks = (blk ^ batch_flip ^ tensor_flip).reshape(4)
    index = jnp.arange(2 * half, dtype=jnp.int32)
    in_block = token_offset(head, index, local_rows).reshape(2, 1, half)
    token_index = q_blocks[None, :, None] * block_rows + in_block
    passed = doc_ends <= token_index[..., None]
    doc_start = jnp.max(jnp.where(passed, doc_ends, 0), axis=-1).astype(jnp.int32)
    position = (token_index - doc_start).reshape(tokens)
    start_lanes = jnp.tile(jnp.transpose(doc_start, (1, 0, 2)).reshape(4, 1, 2 * half), (1, 1, heads))
    k_blocks = q_blocks
    for b in seq_bits:
        k_blocks = jnp.concatenate([k_blocks, k_blocks ^ (1 << b)])
    least_start = jnp.min(doc_start, axis=(0, 2))[:, None]
    last_start = jnp.max(doc_start, axis=(0, 2))[:, None]
    k_first = (k_blocks * block_rows)[None, :]
    none = (k_blocks[None, :] > q_blocks[:, None]) | (k_first + block_rows <= least_start)
    whole = (k_blocks[None, :] < q_blocks[:, None]) & (k_first >= last_start)
    flags = jnp.where(none, 0, jnp.where(whole, 1, 2))
    meta = jnp.concatenate([head[None], q_blocks, k_blocks, flags.reshape(-1)]).astype(jnp.int32)

    inverse_freq = THETA ** (-jnp.arange(head_size // 2, dtype=F32) / (head_size // 2))
    angles = position.astype(F32)[:, None] * inverse_freq[None, :]
    cosine, sine = jnp.cos(angles), jnp.sin(angles)
    cosine = jnp.concatenate([cosine, cosine], axis=1)
    sine = jnp.concatenate([-sine, sine], axis=1)

    def rms(values):
        return lax.rsqrt(jnp.mean(values * values, axis=-1, keepdims=True) + EPS)

    def norm_back(grad, normed, inverse, gain):
        scaled = grad * gain
        return inverse * (scaled - normed * jnp.mean(scaled * normed, axis=-1, keepdims=True))

    gains_in = jnp.stack([attn_gain, mlp_gain]).astype(F32)
    gain_q = query_gain.astype(F32)[None]
    gain_k = key_gain.astype(F32)[None]

    q_columns, k_columns = heads * head_size, head_size
    a_weights = (query_weight, key_matrix, value_matrix)

    def halves(weights, which):
        return jnp.concatenate(
            [lax.dynamic_slice_in_dim(w, which * (w.shape[1] // 2), w.shape[1] // 2, 1) for w in weights], axis=1
        )

    mine, theirs = split_batch(hidden_in)
    other = over_blk(theirs, b_mask)
    a_own, a_other = halves(a_weights, tensor), halves(a_weights, 1 - tensor)
    a_by_t = over_blk(a_other, t_mask)
    a_by_b = over_blk(a_own, b_mask)
    early = over_blk(jnp.concatenate([a_own, halves((down_weight,), tensor)], axis=1), x_mask)
    (mine, other, cosine, sine, start_lanes, meta) = pin((mine, other, cosine, sine, start_lanes, meta))
    if aligned:
        x_low, xa, gains_in = enter(blk, bit_order, mine, other, gains_in)
        gain_a, gain_m = gains_in[0], gains_in[1]
    else:
        gains_in = regroup(gains_in)
        gain_a, gain_m = gains_in[0], gains_in[1]
        x_low = regroup(jnp.concatenate([mine, other], axis=0))
        x_wide = x_low.astype(F32)
        xa = (x_wide * rms(x_wide) * gain_a).astype(BF16)

    plan = Plan()
    a_columns = a_own.shape[1]
    w_a = fresh_for(plan, a_weights)
    by_tb = plan.copy((plan.read(a_other), everything), (w_a, rows_at(3)), b_mask | t_mask)
    lay(plan, a_by_t, w_a, 2, onward=True)
    lay(plan, a_by_b, w_a, 1, onward=True)
    lay(plan, a_own, w_a, 0)
    lay(plan, early, w_a, 4, columns=(0, a_columns))
    here, cot_out = plan.read(cotangent), plan.fresh((2, local_rows, width), BF16)
    plan.copy(
        (here, lambda ref: ref.at[1 - bit_of(lax.axis_index("blk"), batch_bit)]),
        (cot_out, lambda ref: ref.at[1]),
        b_mask,
        point=1,
    )
    plan.local(
        (here, lambda ref: ref.at[bit_of(lax.axis_index("blk"), batch_bit)]),
        (cot_out, lambda ref: ref.at[0]),
        (local_rows, width),
    )
    w_out = fresh_for(plan, (out_weight,))
    send_over(plan, out_weight, w_out, 1, 1)
    send_over(plan, out_weight, w_out, 3, 1)
    send_over(plan, out_weight, w_out, 2, 1)
    keep_own(plan, out_weight, w_out, 0)
    w_down = fresh_for(plan, (down_weight,))
    send_over(plan, down_weight, w_down, 2, 1)
    keep_own(plan, down_weight, w_down, 0, onward=False)
    lay(plan, early, w_down, 4, columns=(a_columns, ff))
    w_gate = fresh_for(plan, (gate_weight,))
    keep_own(plan, gate_weight, w_gate, 1)
    send_on(plan, w_a, (3,), 2, after=by_tb)
    xa, (w_qkv, cot, w_out, w_down, w_gate) = spread(xa, plan)
    w_qkv = whole_weight(w_qkv)
    cot = cot.reshape(2 * local_rows, width)
    cot = enter(blk, bit_order, cot)[0] if aligned else regroup(cot)
    query, key_value, raw = prepare(xa, w_qkv, cosine, sine, gain_q, gain_k, heads)

    plan = Plan()
    kv_out = plan.fresh(key_value.shape, BF16)
    plan.copy((plan.read(key_value), everything), (kv_out, everything), x_mask)
    w_out = plan.through(w_out)
    send_on(plan, w_out, (1, 2, 3), 0)
    w_down = plan.through(w_down)
    send_over(plan, down_weight, w_down, 1, 0)
    send_over(plan, down_weight, w_down, 3, 0)
    send_on(plan, w_down, (2,), 1)
    w_gate = plan.through(w_gate)
    send_over(plan, gate_weight, w_gate, 2, 1)
    cot_all, (kv_x, w_out, w_down, w_gate) = spread(cot, plan)
    w_out = whole_weight(w_out)
    key_value = [key_value, kv_x]
    for b in extra_bits:
        key_value = key_value + [over_blk(c, 1 << b) for c in key_value]
    key_value = jnp.stack(key_value)
    keys = key_value[..., :head_size].reshape(parts, 2, 4, half, head_size)
    values = key_value[..., head_size:].reshape(parts, 2, 4, half, head_size)
    query = query.reshape(2, 4, half, q_columns)
    attn, attn_t, total_e = attend(meta, query, keys, values, start_lanes, scaling)
    attn = attn.reshape(tokens, q_columns)

    plan = Plan()
    w_down = plan.through(w_down)
    send_on(plan, w_down, (1, 3), 0)
    w_gate = plan.through(w_gate)
    send_over(plan, gate_weight, w_gate, 1, 0)
    send_over(plan, gate_weight, w_gate, 3, 0)
    send_on(plan, w_gate, (2,), 0)
    w_up = fresh_for(plan, (up_weight,))
    send_over(plan, up_weight, w_up, 2, 0)
    keep_own(plan, up_weight, w_up, 1)
    x_low = x_low.reshape(share)
    (middle, xm), (w_down, w_gate, w_up) = gather_sum(
        nt(attn, w_out).astype(BF16),
        plan,
        [x_low, gain_m[None]],
        [like(share, F32), like(share, BF16)],
        finish_middle,
    )
    w_down = whole_weight(w_down)

    plan = Plan()
    w_gate = plan.through(w_gate)
    w_up = plan.through(w_up)
    by_b = len(plan.jobs)
    send_over(plan, up_weight, w_up, 1, 0)
    send_on(plan, w_gate, (1, 3), 0)
    send_on(plan, w_up, (2,), 1)
    by_tb = plan.copy(
        (plan.read(up_weight), half_cut(ff, True)), (w_up, rows_at(3)), b_mask | t_mask, after=by_b, point=2
    )
    send_on(plan, w_up, (1,), 2)
    send_on(plan, w_up, (3,), 3, after=by_tb)
    xm, (w_gate, w_up) = spread(xm.reshape(2 * local_rows, width), plan)
    w_gate, w_up = whole_weight(w_gate), whole_weight(w_up)
    d_active = nn(cot_all, w_down)
    gate = nn(xm, w_gate)
    up = nn(xm, w_up)
    sig = jax.nn.sigmoid(gate)
    silu = gate * sig
    active = (silu * up).astype(BF16)
    d_gate = (d_active * up * sig * (1.0 + gate * (1.0 - sig))).astype(BF16)
    d_up = (d_active * silu).astype(BF16)

    keep_down, away_down = weight_sum(cot_all, active)
    got_x = over_blk(away_down, x_mask)
    (d_gate, d_up, away_down) = pin((d_gate, d_up, away_down))
    keep_gate, away_gate = weight_sum(xm, d_gate)
    plan = Plan()
    gate_x = plan.fresh(away_gate.shape, BF16)
    ff_cut = ff // 2
    fold_part(plan, away_gate, gate_x, 0, ff_cut)
    (d_middle, d_mid, gain_m_grad), (gate_x,) = gather_sum(
        back_through((d_gate, d_up), (w_gate, w_up)),
        plan,
        [cot.reshape(share), middle, gain_m[None]],
        [like(share, F32), like(share, BF16), like((1, width), F32)],
        finish_mlp_norm,
    )
    (d_mid, got_x) = pin((d_mid, got_x))
    own_down, away_down = to_settle(keep_down, got_x)
    keep_up, away_up = weight_sum(xm, d_up)

    plan = Plan()
    settle(plan, away_down, 1)
    gate_x = plan.through(gate_x)
    fold_part(plan, away_gate, gate_x, ff_cut, ff - ff_cut)
    up_x = plan.fresh(away_up.shape, BF16)
    fold_part(plan, away_up, up_x, 0, ff_cut)
    d_mid_all, (got_down, gate_x, up_x) = spread(d_mid.reshape(2 * local_rows, width), plan)
    (g_down,) = settled([(own_down, got_down)], (ff,))
    own_gate, away_gate = to_settle(keep_gate, gate_x)
    keep_out, away_out = weight_sum(d_mid_all, attn)
    d_attn = nn(d_mid_all, w_out).astype(BF16).reshape(2, 4, half, q_columns)
    d_query, d_key, d_value = attend_back(
        meta, query, d_attn, keys, values, start_lanes, attn_t, total_e, scaling
    )
    d_key = d_key.reshape(parts, tokens, head_size)
    d_value = d_value.reshape(parts, tokens, head_size)
    for b in reversed(extra_bits):
        n = d_key.shape[0] // 2
        d_key = d_key[:n] + over_blk(d_key[n:].astype(BF16), 1 << b).astype(F32)
        d_value = d_value[:n] + over_blk(d_value[n:].astype(BF16), 1 << b).astype(F32)

    plan = Plan()
    fold(plan, jnp.concatenate([d_key[1], d_value[1]], axis=1).astype(BF16))
    settle(plan, away_gate)
    up_x = plan.through(up_x)
    fold_part(plan, away_up, up_x, ff_cut, ff - ff_cut)
    fold(plan, away_out)
    (mixed,), (got_kv, got_gate, up_x, out_x) = gather_sum(
        back_through((active,), (w_down,)),
        plan,
        [middle],
        [like(share, BF16)],
        functools.partial(finish_mixed, bit_order=local_order),
    )
    (g_gate,) = settled([(own_gate, got_gate)], (ff,))
    own_up, away_up = to_settle(keep_up, up_x)
    own_out, away_out = to_settle(keep_out, out_x)
    mixed = natural(mixed)
    mixed_got = over_blk(mixed[1], b_mask)
    d_qkv, d_xa_partial, gains_qk = prepare_back(
        d_query.reshape(tokens, q_columns), d_key, d_value, got_kv, raw, cosine, sine, gain_q, gain_k, w_qkv, heads
    )
    keep_qkv, away_qkv = weight_sum(xa, d_qkv)
    (away_qkv, mixed_got) = pin((away_qkv, mixed_got))

    plan = Plan()
    settle(plan, away_up)
    fold(plan, away_qkv)
    (input_own, input_away, gain_a_grad), (got_up, got) = gather_sum(
        d_xa_partial,
        plan,
        [x_low, d_middle, gain_a[None]],
        [like((local_rows, width), F32), like((local_rows, width), BF16), like((1, width), F32)],
        functools.partial(finish_input, bit_order=local_order),
    )
    (g_up,) = settled([(own_up, got_up)], (ff,))
    own_qkv, away_qkv = to_settle(keep_qkv, got)

    plan = Plan()
    settle(plan, away_qkv)
    settle(plan, away_out)
    input_got = plan.fresh((local_rows, width), BF16)
    plan.copy((plan.read(natural(input_away)), everything), (input_got, everything), b_mask)
    sums = jnp.concatenate([ungroup(gain_a_grad[0]), gains_qk[0], gains_qk[1], ungroup(gain_m_grad[0])])
    (sums,), (got_a, got_o, input_got) = run(
        plan, total_main(sums.reshape(-1, 128)), next(ids), [1 << i for i in range(bits)]
    )
    g_query, g_key, g_value, g_out = settled(
        [(own_qkv, got_a), (own_out, got_o)], (q_columns, k_columns, k_columns, q_columns)
    )
    mixed = in_order(batch, mixed[:1], mixed_got[None], 0)
    input_grad = in_order(batch, natural(input_own)[None], input_got.astype(F32)[None], 0)
    gains = jnp.split(sums.reshape(-1), [width, width + head_size, width + 2 * head_size])
    return (
        mixed,
        input_grad,
        g_query,
        g_key,
        g_value,
        g_out,
        g_gate,
        g_up,
        g_down,
        *gains,
    )


def solution(mesh):
    rows = P(None, ("blk", "head"), None)
    weight = P("blk", "head")
    return jax.shard_map(
        local,
        mesh=mesh,
        in_specs=(rows, P(), *([weight] * 7), P(), P(), P(), P(), rows),
        out_specs=(rows, rows, *([weight] * 7), P(), P(), P(), P()),
        check_vma=False,
    )
```

```python
import functools
import math

import jax
import jax.numpy as jnp
from jax import lax
from jax.experimental import pallas as pl
from jax.experimental.pallas import tpu as pltpu
from jax.sharding import PartitionSpec as P

EPS = 1e-06
THETA = 1000000.0
LOG2E = 1.4426950408889634
F32 = jnp.float32
BF16 = jnp.bfloat16

MIB = 1024 * 1024
TINY_COST = pl.CostEstimate(flops=0, bytes_accessed=0, transcendentals=0)
VMEM_LIMIT = 32 * MIB
TENSOR_BIT = 1
SEQ_BIT = 0


def nt(a, b):
    return lax.dot_general(a, b, (((1,), (1,)), ((), ())), preferred_element_type=F32)


def tn(a, b):
    return lax.dot_general(a, b, (((0,), (0,)), ((), ())), preferred_element_type=F32)


def nn(a, b):
    return jnp.dot(a, b, preferred_element_type=F32)


def bit_of(value, bit):
    return (value >> bit) & 1


def over_blk(value, mask):
    count = lax.axis_size("blk")
    return lax.ppermute(value, "blk", [(i, i ^ mask) for i in range(count)])


def over_head(value, mask):
    count = lax.axis_size("head")
    return lax.ppermute(value, "head", [(i, i ^ mask) for i in range(count)])


def pin(values):
    return lax.optimization_barrier(values)


def in_order(flag, own, other, axis):
    return jnp.where(
        flag == 0,
        jnp.concatenate([own, other], axis=axis),
        jnp.concatenate([other, own], axis=axis),
    )


def token_offset(head_place, index, sub):
    core, upper, inner = index // (2 * sub), (index // sub) % 2, index % sub
    return (head_place ^ (upper * 2) ^ core) * sub + inner


def allowed_mask(meta_ref, start_row, q_block, k_block, rows, half, q_lanes):
    sub = half // 2
    head_place = meta_ref[0]
    k_index = lax.broadcasted_iota(jnp.int32, (2 * half, 1), 0)
    k_token = token_offset(head_place, k_index, sub) + k_block * (2 * half)
    q_index = lax.broadcasted_iota(jnp.int32, (1, q_lanes), 1) % (2 * half)
    q_token = token_offset(head_place, q_index, sub) + q_block * (2 * half)
    return (k_token <= q_token) & (k_token >= start_row)


def stacked(ref, heads, width):
    return jnp.concatenate(
        [ref[c, 0, :, h * width : (h + 1) * width] for h in range(heads) for c in range(2)], axis=0
    )


def key_rows(ref, part, block):
    return jnp.concatenate([ref[part, 0, block], ref[part, 1, block]], axis=0)


def attend_kernel(meta_ref, q_ref, k_ref, v_ref, start_ref, o_ref, ot_ref, l_ref, vt_ref, acc_ref, sum_ref, *, factor, heads):
    q_pos = pl.program_id(0)
    parts, _, blocks, half, width = k_ref.shape
    lanes = heads * 2 * half

    @pl.when(q_pos == 0)
    def _():
        for part in range(parts):
            for block in range(blocks):
                vt_ref[part * blocks + block] = key_rows(v_ref, part, block).T

    q_rows = stacked(q_ref, heads, width)
    acc_ref[...] = jnp.zeros_like(acc_ref)
    sum_ref[...] = jnp.zeros_like(sum_ref)
    start_row = start_ref[0]
    q_block = meta_ref[1 + q_pos]
    total = parts * blocks

    def add(kb, masked):
        e = jnp.exp2(nt(key_rows(k_ref, kb // blocks, kb % blocks), q_rows) * factor)
        if masked:
            k_block = meta_ref[1 + blocks + kb]
            e = jnp.where(allowed_mask(meta_ref, start_row, q_block, k_block, None, half, lanes), e, 0.0)
        sum_ref[...] += jnp.sum(e, axis=0, keepdims=True)
        acc_ref[...] += nn(vt_ref[kb], e.astype(BF16))

    def step(kb, carry):
        flag = meta_ref[1 + blocks + total + q_pos * total + kb]

        @pl.when(flag == 1)
        def _():
            add(kb, False)

        @pl.when(flag == 2)
        def _():
            add(kb, True)

        return carry

    lax.fori_loop(0, total, step, 0)
    out = acc_ref[...] / sum_ref[...]
    ot_ref[0] = out
    l_ref[0] = sum_ref[...]
    rows = out.T
    for h in range(heads):
        for c in range(2):
            at = (h * 2 + c) * half
            o_ref[c, 0, :, h * width : (h + 1) * width] = rows[at : at + half].astype(BF16)


def attend_back_kernel(
    meta_ref, q_ref, do_ref, k_ref, v_ref, start_ref, ot_ref, l_ref, dq_ref, dk_ref, dv_ref, kt_ref, acc_ref, *, factor, scaling, heads
):
    q_pos = pl.program_id(0)
    parts, _, blocks, half, width = k_ref.shape
    lanes = heads * 2 * half

    @pl.when(q_pos == 0)
    def _():
        dk_ref[...] = jnp.zeros_like(dk_ref)
        dv_ref[...] = jnp.zeros_like(dv_ref)
        for part in range(parts):
            for block in range(blocks):
                kt_ref[part * blocks + block] = key_rows(k_ref, part, block).T

    q_rows = stacked(q_ref, heads, width)
    do_rows = stacked(do_ref, heads, width)
    delta = jnp.sum(do_rows.astype(F32).T * ot_ref[0], axis=0, keepdims=True)
    inverse = 1.0 / l_ref[0]
    acc_ref[...] = jnp.zeros_like(acc_ref)
    start_row = start_ref[0]
    q_block = meta_ref[1 + q_pos]
    total = parts * blocks

    def add(kb, masked):
        part, block = kb // blocks, kb % blocks
        e = jnp.exp2(nt(key_rows(k_ref, part, block), q_rows) * factor)
        if masked:
            k_block = meta_ref[1 + blocks + kb]
            e = jnp.where(allowed_mask(meta_ref, start_row, q_block, k_block, None, half, lanes), e, 0.0)
        p = e * inverse
        dp = nt(key_rows(v_ref, part, block), do_rows)
        ds = (p * (dp - delta)).astype(BF16)
        dv = nn(p.astype(BF16), do_rows)
        dk = nn(ds, q_rows) * scaling
        for c in range(2):
            dv_ref[part, c, block] += dv[c * half : (c + 1) * half]
            dk_ref[part, c, block] += dk[c * half : (c + 1) * half]
        acc_ref[...] += nn(kt_ref[kb], ds)

    def step(kb, carry):
        flag = meta_ref[1 + blocks + total + q_pos * total + kb]

        @pl.when(flag == 1)
        def _():
            add(kb, False)

        @pl.when(flag == 2)
        def _():
            add(kb, True)

        return carry

    lax.fori_loop(0, total, step, 0)
    rows = acc_ref[...].T * scaling
    for h in range(heads):
        for c in range(2):
            at = (h * 2 + c) * half
            dq_ref[c, 0, :, h * width : (h + 1) * width] = rows[at : at + half]


def attend(meta, q, k, v, start, scaling):
    _, blocks, half, columns = q.shape
    parts, width = k.shape[0], k.shape[-1]
    heads = columns // width
    lanes = heads * 2 * half
    total = parts * blocks
    row_spec = pl.BlockSpec((2, 1, half, columns), lambda i: (0, i, 0, 0))
    key_spec = pl.BlockSpec(k.shape, lambda i: (0, 0, 0, 0, 0))
    lane_spec = pl.BlockSpec((1, 1, lanes), lambda i: (i, 0, 0))
    return pl.pallas_call(
        functools.partial(attend_kernel, factor=scaling * LOG2E, heads=heads),
        grid=(blocks,),
        in_specs=[pl.BlockSpec(memory_space=pltpu.SMEM), row_spec, key_spec, key_spec, lane_spec],
        out_specs=[row_spec, pl.BlockSpec((1, width, lanes), lambda i: (i, 0, 0)), lane_spec],
        out_shape=[
            jax.ShapeDtypeStruct(q.shape, BF16),
            jax.ShapeDtypeStruct((blocks, width, lanes), F32),
            jax.ShapeDtypeStruct((blocks, 1, lanes), F32),
        ],
        scratch_shapes=[
            pltpu.VMEM((total, width, 2 * half), BF16),
            pltpu.VMEM((width, lanes), F32),
            pltpu.VMEM((1, lanes), F32),
        ],
        compiler_params=pltpu.CompilerParams(vmem_limit_bytes=VMEM_LIMIT),
        cost_estimate=pl.CostEstimate(
            flops=2 * 2 * lanes * 2 * half * width * blocks * total,
            bytes_accessed=8 * q.size + 8 * k.size,
            transcendentals=lanes * 2 * half * blocks * total,
        ),
    )(meta, q, k, v, start)


def attend_back(meta, q, do, k, v, start, out_t, total_e, scaling):
    _, blocks, half, columns = q.shape
    parts, width = k.shape[0], k.shape[-1]
    heads = columns // width
    lanes = heads * 2 * half
    total = parts * blocks
    row_spec = pl.BlockSpec((2, 1, half, columns), lambda i: (0, i, 0, 0))
    key_spec = pl.BlockSpec(k.shape, lambda i: (0, 0, 0, 0, 0))
    lane_spec = pl.BlockSpec((1, 1, lanes), lambda i: (i, 0, 0))
    return pl.pallas_call(
        functools.partial(attend_back_kernel, factor=scaling * LOG2E, scaling=scaling, heads=heads),
        grid=(blocks,),
        in_specs=[
            pl.BlockSpec(memory_space=pltpu.SMEM),
            row_spec,
            row_spec,
            key_spec,
            key_spec,
            lane_spec,
            pl.BlockSpec((1, width, lanes), lambda i: (i, 0, 0)),
            lane_spec,
        ],
        out_specs=[row_spec, key_spec, key_spec],
        out_shape=[
            jax.ShapeDtypeStruct(q.shape, F32),
            jax.ShapeDtypeStruct(k.shape, F32),
            jax.ShapeDtypeStruct(k.shape, F32),
        ],
        scratch_shapes=[
            pltpu.VMEM((total, width, 2 * half), BF16),
            pltpu.VMEM((width, lanes), F32),
        ],
        compiler_params=pltpu.CompilerParams(vmem_limit_bytes=VMEM_LIMIT),
        cost_estimate=pl.CostEstimate(
            flops=5 * 2 * lanes * 2 * half * width * blocks * total,
            bytes_accessed=12 * q.size + 16 * k.size,
            transcendentals=lanes * 2 * half * blocks * total,
        ),
    )(meta, q, do, k, v, start, out_t, total_e)


def prepare_kernel(x_ref, w_ref, cos_ref, sin_ref, gq_ref, gk_ref, q_ref, kv_ref, raw_ref, *, heads, width):
    acc = jnp.dot(x_ref[...], w_ref[...], preferred_element_type=F32)
    raw_ref[...] = acc[:, : (heads + 1) * width]
    for h in range(heads + 1):
        part = acc[:, h * width : (h + 1) * width]
        normed = part * lax.rsqrt(jnp.mean(part * part, axis=-1, keepdims=True) + EPS)
        scaled = normed * (gq_ref if h < heads else gk_ref)[...]
        turned = (scaled * cos_ref[...] + pltpu.roll(scaled, width // 2, 1) * sin_ref[...]).astype(BF16)
        if h < heads:
            q_ref[:, h * width : (h + 1) * width] = turned
        else:
            kv_ref[:, :width] = turned
    kv_ref[:, width:] = acc[:, (heads + 1) * width :].astype(BF16)


def prepare(x, w, cos, sin, gain_q, gain_k, heads):
    tokens, depth = x.shape
    width, tile = gain_q.shape[1], 256
    row = lambda n: pl.BlockSpec((tile, n), lambda i: (i, 0))
    fixed = lambda a: pl.BlockSpec(a.shape, lambda i: (0, 0))
    return pl.pallas_call(
        functools.partial(prepare_kernel, heads=heads, width=width),
        grid=(tokens // tile,),
        in_specs=[row(depth), fixed(w), row(width), row(width), fixed(gain_q), fixed(gain_k)],
        out_specs=[row(heads * width), row(2 * width), row((heads + 1) * width)],
        out_shape=[
            jax.ShapeDtypeStruct((tokens, heads * width), BF16),
            jax.ShapeDtypeStruct((tokens, 2 * width), BF16),
            jax.ShapeDtypeStruct((tokens, (heads + 1) * width), F32),
        ],
        compiler_params=pltpu.CompilerParams(vmem_limit_bytes=VMEM_LIMIT),
        cost_estimate=TINY_COST,
    )(x, w, cos, sin, gain_q, gain_k)


def prepare_back_kernel(
    dq_ref, dk_ref, dv_ref, got_ref, raw_ref, cos_ref, sin_ref, gq_ref, gk_ref, w_ref, d_ref, p_ref, g_ref, *, heads, width
):
    @pl.when(pl.program_id(0) == 0)
    def _():
        g_ref[...] = jnp.zeros_like(g_ref)

    got = got_ref[...].astype(F32)
    for h in range(heads + 1):
        at = slice(h * width, (h + 1) * width)
        grad = dq_ref[:, at] if h < heads else dk_ref[0] + got[:, :width]
        gain = (gq_ref if h < heads else gk_ref)[...]
        raw = raw_ref[:, at]
        inverse = lax.rsqrt(jnp.mean(raw * raw, axis=-1, keepdims=True) + EPS)
        normed = raw * inverse
        turned = grad * cos_ref[...] - pltpu.roll(grad, width // 2, 1) * sin_ref[...]
        row = 0 if h < heads else 1
        g_ref[row : row + 1, :] += jnp.sum(turned * normed, axis=0, keepdims=True)
        scaled = turned * gain
        d_ref[:, at] = (inverse * (scaled - normed * jnp.mean(scaled * normed, axis=-1, keepdims=True))).astype(BF16)
    d_ref[:, (heads + 1) * width :] = (dv_ref[0] + got[:, width:]).astype(BF16)
    p_ref[...] = nt(d_ref[...], w_ref[...]).astype(BF16)


def prepare_back(dq, dk, dv, got, raw, cos, sin, gain_q, gain_k, w, heads):
    tokens, width, tile = dq.shape[0], gain_q.shape[1], 256
    row = lambda n: pl.BlockSpec((tile, n), lambda i: (i, 0))
    part = pl.BlockSpec((1, tile, width), lambda i: (0, i, 0))
    fixed = lambda a: pl.BlockSpec(a.shape, lambda i: (0, 0))
    return pl.pallas_call(
        functools.partial(prepare_back_kernel, heads=heads, width=width),
        grid=(tokens // tile,),
        in_specs=[
            row(heads * width),
            part,
            part,
            row(2 * width),
            row((heads + 1) * width),
            row(width),
            row(width),
            fixed(gain_q),
            fixed(gain_k),
            fixed(w),
        ],
        out_specs=[row(w.shape[1]), row(w.shape[0]), pl.BlockSpec((8, width), lambda i: (0, 0))],
        out_shape=[
            jax.ShapeDtypeStruct((tokens, w.shape[1]), BF16),
            jax.ShapeDtypeStruct((tokens, w.shape[0]), BF16),
            jax.ShapeDtypeStruct((8, width), F32),
        ],
        compiler_params=pltpu.CompilerParams(vmem_limit_bytes=VMEM_LIMIT),
        cost_estimate=TINY_COST,
    )(dq, dk, dv, got, raw, cos, sin, gain_q, gain_k, w)


def place_of_block(blk, bit_order, p):
    return blk ^ sum(((p >> i) & 1) << b for i, b in enumerate(bit_order))


def enter_kernel(blk_ref, *refs, bit_order, normed):
    if normed:
        mine_ref, other_ref, gain_ref, low_ref, out_ref, gains_ref = refs
    else:
        mine_ref, low_ref = refs
    rows, width = mine_ref.shape
    n = width >> len(bit_order)
    for p in range(1 << len(bit_order)):
        at = pl.ds(pl.multiple_of(place_of_block(blk_ref[0], bit_order, p) * n, n), n)
        low_ref[:rows, p * n : (p + 1) * n] = mine_ref[:, at]
        if normed:
            low_ref[rows:, p * n : (p + 1) * n] = other_ref[:, at]
            gains_ref[:, p * n : (p + 1) * n] = gain_ref[:, at]
    if normed:
        values = low_ref[...].astype(F32)
        inverse = lax.rsqrt(jnp.mean(values * values, axis=-1, keepdims=True) + EPS)
        out_ref[...] = (values * inverse * gains_ref[:1]).astype(BF16)


def enter(blk, bit_order, mine, other=None, gain=None):
    rows, width = mine.shape
    normed = gain is not None
    total = (2 * rows if normed else rows, width)
    vmem = pl.BlockSpec(memory_space=pltpu.VMEM)
    operands = [mine, other, gain] if normed else [mine]
    return pl.pallas_call(
        functools.partial(enter_kernel, bit_order=bit_order, normed=normed),
        in_specs=[pl.BlockSpec(memory_space=pltpu.SMEM), *[vmem] * len(operands)],
        out_specs=[vmem] * (3 if normed else 1),
        out_shape=[
            *[jax.ShapeDtypeStruct(total, BF16)] * (2 if normed else 1),
            *([jax.ShapeDtypeStruct(gain.shape, F32)] if normed else []),
        ],
        compiler_params=pltpu.CompilerParams(vmem_limit_bytes=VMEM_LIMIT),
        cost_estimate=TINY_COST,
    )(blk[None].astype(jnp.int32), *operands)


def assemble_kernel(place_ref, *refs, sources, widths):
    ins, outs = refs[: 2 * sources], refs[2 * sources :]
    place, k, at = place_ref[0], 0, 0
    for own_ref, got_ref in zip(ins[::2], ins[1::2]):
        f, at = own_ref.shape[0], 0
        while at < own_ref.shape[1]:
            w, cut = widths[k], slice(at, at + widths[k])
            mine = pl.ds(pl.multiple_of(place * w, w), w)
            theirs = pl.ds(pl.multiple_of((1 - place) * w, w), w)
            outs[k][:, mine] = own_ref[:, cut] + got_ref[:f, cut].astype(F32)
            outs[k][:, theirs] = got_ref[f : 2 * f, cut].astype(F32) + got_ref[2 * f :, cut].astype(F32)
            at += w
            k += 1


def assemble(place, sources, widths):
    vmem = pl.BlockSpec(memory_space=pltpu.VMEM)
    flat = [a for pair in sources for a in pair]
    return pl.pallas_call(
        functools.partial(assemble_kernel, sources=len(sources), widths=widths),
        in_specs=[pl.BlockSpec(memory_space=pltpu.SMEM), *[vmem] * len(flat)],
        out_specs=[vmem] * len(widths),
        out_shape=[jax.ShapeDtypeStruct((sources[0][0].shape[0], 2 * w), F32) for w in widths],
        compiler_params=pltpu.CompilerParams(vmem_limit_bytes=VMEM_LIMIT),
        cost_estimate=TINY_COST,
    )(place[None].astype(jnp.int32), *flat)


def back_kernel(*refs):
    *ins, out_ref = refs
    n = len(ins) // 2
    out_ref[...] = sum(nt(d[...], w[...]) for d, w in zip(ins[:n], ins[n:])).astype(BF16)


def back_through(grads, weights):
    tokens, depth, tile = grads[0].shape[0], weights[0].shape[0], 256
    return pl.pallas_call(
        back_kernel,
        grid=(depth // tile,),
        in_specs=[
            *[pl.BlockSpec(g.shape, lambda i: (0, 0)) for g in grads],
            *[pl.BlockSpec((tile, w.shape[1]), lambda i: (i, 0)) for w in weights],
        ],
        out_specs=pl.BlockSpec((tokens, tile), lambda i: (0, i)),
        out_shape=jax.ShapeDtypeStruct((tokens, depth), BF16),
        compiler_params=pltpu.CompilerParams(vmem_limit_bytes=VMEM_LIMIT),
        cost_estimate=TINY_COST,
    )(*grads, *weights)


def weight_grad_kernel(a_ref, b_ref, keep_ref, away_ref):
    product = tn(a_ref[...], b_ref[...])
    first = pl.program_id(0) < pl.num_programs(0) // 2

    @pl.when(first)
    def _():
        keep_ref[...] = product

    @pl.when(jnp.logical_not(first))
    def _():
        away_ref[...] = product.astype(BF16)


def weight_grad(a, b):
    tokens, depth = a.shape
    n, tile = b.shape[1], 256
    steps = depth // tile
    return pl.pallas_call(
        weight_grad_kernel,
        grid=(steps,),
        in_specs=[
            pl.BlockSpec((tokens, tile), lambda i: (0, i)),
            pl.BlockSpec((tokens, n), lambda i: (0, 0)),
        ],
        out_specs=[
            pl.BlockSpec((tile, n), lambda i: (jnp.minimum(i, steps // 2 - 1), 0)),
            pl.BlockSpec((tile, n), lambda i: (jnp.maximum(i - steps // 2, 0), 0)),
        ],
        out_shape=[
            jax.ShapeDtypeStruct((depth // 2, n), F32),
            jax.ShapeDtypeStruct((depth // 2, n), BF16),
        ],
        compiler_params=pltpu.CompilerParams(vmem_limit_bytes=VMEM_LIMIT),
        cost_estimate=TINY_COST,
    )(a, b)


def remote(src, dst, send, recv, target):
    copy = pltpu.make_async_remote_copy(
        src_ref=src, dst_ref=dst, send_sem=send, recv_sem=recv, device_id=target, device_id_type=pl.DeviceIdType.MESH
    )
    copy.start()
    return copy


class Plan:
    def __init__(self):
        self.inputs, self.shapes, self.aliases, self.jobs = [], [], {}, []

    def read(self, array):
        self.inputs.append(array)
        return ("in", len(self.inputs) - 1)

    def fresh(self, shape, dtype):
        self.shapes.append(jax.ShapeDtypeStruct(shape, dtype))
        return ("out", len(self.shapes) - 1)

    def through(self, array):
        self.inputs.append(array)
        self.aliases[len(self.inputs) - 1] = len(self.shapes)
        return self.fresh(array.shape, array.dtype)

    def copy(self, src, dst, mask, after=None, point=0):
        self.jobs.append((src, dst, mask, after, point, None))
        return len(self.jobs) - 1

    def local(self, src, dst, shape, point=0):
        self.jobs.append((src, dst, 0, None, point, shape))
        return len(self.jobs) - 1


class Fill:
    def __init__(self, inputs, outputs, step, point):
        self.inputs, self.outputs, self.step, self.point = inputs, outputs, step, point

    def scratch(self):
        shapes = [pltpu.VMEM(a.shape, a.dtype) for a in (*self.inputs, *self.outputs)]
        return [*shapes, pltpu.SemaphoreType.DMA((len(shapes),))]


def fill_weight_grad(a, b, point):
    depth, n, tile = a.shape[1], b.shape[1], 256
    half = depth // 2

    def step(ins, outs):
        (a_ref, b_ref), (keep_ref, away_ref) = ins, outs

        def one(i, carry):
            at = pl.ds(pl.multiple_of(i * tile, tile), tile)
            keep_ref[at, :] = tn(a_ref[:, at], b_ref[...])
            far = pl.ds(pl.multiple_of(half + i * tile, tile), tile)
            away_ref[at, :] = tn(a_ref[:, far], b_ref[...]).astype(BF16)
            return carry

        lax.fori_loop(0, half // tile, one, 0)

    outputs = [jax.ShapeDtypeStruct((half, n), F32), jax.ShapeDtypeStruct((half, n), BF16)]
    return Fill([a, b], outputs, step, point)


def fill_back(grad, weight, point):
    tokens, depth, tile = grad.shape[0], weight.shape[0], 256

    def step(ins, outs):
        (g_ref, w_ref), (out_ref,) = ins, outs

        def one(i, carry):
            at = pl.ds(pl.multiple_of(i * tile, tile), tile)
            out_ref[:, at] = nt(g_ref[...], w_ref[at, :]).astype(BF16)
            return carry

        lax.fori_loop(0, depth // tile, one, 0)

    return Fill([grad, weight], [jax.ShapeDtypeStruct((tokens, depth), BF16)], step, point)


def fill_product(left, right, point):
    tokens, n, tile = left.shape[0], right.shape[1], 256

    def step(ins, outs):
        (l_ref, r_ref), (out_ref,) = ins, outs

        def one(i, carry):
            at = pl.ds(pl.multiple_of(i * tile, tile), tile)
            out_ref[at, :] = nn(l_ref[at, :], r_ref[...])
            return carry

        lax.fori_loop(0, tokens // tile, one, 0)

    return Fill([left, right], [jax.ShapeDtypeStruct((tokens, n), F32)], step, point)


def run(plan, main, collective_id, greeted=(), fills=(), limit=None):
    inputs, in_specs, out_shapes, out_specs, scratch, body, own_limit = main
    limit = limit or own_limit + sum(math.prod(s.shape) * s.dtype.itemsize for f in fills for s in f.scratch()[:-1])
    f_in, f_out = [a for f in fills for a in f.inputs], [a for f in fills for a in f.outputs]
    n_in, n_out = len(inputs), len(out_shapes)
    m_in, m_out = len(plan.inputs), len(plan.shapes)
    jobs = plan.jobs
    local_jobs = [i for i, job in enumerate(jobs) if not job[2]]
    masks = sorted({*greeted, *[job[2] for job in jobs if job[2]]} - {1 << TENSOR_BIT})
    any_spec = pl.BlockSpec(memory_space=pltpu.HBM)

    def kernel(*refs):
        main_in, refs = refs[:n_in], refs[n_in:]
        plan_in, refs = refs[:m_in], refs[m_in:]
        fill_in, refs = refs[: len(f_in)], refs[len(f_in) :]
        main_out, refs = refs[:n_out], refs[n_out:]
        plan_out, refs = refs[:m_out], refs[m_out:]
        fill_out, refs = refs[: len(f_out)], refs[len(f_out) :]
        send, recv, *rest = refs
        bounce = dict(zip(local_jobs, rest))
        rest = rest[len(local_jobs) :]
        parts = []
        for f in fills:
            k, m = len(f.inputs), len(f.outputs)
            (*held, sems), rest = rest[: k + m + 1], rest[k + m + 1 :]
            loads = [pltpu.make_async_copy(fill_in[i], held[i], sems.at[i]) for i in range(k)]
            stores = [pltpu.make_async_copy(held[k + i], fill_out[i], sems.at[k + i]) for i in range(m)]
            fill_in, fill_out = fill_in[k:], fill_out[m:]
            for copy in loads:
                copy.start()
            parts.append((f, held[:k], held[k:], loads, stores))

        def compute(point):
            for f, ins, outs, loads, stores in parts:
                if f.point == point:
                    for copy in loads:
                        copy.wait()
                    f.step(ins, outs)
                    for copy in stores:
                        copy.start()

        blk, head = lax.axis_index("blk"), lax.axis_index("head")
        core, near, across = (blk, head ^ 1), (blk, head ^ 2), (blk ^ (1 << TENSOR_BIT), head)
        barrier = pltpu.get_barrier_semaphore()
        partners = [core, near, across, *[(blk ^ m, head) for m in masks]]
        for target in partners:
            pl.semaphore_signal(barrier, inc=1, device_id=target, device_id_type=pl.DeviceIdType.MESH)
        pl.semaphore_wait(barrier, len(partners))
        started, arrived, halfway = {}, set(), []

        def arrive(i):
            if i not in arrived:
                arrived.add(i)
                (started[i].wait_recv if jobs[i][2] else started[i].wait)()

        def part(side):
            (kind, index), cut = side
            if kind == "fill":
                return cut(parts[index[0]][2][index[1]])
            return cut((plan_in if kind == "in" else plan_out)[index])

        def issue(point):
            for i in list(halfway):
                started[i].wait()
                started[i] = pltpu.make_async_copy(bounce[i], part(jobs[i][1]), recv.at[i])
                started[i].start()
                halfway.remove(i)
            for i, (src, dst, mask, after, at, shape) in enumerate(jobs):
                if i in started or (at != point and point is not None):
                    continue
                if after is not None:
                    arrive(after)
                if mask:
                    started[i] = remote(part(src), part(dst), send.at[i], recv.at[i], (blk ^ mask, head))
                else:
                    started[i] = pltpu.make_async_copy(part(src), bounce[i], send.at[i])
                    started[i].start()
                    halfway.append(i)

        point = 0
        for _ in body((core, near, across), main_in, main_out, rest):
            issue(point)
            compute(point)
            point += 1
        issue(None)
        issue(None)
        for i in range(len(jobs)):
            arrive(i)
            if jobs[i][2]:
                started[i].wait_send()
        for *_, stores in parts:
            for copy in stores:
                copy.wait()

    results = pl.pallas_call(
        kernel,
        out_shape=[*out_shapes, *plan.shapes, *f_out],
        in_specs=[*in_specs, *[any_spec] * (m_in + len(f_in))],
        out_specs=[*out_specs, *[any_spec] * (m_out + len(f_out))],
        scratch_shapes=[
            pltpu.SemaphoreType.DMA((max(1, len(jobs)),)),
            pltpu.SemaphoreType.DMA((max(1, len(jobs)),)),
            *[pltpu.VMEM(jobs[i][5], BF16) for i in local_jobs],
            *[s for f in fills for s in f.scratch()],
            *scratch,
        ],
        input_output_aliases={n_in + i: n_out + o for i, o in plan.aliases.items()},
        compiler_params=pltpu.CompilerParams(
            collective_id=collective_id, has_side_effects=True, vmem_limit_bytes=limit
        ),
        cost_estimate=TINY_COST,
    )(*inputs, *plan.inputs, *f_in)
    return results[:n_out], results[n_out:]


def spread_main(flat, chunk):
    rows, width = flat.shape[0] // 2, flat.shape[1]
    pieces = width // chunk

    def body(partners, ins, outs, scratch):
        core, near, across = partners
        (s_ref,), (o_ref,), (hold, local_sem, send, recv) = ins, outs, scratch
        first = remote(s_ref, o_ref.at[0, :, 0, 1], send.at[0], recv.at[0], near)
        second = [
            remote(
                s_ref.at[:, :, pl.ds(i * chunk, chunk)],
                o_ref.at[0, :, 1, 0, :, pl.ds((i ^ 1) * chunk, chunk)],
                send.at[6 + i],
                recv.at[6 + i],
                across,
            )
            for i in range(pieces)
        ]
        third = remote(s_ref, o_ref.at[1, :, 0, 0], send.at[1], recv.at[1], core)
        held = pltpu.make_async_copy(s_ref, hold, local_sem.at[0])
        held.start()
        yield
        held.wait()
        own = pltpu.make_async_copy(hold, o_ref.at[0, :, 0, 0], local_sem.at[1])
        own.start()
        for copy in second:
            copy.wait_recv()
        fourth = remote(o_ref.at[0, :, 1, 0], o_ref.at[0, :, 1, 1], send.at[2], recv.at[2], near)
        fifth = remote(o_ref.at[0, :, 1, 0], o_ref.at[1, :, 1, 0], send.at[3], recv.at[3], core)
        yield
        first.wait_recv()
        sixth = remote(o_ref.at[0, :, 0, 1], o_ref.at[1, :, 0, 1], send.at[4], recv.at[4], core)
        yield
        fourth.wait_recv()
        seventh = remote(o_ref.at[0, :, 1, 1], o_ref.at[1, :, 1, 1], send.at[5], recv.at[5], core)
        yield
        own.wait()
        for copy in (first, *second, third, fourth, fifth, sixth, seventh):
            copy.wait_send()
        for copy in (third, fifth, sixth, seventh):
            copy.wait_recv()

    any_spec = pl.BlockSpec(memory_space=pltpu.HBM)
    return (
        [flat.reshape(2, rows, width)],
        [any_spec],
        [jax.ShapeDtypeStruct((2, 2, 2, 2, rows, width), flat.dtype)],
        [any_spec],
        [
            pltpu.VMEM((2, rows, width), flat.dtype),
            pltpu.SemaphoreType.DMA((2,)),
            pltpu.SemaphoreType.DMA((6 + pieces,)),
            pltpu.SemaphoreType.DMA((6 + pieces,)),
        ],
        body,
        8 * MIB,
    )


def gather_main(partial, chunk, extra, outs_like, finish):
    rows, width = partial.shape[0] // 16, partial.shape[1]
    share = (2, rows, width)
    pieces = width // chunk

    def body(partners, ins, outs, scratch):
        core, near, across = partners
        p_ref, *extra_refs = ins
        core_in, out_y, in_y, out_t, in_t, hold, send, recv = scratch
        order = ((1, 1), (0, 1), (1, 0), (0, 0))
        from_core = [
            remote(p_ref.at[1, :, t, y], core_in.at[i], send.at[i], recv.at[i], core) for i, (t, y) in enumerate(order)
        ]
        from_y = []
        for i in range(2):
            t, y = order[i]
            from_core[i].wait_recv()
            out_y[i] = (p_ref[0, :, t, y].astype(F32) + core_in[i].astype(F32)).astype(BF16)
            from_y.append(remote(out_y.at[i], in_y.at[i], send.at[4 + i], recv.at[4 + i], near))
        yield
        from_core[2].wait_recv()
        hold[...] = p_ref[0, :, 1, 0].astype(F32) + core_in[2].astype(F32)
        from_y[0].wait_recv()
        for i in range(pieces):
            a, b = slice(i * chunk, (i + 1) * chunk), slice((i ^ 1) * chunk, ((i ^ 1) + 1) * chunk)
            out_t[:, :, b] = (hold[:, :, a] + in_y[0, :, :, a].astype(F32)).astype(BF16)
        from_t = remote(out_t, in_t, send.at[6], recv.at[6], across)
        yield
        from_core[3].wait_recv()
        hold[...] = p_ref[0, :, 0, 0].astype(F32) + core_in[3].astype(F32)
        from_y[1].wait_recv()
        hold[...] += in_y[1].astype(F32)
        yield
        from_t.wait_recv()
        hold[...] += in_t[...].astype(F32)
        finish(hold, extra_refs, outs)
        for copy in (*from_core, *from_y, from_t):
            copy.wait_send()

    vmem_spec = pl.BlockSpec(memory_space=pltpu.VMEM)
    return (
        [partial.reshape(2, 2, 2, 2, rows, width), *extra],
        [vmem_spec] * (1 + len(extra)),
        outs_like,
        [vmem_spec] * len(outs_like),
        [
            pltpu.VMEM((4, *share), BF16),
            pltpu.VMEM((2, *share), BF16),
            pltpu.VMEM((2, *share), BF16),
            pltpu.VMEM(share, BF16),
            pltpu.VMEM(share, BF16),
            pltpu.VMEM(share, F32),
            pltpu.SemaphoreType.DMA((7,)),
            pltpu.SemaphoreType.DMA((7,)),
        ],
        body,
        24 * MIB,
    )


def inverse_rms(values):
    return lax.rsqrt(jnp.mean(values * values, axis=-1, keepdims=True) + EPS)


def finish_middle(total, extra, outs):
    (low_ref, gain_ref), (middle_ref, normed_ref) = extra, outs
    for m in range(2):
        middle = low_ref[m].astype(F32) + total[m]
        middle_ref[m] = middle
        normed_ref[m] = (middle * inverse_rms(middle) * gain_ref[...]).astype(BF16)


def norm_grad(total, values, gain, gain_grad_ref, m):
    inverse = inverse_rms(values)
    normal = values * inverse
    part = jnp.sum(total * normal, axis=0, keepdims=True)
    gain_grad_ref[...] = part if m == 0 else gain_grad_ref[...] + part
    scaled = total * gain
    return inverse * (scaled - normal * jnp.mean(scaled * normal, axis=-1, keepdims=True))


def finish_mlp_norm(total, extra, outs):
    (cot_ref, middle_ref, gain_ref), (grad_ref, low_ref, gain_grad_ref) = extra, outs
    for m in range(2):
        grad = cot_ref[m].astype(F32) + norm_grad(total[m], middle_ref[m], gain_ref[...], gain_grad_ref, m)
        grad_ref[m] = grad
        low_ref[m] = grad.astype(BF16)


def store_ungrouped(value, ref, blk, bit_order, lead=()):
    n = value.shape[-1] >> len(bit_order)
    for p in range(1 << len(bit_order)):
        block = value[:, p * n : (p + 1) * n]
        if bit_order and n % 128 == 0:
            at = pl.ds(pl.multiple_of(place_of_block(blk, bit_order, p) * n, n), n)
        else:
            at = pl.ds(p * n, n)
        ref[(*lead, slice(None), at)] = block.astype(ref.dtype)


def finish_mixed(total, extra, outs, *, bit_order):
    (middle_ref,), (mixed_ref,) = extra, outs
    blk = lax.axis_index("blk")
    for m in range(2):
        store_ungrouped(middle_ref[m] + total[m], mixed_ref, blk, bit_order, (m,))


def finish_input(total, extra, outs, *, bit_order):
    (low_ref, mid_ref, gain_ref), (own_ref, away_ref, gain_grad_ref) = extra, outs
    blk = lax.axis_index("blk")
    for m in range(2):
        grad = mid_ref[m] + norm_grad(total[m], low_ref[m].astype(F32), gain_ref[...], gain_grad_ref, m)
        store_ungrouped(grad, own_ref if m == 0 else away_ref, blk, bit_order)


def total_main(values):
    rows, width = values.shape
    rounds = 2 + lax.axis_size("blk").bit_length() - 1

    def body(partners, ins, outs, scratch):
        (v_ref,), (o_ref,) = ins, outs
        out_buf, in_buf, send, recv = scratch
        blk, head = lax.axis_index("blk"), lax.axis_index("head")
        o_ref[...] = v_ref[...]
        yield
        for i in range(rounds):
            target = (blk, head ^ (1 << i)) if i < 2 else (blk ^ (1 << (i - 2)), head)
            out_buf[i] = o_ref[...]
            copy = remote(out_buf.at[i], in_buf.at[i], send.at[i], recv.at[i], target)
            copy.wait_recv()
            o_ref[...] += in_buf[i]
            copy.wait_send()
        yield

    vmem_spec = pl.BlockSpec(memory_space=pltpu.VMEM)
    return (
        [values],
        [vmem_spec],
        [jax.ShapeDtypeStruct(values.shape, F32)],
        [vmem_spec],
        [
            pltpu.VMEM((rounds, rows, width), F32),
            pltpu.VMEM((rounds, rows, width), F32),
            pltpu.SemaphoreType.DMA((rounds,)),
            pltpu.SemaphoreType.DMA((rounds,)),
        ],
        body,
        8 * MIB,
    )


def local(
    hidden_in,
    lengths,
    query_weight,
    key_matrix,
    value_matrix,
    out_weight,
    gate_weight,
    up_weight,
    down_weight,
    attn_gain,
    query_gain,
    key_gain,
    mlp_gain,
    cotangent,
):
    ring = lax.axis_size("blk")
    bits = ring.bit_length() - 1
    batch_bit = bits - 1
    extra_bits = [i for i in range(bits) if i not in (TENSOR_BIT, SEQ_BIT, batch_bit)]
    seq_bits = [SEQ_BIT, *extra_bits]
    parts = 1 << len(seq_bits)
    bit_order = [batch_bit, TENSOR_BIT, SEQ_BIT, *extra_bits]
    b_mask, t_mask, x_mask = 1 << batch_bit, 1 << TENSOR_BIT, 1 << SEQ_BIT
    blk, head = lax.axis_index("blk"), lax.axis_index("head")
    batch, tensor = bit_of(blk, batch_bit), bit_of(blk, TENSOR_BIT)

    local_rows, width = hidden_in.shape[1:]
    block_rows = local_rows * lax.axis_size("head")
    half = block_rows // 2
    row_features = width // ring
    head_size = query_gain.shape[0]
    scaling = head_size ** (-0.5)
    tokens = 16 * local_rows
    heads = query_weight.shape[1] // (2 * head_size)
    ff = gate_weight.shape[1] // 2

    def moved(values, place_of):
        axis = values.ndim - 1
        return jnp.concatenate(
            [
                lax.dynamic_slice_in_dim(values, place_of(i) * row_features, row_features, axis)
                for i in range(ring)
            ],
            axis=axis,
        )

    def regroup(values):
        return moved(values, lambda p: blk ^ sum(((p >> i) & 1) << b for i, b in enumerate(bit_order)))

    def ungroup(values):
        return moved(values, lambda n: sum(bit_of(blk ^ n, b) << i for i, b in enumerate(bit_order)))

    def everything(ref):
        return ref

    def mask_of(p):
        return sum(((p >> i) & 1) << b for i, b in enumerate(bit_order))

    def rows_at(p):
        return lambda ref: ref.at[pl.ds(p * row_features, row_features), :]

    def half_cut(n, other):
        def cut(ref):
            place = bit_of(lax.axis_index("blk"), TENSOR_BIT)
            place = 1 - place if other else place
            return ref.at[:, pl.ds(pl.multiple_of(place * n, n), n)]

        return cut

    def send_over(plan, weight, buffer, p, point):
        mask, n = mask_of(p), weight.shape[1] // 2
        plan.copy((plan.read(weight), half_cut(n, mask & t_mask)), (buffer, rows_at(p)), mask, point=point)

    def keep_own(plan, weight, buffer, point, onward=True):
        here, n = plan.read(weight), weight.shape[1] // 2
        if onward:
            plan.copy((here, half_cut(n, 0)), (buffer, rows_at(4)), x_mask, point=point)
        plan.local((here, half_cut(n, 0)), (buffer, rows_at(0)), (row_features, n), point=point)

    def send_on(plan, buffer, places, point, after=None):
        for p in places:
            plan.copy((buffer, rows_at(p)), (buffer, rows_at(p + 4)), x_mask, after=after, point=point)

    def lay(plan, array, buffer, p, point=0, columns=None, onward=False):
        here = plan.read(array)
        cut = (lambda ref: ref.at[:, pl.ds(*columns)]) if columns else everything
        if onward:
            plan.copy((here, cut), (buffer, rows_at(p + 4)), x_mask, point=point)
        plan.local((here, cut), (buffer, rows_at(p)), (row_features, columns[1] if columns else array.shape[1]), point)

    def fresh_for(plan, weights):
        return plan.fresh(buffer_shape(weights), BF16)

    def buffer_shape(weights):
        return (8 * row_features, sum(w.shape[1] for w in weights) // 2)

    def whole_weight(buffer):
        pieces = [buffer]
        for b in extra_bits:
            pieces = pieces + [over_blk(c, 1 << b) for c in pieces]
        return jnp.concatenate(pieces, axis=0) if extra_bits else buffer

    def split_grad(grad):
        for b in reversed(extra_bits):
            n = grad.shape[0] // 2
            grad = grad[:n] + over_blk(grad[n:].astype(BF16), 1 << b).astype(F32)
        n = grad.shape[0] // 2
        return grad[:n], grad[n:].astype(BF16)

    def weight_sum(a, b):
        return split_grad(tn(a, b)) if extra_bits else weight_grad(a, b)

    def fold(plan, source, shape, point=0):
        plan.copy((source, everything), (plan.fresh(shape, BF16), everything), x_mask, point=point)

    def fold_part(plan, source, buffer, start, n, point=0):
        def part(ref):
            return ref.at[:, pl.ds(start, n)]

        plan.copy((source, part), (buffer, part), x_mask, point=point)

    def to_settle(keep, got):
        total = keep + got.astype(F32)
        return total[:row_features], total[row_features:].astype(BF16)

    def settle(plan, away, t_point=0):
        out, here = plan.fresh(away.shape, away.dtype), plan.read(away)
        for i, mask in ((0, b_mask), (2, b_mask | t_mask), (1, t_mask)):
            plan.copy((here, rows_at(i)), (out, rows_at(i)), mask, point=t_point if mask == t_mask else 0)

    def settled(sources, column_widths):
        if all(w % 128 == 0 for w in column_widths):
            return assemble(tensor, sources, column_widths)
        f, results = row_features, []
        widths = iter(column_widths)
        for own, got in sources:
            own = own + got[:f].astype(F32)
            other = got[f : 2 * f].astype(F32) + got[2 * f :].astype(F32)
            at = 0
            while at < own.shape[1]:
                w = next(widths)
                results.append(in_order(tensor, own[:, at : at + w], other[:, at : at + w], 1))
                at += w
        return results

    chunk = 2 * row_features
    ids = iter(range(100))

    def spread(flat, plan, fills=(), limit=None):
        (out,), rest = run(plan, spread_main(flat, chunk), next(ids), fills=fills, limit=limit)
        return out.reshape(tokens, width), rest

    share = (2, local_rows, width)

    def gather_sum(partial, plan, extra, outs_like, finish, fills=()):
        return run(plan, gather_main(partial, chunk, extra, outs_like, finish), next(ids), fills=fills)

    def like(shape, dtype):
        return jax.ShapeDtypeStruct(shape, dtype)

    aligned = row_features % 128 == 0
    local_order = bit_order if aligned else []

    def split_batch(rows):
        mine = lax.dynamic_index_in_dim(rows, batch, 0, keepdims=False)
        theirs = lax.dynamic_index_in_dim(rows, 1 - batch, 0, keepdims=False)
        return mine, theirs

    def natural(rows):
        return rows if aligned else ungroup(rows)

    length_row = lax.dynamic_index_in_dim(lengths, batch, 0, keepdims=False)
    doc_ends = jnp.cumsum(length_row)
    batch_flip = jnp.arange(2, dtype=jnp.int32)[:, None] << batch_bit
    tensor_flip = jnp.arange(2, dtype=jnp.int32)[None, :] << TENSOR_BIT
    q_blocks = (blk ^ batch_flip ^ tensor_flip).reshape(4)
    index = jnp.arange(2 * half, dtype=jnp.int32)
    in_block = token_offset(head, index, local_rows).reshape(2, 1, half)
    token_index = q_blocks[None, :, None] * block_rows + in_block
    passed = doc_ends <= token_index[..., None]
    doc_start = jnp.max(jnp.where(passed, doc_ends, 0), axis=-1).astype(jnp.int32)
    position = (token_index - doc_start).reshape(tokens)
    start_lanes = jnp.tile(jnp.transpose(doc_start, (1, 0, 2)).reshape(4, 1, 2 * half), (1, 1, heads))
    k_blocks = q_blocks
    for b in seq_bits:
        k_blocks = jnp.concatenate([k_blocks, k_blocks ^ (1 << b)])
    least_start = jnp.min(doc_start, axis=(0, 2))[:, None]
    last_start = jnp.max(doc_start, axis=(0, 2))[:, None]
    k_first = (k_blocks * block_rows)[None, :]
    none = (k_blocks[None, :] > q_blocks[:, None]) | (k_first + block_rows <= least_start)
    whole = (k_blocks[None, :] < q_blocks[:, None]) & (k_first >= last_start)
    flags = jnp.where(none, 0, jnp.where(whole, 1, 2))
    meta = jnp.concatenate([head[None], q_blocks, k_blocks, flags.reshape(-1)]).astype(jnp.int32)

    inverse_freq = THETA ** (-jnp.arange(head_size // 2, dtype=F32) / (head_size // 2))
    angles = position.astype(F32)[:, None] * inverse_freq[None, :]
    cosine, sine = jnp.cos(angles), jnp.sin(angles)
    cosine = jnp.concatenate([cosine, cosine], axis=1)
    sine = jnp.concatenate([-sine, sine], axis=1)

    def rms(values):
        return lax.rsqrt(jnp.mean(values * values, axis=-1, keepdims=True) + EPS)

    def norm_back(grad, normed, inverse, gain):
        scaled = grad * gain
        return inverse * (scaled - normed * jnp.mean(scaled * normed, axis=-1, keepdims=True))

    gains_in = jnp.stack([attn_gain, mlp_gain]).astype(F32)
    gain_q = query_gain.astype(F32)[None]
    gain_k = key_gain.astype(F32)[None]

    q_columns, k_columns = heads * head_size, head_size
    a_weights = (query_weight, key_matrix, value_matrix)

    def halves(weights, which):
        return jnp.concatenate(
            [lax.dynamic_slice_in_dim(w, which * (w.shape[1] // 2), w.shape[1] // 2, 1) for w in weights], axis=1
        )

    mine, theirs = split_batch(hidden_in)
    other = over_blk(theirs, b_mask)
    a_own, a_other = halves(a_weights, tensor), halves(a_weights, 1 - tensor)
    a_by_t = over_blk(a_other, t_mask)
    a_by_b = over_blk(a_own, b_mask)
    early = over_blk(jnp.concatenate([a_own, halves((down_weight,), tensor)], axis=1), x_mask)
    (mine, other, cosine, sine, start_lanes, meta) = pin((mine, other, cosine, sine, start_lanes, meta))
    if aligned:
        x_low, xa, gains_in = enter(blk, bit_order, mine, other, gains_in)
        gain_a, gain_m = gains_in[0], gains_in[1]
    else:
        gains_in = regroup(gains_in)
        gain_a, gain_m = gains_in[0], gains_in[1]
        x_low = regroup(jnp.concatenate([mine, other], axis=0))
        x_wide = x_low.astype(F32)
        xa = (x_wide * rms(x_wide) * gain_a).astype(BF16)

    plan = Plan()
    a_columns = a_own.shape[1]
    w_a = fresh_for(plan, a_weights)
    by_tb = plan.copy((plan.read(a_other), everything), (w_a, rows_at(3)), b_mask | t_mask)
    lay(plan, a_by_t, w_a, 2, onward=True)
    lay(plan, a_by_b, w_a, 1, onward=True)
    lay(plan, a_own, w_a, 0)
    lay(plan, early, w_a, 4, columns=(0, a_columns))
    here, cot_out = plan.read(cotangent), plan.fresh((2, local_rows, width), BF16)
    plan.copy(
        (here, lambda ref: ref.at[1 - bit_of(lax.axis_index("blk"), batch_bit)]),
        (cot_out, lambda ref: ref.at[1]),
        b_mask,
        point=1,
    )
    plan.local(
        (here, lambda ref: ref.at[bit_of(lax.axis_index("blk"), batch_bit)]),
        (cot_out, lambda ref: ref.at[0]),
        (local_rows, width),
    )
    w_out = fresh_for(plan, (out_weight,))
    send_over(plan, out_weight, w_out, 1, 1)
    send_over(plan, out_weight, w_out, 3, 1)
    send_over(plan, out_weight, w_out, 2, 1)
    keep_own(plan, out_weight, w_out, 0)
    w_down = fresh_for(plan, (down_weight,))
    send_over(plan, down_weight, w_down, 2, 1)
    keep_own(plan, down_weight, w_down, 0, onward=False)
    lay(plan, early, w_down, 4, columns=(a_columns, ff))
    w_gate = fresh_for(plan, (gate_weight,))
    keep_own(plan, gate_weight, w_gate, 1)
    send_on(plan, w_a, (3,), 2, after=by_tb)
    xa, (w_qkv, cot, w_out, w_down, w_gate) = spread(xa, plan, limit=56 * MIB)
    w_qkv = whole_weight(w_qkv)
    cot = cot.reshape(2 * local_rows, width)
    cot = enter(blk, bit_order, cot)[0] if aligned else regroup(cot)
    query, key_value, raw = prepare(xa, w_qkv, cosine, sine, gain_q, gain_k, heads)

    plan = Plan()
    kv_out = plan.fresh(key_value.shape, BF16)
    plan.copy((plan.read(key_value), everything), (kv_out, everything), x_mask)
    w_out = plan.through(w_out)
    send_on(plan, w_out, (1, 2, 3), 0)
    w_down = plan.through(w_down)
    send_over(plan, down_weight, w_down, 1, 0)
    send_over(plan, down_weight, w_down, 3, 0)
    send_on(plan, w_down, (2,), 1)
    w_gate = plan.through(w_gate)
    send_over(plan, gate_weight, w_gate, 2, 1)
    cot_all, (kv_x, w_out, w_down, w_gate) = spread(cot, plan)
    w_out = whole_weight(w_out)
    key_value = [key_value, kv_x]
    for b in extra_bits:
        key_value = key_value + [over_blk(c, 1 << b) for c in key_value]
    key_value = jnp.stack(key_value)
    keys = key_value[..., :head_size].reshape(parts, 2, 4, half, head_size)
    values = key_value[..., head_size:].reshape(parts, 2, 4, half, head_size)
    query = query.reshape(2, 4, half, q_columns)
    attn, attn_t, total_e = attend(meta, query, keys, values, start_lanes, scaling)
    attn = attn.reshape(tokens, q_columns)

    plan = Plan()
    w_down = plan.through(w_down)
    send_on(plan, w_down, (1, 3), 0)
    w_gate = plan.through(w_gate)
    send_over(plan, gate_weight, w_gate, 1, 0)
    send_over(plan, gate_weight, w_gate, 3, 0)
    send_on(plan, w_gate, (2,), 0)
    w_up = fresh_for(plan, (up_weight,))
    send_over(plan, up_weight, w_up, 2, 0)
    keep_own(plan, up_weight, w_up, 1)
    x_low = x_low.reshape(share)
    (middle, xm), (w_down, w_gate, w_up) = gather_sum(
        nt(attn, w_out).astype(BF16),
        plan,
        [x_low, gain_m[None]],
        [like(share, F32), like(share, BF16)],
        finish_middle,
    )
    w_down = whole_weight(w_down)

    plan = Plan()
    w_gate = plan.through(w_gate)
    w_up = plan.through(w_up)
    by_b = len(plan.jobs)
    send_over(plan, up_weight, w_up, 1, 0)
    send_on(plan, w_gate, (1, 3), 0)
    send_on(plan, w_up, (2,), 1)
    by_tb = plan.copy(
        (plan.read(up_weight), half_cut(ff, True)), (w_up, rows_at(3)), b_mask | t_mask, after=by_b, point=2
    )
    send_on(plan, w_up, (1,), 2)
    send_on(plan, w_up, (3,), 3, after=by_tb)
    xm, (w_gate, w_up, d_active) = spread(
        xm.reshape(2 * local_rows, width), plan, [fill_product(cot_all, w_down, 0)]
    )
    w_gate, w_up = whole_weight(w_gate), whole_weight(w_up)
    gate = nn(xm, w_gate)
    up = nn(xm, w_up)
    sig = jax.nn.sigmoid(gate)
    silu = gate * sig
    active = (silu * up).astype(BF16)
    d_gate = (d_active * up * sig * (1.0 + gate * (1.0 - sig))).astype(BF16)
    d_up = (d_active * silu).astype(BF16)

    keep_down, away_down = weight_sum(cot_all, active)
    got_x = over_blk(away_down, x_mask)
    (d_gate, d_up, away_down) = pin((d_gate, d_up, away_down))
    ff_cut = ff // 2
    plan, fills = Plan(), []
    if extra_bits:
        keep_gate, away_gate = weight_sum(xm, d_gate)
        keep_up, away_up = weight_sum(xm, d_up)
        source, point = plan.read(away_gate), 0
    else:
        fills = [fill_weight_grad(xm, d_gate, 0), fill_weight_grad(xm, d_up, 1)]
        source, point = ("fill", (0, 1)), 1
    gate_x = plan.fresh((4 * row_features, ff), BF16)
    fold_part(plan, source, gate_x, 0, ff_cut, point)
    (d_middle, d_mid, gain_m_grad), (gate_x, *filled) = gather_sum(
        back_through((d_gate, d_up), (w_gate, w_up)),
        plan,
        [cot.reshape(share), middle, gain_m[None]],
        [like(share, F32), like(share, BF16), like((1, width), F32)],
        finish_mlp_norm,
        fills,
    )
    if filled:
        keep_gate, away_gate, keep_up, away_up = filled
    (d_mid, got_x) = pin((d_mid, got_x))
    own_down, away_down = to_settle(keep_down, got_x)

    plan = Plan()
    settle(plan, away_down, 1)
    gate_x = plan.through(gate_x)
    fold_part(plan, plan.read(away_gate), gate_x, ff_cut, ff - ff_cut)
    up_x = plan.fresh(away_up.shape, BF16)
    fold_part(plan, plan.read(away_up), up_x, 0, ff_cut)
    d_mid_all, (got_down, gate_x, up_x, mixed_partial) = spread(
        d_mid.reshape(2 * local_rows, width), plan, [fill_back(active, w_down, 0)]
    )
    (g_down,) = settled([(own_down, got_down)], (ff,))
    own_gate, away_gate = to_settle(keep_gate, gate_x)
    d_attn = nn(d_mid_all, w_out).astype(BF16).reshape(2, 4, half, q_columns)
    d_query, d_key, d_value = attend_back(
        meta, query, d_attn, keys, values, start_lanes, attn_t, total_e, scaling
    )
    d_key = d_key.reshape(parts, tokens, head_size)
    d_value = d_value.reshape(parts, tokens, head_size)
    for b in reversed(extra_bits):
        n = d_key.shape[0] // 2
        d_key = d_key[:n] + over_blk(d_key[n:].astype(BF16), 1 << b).astype(F32)
        d_value = d_value[:n] + over_blk(d_value[n:].astype(BF16), 1 << b).astype(F32)

    plan = Plan()
    away_kv = jnp.concatenate([d_key[1], d_value[1]], axis=1).astype(BF16)
    fold(plan, plan.read(away_kv), away_kv.shape)
    settle(plan, away_gate)
    up_x = plan.through(up_x)
    fold_part(plan, plan.read(away_up), up_x, ff_cut, ff - ff_cut)
    (mixed,), (got_kv, got_gate, up_x, *filled) = gather_sum(
        mixed_partial,
        plan,
        [middle],
        [like(share, BF16)],
        functools.partial(finish_mixed, bit_order=local_order),
        [] if extra_bits else [fill_weight_grad(d_mid_all, attn, 0)],
    )
    keep_out, away_out = filled if filled else weight_sum(d_mid_all, attn)
    (g_gate,) = settled([(own_gate, got_gate)], (ff,))
    own_up, away_up = to_settle(keep_up, up_x)
    mixed = natural(mixed)
    mixed_got = over_blk(mixed[1], b_mask)
    d_qkv, d_xa_partial, gains_qk = prepare_back(
        d_query.reshape(tokens, q_columns), d_key, d_value, got_kv, raw, cosine, sine, gain_q, gain_k, w_qkv, heads
    )
    (d_xa_partial, mixed_got) = pin((d_xa_partial, mixed_got))

    plan, fills = Plan(), []
    settle(plan, away_up)
    fold(plan, plan.read(away_out), away_out.shape)
    if extra_bits:
        keep_qkv, away_qkv = weight_sum(xa, d_qkv)
        fold(plan, plan.read(away_qkv), away_qkv.shape)
    else:
        fills = [fill_weight_grad(xa, d_qkv, 0)]
        fold(plan, ("fill", (0, 1)), (4 * row_features, a_columns), 1)
    (input_own, input_away, gain_a_grad), (got_up, out_x, got, *filled) = gather_sum(
        d_xa_partial,
        plan,
        [x_low, d_middle, gain_a[None]],
        [like((local_rows, width), F32), like((local_rows, width), BF16), like((1, width), F32)],
        functools.partial(finish_input, bit_order=local_order),
        fills,
    )
    if filled:
        keep_qkv = filled[0]
    own_out, away_out = to_settle(keep_out, out_x)
    (g_up,) = settled([(own_up, got_up)], (ff,))
    own_qkv, away_qkv = to_settle(keep_qkv, got)

    plan = Plan()
    settle(plan, away_qkv)
    settle(plan, away_out)
    input_got = plan.fresh((local_rows, width), BF16)
    plan.copy((plan.read(natural(input_away)), everything), (input_got, everything), b_mask)
    sums = jnp.concatenate([ungroup(gain_a_grad[0]), gains_qk[0], gains_qk[1], ungroup(gain_m_grad[0])])
    (sums,), (got_a, got_o, input_got) = run(
        plan, total_main(sums.reshape(-1, 128)), next(ids), [1 << i for i in range(bits)]
    )
    g_query, g_key, g_value, g_out = settled(
        [(own_qkv, got_a), (own_out, got_o)], (q_columns, k_columns, k_columns, q_columns)
    )
    mixed = in_order(batch, mixed[:1], mixed_got[None], 0)
    input_grad = in_order(batch, natural(input_own)[None], input_got.astype(F32)[None], 0)
    gains = jnp.split(sums.reshape(-1), [width, width + head_size, width + 2 * head_size])
    return (
        mixed,
        input_grad,
        g_query,
        g_key,
        g_value,
        g_out,
        g_gate,
        g_up,
        g_down,
        *gains,
    )


def solution(mesh):
    rows = P(None, ("blk", "head"), None)
    weight = P("blk", "head")
    return jax.shard_map(
        local,
        mesh=mesh,
        in_specs=(rows, P(), *([weight] * 7), P(), P(), P(), P(), rows),
        out_specs=(rows, rows, *([weight] * 7), P(), P(), P(), P()),
        check_vma=False,
    )
```

```python
import functools
import math

import jax
import jax.numpy as jnp
from jax import lax
from jax.experimental import pallas as pl
from jax.experimental.pallas import tpu as pltpu
from jax.sharding import PartitionSpec as P

EPS = 1e-06
THETA = 1000000.0
LOG2E = 1.4426950408889634
F32 = jnp.float32
BF16 = jnp.bfloat16

MIB = 1024 * 1024
TINY_COST = pl.CostEstimate(flops=0, bytes_accessed=0, transcendentals=0)
VMEM_LIMIT = 32 * MIB
TENSOR_BIT = 1
SEQ_BIT = 0


def nt(a, b):
    return lax.dot_general(a, b, (((1,), (1,)), ((), ())), preferred_element_type=F32)


def tn(a, b):
    return lax.dot_general(a, b, (((0,), (0,)), ((), ())), preferred_element_type=F32)


def nn(a, b):
    return jnp.dot(a, b, preferred_element_type=F32)


def bit_of(value, bit):
    return (value >> bit) & 1


def over_blk(value, mask):
    count = lax.axis_size("blk")
    return lax.ppermute(value, "blk", [(i, i ^ mask) for i in range(count)])


def over_head(value, mask):
    count = lax.axis_size("head")
    return lax.ppermute(value, "head", [(i, i ^ mask) for i in range(count)])


def pin(values):
    return lax.optimization_barrier(values)


def in_order(flag, own, other, axis):
    return jnp.where(
        flag == 0,
        jnp.concatenate([own, other], axis=axis),
        jnp.concatenate([other, own], axis=axis),
    )


def token_offset(head_place, index, sub):
    core, upper, inner = index // (2 * sub), (index // sub) % 2, index % sub
    return (head_place ^ (upper * 2) ^ core) * sub + inner


def allowed_mask(meta_ref, start_row, q_block, k_block, rows, half, q_lanes):
    sub = half // 2
    head_place = meta_ref[0]
    k_index = lax.broadcasted_iota(jnp.int32, (2 * half, 1), 0)
    k_token = token_offset(head_place, k_index, sub) + k_block * (2 * half)
    q_index = lax.broadcasted_iota(jnp.int32, (1, q_lanes), 1) % (2 * half)
    q_token = token_offset(head_place, q_index, sub) + q_block * (2 * half)
    return (k_token <= q_token) & (k_token >= start_row)


def stacked(ref, heads, width):
    return jnp.concatenate(
        [ref[c, 0, :, h * width : (h + 1) * width] for h in range(heads) for c in range(2)], axis=0
    )


def key_rows(ref, part, block):
    return jnp.concatenate([ref[part, 0, block], ref[part, 1, block]], axis=0)


def attend_kernel(meta_ref, q_ref, k_ref, v_ref, start_ref, o_ref, ot_ref, l_ref, vt_ref, acc_ref, sum_ref, *, factor, heads):
    q_pos = pl.program_id(0)
    parts, _, blocks, half, width = k_ref.shape
    lanes = heads * 2 * half

    @pl.when(q_pos == 0)
    def _():
        for part in range(parts):
            for block in range(blocks):
                vt_ref[part * blocks + block] = key_rows(v_ref, part, block).T

    q_rows = stacked(q_ref, heads, width)
    acc_ref[...] = jnp.zeros_like(acc_ref)
    sum_ref[...] = jnp.zeros_like(sum_ref)
    start_row = start_ref[0]
    q_block = meta_ref[1 + q_pos]
    total = parts * blocks

    def add(kb, masked):
        e = jnp.exp2(nt(key_rows(k_ref, kb // blocks, kb % blocks), q_rows) * factor)
        if masked:
            k_block = meta_ref[1 + blocks + kb]
            e = jnp.where(allowed_mask(meta_ref, start_row, q_block, k_block, None, half, lanes), e, 0.0)
        sum_ref[...] += jnp.sum(e, axis=0, keepdims=True)
        acc_ref[...] += nn(vt_ref[kb], e.astype(BF16))

    def step(kb, carry):
        flag = meta_ref[1 + blocks + total + q_pos * total + kb]

        @pl.when(flag == 1)
        def _():
            add(kb, False)

        @pl.when(flag == 2)
        def _():
            add(kb, True)

        return carry

    lax.fori_loop(0, total, step, 0)
    out = acc_ref[...] / sum_ref[...]
    ot_ref[0] = out
    l_ref[0] = sum_ref[...]
    rows = out.T
    for h in range(heads):
        for c in range(2):
            at = (h * 2 + c) * half
            o_ref[c, 0, :, h * width : (h + 1) * width] = rows[at : at + half].astype(BF16)


def attend_back_kernel(
    meta_ref, q_ref, do_ref, k_ref, v_ref, start_ref, ot_ref, l_ref, dq_ref, dk_ref, dv_ref, kt_ref, acc_ref, *, factor, scaling, heads
):
    q_pos = pl.program_id(0)
    parts, _, blocks, half, width = k_ref.shape
    lanes = heads * 2 * half

    @pl.when(q_pos == 0)
    def _():
        dk_ref[...] = jnp.zeros_like(dk_ref)
        dv_ref[...] = jnp.zeros_like(dv_ref)
        for part in range(parts):
            for block in range(blocks):
                kt_ref[part * blocks + block] = key_rows(k_ref, part, block).T

    q_rows = stacked(q_ref, heads, width)
    do_rows = stacked(do_ref, heads, width)
    delta = jnp.sum(do_rows.astype(F32).T * ot_ref[0], axis=0, keepdims=True)
    inverse = 1.0 / l_ref[0]
    acc_ref[...] = jnp.zeros_like(acc_ref)
    start_row = start_ref[0]
    q_block = meta_ref[1 + q_pos]
    total = parts * blocks

    def add(kb, masked):
        part, block = kb // blocks, kb % blocks
        e = jnp.exp2(nt(key_rows(k_ref, part, block), q_rows) * factor)
        if masked:
            k_block = meta_ref[1 + blocks + kb]
            e = jnp.where(allowed_mask(meta_ref, start_row, q_block, k_block, None, half, lanes), e, 0.0)
        p = e * inverse
        dp = nt(key_rows(v_ref, part, block), do_rows)
        ds = (p * (dp - delta)).astype(BF16)
        dv = nn(p.astype(BF16), do_rows)
        dk = nn(ds, q_rows) * scaling
        for c in range(2):
            dv_ref[part, c, block] += dv[c * half : (c + 1) * half]
            dk_ref[part, c, block] += dk[c * half : (c + 1) * half]
        acc_ref[...] += nn(kt_ref[kb], ds)

    def step(kb, carry):
        flag = meta_ref[1 + blocks + total + q_pos * total + kb]

        @pl.when(flag == 1)
        def _():
            add(kb, False)

        @pl.when(flag == 2)
        def _():
            add(kb, True)

        return carry

    lax.fori_loop(0, total, step, 0)
    rows = acc_ref[...].T * scaling
    for h in range(heads):
        for c in range(2):
            at = (h * 2 + c) * half
            dq_ref[c, 0, :, h * width : (h + 1) * width] = rows[at : at + half]


def attend(meta, q, k, v, start, scaling):
    _, blocks, half, columns = q.shape
    parts, width = k.shape[0], k.shape[-1]
    heads = columns // width
    lanes = heads * 2 * half
    total = parts * blocks
    row_spec = pl.BlockSpec((2, 1, half, columns), lambda i: (0, i, 0, 0))
    key_spec = pl.BlockSpec(k.shape, lambda i: (0, 0, 0, 0, 0))
    lane_spec = pl.BlockSpec((1, 1, lanes), lambda i: (i, 0, 0))
    return pl.pallas_call(
        functools.partial(attend_kernel, factor=scaling * LOG2E, heads=heads),
        grid=(blocks,),
        in_specs=[pl.BlockSpec(memory_space=pltpu.SMEM), row_spec, key_spec, key_spec, lane_spec],
        out_specs=[row_spec, pl.BlockSpec((1, width, lanes), lambda i: (i, 0, 0)), lane_spec],
        out_shape=[
            jax.ShapeDtypeStruct(q.shape, BF16),
            jax.ShapeDtypeStruct((blocks, width, lanes), F32),
            jax.ShapeDtypeStruct((blocks, 1, lanes), F32),
        ],
        scratch_shapes=[
            pltpu.VMEM((total, width, 2 * half), BF16),
            pltpu.VMEM((width, lanes), F32),
            pltpu.VMEM((1, lanes), F32),
        ],
        compiler_params=pltpu.CompilerParams(vmem_limit_bytes=VMEM_LIMIT),
        cost_estimate=pl.CostEstimate(
            flops=2 * 2 * lanes * 2 * half * width * blocks * total,
            bytes_accessed=8 * q.size + 8 * k.size,
            transcendentals=lanes * 2 * half * blocks * total,
        ),
    )(meta, q, k, v, start)


def attend_back(meta, q, do, k, v, start, out_t, total_e, scaling):
    _, blocks, half, columns = q.shape
    parts, width = k.shape[0], k.shape[-1]
    heads = columns // width
    lanes = heads * 2 * half
    total = parts * blocks
    row_spec = pl.BlockSpec((2, 1, half, columns), lambda i: (0, i, 0, 0))
    key_spec = pl.BlockSpec(k.shape, lambda i: (0, 0, 0, 0, 0))
    lane_spec = pl.BlockSpec((1, 1, lanes), lambda i: (i, 0, 0))
    return pl.pallas_call(
        functools.partial(attend_back_kernel, factor=scaling * LOG2E, scaling=scaling, heads=heads),
        grid=(blocks,),
        in_specs=[
            pl.BlockSpec(memory_space=pltpu.SMEM),
            row_spec,
            row_spec,
            key_spec,
            key_spec,
            lane_spec,
            pl.BlockSpec((1, width, lanes), lambda i: (i, 0, 0)),
            lane_spec,
        ],
        out_specs=[row_spec, key_spec, key_spec],
        out_shape=[
            jax.ShapeDtypeStruct(q.shape, F32),
            jax.ShapeDtypeStruct(k.shape, F32),
            jax.ShapeDtypeStruct(k.shape, F32),
        ],
        scratch_shapes=[
            pltpu.VMEM((total, width, 2 * half), BF16),
            pltpu.VMEM((width, lanes), F32),
        ],
        compiler_params=pltpu.CompilerParams(vmem_limit_bytes=VMEM_LIMIT),
        cost_estimate=pl.CostEstimate(
            flops=5 * 2 * lanes * 2 * half * width * blocks * total,
            bytes_accessed=12 * q.size + 16 * k.size,
            transcendentals=lanes * 2 * half * blocks * total,
        ),
    )(meta, q, do, k, v, start, out_t, total_e)


def prepare_kernel(x_ref, w_ref, cos_ref, sin_ref, gq_ref, gk_ref, q_ref, kv_ref, raw_ref, *, heads, width):
    acc = jnp.dot(x_ref[...], w_ref[...], preferred_element_type=F32)
    raw_ref[...] = acc[:, : (heads + 1) * width]
    for h in range(heads + 1):
        part = acc[:, h * width : (h + 1) * width]
        normed = part * lax.rsqrt(jnp.mean(part * part, axis=-1, keepdims=True) + EPS)
        scaled = normed * (gq_ref if h < heads else gk_ref)[...]
        turned = (scaled * cos_ref[...] + pltpu.roll(scaled, width // 2, 1) * sin_ref[...]).astype(BF16)
        if h < heads:
            q_ref[:, h * width : (h + 1) * width] = turned
        else:
            kv_ref[:, :width] = turned
    kv_ref[:, width:] = acc[:, (heads + 1) * width :].astype(BF16)


def prepare(x, w, cos, sin, gain_q, gain_k, heads):
    tokens, depth = x.shape
    width, tile = gain_q.shape[1], 256
    row = lambda n: pl.BlockSpec((tile, n), lambda i: (i, 0))
    fixed = lambda a: pl.BlockSpec(a.shape, lambda i: (0, 0))
    return pl.pallas_call(
        functools.partial(prepare_kernel, heads=heads, width=width),
        grid=(tokens // tile,),
        in_specs=[row(depth), fixed(w), row(width), row(width), fixed(gain_q), fixed(gain_k)],
        out_specs=[row(heads * width), row(2 * width), row((heads + 1) * width)],
        out_shape=[
            jax.ShapeDtypeStruct((tokens, heads * width), BF16),
            jax.ShapeDtypeStruct((tokens, 2 * width), BF16),
            jax.ShapeDtypeStruct((tokens, (heads + 1) * width), F32),
        ],
        compiler_params=pltpu.CompilerParams(vmem_limit_bytes=VMEM_LIMIT),
        cost_estimate=TINY_COST,
    )(x, w, cos, sin, gain_q, gain_k)


def prepare_back_kernel(
    dq_ref, dk_ref, dv_ref, got_ref, raw_ref, cos_ref, sin_ref, gq_ref, gk_ref, w_ref, d_ref, p_ref, g_ref, *, heads, width
):
    @pl.when(pl.program_id(0) == 0)
    def _():
        g_ref[...] = jnp.zeros_like(g_ref)

    got = got_ref[...].astype(F32)
    for h in range(heads + 1):
        at = slice(h * width, (h + 1) * width)
        grad = dq_ref[:, at] if h < heads else dk_ref[0] + got[:, :width]
        gain = (gq_ref if h < heads else gk_ref)[...]
        raw = raw_ref[:, at]
        inverse = lax.rsqrt(jnp.mean(raw * raw, axis=-1, keepdims=True) + EPS)
        normed = raw * inverse
        turned = grad * cos_ref[...] - pltpu.roll(grad, width // 2, 1) * sin_ref[...]
        row = 0 if h < heads else 1
        g_ref[row : row + 1, :] += jnp.sum(turned * normed, axis=0, keepdims=True)
        scaled = turned * gain
        d_ref[:, at] = (inverse * (scaled - normed * jnp.mean(scaled * normed, axis=-1, keepdims=True))).astype(BF16)
    d_ref[:, (heads + 1) * width :] = (dv_ref[0] + got[:, width:]).astype(BF16)
    p_ref[...] = nt(d_ref[...], w_ref[...]).astype(BF16)


def prepare_back(dq, dk, dv, got, raw, cos, sin, gain_q, gain_k, w, heads):
    tokens, width, tile = dq.shape[0], gain_q.shape[1], 256
    row = lambda n: pl.BlockSpec((tile, n), lambda i: (i, 0))
    part = pl.BlockSpec((1, tile, width), lambda i: (0, i, 0))
    fixed = lambda a: pl.BlockSpec(a.shape, lambda i: (0, 0))
    return pl.pallas_call(
        functools.partial(prepare_back_kernel, heads=heads, width=width),
        grid=(tokens // tile,),
        in_specs=[
            row(heads * width),
            part,
            part,
            row(2 * width),
            row((heads + 1) * width),
            row(width),
            row(width),
            fixed(gain_q),
            fixed(gain_k),
            fixed(w),
        ],
        out_specs=[row(w.shape[1]), row(w.shape[0]), pl.BlockSpec((8, width), lambda i: (0, 0))],
        out_shape=[
            jax.ShapeDtypeStruct((tokens, w.shape[1]), BF16),
            jax.ShapeDtypeStruct((tokens, w.shape[0]), BF16),
            jax.ShapeDtypeStruct((8, width), F32),
        ],
        compiler_params=pltpu.CompilerParams(vmem_limit_bytes=VMEM_LIMIT),
        cost_estimate=TINY_COST,
    )(dq, dk, dv, got, raw, cos, sin, gain_q, gain_k, w)


def place_of_block(blk, bit_order, p):
    return blk ^ sum(((p >> i) & 1) << b for i, b in enumerate(bit_order))


def enter_kernel(blk_ref, *refs, bit_order, normed):
    if normed:
        mine_ref, other_ref, gain_ref, low_ref, out_ref, gains_ref = refs
    else:
        mine_ref, low_ref = refs
    rows, width = mine_ref.shape
    n = width >> len(bit_order)
    for p in range(1 << len(bit_order)):
        at = pl.ds(pl.multiple_of(place_of_block(blk_ref[0], bit_order, p) * n, n), n)
        low_ref[:rows, p * n : (p + 1) * n] = mine_ref[:, at]
        if normed:
            low_ref[rows:, p * n : (p + 1) * n] = other_ref[:, at]
            gains_ref[:, p * n : (p + 1) * n] = gain_ref[:, at]
    if normed:
        values = low_ref[...].astype(F32)
        inverse = lax.rsqrt(jnp.mean(values * values, axis=-1, keepdims=True) + EPS)
        out_ref[...] = (values * inverse * gains_ref[:1]).astype(BF16)


def enter(blk, bit_order, mine, other=None, gain=None):
    rows, width = mine.shape
    normed = gain is not None
    total = (2 * rows if normed else rows, width)
    vmem = pl.BlockSpec(memory_space=pltpu.VMEM)
    operands = [mine, other, gain] if normed else [mine]
    return pl.pallas_call(
        functools.partial(enter_kernel, bit_order=bit_order, normed=normed),
        in_specs=[pl.BlockSpec(memory_space=pltpu.SMEM), *[vmem] * len(operands)],
        out_specs=[vmem] * (3 if normed else 1),
        out_shape=[
            *[jax.ShapeDtypeStruct(total, BF16)] * (2 if normed else 1),
            *([jax.ShapeDtypeStruct(gain.shape, F32)] if normed else []),
        ],
        compiler_params=pltpu.CompilerParams(vmem_limit_bytes=VMEM_LIMIT),
        cost_estimate=TINY_COST,
    )(blk[None].astype(jnp.int32), *operands)


def assemble_kernel(place_ref, *refs, sources, widths):
    ins, outs = refs[: 2 * sources], refs[2 * sources :]
    place, k, at = place_ref[0], 0, 0
    for own_ref, got_ref in zip(ins[::2], ins[1::2]):
        f, at = own_ref.shape[0], 0
        while at < own_ref.shape[1]:
            w, cut = widths[k], slice(at, at + widths[k])
            mine = pl.ds(pl.multiple_of(place * w, w), w)
            theirs = pl.ds(pl.multiple_of((1 - place) * w, w), w)
            outs[k][:, mine] = own_ref[:, cut] + got_ref[:f, cut].astype(F32)
            outs[k][:, theirs] = got_ref[f : 2 * f, cut].astype(F32) + got_ref[2 * f :, cut].astype(F32)
            at += w
            k += 1


def assemble(place, sources, widths):
    vmem = pl.BlockSpec(memory_space=pltpu.VMEM)
    flat = [a for pair in sources for a in pair]
    return pl.pallas_call(
        functools.partial(assemble_kernel, sources=len(sources), widths=widths),
        in_specs=[pl.BlockSpec(memory_space=pltpu.SMEM), *[vmem] * len(flat)],
        out_specs=[vmem] * len(widths),
        out_shape=[jax.ShapeDtypeStruct((sources[0][0].shape[0], 2 * w), F32) for w in widths],
        compiler_params=pltpu.CompilerParams(vmem_limit_bytes=VMEM_LIMIT),
        cost_estimate=TINY_COST,
    )(place[None].astype(jnp.int32), *flat)


def back_kernel(*refs):
    *ins, out_ref = refs
    n = len(ins) // 2
    out_ref[...] = sum(nt(d[...], w[...]) for d, w in zip(ins[:n], ins[n:])).astype(BF16)


def back_through(grads, weights):
    tokens, depth, tile = grads[0].shape[0], weights[0].shape[0], 256
    return pl.pallas_call(
        back_kernel,
        grid=(depth // tile,),
        in_specs=[
            *[pl.BlockSpec(g.shape, lambda i: (0, 0)) for g in grads],
            *[pl.BlockSpec((tile, w.shape[1]), lambda i: (i, 0)) for w in weights],
        ],
        out_specs=pl.BlockSpec((tokens, tile), lambda i: (0, i)),
        out_shape=jax.ShapeDtypeStruct((tokens, depth), BF16),
        compiler_params=pltpu.CompilerParams(vmem_limit_bytes=VMEM_LIMIT),
        cost_estimate=TINY_COST,
    )(*grads, *weights)


def weight_grad_kernel(a_ref, b_ref, keep_ref, away_ref):
    product = tn(a_ref[...], b_ref[...])
    first = pl.program_id(0) < pl.num_programs(0) // 2

    @pl.when(first)
    def _():
        keep_ref[...] = product

    @pl.when(jnp.logical_not(first))
    def _():
        away_ref[...] = product.astype(BF16)


def weight_grad(a, b):
    tokens, depth = a.shape
    n, tile = b.shape[1], 256
    steps = depth // tile
    return pl.pallas_call(
        weight_grad_kernel,
        grid=(steps,),
        in_specs=[
            pl.BlockSpec((tokens, tile), lambda i: (0, i)),
            pl.BlockSpec((tokens, n), lambda i: (0, 0)),
        ],
        out_specs=[
            pl.BlockSpec((tile, n), lambda i: (jnp.minimum(i, steps // 2 - 1), 0)),
            pl.BlockSpec((tile, n), lambda i: (jnp.maximum(i - steps // 2, 0), 0)),
        ],
        out_shape=[
            jax.ShapeDtypeStruct((depth // 2, n), F32),
            jax.ShapeDtypeStruct((depth // 2, n), BF16),
        ],
        compiler_params=pltpu.CompilerParams(vmem_limit_bytes=VMEM_LIMIT),
        cost_estimate=TINY_COST,
    )(a, b)


def remote(src, dst, send, recv, target):
    copy = pltpu.make_async_remote_copy(
        src_ref=src, dst_ref=dst, send_sem=send, recv_sem=recv, device_id=target, device_id_type=pl.DeviceIdType.MESH
    )
    copy.start()
    return copy


class Plan:
    def __init__(self):
        self.inputs, self.shapes, self.aliases, self.jobs = [], [], {}, []

    def read(self, array):
        self.inputs.append(array)
        return ("in", len(self.inputs) - 1)

    def fresh(self, shape, dtype):
        self.shapes.append(jax.ShapeDtypeStruct(shape, dtype))
        return ("out", len(self.shapes) - 1)

    def through(self, array):
        self.inputs.append(array)
        self.aliases[len(self.inputs) - 1] = len(self.shapes)
        return self.fresh(array.shape, array.dtype)

    def copy(self, src, dst, mask, after=None, point=0):
        self.jobs.append((src, dst, mask, after, point, None))
        return len(self.jobs) - 1

    def local(self, src, dst, shape, point=0):
        self.jobs.append((src, dst, 0, None, point, shape))
        return len(self.jobs) - 1


class Fill:
    def __init__(self, inputs, outputs, step, point):
        self.inputs, self.outputs, self.step, self.point = inputs, outputs, step, point

    def scratch(self):
        shapes = [pltpu.VMEM(a.shape, a.dtype) for a in (*self.inputs, *self.outputs)]
        return [*shapes, pltpu.SemaphoreType.DMA((len(shapes),))]


def fill_weight_grad(a, b, point):
    depth, n, tile = a.shape[1], b.shape[1], 256
    half = depth // 2

    def step(ins, outs):
        (a_ref, b_ref), (keep_ref, away_ref) = ins, outs

        def one(i, carry):
            at = pl.ds(pl.multiple_of(i * tile, tile), tile)
            keep_ref[at, :] = tn(a_ref[:, at], b_ref[...])
            far = pl.ds(pl.multiple_of(half + i * tile, tile), tile)
            away_ref[at, :] = tn(a_ref[:, far], b_ref[...]).astype(BF16)
            return carry

        lax.fori_loop(0, half // tile, one, 0)

    outputs = [jax.ShapeDtypeStruct((half, n), F32), jax.ShapeDtypeStruct((half, n), BF16)]
    return Fill([a, b], outputs, step, point)


def fill_back(grad, weight, point):
    tokens, depth, tile = grad.shape[0], weight.shape[0], 256

    def step(ins, outs):
        (g_ref, w_ref), (out_ref,) = ins, outs

        def one(i, carry):
            at = pl.ds(pl.multiple_of(i * tile, tile), tile)
            out_ref[:, at] = nt(g_ref[...], w_ref[at, :]).astype(BF16)
            return carry

        lax.fori_loop(0, depth // tile, one, 0)

    return Fill([grad, weight], [jax.ShapeDtypeStruct((tokens, depth), BF16)], step, point)


def fill_product(left, right, point):
    tokens, n, tile = left.shape[0], right.shape[1], 256

    def step(ins, outs):
        (l_ref, r_ref), (out_ref,) = ins, outs

        def one(i, carry):
            at = pl.ds(pl.multiple_of(i * tile, tile), tile)
            out_ref[at, :] = nn(l_ref[at, :], r_ref[...])
            return carry

        lax.fori_loop(0, tokens // tile, one, 0)

    return Fill([left, right], [jax.ShapeDtypeStruct((tokens, n), F32)], step, point)


def run(plan, main, collective_id, greeted=(), fills=(), limit=None):
    inputs, in_specs, out_shapes, out_specs, scratch, body, own_limit = main
    limit = limit or own_limit + sum(math.prod(s.shape) * s.dtype.itemsize for f in fills for s in f.scratch()[:-1])
    f_in, f_out = [a for f in fills for a in f.inputs], [a for f in fills for a in f.outputs]
    n_in, n_out = len(inputs), len(out_shapes)
    m_in, m_out = len(plan.inputs), len(plan.shapes)
    jobs = plan.jobs
    local_jobs = [i for i, job in enumerate(jobs) if not job[2]]
    masks = sorted({*greeted, *[job[2] for job in jobs if job[2]]} - {1 << TENSOR_BIT})
    any_spec = pl.BlockSpec(memory_space=pltpu.HBM)

    def kernel(*refs):
        main_in, refs = refs[:n_in], refs[n_in:]
        plan_in, refs = refs[:m_in], refs[m_in:]
        fill_in, refs = refs[: len(f_in)], refs[len(f_in) :]
        main_out, refs = refs[:n_out], refs[n_out:]
        plan_out, refs = refs[:m_out], refs[m_out:]
        fill_out, refs = refs[: len(f_out)], refs[len(f_out) :]
        send, recv, *rest = refs
        bounce = dict(zip(local_jobs, rest))
        rest = rest[len(local_jobs) :]
        parts = []
        for f in fills:
            k, m = len(f.inputs), len(f.outputs)
            (*held, sems), rest = rest[: k + m + 1], rest[k + m + 1 :]
            loads = [pltpu.make_async_copy(fill_in[i], held[i], sems.at[i]) for i in range(k)]
            stores = [pltpu.make_async_copy(held[k + i], fill_out[i], sems.at[k + i]) for i in range(m)]
            fill_in, fill_out = fill_in[k:], fill_out[m:]
            for copy in loads:
                copy.start()
            parts.append((f, held[:k], held[k:], loads, stores))

        def compute(point):
            for f, ins, outs, loads, stores in parts:
                if f.point == point:
                    for copy in loads:
                        copy.wait()
                    f.step(ins, outs)
                    for copy in stores:
                        copy.start()

        blk, head = lax.axis_index("blk"), lax.axis_index("head")
        core, near, across = (blk, head ^ 1), (blk, head ^ 2), (blk ^ (1 << TENSOR_BIT), head)
        barrier = pltpu.get_barrier_semaphore()
        partners = [core, near, across, *[(blk ^ m, head) for m in masks]]
        for target in partners:
            pl.semaphore_signal(barrier, inc=1, device_id=target, device_id_type=pl.DeviceIdType.MESH)
        pl.semaphore_wait(barrier, len(partners))
        started, arrived, halfway = {}, set(), []

        def arrive(i):
            if i not in arrived:
                arrived.add(i)
                (started[i].wait_recv if jobs[i][2] else started[i].wait)()

        def part(side):
            (kind, index), cut = side
            if kind == "fill":
                return cut(parts[index[0]][2][index[1]])
            return cut((plan_in if kind == "in" else plan_out)[index])

        def issue(point):
            for i in list(halfway):
                started[i].wait()
                started[i] = pltpu.make_async_copy(bounce[i], part(jobs[i][1]), recv.at[i])
                started[i].start()
                halfway.remove(i)
            for i, (src, dst, mask, after, at, shape) in enumerate(jobs):
                if i in started or (at != point and point is not None):
                    continue
                if after is not None:
                    arrive(after)
                if mask:
                    started[i] = remote(part(src), part(dst), send.at[i], recv.at[i], (blk ^ mask, head))
                else:
                    started[i] = pltpu.make_async_copy(part(src), bounce[i], send.at[i])
                    started[i].start()
                    halfway.append(i)

        point = 0
        for _ in body((core, near, across), main_in, main_out, rest):
            issue(point)
            compute(point)
            point += 1
        issue(None)
        issue(None)
        for i in range(len(jobs)):
            arrive(i)
            if jobs[i][2]:
                started[i].wait_send()
        for *_, stores in parts:
            for copy in stores:
                copy.wait()

    results = pl.pallas_call(
        kernel,
        out_shape=[*out_shapes, *plan.shapes, *f_out],
        in_specs=[*in_specs, *[any_spec] * (m_in + len(f_in))],
        out_specs=[*out_specs, *[any_spec] * (m_out + len(f_out))],
        scratch_shapes=[
            pltpu.SemaphoreType.DMA((max(1, len(jobs)),)),
            pltpu.SemaphoreType.DMA((max(1, len(jobs)),)),
            *[pltpu.VMEM(jobs[i][5], BF16) for i in local_jobs],
            *[s for f in fills for s in f.scratch()],
            *scratch,
        ],
        input_output_aliases={n_in + i: n_out + o for i, o in plan.aliases.items()},
        compiler_params=pltpu.CompilerParams(
            collective_id=collective_id, has_side_effects=True, vmem_limit_bytes=limit
        ),
        cost_estimate=TINY_COST,
    )(*inputs, *plan.inputs, *f_in)
    return results[:n_out], results[n_out:]


def spread_main(flat, chunk):
    rows, width = flat.shape[0] // 2, flat.shape[1]
    pieces = width // chunk

    def body(partners, ins, outs, scratch):
        core, near, across = partners
        (s_ref,), (o_ref,), (hold, local_sem, send, recv) = ins, outs, scratch
        first = remote(s_ref, o_ref.at[0, :, 0, 1], send.at[0], recv.at[0], near)
        second = [
            remote(
                s_ref.at[:, :, pl.ds(i * chunk, chunk)],
                o_ref.at[0, :, 1, 0, :, pl.ds((i ^ 1) * chunk, chunk)],
                send.at[6 + i],
                recv.at[6 + i],
                across,
            )
            for i in range(pieces)
        ]
        third = remote(s_ref, o_ref.at[1, :, 0, 0], send.at[1], recv.at[1], core)
        held = pltpu.make_async_copy(s_ref, hold, local_sem.at[0])
        held.start()
        yield
        held.wait()
        own = pltpu.make_async_copy(hold, o_ref.at[0, :, 0, 0], local_sem.at[1])
        own.start()
        for copy in second:
            copy.wait_recv()
        fourth = remote(o_ref.at[0, :, 1, 0], o_ref.at[0, :, 1, 1], send.at[2], recv.at[2], near)
        fifth = remote(o_ref.at[0, :, 1, 0], o_ref.at[1, :, 1, 0], send.at[3], recv.at[3], core)
        yield
        first.wait_recv()
        sixth = remote(o_ref.at[0, :, 0, 1], o_ref.at[1, :, 0, 1], send.at[4], recv.at[4], core)
        yield
        fourth.wait_recv()
        seventh = remote(o_ref.at[0, :, 1, 1], o_ref.at[1, :, 1, 1], send.at[5], recv.at[5], core)
        yield
        own.wait()
        for copy in (first, *second, third, fourth, fifth, sixth, seventh):
            copy.wait_send()
        for copy in (third, fifth, sixth, seventh):
            copy.wait_recv()

    any_spec = pl.BlockSpec(memory_space=pltpu.HBM)
    return (
        [flat.reshape(2, rows, width)],
        [any_spec],
        [jax.ShapeDtypeStruct((2, 2, 2, 2, rows, width), flat.dtype)],
        [any_spec],
        [
            pltpu.VMEM((2, rows, width), flat.dtype),
            pltpu.SemaphoreType.DMA((2,)),
            pltpu.SemaphoreType.DMA((6 + pieces,)),
            pltpu.SemaphoreType.DMA((6 + pieces,)),
        ],
        body,
        8 * MIB,
    )


def gather_main(partial, chunk, extra, outs_like, finish):
    rows, width = partial.shape[0] // 16, partial.shape[1]
    share = (2, rows, width)
    pieces = width // chunk

    def body(partners, ins, outs, scratch):
        core, near, across = partners
        p_ref, *extra_refs = ins
        core_in, out_y, in_y, out_t, in_t, hold, send, recv = scratch
        order = ((1, 1), (0, 1), (1, 0), (0, 0))
        from_core = [
            remote(p_ref.at[1, :, t, y], core_in.at[i], send.at[i], recv.at[i], core) for i, (t, y) in enumerate(order)
        ]
        from_y = []
        for i in range(2):
            t, y = order[i]
            from_core[i].wait_recv()
            out_y[i] = (p_ref[0, :, t, y].astype(F32) + core_in[i].astype(F32)).astype(BF16)
            from_y.append(remote(out_y.at[i], in_y.at[i], send.at[4 + i], recv.at[4 + i], near))
        yield
        from_core[2].wait_recv()
        hold[...] = p_ref[0, :, 1, 0].astype(F32) + core_in[2].astype(F32)
        from_y[0].wait_recv()
        for i in range(pieces):
            a, b = slice(i * chunk, (i + 1) * chunk), slice((i ^ 1) * chunk, ((i ^ 1) + 1) * chunk)
            out_t[:, :, b] = (hold[:, :, a] + in_y[0, :, :, a].astype(F32)).astype(BF16)
        from_t = remote(out_t, in_t, send.at[6], recv.at[6], across)
        yield
        from_core[3].wait_recv()
        hold[...] = p_ref[0, :, 0, 0].astype(F32) + core_in[3].astype(F32)
        from_y[1].wait_recv()
        hold[...] += in_y[1].astype(F32)
        yield
        from_t.wait_recv()
        hold[...] += in_t[...].astype(F32)
        finish(hold, extra_refs, outs)
        for copy in (*from_core, *from_y, from_t):
            copy.wait_send()

    vmem_spec = pl.BlockSpec(memory_space=pltpu.VMEM)
    return (
        [partial.reshape(2, 2, 2, 2, rows, width), *extra],
        [vmem_spec] * (1 + len(extra)),
        outs_like,
        [vmem_spec] * len(outs_like),
        [
            pltpu.VMEM((4, *share), BF16),
            pltpu.VMEM((2, *share), BF16),
            pltpu.VMEM((2, *share), BF16),
            pltpu.VMEM(share, BF16),
            pltpu.VMEM(share, BF16),
            pltpu.VMEM(share, F32),
            pltpu.SemaphoreType.DMA((7,)),
            pltpu.SemaphoreType.DMA((7,)),
        ],
        body,
        24 * MIB,
    )


def inverse_rms(values):
    return lax.rsqrt(jnp.mean(values * values, axis=-1, keepdims=True) + EPS)


def finish_middle(total, extra, outs):
    (low_ref, gain_ref), (middle_ref, normed_ref) = extra, outs
    for m in range(2):
        middle = low_ref[m].astype(F32) + total[m]
        middle_ref[m] = middle
        normed_ref[m] = (middle * inverse_rms(middle) * gain_ref[...]).astype(BF16)


def norm_grad(total, values, gain, gain_grad_ref, m):
    inverse = inverse_rms(values)
    normal = values * inverse
    part = jnp.sum(total * normal, axis=0, keepdims=True)
    gain_grad_ref[...] = part if m == 0 else gain_grad_ref[...] + part
    scaled = total * gain
    return inverse * (scaled - normal * jnp.mean(scaled * normal, axis=-1, keepdims=True))


def finish_mlp_norm(total, extra, outs):
    (cot_ref, middle_ref, gain_ref), (grad_ref, low_ref, gain_grad_ref) = extra, outs
    for m in range(2):
        grad = cot_ref[m].astype(F32) + norm_grad(total[m], middle_ref[m], gain_ref[...], gain_grad_ref, m)
        grad_ref[m] = grad
        low_ref[m] = grad.astype(BF16)


def store_ungrouped(value, ref, blk, bit_order, lead=()):
    n = value.shape[-1] >> len(bit_order)
    for p in range(1 << len(bit_order)):
        block = value[:, p * n : (p + 1) * n]
        if bit_order and n % 128 == 0:
            at = pl.ds(pl.multiple_of(place_of_block(blk, bit_order, p) * n, n), n)
        else:
            at = pl.ds(p * n, n)
        ref[(*lead, slice(None), at)] = block.astype(ref.dtype)


def finish_mixed(total, extra, outs, *, bit_order):
    (middle_ref,), (mixed_ref,) = extra, outs
    blk = lax.axis_index("blk")
    for m in range(2):
        store_ungrouped(middle_ref[m] + total[m], mixed_ref, blk, bit_order, (m,))


def finish_input(total, extra, outs, *, bit_order):
    (low_ref, mid_ref, gain_ref), (own_ref, away_ref, gain_grad_ref) = extra, outs
    blk = lax.axis_index("blk")
    for m in range(2):
        grad = mid_ref[m] + norm_grad(total[m], low_ref[m].astype(F32), gain_ref[...], gain_grad_ref, m)
        store_ungrouped(grad, own_ref if m == 0 else away_ref, blk, bit_order)


def total_main(values):
    rows, width = values.shape
    rounds = 2 + lax.axis_size("blk").bit_length() - 1

    def body(partners, ins, outs, scratch):
        (v_ref,), (o_ref,) = ins, outs
        out_buf, in_buf, send, recv = scratch
        blk, head = lax.axis_index("blk"), lax.axis_index("head")
        o_ref[...] = v_ref[...]
        yield
        for i in range(rounds):
            target = (blk, head ^ (1 << i)) if i < 2 else (blk ^ (1 << (i - 2)), head)
            out_buf[i] = o_ref[...]
            copy = remote(out_buf.at[i], in_buf.at[i], send.at[i], recv.at[i], target)
            copy.wait_recv()
            o_ref[...] += in_buf[i]
            copy.wait_send()
        yield

    vmem_spec = pl.BlockSpec(memory_space=pltpu.VMEM)
    return (
        [values],
        [vmem_spec],
        [jax.ShapeDtypeStruct(values.shape, F32)],
        [vmem_spec],
        [
            pltpu.VMEM((rounds, rows, width), F32),
            pltpu.VMEM((rounds, rows, width), F32),
            pltpu.SemaphoreType.DMA((rounds,)),
            pltpu.SemaphoreType.DMA((rounds,)),
        ],
        body,
        8 * MIB,
    )


class Moving:
    def __init__(self, copy, away):
        self.copy, self.away, self.here, self.gone = copy, away, False, not away

    def arrive(self):
        if not self.here:
            self.here = True
            (self.copy.wait_recv if self.away else self.copy.wait)()

    def sent(self):
        if not self.gone:
            self.gone = True
            self.copy.wait_send()


class Links:
    def __init__(self, send, recv, batch_mask):
        self.send, self.recv, self.all = send, recv, []
        blk, head = lax.axis_index("blk"), lax.axis_index("head")
        self.core, self.near, self.across = (blk, head ^ 1), (blk, head ^ 2), (blk ^ (1 << TENSOR_BIT), head)
        self.seq, self.batch = (blk ^ (1 << SEQ_BIT), head), (blk ^ batch_mask, head)
        self.both = (blk ^ (batch_mask | (1 << TENSOR_BIT)), head)
        self.place = bit_of(blk, TENSOR_BIT)
        self.blk = blk

    def greet(self):
        barrier = pltpu.get_barrier_semaphore()
        partners = (self.core, self.near, self.across, self.seq, self.batch, self.both)
        for target in partners:
            pl.semaphore_signal(barrier, inc=1, device_id=target, device_id_type=pl.DeviceIdType.MESH)
        pl.semaphore_wait(barrier, len(partners))

    def to(self, target, src, dst):
        i = len(self.all)
        self.all.append(Moving(remote(src, dst, self.send.at[i], self.recv.at[i], target), True))
        return self.all[-1]

    def load(self, src, dst):
        copy = pltpu.make_async_copy(src, dst, self.recv.at[len(self.all)])
        copy.start()
        self.all.append(Moving(copy, False))
        return self.all[-1]

    def finish(self):
        for moving in self.all:
            moving.arrive()
            moving.sent()

    def half(self, ref, other):
        n = ref.shape[1] // 2
        place = 1 - self.place if other else self.place
        return ref.at[:, pl.ds(pl.multiple_of(place * n, n), n)]


def nothing(stage):
    pass


def spread_in(links, s_ref, o_ref, chunk, between=nothing, in_vmem=True):
    pieces = s_ref.shape[-1] // chunk
    across = [
        links.to(
            links.across,
            s_ref.at[:, :, pl.ds(i * chunk, chunk)],
            o_ref.at[0, :, 1, 0, :, pl.ds((i ^ 1) * chunk, chunk)],
        )
        for i in range(pieces)
    ]
    near = links.to(links.near, s_ref, o_ref.at[0, :, 0, 1])
    core = [links.to(links.core, s_ref, o_ref.at[1, :, 0, 0])]
    if in_vmem:
        o_ref[0, :, 0, 0] = s_ref[...]
    else:
        links.load(s_ref, o_ref.at[0, :, 0, 0])
    between(0)
    for copy in across:
        copy.arrive()
    onward = links.to(links.near, o_ref.at[0, :, 1, 0], o_ref.at[0, :, 1, 1])
    core.append(links.to(links.core, o_ref.at[0, :, 1, 0], o_ref.at[1, :, 1, 0]))
    near.arrive()
    core.append(links.to(links.core, o_ref.at[0, :, 0, 1], o_ref.at[1, :, 0, 1]))
    between(1)
    onward.arrive()
    core.append(links.to(links.core, o_ref.at[0, :, 1, 1], o_ref.at[1, :, 1, 1]))
    between(2)
    for copy in core:
        copy.arrive()
    for copy in (*across, near, core[0]):
        copy.sent()


def sum_in(links, bufs, chunk, partial, between=nothing):
    p_ref, core_in, out_y, in_y, out_t, in_t, hold = bufs
    order = ((1, 1), (0, 1), (1, 0), (0, 0))
    partial(1)
    core = [links.to(links.core, p_ref.at[1, :, t, y], core_in.at[i]) for i, (t, y) in enumerate(order)]
    partial(0)
    near = []
    for i in range(2):
        t, y = order[i]
        core[i].arrive()
        out_y[i] = (p_ref[0, :, t, y].astype(F32) + core_in[i].astype(F32)).astype(BF16)
        near.append(links.to(links.near, out_y.at[i], in_y.at[i]))
    between(0)
    core[2].arrive()
    hold[...] = p_ref[0, :, 1, 0].astype(F32) + core_in[2].astype(F32)
    near[0].arrive()
    for i in range(p_ref.shape[-1] // chunk):
        a, b = slice(i * chunk, (i + 1) * chunk), slice((i ^ 1) * chunk, ((i ^ 1) + 1) * chunk)
        out_t[:, :, b] = (hold[:, :, a] + in_y[0, :, :, a].astype(F32)).astype(BF16)
    across = links.to(links.across, out_t, in_t)
    between(1)
    core[3].arrive()
    hold[...] = p_ref[0, :, 0, 0].astype(F32) + core_in[3].astype(F32)
    near[1].arrive()
    hold[...] += in_y[1].astype(F32)
    between(2)
    across.arrive()
    hold[...] += in_t[...].astype(F32)
    for copy in (*core, *near, across):
        copy.sent()


def loop(count, step):
    def one(i, carry):
        step(i)
        return carry

    lax.fori_loop(0, count, one, 0)


def rows_of(ref, i):
    value = ref[i // 2, i % 2]
    return value.reshape(-1, value.shape[-1])


def away_rows(a_cols, b_ref, away_ref):
    depth, tile = away_ref.shape[0], 512

    def step(i):
        product = tn(a_cols(pl.multiple_of(depth + i * tile, tile), tile), b_ref[...])
        away_ref[pl.ds(pl.multiple_of(i * tile, tile), tile), :] = product.astype(BF16)

    loop(depth // tile, step)


def keep_rows(a_cols, b_ref, fold_ref, own_ref, send_ref):
    f = own_ref.shape[0]
    own_ref[...] = tn(a_cols(0, f), b_ref[...]) + fold_ref[:f, :].astype(F32)

    def step(i):
        at = pl.multiple_of(i * f, f)
        product = tn(a_cols(pl.multiple_of(at + f, f), f), b_ref[...])
        send_ref[pl.ds(at, f), :] = (product + fold_ref[pl.ds(pl.multiple_of(at + f, f), f), :].astype(F32)).astype(BF16)

    loop(3, step)


def middle_kernel(
    low_ref, cot_ref, gain_ref, attn_ref, wo_ref, c_ref, wd_ref, wg_ref, gate_ref, up_ref,
    middle_ref, dmid_ref, gain_grad_ref, dall_ref, mixed_ref, own_d_ref, got_d_ref, own_g_ref, send_g_ref, keep_u_ref, away_u_ref,
    attn, wo, p, core_in, out_y, in_y, out_t, in_t, hold, xm_s, xm, c, wd, wg, wu, dact, gate, act, dg, du,
    away_d, fold_d, away_g, fold_g, own_d, send_d, own_g, send_g, up_tile, send, recv, *, batch_mask, chunk,
):
    links = Links(send, recv, batch_mask)
    f, ff = own_d.shape[0], act.shape[1]
    to, load = links.to, links.load
    loads = [load(attn_ref, attn), load(wo_ref, wo)]
    links.greet()

    def rows(ref, q):
        return ref.at[pl.ds(q * f, f), :]

    down = [to(links.seq, rows(wd_ref, q), rows(wd, q + 4)) for q in (1, 3)]
    gate_z = [to(links.batch, links.half(gate_ref, 0), rows(wg, 1)), to(links.both, links.half(gate_ref, 1), rows(wg, 3))]
    gates = [to(links.seq, rows(wg_ref, 2), rows(wg, 6))]
    up_t = to(links.across, links.half(up_ref, 1), rows(wu, 2))
    ups = []
    for copy in loads:
        copy.arrive()
    down += [load(rows(wd_ref, q), rows(wd, q)) for q in (0, 1, 2, 3, 4, 6)]
    gates += [load(rows(wg_ref, q), rows(wg, q)) for q in (0, 2, 4)]
    c_load = load(c_ref, c)
    up_own = load(links.half(up_ref, 0), rows(wu, 0))
    bufs = (p, core_in, out_y, in_y, out_t, in_t, hold)

    def out_partial(k):
        for m in range(2):
            at = (k * 2 + m) * attn.shape[0] // 4
            p[k, m] = nt(attn[at : at + attn.shape[0] // 4], wo[...]).astype(BF16).reshape(p.shape[2:])

    def while_out(stage):
        if stage == 0:
            ups.append(to(links.seq, links.half(up_ref, 0), rows(wu, 4)))
        if stage == 1:
            up_t.arrive()
            ups.append(to(links.seq, rows(wu, 2), rows(wu, 6)))

    sum_in(links, bufs, chunk, out_partial, while_out)
    for m in range(2):
        middle = low_ref[m].astype(F32) + hold[m]
        middle_ref[m] = middle
        xm_s[m] = (middle * inverse_rms(middle) * gain_ref[...]).astype(BF16)

    up_z = []

    def while_xm(stage):
        if stage == 0:
            for copy in gate_z:
                copy.arrive()
            up_z.append(to(links.batch, links.half(up_ref, 0), rows(wu, 1)))
            gates.extend(to(links.seq, rows(wg, q), rows(wg, q + 4)) for q in (1, 3))
            for copy in (*down, c_load):
                copy.arrive()

            def step(i):
                at = pl.ds(pl.multiple_of(i * 512, 512), 512)
                dact[at, :] = nn(c[at, :], wd[...])

            loop(c.shape[0] // 512, step)
        if stage == 2:
            up_z[0].arrive()
            up_z.append(to(links.both, links.half(up_ref, 1), rows(wu, 3)))
            ups.append(to(links.seq, rows(wu, 1), rows(wu, 5)))

    spread_in(links, xm_s, xm, chunk, while_xm)
    for copy in gates:
        copy.arrive()

    def gate_step(i):
        at = pl.ds(pl.multiple_of(i * 256, 256), 256)
        gate[at, :] = nn(rows_of(xm, i), wg[...])

    loop(4, gate_step)
    up_z[1].arrive()
    ups.append(to(links.seq, rows(wu, 3), rows(wu, 7)))
    up_own.arrive()
    for copy in ups:
        copy.arrive()

    def up_step(i):
        base = pl.multiple_of(i * 256, 256)
        up_tile[...] = nn(rows_of(xm, i), wu[...])

        def part(j):
            at, here = pl.ds(pl.multiple_of(base + j * 32, 32), 32), pl.ds(pl.multiple_of(j * 32, 32), 32)
            g, u, d = gate[at, :], up_tile[here, :], dact[at, :]
            sig = 1.0 / (1.0 + jnp.exp(-g))
            silu = g * sig
            act[at, :] = (silu * u).astype(BF16)
            dg[at, :] = (d * u * sig * (1.0 + g * (1.0 - sig))).astype(BF16)
            du[at, :] = (d * silu).astype(BF16)

        loop(8, part)

    loop(4, up_step)

    def c_cols(at, n):
        return c[:, pl.ds(at, n)]

    def xm_cols(at, n):
        return xm[:, :, :, :, :, pl.ds(at, n)].reshape(-1, n)

    away_rows(c_cols, act, away_d)
    fold = to(links.seq, away_d, fold_d)

    def back_partial(k):
        def step(m):
            at = pl.ds(pl.multiple_of((k * 2 + m) * 256, 256), 256)
            value = nt(dg[at, :], wg[...]) + nt(du[at, :], wu[...])
            p[k, m] = value.astype(BF16).reshape(p.shape[2:])

        loop(2, step)

    later = []

    def while_back(stage):
        if stage == 0:
            away_rows(xm_cols, dg, away_g)
            later.append(to(links.seq, away_g, fold_g))
        if stage == 1:
            def step(i):
                at = pl.ds(pl.multiple_of(i * 512, 512), 512)
                dact[at, :] = tn(xm_cols(pl.multiple_of(i * 512, 512), 512), du[...])

            loop(2, step)
            later.append(load(dact, keep_u_ref))

    sum_in(links, bufs, chunk, back_partial, while_back)
    for m in range(2):
        middle = middle_ref[m]
        grad = cot_ref[m].astype(F32) + norm_grad(hold[m], middle, gain_ref[...], gain_grad_ref, m)
        dmid_ref[m] = grad
        xm_s[m] = grad.astype(BF16)

    settles = []

    def while_mid(stage):
        if stage == 0:
            fold.arrive()
            fold.sent()
            keep_rows(c_cols, act, fold_d, own_d, send_d)
            for q, target in ((0, links.batch), (2, links.both), (1, links.across)):
                settles.append(to(target, rows(send_d, q), rows(got_d_ref, q)))
            settles.append(load(own_d, own_d_ref))
            away_rows(xm_cols, du, away_d)
            settles.append(load(away_d, away_u_ref))
        if stage == 1:

            def step(i):
                at = pl.ds(pl.multiple_of(i * 256, 256), 256)
                p[i // 2, i % 2] = nt(act[at, :], wd[...]).astype(BF16).reshape(p.shape[2:])

            loop(4, step)
            settles.append(load(p, mixed_ref))

    spread_in(links, xm_s, dall_ref, chunk, while_mid, in_vmem=False)
    later[0].arrive()
    keep_rows(xm_cols, dg, fold_g, own_g, send_g)
    load(own_g, own_g_ref)
    load(send_g, send_g_ref)
    links.finish()


def middle_call(batch_mask, low, cot, gain, attn, w_out, cot_all, w_down, w_gate, gate_weight, up_weight, collective_id):
    _, rows, width = low.shape
    tokens, columns = attn.shape
    ff = w_down.shape[1]
    f = w_down.shape[0] // 8
    share, full = (2, rows, width), (2, 2, 2, 2, rows, width)
    vmem, hbm = pl.BlockSpec(memory_space=pltpu.VMEM), pl.BlockSpec(memory_space=pltpu.HBM)
    like = jax.ShapeDtypeStruct
    return pl.pallas_call(
        functools.partial(middle_kernel, batch_mask=batch_mask, chunk=2 * width // 8),
        in_specs=[vmem] * 3 + [hbm] * 7,
        out_specs=[vmem] * 3 + [hbm] * 8,
        out_shape=[
            like(share, F32),
            like(share, F32),
            like((1, width), F32),
            like(full, BF16),
            like(full, BF16),
            like((f, ff), F32),
            like((3 * f, ff), BF16),
            like((f, ff), F32),
            like((3 * f, ff), BF16),
            like((4 * f, ff), F32),
            like((4 * f, ff), BF16),
        ],
        scratch_shapes=[
            pltpu.VMEM((tokens, columns), BF16),
            pltpu.VMEM((width, columns), BF16),
            pltpu.VMEM(full, BF16),
            pltpu.VMEM((4, *share), BF16),
            pltpu.VMEM((2, *share), BF16),
            pltpu.VMEM((2, *share), BF16),
            pltpu.VMEM(share, BF16),
            pltpu.VMEM(share, BF16),
            pltpu.VMEM(share, F32),
            pltpu.VMEM(share, BF16),
            pltpu.VMEM(full, BF16),
            pltpu.VMEM((tokens, width), BF16),
            *[pltpu.VMEM((width, ff), BF16)] * 3,
            *[pltpu.VMEM((tokens, ff), F32)] * 2,
            *[pltpu.VMEM((tokens, ff), BF16)] * 3,
            *[pltpu.VMEM((4 * f, ff), BF16)] * 4,
            pltpu.VMEM((f, ff), F32),
            pltpu.VMEM((3 * f, ff), BF16),
            pltpu.VMEM((f, ff), F32),
            pltpu.VMEM((3 * f, ff), BF16),
            pltpu.VMEM((256, ff), F32),
            pltpu.SemaphoreType.DMA((96,)),
            pltpu.SemaphoreType.DMA((96,)),
        ],
        compiler_params=pltpu.CompilerParams(
            collective_id=collective_id, has_side_effects=True, vmem_limit_bytes=60 * MIB
        ),
        cost_estimate=TINY_COST,
    )(low, cot, gain, attn, w_out, cot_all, w_down, w_gate, gate_weight, up_weight)


def local(
    hidden_in,
    lengths,
    query_weight,
    key_matrix,
    value_matrix,
    out_weight,
    gate_weight,
    up_weight,
    down_weight,
    attn_gain,
    query_gain,
    key_gain,
    mlp_gain,
    cotangent,
):
    ring = lax.axis_size("blk")
    bits = ring.bit_length() - 1
    batch_bit = bits - 1
    extra_bits = [i for i in range(bits) if i not in (TENSOR_BIT, SEQ_BIT, batch_bit)]
    seq_bits = [SEQ_BIT, *extra_bits]
    parts = 1 << len(seq_bits)
    bit_order = [batch_bit, TENSOR_BIT, SEQ_BIT, *extra_bits]
    b_mask, t_mask, x_mask = 1 << batch_bit, 1 << TENSOR_BIT, 1 << SEQ_BIT
    blk, head = lax.axis_index("blk"), lax.axis_index("head")
    batch, tensor = bit_of(blk, batch_bit), bit_of(blk, TENSOR_BIT)

    local_rows, width = hidden_in.shape[1:]
    block_rows = local_rows * lax.axis_size("head")
    half = block_rows // 2
    row_features = width // ring
    head_size = query_gain.shape[0]
    scaling = head_size ** (-0.5)
    tokens = 16 * local_rows
    heads = query_weight.shape[1] // (2 * head_size)
    ff = gate_weight.shape[1] // 2

    def moved(values, place_of):
        axis = values.ndim - 1
        return jnp.concatenate(
            [
                lax.dynamic_slice_in_dim(values, place_of(i) * row_features, row_features, axis)
                for i in range(ring)
            ],
            axis=axis,
        )

    def regroup(values):
        return moved(values, lambda p: blk ^ sum(((p >> i) & 1) << b for i, b in enumerate(bit_order)))

    def ungroup(values):
        return moved(values, lambda n: sum(bit_of(blk ^ n, b) << i for i, b in enumerate(bit_order)))

    def everything(ref):
        return ref

    def mask_of(p):
        return sum(((p >> i) & 1) << b for i, b in enumerate(bit_order))

    def rows_at(p):
        return lambda ref: ref.at[pl.ds(p * row_features, row_features), :]

    def half_cut(n, other):
        def cut(ref):
            place = bit_of(lax.axis_index("blk"), TENSOR_BIT)
            place = 1 - place if other else place
            return ref.at[:, pl.ds(pl.multiple_of(place * n, n), n)]

        return cut

    def send_over(plan, weight, buffer, p, point):
        mask, n = mask_of(p), weight.shape[1] // 2
        plan.copy((plan.read(weight), half_cut(n, mask & t_mask)), (buffer, rows_at(p)), mask, point=point)

    def keep_own(plan, weight, buffer, point, onward=True):
        here, n = plan.read(weight), weight.shape[1] // 2
        if onward:
            plan.copy((here, half_cut(n, 0)), (buffer, rows_at(4)), x_mask, point=point)
        plan.local((here, half_cut(n, 0)), (buffer, rows_at(0)), (row_features, n), point=point)

    def send_on(plan, buffer, places, point, after=None):
        for p in places:
            plan.copy((buffer, rows_at(p)), (buffer, rows_at(p + 4)), x_mask, after=after, point=point)

    def lay(plan, array, buffer, p, point=0, columns=None, onward=False):
        here = plan.read(array)
        cut = (lambda ref: ref.at[:, pl.ds(*columns)]) if columns else everything
        if onward:
            plan.copy((here, cut), (buffer, rows_at(p + 4)), x_mask, point=point)
        plan.local((here, cut), (buffer, rows_at(p)), (row_features, columns[1] if columns else array.shape[1]), point)

    def fresh_for(plan, weights):
        return plan.fresh(buffer_shape(weights), BF16)

    def buffer_shape(weights):
        return (8 * row_features, sum(w.shape[1] for w in weights) // 2)

    def whole_weight(buffer):
        pieces = [buffer]
        for b in extra_bits:
            pieces = pieces + [over_blk(c, 1 << b) for c in pieces]
        return jnp.concatenate(pieces, axis=0) if extra_bits else buffer

    def split_grad(grad):
        for b in reversed(extra_bits):
            n = grad.shape[0] // 2
            grad = grad[:n] + over_blk(grad[n:].astype(BF16), 1 << b).astype(F32)
        n = grad.shape[0] // 2
        return grad[:n], grad[n:].astype(BF16)

    def weight_sum(a, b):
        return split_grad(tn(a, b)) if extra_bits else weight_grad(a, b)

    def fold(plan, source, shape, point=0):
        plan.copy((source, everything), (plan.fresh(shape, BF16), everything), x_mask, point=point)

    def fold_part(plan, source, buffer, start, n, point=0):
        def part(ref):
            return ref.at[:, pl.ds(start, n)]

        plan.copy((source, part), (buffer, part), x_mask, point=point)

    def to_settle(keep, got):
        total = keep + got.astype(F32)
        return total[:row_features], total[row_features:].astype(BF16)

    def settle(plan, away, t_point=0):
        out, here = plan.fresh(away.shape, away.dtype), plan.read(away)
        for i, mask in ((0, b_mask), (2, b_mask | t_mask), (1, t_mask)):
            plan.copy((here, rows_at(i)), (out, rows_at(i)), mask, point=t_point if mask == t_mask else 0)

    def settled(sources, column_widths):
        if all(w % 128 == 0 for w in column_widths):
            return assemble(tensor, sources, column_widths)
        f, results = row_features, []
        widths = iter(column_widths)
        for own, got in sources:
            own = own + got[:f].astype(F32)
            other = got[f : 2 * f].astype(F32) + got[2 * f :].astype(F32)
            at = 0
            while at < own.shape[1]:
                w = next(widths)
                results.append(in_order(tensor, own[:, at : at + w], other[:, at : at + w], 1))
                at += w
        return results

    chunk = 2 * row_features
    ids = iter(range(100))

    def spread(flat, plan, fills=(), limit=None):
        (out,), rest = run(plan, spread_main(flat, chunk), next(ids), fills=fills, limit=limit)
        return out.reshape(tokens, width), rest

    share = (2, local_rows, width)

    def gather_sum(partial, plan, extra, outs_like, finish, fills=()):
        return run(plan, gather_main(partial, chunk, extra, outs_like, finish), next(ids), fills=fills)

    def like(shape, dtype):
        return jax.ShapeDtypeStruct(shape, dtype)

    aligned = row_features % 128 == 0
    local_order = bit_order if aligned else []

    def split_batch(rows):
        mine = lax.dynamic_index_in_dim(rows, batch, 0, keepdims=False)
        theirs = lax.dynamic_index_in_dim(rows, 1 - batch, 0, keepdims=False)
        return mine, theirs

    def natural(rows):
        return rows if aligned else ungroup(rows)

    length_row = lax.dynamic_index_in_dim(lengths, batch, 0, keepdims=False)
    doc_ends = jnp.cumsum(length_row)
    batch_flip = jnp.arange(2, dtype=jnp.int32)[:, None] << batch_bit
    tensor_flip = jnp.arange(2, dtype=jnp.int32)[None, :] << TENSOR_BIT
    q_blocks = (blk ^ batch_flip ^ tensor_flip).reshape(4)
    index = jnp.arange(2 * half, dtype=jnp.int32)
    in_block = token_offset(head, index, local_rows).reshape(2, 1, half)
    token_index = q_blocks[None, :, None] * block_rows + in_block
    passed = doc_ends <= token_index[..., None]
    doc_start = jnp.max(jnp.where(passed, doc_ends, 0), axis=-1).astype(jnp.int32)
    position = (token_index - doc_start).reshape(tokens)
    start_lanes = jnp.tile(jnp.transpose(doc_start, (1, 0, 2)).reshape(4, 1, 2 * half), (1, 1, heads))
    k_blocks = q_blocks
    for b in seq_bits:
        k_blocks = jnp.concatenate([k_blocks, k_blocks ^ (1 << b)])
    least_start = jnp.min(doc_start, axis=(0, 2))[:, None]
    last_start = jnp.max(doc_start, axis=(0, 2))[:, None]
    k_first = (k_blocks * block_rows)[None, :]
    none = (k_blocks[None, :] > q_blocks[:, None]) | (k_first + block_rows <= least_start)
    whole = (k_blocks[None, :] < q_blocks[:, None]) & (k_first >= last_start)
    flags = jnp.where(none, 0, jnp.where(whole, 1, 2))
    meta = jnp.concatenate([head[None], q_blocks, k_blocks, flags.reshape(-1)]).astype(jnp.int32)

    inverse_freq = THETA ** (-jnp.arange(head_size // 2, dtype=F32) / (head_size // 2))
    angles = position.astype(F32)[:, None] * inverse_freq[None, :]
    cosine, sine = jnp.cos(angles), jnp.sin(angles)
    cosine = jnp.concatenate([cosine, cosine], axis=1)
    sine = jnp.concatenate([-sine, sine], axis=1)

    def rms(values):
        return lax.rsqrt(jnp.mean(values * values, axis=-1, keepdims=True) + EPS)

    def norm_back(grad, normed, inverse, gain):
        scaled = grad * gain
        return inverse * (scaled - normed * jnp.mean(scaled * normed, axis=-1, keepdims=True))

    gains_in = jnp.stack([attn_gain, mlp_gain]).astype(F32)
    gain_q = query_gain.astype(F32)[None]
    gain_k = key_gain.astype(F32)[None]

    q_columns, k_columns = heads * head_size, head_size
    a_weights = (query_weight, key_matrix, value_matrix)

    def halves(weights, which):
        return jnp.concatenate(
            [lax.dynamic_slice_in_dim(w, which * (w.shape[1] // 2), w.shape[1] // 2, 1) for w in weights], axis=1
        )

    mine, theirs = split_batch(hidden_in)
    other = over_blk(theirs, b_mask)
    a_own, a_other = halves(a_weights, tensor), halves(a_weights, 1 - tensor)
    a_by_t = over_blk(a_other, t_mask)
    a_by_b = over_blk(a_own, b_mask)
    early = over_blk(jnp.concatenate([a_own, halves((down_weight,), tensor)], axis=1), x_mask)
    (mine, other, cosine, sine, start_lanes, meta) = pin((mine, other, cosine, sine, start_lanes, meta))
    if aligned:
        x_low, xa, gains_in = enter(blk, bit_order, mine, other, gains_in)
        gain_a, gain_m = gains_in[0], gains_in[1]
    else:
        gains_in = regroup(gains_in)
        gain_a, gain_m = gains_in[0], gains_in[1]
        x_low = regroup(jnp.concatenate([mine, other], axis=0))
        x_wide = x_low.astype(F32)
        xa = (x_wide * rms(x_wide) * gain_a).astype(BF16)

    plan = Plan()
    a_columns = a_own.shape[1]
    w_a = fresh_for(plan, a_weights)
    by_tb = plan.copy((plan.read(a_other), everything), (w_a, rows_at(3)), b_mask | t_mask)
    lay(plan, a_by_t, w_a, 2, onward=True)
    lay(plan, a_by_b, w_a, 1, onward=True)
    lay(plan, a_own, w_a, 0)
    lay(plan, early, w_a, 4, columns=(0, a_columns))
    here, cot_out = plan.read(cotangent), plan.fresh((2, local_rows, width), BF16)
    plan.copy(
        (here, lambda ref: ref.at[1 - bit_of(lax.axis_index("blk"), batch_bit)]),
        (cot_out, lambda ref: ref.at[1]),
        b_mask,
        point=1,
    )
    plan.local(
        (here, lambda ref: ref.at[bit_of(lax.axis_index("blk"), batch_bit)]),
        (cot_out, lambda ref: ref.at[0]),
        (local_rows, width),
    )
    w_out = fresh_for(plan, (out_weight,))
    send_over(plan, out_weight, w_out, 1, 1)
    send_over(plan, out_weight, w_out, 3, 1)
    send_over(plan, out_weight, w_out, 2, 1)
    keep_own(plan, out_weight, w_out, 0)
    w_down = fresh_for(plan, (down_weight,))
    send_over(plan, down_weight, w_down, 2, 1)
    keep_own(plan, down_weight, w_down, 0, onward=False)
    lay(plan, early, w_down, 4, columns=(a_columns, ff))
    w_gate = fresh_for(plan, (gate_weight,))
    keep_own(plan, gate_weight, w_gate, 1)
    send_on(plan, w_a, (3,), 2, after=by_tb)
    xa, (w_qkv, cot, w_out, w_down, w_gate) = spread(xa, plan, limit=56 * MIB)
    w_qkv = whole_weight(w_qkv)
    cot = cot.reshape(2 * local_rows, width)
    cot = enter(blk, bit_order, cot)[0] if aligned else regroup(cot)
    query, key_value, raw = prepare(xa, w_qkv, cosine, sine, gain_q, gain_k, heads)

    plan = Plan()
    kv_out = plan.fresh(key_value.shape, BF16)
    plan.copy((plan.read(key_value), everything), (kv_out, everything), x_mask)
    w_out = plan.through(w_out)
    send_on(plan, w_out, (1, 2, 3), 0)
    w_down = plan.through(w_down)
    send_over(plan, down_weight, w_down, 1, 0)
    send_over(plan, down_weight, w_down, 3, 0)
    send_on(plan, w_down, (2,), 1)
    w_gate = plan.through(w_gate)
    send_over(plan, gate_weight, w_gate, 2, 1)
    cot_all, (kv_x, w_out, w_down, w_gate) = spread(cot, plan)
    w_out = whole_weight(w_out)
    key_value = [key_value, kv_x]
    for b in extra_bits:
        key_value = key_value + [over_blk(c, 1 << b) for c in key_value]
    key_value = jnp.stack(key_value)
    keys = key_value[..., :head_size].reshape(parts, 2, 4, half, head_size)
    values = key_value[..., head_size:].reshape(parts, 2, 4, half, head_size)
    query = query.reshape(2, 4, half, q_columns)
    attn, attn_t, total_e = attend(meta, query, keys, values, start_lanes, scaling)
    attn = attn.reshape(tokens, q_columns)

    x_low = x_low.reshape(share)
    if extra_bits:
        plan = Plan()
        w_down = plan.through(w_down)
        send_on(plan, w_down, (1, 3), 0)
        w_gate = plan.through(w_gate)
        send_over(plan, gate_weight, w_gate, 1, 0)
        send_over(plan, gate_weight, w_gate, 3, 0)
        send_on(plan, w_gate, (2,), 0)
        w_up = fresh_for(plan, (up_weight,))
        send_over(plan, up_weight, w_up, 2, 0)
        keep_own(plan, up_weight, w_up, 1)
        (middle, xm), (w_down, w_gate, w_up) = gather_sum(
            nt(attn, w_out).astype(BF16),
            plan,
            [x_low, gain_m[None]],
            [like(share, F32), like(share, BF16)],
            finish_middle,
        )
        w_down = whole_weight(w_down)

        plan = Plan()
        w_gate = plan.through(w_gate)
        w_up = plan.through(w_up)
        by_b = len(plan.jobs)
        send_over(plan, up_weight, w_up, 1, 0)
        send_on(plan, w_gate, (1, 3), 0)
        send_on(plan, w_up, (2,), 1)
        by_tb = plan.copy(
            (plan.read(up_weight), half_cut(ff, True)), (w_up, rows_at(3)), b_mask | t_mask, after=by_b, point=2
        )
        send_on(plan, w_up, (1,), 2)
        send_on(plan, w_up, (3,), 3, after=by_tb)
        xm, (w_gate, w_up, d_active) = spread(
            xm.reshape(2 * local_rows, width), plan, [fill_product(cot_all, w_down, 0)]
        )
        w_gate, w_up = whole_weight(w_gate), whole_weight(w_up)
        gate = nn(xm, w_gate)
        up = nn(xm, w_up)
        sig = jax.nn.sigmoid(gate)
        silu = gate * sig
        active = (silu * up).astype(BF16)
        d_gate = (d_active * up * sig * (1.0 + gate * (1.0 - sig))).astype(BF16)
        d_up = (d_active * silu).astype(BF16)

        keep_down, away_down = weight_sum(cot_all, active)
        got_x = over_blk(away_down, x_mask)
        (d_gate, d_up, away_down) = pin((d_gate, d_up, away_down))
        ff_cut = ff // 2
        plan, fills = Plan(), []
        if extra_bits:
            keep_gate, away_gate = weight_sum(xm, d_gate)
            keep_up, away_up = weight_sum(xm, d_up)
            source, point = plan.read(away_gate), 0
        else:
            fills = [fill_weight_grad(xm, d_gate, 0), fill_weight_grad(xm, d_up, 1)]
            source, point = ("fill", (0, 1)), 1
        gate_x = plan.fresh((4 * row_features, ff), BF16)
        fold_part(plan, source, gate_x, 0, ff_cut, point)
        (d_middle, d_mid, gain_m_grad), (gate_x, *filled) = gather_sum(
            back_through((d_gate, d_up), (w_gate, w_up)),
            plan,
            [cot.reshape(share), middle, gain_m[None]],
            [like(share, F32), like(share, BF16), like((1, width), F32)],
            finish_mlp_norm,
            fills,
        )
        if filled:
            keep_gate, away_gate, keep_up, away_up = filled
        (d_mid, got_x) = pin((d_mid, got_x))
        own_down, away_down = to_settle(keep_down, got_x)

        plan = Plan()
        settle(plan, away_down, 1)
        gate_x = plan.through(gate_x)
        fold_part(plan, plan.read(away_gate), gate_x, ff_cut, ff - ff_cut)
        up_x = plan.fresh(away_up.shape, BF16)
        fold_part(plan, plan.read(away_up), up_x, 0, ff_cut)
        d_mid_all, (got_down, gate_x, up_x, mixed_partial) = spread(
            d_mid.reshape(2 * local_rows, width), plan, [fill_back(active, w_down, 0)]
        )
        (g_down,) = settled([(own_down, got_down)], (ff,))
        own_gate, away_gate = to_settle(keep_gate, gate_x)
    else:
        (
            middle, d_middle, gain_m_grad, d_mid_all, mixed_partial, own_down, got_down, own_gate, away_gate, keep_up, away_up,
        ) = middle_call(
            b_mask, x_low, cot.reshape(share), gain_m[None], attn, w_out, cot_all, w_down, w_gate, gate_weight, up_weight, next(ids)
        )
        d_mid_all = d_mid_all.reshape(tokens, width)
        mixed_partial = mixed_partial.reshape(tokens, width)
        (g_down,) = settled([(own_down, got_down)], (ff,))
        up_x = None
    d_attn = nn(d_mid_all, w_out).astype(BF16).reshape(2, 4, half, q_columns)
    d_query, d_key, d_value = attend_back(
        meta, query, d_attn, keys, values, start_lanes, attn_t, total_e, scaling
    )
    d_key = d_key.reshape(parts, tokens, head_size)
    d_value = d_value.reshape(parts, tokens, head_size)
    for b in reversed(extra_bits):
        n = d_key.shape[0] // 2
        d_key = d_key[:n] + over_blk(d_key[n:].astype(BF16), 1 << b).astype(F32)
        d_value = d_value[:n] + over_blk(d_value[n:].astype(BF16), 1 << b).astype(F32)

    plan = Plan()
    away_kv = jnp.concatenate([d_key[1], d_value[1]], axis=1).astype(BF16)
    fold(plan, plan.read(away_kv), away_kv.shape)
    settle(plan, away_gate)
    if up_x is None:
        fold(plan, plan.read(away_up), away_up.shape)
    else:
        up_x = plan.through(up_x)
        fold_part(plan, plan.read(away_up), up_x, ff_cut, ff - ff_cut)
    (mixed,), (got_kv, got_gate, up_x, *filled) = gather_sum(
        mixed_partial,
        plan,
        [middle],
        [like(share, BF16)],
        functools.partial(finish_mixed, bit_order=local_order),
        [] if extra_bits else [fill_weight_grad(d_mid_all, attn, 0)],
    )
    keep_out, away_out = filled if filled else weight_sum(d_mid_all, attn)
    (g_gate,) = settled([(own_gate, got_gate)], (ff,))
    own_up, away_up = to_settle(keep_up, up_x)
    mixed = natural(mixed)
    mixed_got = over_blk(mixed[1], b_mask)
    d_qkv, d_xa_partial, gains_qk = prepare_back(
        d_query.reshape(tokens, q_columns), d_key, d_value, got_kv, raw, cosine, sine, gain_q, gain_k, w_qkv, heads
    )
    (d_xa_partial, mixed_got) = pin((d_xa_partial, mixed_got))

    plan, fills = Plan(), []
    settle(plan, away_up)
    fold(plan, plan.read(away_out), away_out.shape)
    if extra_bits:
        keep_qkv, away_qkv = weight_sum(xa, d_qkv)
        fold(plan, plan.read(away_qkv), away_qkv.shape)
    else:
        fills = [fill_weight_grad(xa, d_qkv, 0)]
        fold(plan, ("fill", (0, 1)), (4 * row_features, a_columns), 1)
    (input_own, input_away, gain_a_grad), (got_up, out_x, got, *filled) = gather_sum(
        d_xa_partial,
        plan,
        [x_low, d_middle, gain_a[None]],
        [like((local_rows, width), F32), like((local_rows, width), BF16), like((1, width), F32)],
        functools.partial(finish_input, bit_order=local_order),
        fills,
    )
    if filled:
        keep_qkv = filled[0]
    own_out, away_out = to_settle(keep_out, out_x)
    (g_up,) = settled([(own_up, got_up)], (ff,))
    own_qkv, away_qkv = to_settle(keep_qkv, got)

    plan = Plan()
    settle(plan, away_qkv)
    settle(plan, away_out)
    input_got = plan.fresh((local_rows, width), BF16)
    plan.copy((plan.read(natural(input_away)), everything), (input_got, everything), b_mask)
    sums = jnp.concatenate([ungroup(gain_a_grad[0]), gains_qk[0], gains_qk[1], ungroup(gain_m_grad[0])])
    (sums,), (got_a, got_o, input_got) = run(
        plan, total_main(sums.reshape(-1, 128)), next(ids), [1 << i for i in range(bits)]
    )
    g_query, g_key, g_value, g_out = settled(
        [(own_qkv, got_a), (own_out, got_o)], (q_columns, k_columns, k_columns, q_columns)
    )
    mixed = in_order(batch, mixed[:1], mixed_got[None], 0)
    input_grad = in_order(batch, natural(input_own)[None], input_got.astype(F32)[None], 0)
    gains = jnp.split(sums.reshape(-1), [width, width + head_size, width + 2 * head_size])
    return (
        mixed,
        input_grad,
        g_query,
        g_key,
        g_value,
        g_out,
        g_gate,
        g_up,
        g_down,
        *gains,
    )


def solution(mesh):
    rows = P(None, ("blk", "head"), None)
    weight = P("blk", "head")
    return jax.shard_map(
        local,
        mesh=mesh,
        in_specs=(rows, P(), *([weight] * 7), P(), P(), P(), P(), rows),
        out_specs=(rows, rows, *([weight] * 7), P(), P(), P(), P()),
        check_vma=False,
    )
```

```python
import functools
import math

import jax
import jax.numpy as jnp
from jax import lax
from jax.experimental import pallas as pl
from jax.experimental.pallas import tpu as pltpu
from jax.sharding import PartitionSpec as P

EPS = 1e-06
THETA = 1000000.0
LOG2E = 1.4426950408889634
F32 = jnp.float32
BF16 = jnp.bfloat16

MIB = 1024 * 1024
TINY_COST = pl.CostEstimate(flops=0, bytes_accessed=0, transcendentals=0)
VMEM_LIMIT = 32 * MIB
TENSOR_BIT = 1
SEQ_BIT = 0


def nt(a, b):
    return lax.dot_general(a, b, (((1,), (1,)), ((), ())), preferred_element_type=F32)


def tn(a, b):
    return lax.dot_general(a, b, (((0,), (0,)), ((), ())), preferred_element_type=F32)


def nn(a, b):
    return jnp.dot(a, b, preferred_element_type=F32)


def bit_of(value, bit):
    return (value >> bit) & 1


def over_blk(value, mask):
    count = lax.axis_size("blk")
    return lax.ppermute(value, "blk", [(i, i ^ mask) for i in range(count)])


def over_head(value, mask):
    count = lax.axis_size("head")
    return lax.ppermute(value, "head", [(i, i ^ mask) for i in range(count)])


def pin(values):
    return lax.optimization_barrier(values)


def in_order(flag, own, other, axis):
    return jnp.where(
        flag == 0,
        jnp.concatenate([own, other], axis=axis),
        jnp.concatenate([other, own], axis=axis),
    )


def token_offset(head_place, index, sub):
    core, upper, inner = index // (2 * sub), (index // sub) % 2, index % sub
    return (head_place ^ (upper * 2) ^ core) * sub + inner


def allowed_mask(meta_ref, start_row, q_block, k_block, rows, half, q_lanes):
    sub = half // 2
    head_place = meta_ref[0]
    k_index = lax.broadcasted_iota(jnp.int32, (2 * half, 1), 0)
    k_token = token_offset(head_place, k_index, sub) + k_block * (2 * half)
    q_index = lax.broadcasted_iota(jnp.int32, (1, q_lanes), 1) % (2 * half)
    q_token = token_offset(head_place, q_index, sub) + q_block * (2 * half)
    return (k_token <= q_token) & (k_token >= start_row)


def stacked(ref, heads, width):
    return jnp.concatenate(
        [ref[c, 0, :, h * width : (h + 1) * width] for h in range(heads) for c in range(2)], axis=0
    )


def key_rows(ref, part, block):
    return jnp.concatenate([ref[part, 0, block], ref[part, 1, block]], axis=0)


def attend_kernel(meta_ref, q_ref, k_ref, v_ref, start_ref, o_ref, ot_ref, l_ref, vt_ref, acc_ref, sum_ref, *, factor, heads):
    q_pos = pl.program_id(0)
    parts, _, blocks, half, width = k_ref.shape
    lanes = heads * 2 * half

    @pl.when(q_pos == 0)
    def _():
        for part in range(parts):
            for block in range(blocks):
                vt_ref[part * blocks + block] = key_rows(v_ref, part, block).T

    q_rows = stacked(q_ref, heads, width)
    acc_ref[...] = jnp.zeros_like(acc_ref)
    sum_ref[...] = jnp.zeros_like(sum_ref)
    start_row = start_ref[0]
    q_block = meta_ref[1 + q_pos]
    total = parts * blocks

    def add(kb, masked):
        e = jnp.exp2(nt(key_rows(k_ref, kb // blocks, kb % blocks), q_rows) * factor)
        if masked:
            k_block = meta_ref[1 + blocks + kb]
            e = jnp.where(allowed_mask(meta_ref, start_row, q_block, k_block, None, half, lanes), e, 0.0)
        sum_ref[...] += jnp.sum(e, axis=0, keepdims=True)
        acc_ref[...] += nn(vt_ref[kb], e.astype(BF16))

    def step(kb, carry):
        flag = meta_ref[1 + blocks + total + q_pos * total + kb]

        @pl.when(flag == 1)
        def _():
            add(kb, False)

        @pl.when(flag == 2)
        def _():
            add(kb, True)

        return carry

    lax.fori_loop(0, total, step, 0)
    out = acc_ref[...] / sum_ref[...]
    ot_ref[0] = out
    l_ref[0] = sum_ref[...]
    rows = out.T
    for h in range(heads):
        for c in range(2):
            at = (h * 2 + c) * half
            o_ref[c, 0, :, h * width : (h + 1) * width] = rows[at : at + half].astype(BF16)


def attend_back_kernel(
    meta_ref, q_ref, do_ref, k_ref, v_ref, start_ref, ot_ref, l_ref, dq_ref, dk_ref, dv_ref, kt_ref, acc_ref, *, factor, scaling, heads
):
    q_pos = pl.program_id(0)
    parts, _, blocks, half, width = k_ref.shape
    lanes = heads * 2 * half

    @pl.when(q_pos == 0)
    def _():
        dk_ref[...] = jnp.zeros_like(dk_ref)
        dv_ref[...] = jnp.zeros_like(dv_ref)
        for part in range(parts):
            for block in range(blocks):
                kt_ref[part * blocks + block] = key_rows(k_ref, part, block).T

    q_rows = stacked(q_ref, heads, width)
    do_rows = stacked(do_ref, heads, width)
    delta = jnp.sum(do_rows.astype(F32).T * ot_ref[0], axis=0, keepdims=True)
    inverse = 1.0 / l_ref[0]
    acc_ref[...] = jnp.zeros_like(acc_ref)
    start_row = start_ref[0]
    q_block = meta_ref[1 + q_pos]
    total = parts * blocks

    def add(kb, masked):
        part, block = kb // blocks, kb % blocks
        e = jnp.exp2(nt(key_rows(k_ref, part, block), q_rows) * factor)
        if masked:
            k_block = meta_ref[1 + blocks + kb]
            e = jnp.where(allowed_mask(meta_ref, start_row, q_block, k_block, None, half, lanes), e, 0.0)
        p = e * inverse
        dp = nt(key_rows(v_ref, part, block), do_rows)
        ds = (p * (dp - delta)).astype(BF16)
        dv = nn(p.astype(BF16), do_rows)
        dk = nn(ds, q_rows) * scaling
        for c in range(2):
            dv_ref[part, c, block] += dv[c * half : (c + 1) * half]
            dk_ref[part, c, block] += dk[c * half : (c + 1) * half]
        acc_ref[...] += nn(kt_ref[kb], ds)

    def step(kb, carry):
        flag = meta_ref[1 + blocks + total + q_pos * total + kb]

        @pl.when(flag == 1)
        def _():
            add(kb, False)

        @pl.when(flag == 2)
        def _():
            add(kb, True)

        return carry

    lax.fori_loop(0, total, step, 0)
    rows = acc_ref[...].T * scaling
    for h in range(heads):
        for c in range(2):
            at = (h * 2 + c) * half
            dq_ref[c, 0, :, h * width : (h + 1) * width] = rows[at : at + half]


def attend(meta, q, k, v, start, scaling):
    _, blocks, half, columns = q.shape
    parts, width = k.shape[0], k.shape[-1]
    heads = columns // width
    lanes = heads * 2 * half
    total = parts * blocks
    row_spec = pl.BlockSpec((2, 1, half, columns), lambda i: (0, i, 0, 0))
    key_spec = pl.BlockSpec(k.shape, lambda i: (0, 0, 0, 0, 0))
    lane_spec = pl.BlockSpec((1, 1, lanes), lambda i: (i, 0, 0))
    return pl.pallas_call(
        functools.partial(attend_kernel, factor=scaling * LOG2E, heads=heads),
        grid=(blocks,),
        in_specs=[pl.BlockSpec(memory_space=pltpu.SMEM), row_spec, key_spec, key_spec, lane_spec],
        out_specs=[row_spec, pl.BlockSpec((1, width, lanes), lambda i: (i, 0, 0)), lane_spec],
        out_shape=[
            jax.ShapeDtypeStruct(q.shape, BF16),
            jax.ShapeDtypeStruct((blocks, width, lanes), F32),
            jax.ShapeDtypeStruct((blocks, 1, lanes), F32),
        ],
        scratch_shapes=[
            pltpu.VMEM((total, width, 2 * half), BF16),
            pltpu.VMEM((width, lanes), F32),
            pltpu.VMEM((1, lanes), F32),
        ],
        compiler_params=pltpu.CompilerParams(vmem_limit_bytes=VMEM_LIMIT),
        cost_estimate=pl.CostEstimate(
            flops=2 * 2 * lanes * 2 * half * width * blocks * total,
            bytes_accessed=8 * q.size + 8 * k.size,
            transcendentals=lanes * 2 * half * blocks * total,
        ),
    )(meta, q, k, v, start)


def attend_back(meta, q, do, k, v, start, out_t, total_e, scaling):
    _, blocks, half, columns = q.shape
    parts, width = k.shape[0], k.shape[-1]
    heads = columns // width
    lanes = heads * 2 * half
    total = parts * blocks
    row_spec = pl.BlockSpec((2, 1, half, columns), lambda i: (0, i, 0, 0))
    key_spec = pl.BlockSpec(k.shape, lambda i: (0, 0, 0, 0, 0))
    lane_spec = pl.BlockSpec((1, 1, lanes), lambda i: (i, 0, 0))
    return pl.pallas_call(
        functools.partial(attend_back_kernel, factor=scaling * LOG2E, scaling=scaling, heads=heads),
        grid=(blocks,),
        in_specs=[
            pl.BlockSpec(memory_space=pltpu.SMEM),
            row_spec,
            row_spec,
            key_spec,
            key_spec,
            lane_spec,
            pl.BlockSpec((1, width, lanes), lambda i: (i, 0, 0)),
            lane_spec,
        ],
        out_specs=[row_spec, key_spec, key_spec],
        out_shape=[
            jax.ShapeDtypeStruct(q.shape, F32),
            jax.ShapeDtypeStruct(k.shape, F32),
            jax.ShapeDtypeStruct(k.shape, F32),
        ],
        scratch_shapes=[
            pltpu.VMEM((total, width, 2 * half), BF16),
            pltpu.VMEM((width, lanes), F32),
        ],
        compiler_params=pltpu.CompilerParams(vmem_limit_bytes=VMEM_LIMIT),
        cost_estimate=pl.CostEstimate(
            flops=5 * 2 * lanes * 2 * half * width * blocks * total,
            bytes_accessed=12 * q.size + 16 * k.size,
            transcendentals=lanes * 2 * half * blocks * total,
        ),
    )(meta, q, do, k, v, start, out_t, total_e)


def prepare_kernel(x_ref, w_ref, cos_ref, sin_ref, gq_ref, gk_ref, q_ref, kv_ref, raw_ref, *, heads, width):
    acc = jnp.dot(x_ref[...], w_ref[...], preferred_element_type=F32)
    raw_ref[...] = acc[:, : (heads + 1) * width]
    for h in range(heads + 1):
        part = acc[:, h * width : (h + 1) * width]
        normed = part * lax.rsqrt(jnp.mean(part * part, axis=-1, keepdims=True) + EPS)
        scaled = normed * (gq_ref if h < heads else gk_ref)[...]
        turned = (scaled * cos_ref[...] + pltpu.roll(scaled, width // 2, 1) * sin_ref[...]).astype(BF16)
        if h < heads:
            q_ref[:, h * width : (h + 1) * width] = turned
        else:
            kv_ref[:, :width] = turned
    kv_ref[:, width:] = acc[:, (heads + 1) * width :].astype(BF16)


def prepare(x, w, cos, sin, gain_q, gain_k, heads):
    tokens, depth = x.shape
    width, tile = gain_q.shape[1], 256
    row = lambda n: pl.BlockSpec((tile, n), lambda i: (i, 0))
    fixed = lambda a: pl.BlockSpec(a.shape, lambda i: (0, 0))
    return pl.pallas_call(
        functools.partial(prepare_kernel, heads=heads, width=width),
        grid=(tokens // tile,),
        in_specs=[row(depth), fixed(w), row(width), row(width), fixed(gain_q), fixed(gain_k)],
        out_specs=[row(heads * width), row(2 * width), row((heads + 1) * width)],
        out_shape=[
            jax.ShapeDtypeStruct((tokens, heads * width), BF16),
            jax.ShapeDtypeStruct((tokens, 2 * width), BF16),
            jax.ShapeDtypeStruct((tokens, (heads + 1) * width), F32),
        ],
        compiler_params=pltpu.CompilerParams(vmem_limit_bytes=VMEM_LIMIT),
        cost_estimate=TINY_COST,
    )(x, w, cos, sin, gain_q, gain_k)


def prepare_back_kernel(
    dq_ref, dk_ref, dv_ref, got_ref, raw_ref, cos_ref, sin_ref, gq_ref, gk_ref, w_ref, d_ref, p_ref, g_ref, *, heads, width
):
    @pl.when(pl.program_id(0) == 0)
    def _():
        g_ref[...] = jnp.zeros_like(g_ref)

    got = got_ref[...].astype(F32)
    for h in range(heads + 1):
        at = slice(h * width, (h + 1) * width)
        grad = dq_ref[:, at] if h < heads else dk_ref[0] + got[:, :width]
        gain = (gq_ref if h < heads else gk_ref)[...]
        raw = raw_ref[:, at]
        inverse = lax.rsqrt(jnp.mean(raw * raw, axis=-1, keepdims=True) + EPS)
        normed = raw * inverse
        turned = grad * cos_ref[...] - pltpu.roll(grad, width // 2, 1) * sin_ref[...]
        row = 0 if h < heads else 1
        g_ref[row : row + 1, :] += jnp.sum(turned * normed, axis=0, keepdims=True)
        scaled = turned * gain
        d_ref[:, at] = (inverse * (scaled - normed * jnp.mean(scaled * normed, axis=-1, keepdims=True))).astype(BF16)
    d_ref[:, (heads + 1) * width :] = (dv_ref[0] + got[:, width:]).astype(BF16)
    p_ref[...] = nt(d_ref[...], w_ref[...]).astype(BF16)


def prepare_back(dq, dk, dv, got, raw, cos, sin, gain_q, gain_k, w, heads):
    tokens, width, tile = dq.shape[0], gain_q.shape[1], 256
    row = lambda n: pl.BlockSpec((tile, n), lambda i: (i, 0))
    part = pl.BlockSpec((1, tile, width), lambda i: (0, i, 0))
    fixed = lambda a: pl.BlockSpec(a.shape, lambda i: (0, 0))
    return pl.pallas_call(
        functools.partial(prepare_back_kernel, heads=heads, width=width),
        grid=(tokens // tile,),
        in_specs=[
            row(heads * width),
            part,
            part,
            row(2 * width),
            row((heads + 1) * width),
            row(width),
            row(width),
            fixed(gain_q),
            fixed(gain_k),
            fixed(w),
        ],
        out_specs=[row(w.shape[1]), row(w.shape[0]), pl.BlockSpec((8, width), lambda i: (0, 0))],
        out_shape=[
            jax.ShapeDtypeStruct((tokens, w.shape[1]), BF16),
            jax.ShapeDtypeStruct((tokens, w.shape[0]), BF16),
            jax.ShapeDtypeStruct((8, width), F32),
        ],
        compiler_params=pltpu.CompilerParams(vmem_limit_bytes=VMEM_LIMIT),
        cost_estimate=TINY_COST,
    )(dq, dk, dv, got, raw, cos, sin, gain_q, gain_k, w)


def place_of_block(blk, bit_order, p):
    return blk ^ sum(((p >> i) & 1) << b for i, b in enumerate(bit_order))


def enter_kernel(blk_ref, *refs, bit_order, normed):
    if normed:
        mine_ref, other_ref, gain_ref, low_ref, out_ref, gains_ref = refs
    else:
        mine_ref, low_ref = refs
    rows, width = mine_ref.shape
    n = width >> len(bit_order)
    for p in range(1 << len(bit_order)):
        at = pl.ds(pl.multiple_of(place_of_block(blk_ref[0], bit_order, p) * n, n), n)
        low_ref[:rows, p * n : (p + 1) * n] = mine_ref[:, at]
        if normed:
            low_ref[rows:, p * n : (p + 1) * n] = other_ref[:, at]
            gains_ref[:, p * n : (p + 1) * n] = gain_ref[:, at]
    if normed:
        values = low_ref[...].astype(F32)
        inverse = lax.rsqrt(jnp.mean(values * values, axis=-1, keepdims=True) + EPS)
        out_ref[...] = (values * inverse * gains_ref[:1]).astype(BF16)


def enter(blk, bit_order, mine, other=None, gain=None):
    rows, width = mine.shape
    normed = gain is not None
    total = (2 * rows if normed else rows, width)
    vmem = pl.BlockSpec(memory_space=pltpu.VMEM)
    operands = [mine, other, gain] if normed else [mine]
    return pl.pallas_call(
        functools.partial(enter_kernel, bit_order=bit_order, normed=normed),
        in_specs=[pl.BlockSpec(memory_space=pltpu.SMEM), *[vmem] * len(operands)],
        out_specs=[vmem] * (3 if normed else 1),
        out_shape=[
            *[jax.ShapeDtypeStruct(total, BF16)] * (2 if normed else 1),
            *([jax.ShapeDtypeStruct(gain.shape, F32)] if normed else []),
        ],
        compiler_params=pltpu.CompilerParams(vmem_limit_bytes=VMEM_LIMIT),
        cost_estimate=TINY_COST,
    )(blk[None].astype(jnp.int32), *operands)


def assemble_kernel(place_ref, *refs, sources, widths):
    ins, outs = refs[: 2 * sources], refs[2 * sources :]
    place, k, at = place_ref[0], 0, 0
    for own_ref, got_ref in zip(ins[::2], ins[1::2]):
        f, at = own_ref.shape[0], 0
        while at < own_ref.shape[1]:
            w, cut = widths[k], slice(at, at + widths[k])
            mine = pl.ds(pl.multiple_of(place * w, w), w)
            theirs = pl.ds(pl.multiple_of((1 - place) * w, w), w)
            outs[k][:, mine] = own_ref[:, cut] + got_ref[:f, cut].astype(F32)
            outs[k][:, theirs] = got_ref[f : 2 * f, cut].astype(F32) + got_ref[2 * f :, cut].astype(F32)
            at += w
            k += 1


def assemble(place, sources, widths):
    vmem = pl.BlockSpec(memory_space=pltpu.VMEM)
    flat = [a for pair in sources for a in pair]
    return pl.pallas_call(
        functools.partial(assemble_kernel, sources=len(sources), widths=widths),
        in_specs=[pl.BlockSpec(memory_space=pltpu.SMEM), *[vmem] * len(flat)],
        out_specs=[vmem] * len(widths),
        out_shape=[jax.ShapeDtypeStruct((sources[0][0].shape[0], 2 * w), F32) for w in widths],
        compiler_params=pltpu.CompilerParams(vmem_limit_bytes=VMEM_LIMIT),
        cost_estimate=TINY_COST,
    )(place[None].astype(jnp.int32), *flat)


def back_kernel(*refs):
    *ins, out_ref = refs
    n = len(ins) // 2
    out_ref[...] = sum(nt(d[...], w[...]) for d, w in zip(ins[:n], ins[n:])).astype(BF16)


def back_through(grads, weights):
    tokens, depth, tile = grads[0].shape[0], weights[0].shape[0], 256
    return pl.pallas_call(
        back_kernel,
        grid=(depth // tile,),
        in_specs=[
            *[pl.BlockSpec(g.shape, lambda i: (0, 0)) for g in grads],
            *[pl.BlockSpec((tile, w.shape[1]), lambda i: (i, 0)) for w in weights],
        ],
        out_specs=pl.BlockSpec((tokens, tile), lambda i: (0, i)),
        out_shape=jax.ShapeDtypeStruct((tokens, depth), BF16),
        compiler_params=pltpu.CompilerParams(vmem_limit_bytes=VMEM_LIMIT),
        cost_estimate=TINY_COST,
    )(*grads, *weights)


def weight_grad_kernel(a_ref, b_ref, keep_ref, away_ref):
    product = tn(a_ref[...], b_ref[...])
    first = pl.program_id(0) < pl.num_programs(0) // 2

    @pl.when(first)
    def _():
        keep_ref[...] = product

    @pl.when(jnp.logical_not(first))
    def _():
        away_ref[...] = product.astype(BF16)


def weight_grad(a, b):
    tokens, depth = a.shape
    n, tile = b.shape[1], 256
    steps = depth // tile
    return pl.pallas_call(
        weight_grad_kernel,
        grid=(steps,),
        in_specs=[
            pl.BlockSpec((tokens, tile), lambda i: (0, i)),
            pl.BlockSpec((tokens, n), lambda i: (0, 0)),
        ],
        out_specs=[
            pl.BlockSpec((tile, n), lambda i: (jnp.minimum(i, steps // 2 - 1), 0)),
            pl.BlockSpec((tile, n), lambda i: (jnp.maximum(i - steps // 2, 0), 0)),
        ],
        out_shape=[
            jax.ShapeDtypeStruct((depth // 2, n), F32),
            jax.ShapeDtypeStruct((depth // 2, n), BF16),
        ],
        compiler_params=pltpu.CompilerParams(vmem_limit_bytes=VMEM_LIMIT),
        cost_estimate=TINY_COST,
    )(a, b)


def remote(src, dst, send, recv, target):
    copy = pltpu.make_async_remote_copy(
        src_ref=src, dst_ref=dst, send_sem=send, recv_sem=recv, device_id=target, device_id_type=pl.DeviceIdType.MESH
    )
    copy.start()
    return copy


class Plan:
    def __init__(self):
        self.inputs, self.shapes, self.aliases, self.jobs = [], [], {}, []

    def read(self, array):
        self.inputs.append(array)
        return ("in", len(self.inputs) - 1)

    def fresh(self, shape, dtype):
        self.shapes.append(jax.ShapeDtypeStruct(shape, dtype))
        return ("out", len(self.shapes) - 1)

    def through(self, array):
        self.inputs.append(array)
        self.aliases[len(self.inputs) - 1] = len(self.shapes)
        return self.fresh(array.shape, array.dtype)

    def copy(self, src, dst, mask, after=None, point=0):
        self.jobs.append((src, dst, mask, after, point, None))
        return len(self.jobs) - 1

    def local(self, src, dst, shape, point=0):
        self.jobs.append((src, dst, 0, None, point, shape))
        return len(self.jobs) - 1


class Fill:
    def __init__(self, inputs, outputs, step, point):
        self.inputs, self.outputs, self.step, self.point = inputs, outputs, step, point

    def scratch(self):
        shapes = [pltpu.VMEM(a.shape, a.dtype) for a in (*self.inputs, *self.outputs)]
        return [*shapes, pltpu.SemaphoreType.DMA((len(shapes),))]


def fill_weight_grad(a, b, point):
    depth, n, tile = a.shape[1], b.shape[1], 256
    half = depth // 2

    def step(ins, outs):
        (a_ref, b_ref), (keep_ref, away_ref) = ins, outs

        def one(i, carry):
            at = pl.ds(pl.multiple_of(i * tile, tile), tile)
            keep_ref[at, :] = tn(a_ref[:, at], b_ref[...])
            far = pl.ds(pl.multiple_of(half + i * tile, tile), tile)
            away_ref[at, :] = tn(a_ref[:, far], b_ref[...]).astype(BF16)
            return carry

        lax.fori_loop(0, half // tile, one, 0)

    outputs = [jax.ShapeDtypeStruct((half, n), F32), jax.ShapeDtypeStruct((half, n), BF16)]
    return Fill([a, b], outputs, step, point)


def fill_back(grad, weight, point):
    tokens, depth, tile = grad.shape[0], weight.shape[0], 256

    def step(ins, outs):
        (g_ref, w_ref), (out_ref,) = ins, outs

        def one(i, carry):
            at = pl.ds(pl.multiple_of(i * tile, tile), tile)
            out_ref[:, at] = nt(g_ref[...], w_ref[at, :]).astype(BF16)
            return carry

        lax.fori_loop(0, depth // tile, one, 0)

    return Fill([grad, weight], [jax.ShapeDtypeStruct((tokens, depth), BF16)], step, point)


def fill_product(left, right, point):
    tokens, n, tile = left.shape[0], right.shape[1], 256

    def step(ins, outs):
        (l_ref, r_ref), (out_ref,) = ins, outs

        def one(i, carry):
            at = pl.ds(pl.multiple_of(i * tile, tile), tile)
            out_ref[at, :] = nn(l_ref[at, :], r_ref[...])
            return carry

        lax.fori_loop(0, tokens // tile, one, 0)

    return Fill([left, right], [jax.ShapeDtypeStruct((tokens, n), F32)], step, point)


def run(plan, main, collective_id, greeted=(), fills=(), limit=None):
    inputs, in_specs, out_shapes, out_specs, scratch, body, own_limit = main
    limit = limit or own_limit + sum(math.prod(s.shape) * s.dtype.itemsize for f in fills for s in f.scratch()[:-1])
    f_in, f_out = [a for f in fills for a in f.inputs], [a for f in fills for a in f.outputs]
    n_in, n_out = len(inputs), len(out_shapes)
    m_in, m_out = len(plan.inputs), len(plan.shapes)
    jobs = plan.jobs
    local_jobs = [i for i, job in enumerate(jobs) if not job[2]]
    masks = sorted({*greeted, *[job[2] for job in jobs if job[2]]} - {1 << TENSOR_BIT})
    any_spec = pl.BlockSpec(memory_space=pltpu.HBM)

    def kernel(*refs):
        main_in, refs = refs[:n_in], refs[n_in:]
        plan_in, refs = refs[:m_in], refs[m_in:]
        fill_in, refs = refs[: len(f_in)], refs[len(f_in) :]
        main_out, refs = refs[:n_out], refs[n_out:]
        plan_out, refs = refs[:m_out], refs[m_out:]
        fill_out, refs = refs[: len(f_out)], refs[len(f_out) :]
        send, recv, *rest = refs
        bounce = dict(zip(local_jobs, rest))
        rest = rest[len(local_jobs) :]
        parts = []
        for f in fills:
            k, m = len(f.inputs), len(f.outputs)
            (*held, sems), rest = rest[: k + m + 1], rest[k + m + 1 :]
            loads = [pltpu.make_async_copy(fill_in[i], held[i], sems.at[i]) for i in range(k)]
            stores = [pltpu.make_async_copy(held[k + i], fill_out[i], sems.at[k + i]) for i in range(m)]
            fill_in, fill_out = fill_in[k:], fill_out[m:]
            for copy in loads:
                copy.start()
            parts.append((f, held[:k], held[k:], loads, stores))

        def compute(point):
            for f, ins, outs, loads, stores in parts:
                if f.point == point:
                    for copy in loads:
                        copy.wait()
                    f.step(ins, outs)
                    for copy in stores:
                        copy.start()

        blk, head = lax.axis_index("blk"), lax.axis_index("head")
        core, near, across = (blk, head ^ 1), (blk, head ^ 2), (blk ^ (1 << TENSOR_BIT), head)
        barrier = pltpu.get_barrier_semaphore()
        partners = [core, near, across, *[(blk ^ m, head) for m in masks]]
        for target in partners:
            pl.semaphore_signal(barrier, inc=1, device_id=target, device_id_type=pl.DeviceIdType.MESH)
        pl.semaphore_wait(barrier, len(partners))
        started, arrived, halfway = {}, set(), []

        def arrive(i):
            if i not in arrived:
                arrived.add(i)
                (started[i].wait_recv if jobs[i][2] else started[i].wait)()

        def part(side):
            (kind, index), cut = side
            if kind == "fill":
                return cut(parts[index[0]][2][index[1]])
            return cut((plan_in if kind == "in" else plan_out)[index])

        def issue(point):
            for i in list(halfway):
                started[i].wait()
                started[i] = pltpu.make_async_copy(bounce[i], part(jobs[i][1]), recv.at[i])
                started[i].start()
                halfway.remove(i)
            for i, (src, dst, mask, after, at, shape) in enumerate(jobs):
                if i in started or (at != point and point is not None):
                    continue
                if after is not None:
                    arrive(after)
                if mask:
                    started[i] = remote(part(src), part(dst), send.at[i], recv.at[i], (blk ^ mask, head))
                else:
                    started[i] = pltpu.make_async_copy(part(src), bounce[i], send.at[i])
                    started[i].start()
                    halfway.append(i)

        point = 0
        for _ in body((core, near, across), main_in, main_out, rest):
            issue(point)
            compute(point)
            point += 1
        issue(None)
        issue(None)
        for i in range(len(jobs)):
            arrive(i)
            if jobs[i][2]:
                started[i].wait_send()
        for *_, stores in parts:
            for copy in stores:
                copy.wait()

    results = pl.pallas_call(
        kernel,
        out_shape=[*out_shapes, *plan.shapes, *f_out],
        in_specs=[*in_specs, *[any_spec] * (m_in + len(f_in))],
        out_specs=[*out_specs, *[any_spec] * (m_out + len(f_out))],
        scratch_shapes=[
            pltpu.SemaphoreType.DMA((max(1, len(jobs)),)),
            pltpu.SemaphoreType.DMA((max(1, len(jobs)),)),
            *[pltpu.VMEM(jobs[i][5], BF16) for i in local_jobs],
            *[s for f in fills for s in f.scratch()],
            *scratch,
        ],
        input_output_aliases={n_in + i: n_out + o for i, o in plan.aliases.items()},
        compiler_params=pltpu.CompilerParams(
            collective_id=collective_id, has_side_effects=True, vmem_limit_bytes=limit
        ),
        cost_estimate=TINY_COST,
    )(*inputs, *plan.inputs, *f_in)
    return results[:n_out], results[n_out:]


def spread_main(flat, chunk):
    rows, width = flat.shape[0] // 2, flat.shape[1]
    pieces = width // chunk

    def body(partners, ins, outs, scratch):
        core, near, across = partners
        (s_ref,), (o_ref,), (hold, local_sem, send, recv) = ins, outs, scratch
        first = remote(s_ref, o_ref.at[0, :, 0, 1], send.at[0], recv.at[0], near)
        second = [
            remote(
                s_ref.at[:, :, pl.ds(i * chunk, chunk)],
                o_ref.at[0, :, 1, 0, :, pl.ds((i ^ 1) * chunk, chunk)],
                send.at[6 + i],
                recv.at[6 + i],
                across,
            )
            for i in range(pieces)
        ]
        third = remote(s_ref, o_ref.at[1, :, 0, 0], send.at[1], recv.at[1], core)
        held = pltpu.make_async_copy(s_ref, hold, local_sem.at[0])
        held.start()
        yield
        held.wait()
        own = pltpu.make_async_copy(hold, o_ref.at[0, :, 0, 0], local_sem.at[1])
        own.start()
        for copy in second:
            copy.wait_recv()
        fourth = remote(o_ref.at[0, :, 1, 0], o_ref.at[0, :, 1, 1], send.at[2], recv.at[2], near)
        fifth = remote(o_ref.at[0, :, 1, 0], o_ref.at[1, :, 1, 0], send.at[3], recv.at[3], core)
        yield
        first.wait_recv()
        sixth = remote(o_ref.at[0, :, 0, 1], o_ref.at[1, :, 0, 1], send.at[4], recv.at[4], core)
        yield
        fourth.wait_recv()
        seventh = remote(o_ref.at[0, :, 1, 1], o_ref.at[1, :, 1, 1], send.at[5], recv.at[5], core)
        yield
        own.wait()
        for copy in (first, *second, third, fourth, fifth, sixth, seventh):
            copy.wait_send()
        for copy in (third, fifth, sixth, seventh):
            copy.wait_recv()

    any_spec = pl.BlockSpec(memory_space=pltpu.HBM)
    return (
        [flat.reshape(2, rows, width)],
        [any_spec],
        [jax.ShapeDtypeStruct((2, 2, 2, 2, rows, width), flat.dtype)],
        [any_spec],
        [
            pltpu.VMEM((2, rows, width), flat.dtype),
            pltpu.SemaphoreType.DMA((2,)),
            pltpu.SemaphoreType.DMA((6 + pieces,)),
            pltpu.SemaphoreType.DMA((6 + pieces,)),
        ],
        body,
        8 * MIB,
    )


def gather_main(partial, chunk, extra, outs_like, finish):
    rows, width = partial.shape[0] // 16, partial.shape[1]
    share = (2, rows, width)
    pieces = width // chunk

    def body(partners, ins, outs, scratch):
        core, near, across = partners
        p_ref, *extra_refs = ins
        core_in, out_y, in_y, out_t, in_t, hold, send, recv = scratch
        order = ((1, 1), (0, 1), (1, 0), (0, 0))
        from_core = [
            remote(p_ref.at[1, :, t, y], core_in.at[i], send.at[i], recv.at[i], core) for i, (t, y) in enumerate(order)
        ]
        from_y = []
        for i in range(2):
            t, y = order[i]
            from_core[i].wait_recv()
            out_y[i] = (p_ref[0, :, t, y].astype(F32) + core_in[i].astype(F32)).astype(BF16)
            from_y.append(remote(out_y.at[i], in_y.at[i], send.at[4 + i], recv.at[4 + i], near))
        yield
        from_core[2].wait_recv()
        hold[...] = p_ref[0, :, 1, 0].astype(F32) + core_in[2].astype(F32)
        from_y[0].wait_recv()
        for i in range(pieces):
            a, b = slice(i * chunk, (i + 1) * chunk), slice((i ^ 1) * chunk, ((i ^ 1) + 1) * chunk)
            out_t[:, :, b] = (hold[:, :, a] + in_y[0, :, :, a].astype(F32)).astype(BF16)
        from_t = remote(out_t, in_t, send.at[6], recv.at[6], across)
        yield
        from_core[3].wait_recv()
        hold[...] = p_ref[0, :, 0, 0].astype(F32) + core_in[3].astype(F32)
        from_y[1].wait_recv()
        hold[...] += in_y[1].astype(F32)
        yield
        from_t.wait_recv()
        hold[...] += in_t[...].astype(F32)
        finish(hold, extra_refs, outs)
        for copy in (*from_core, *from_y, from_t):
            copy.wait_send()

    vmem_spec = pl.BlockSpec(memory_space=pltpu.VMEM)
    return (
        [partial.reshape(2, 2, 2, 2, rows, width), *extra],
        [vmem_spec] * (1 + len(extra)),
        outs_like,
        [vmem_spec] * len(outs_like),
        [
            pltpu.VMEM((4, *share), BF16),
            pltpu.VMEM((2, *share), BF16),
            pltpu.VMEM((2, *share), BF16),
            pltpu.VMEM(share, BF16),
            pltpu.VMEM(share, BF16),
            pltpu.VMEM(share, F32),
            pltpu.SemaphoreType.DMA((7,)),
            pltpu.SemaphoreType.DMA((7,)),
        ],
        body,
        24 * MIB,
    )


def inverse_rms(values):
    return lax.rsqrt(jnp.mean(values * values, axis=-1, keepdims=True) + EPS)


def finish_middle(total, extra, outs):
    (low_ref, gain_ref), (middle_ref, normed_ref) = extra, outs
    for m in range(2):
        middle = low_ref[m].astype(F32) + total[m]
        middle_ref[m] = middle
        normed_ref[m] = (middle * inverse_rms(middle) * gain_ref[...]).astype(BF16)


def norm_grad(total, values, gain, gain_grad_ref, m):
    inverse = inverse_rms(values)
    normal = values * inverse
    part = jnp.sum(total * normal, axis=0, keepdims=True)
    gain_grad_ref[...] = part if m == 0 else gain_grad_ref[...] + part
    scaled = total * gain
    return inverse * (scaled - normal * jnp.mean(scaled * normal, axis=-1, keepdims=True))


def finish_mlp_norm(total, extra, outs):
    (cot_ref, middle_ref, gain_ref), (grad_ref, low_ref, gain_grad_ref) = extra, outs
    for m in range(2):
        grad = cot_ref[m].astype(F32) + norm_grad(total[m], middle_ref[m], gain_ref[...], gain_grad_ref, m)
        grad_ref[m] = grad
        low_ref[m] = grad.astype(BF16)


def store_ungrouped(value, ref, blk, bit_order, lead=()):
    n = value.shape[-1] >> len(bit_order)
    for p in range(1 << len(bit_order)):
        block = value[:, p * n : (p + 1) * n]
        if bit_order and n % 128 == 0:
            at = pl.ds(pl.multiple_of(place_of_block(blk, bit_order, p) * n, n), n)
        else:
            at = pl.ds(p * n, n)
        ref[(*lead, slice(None), at)] = block.astype(ref.dtype)


def finish_mixed(total, extra, outs, *, bit_order):
    (middle_ref,), (mixed_ref,) = extra, outs
    blk = lax.axis_index("blk")
    for m in range(2):
        store_ungrouped(middle_ref[m] + total[m], mixed_ref, blk, bit_order, (m,))


def finish_input(total, extra, outs, *, bit_order):
    (low_ref, mid_ref, gain_ref), (own_ref, away_ref, gain_grad_ref) = extra, outs
    blk = lax.axis_index("blk")
    for m in range(2):
        grad = mid_ref[m] + norm_grad(total[m], low_ref[m].astype(F32), gain_ref[...], gain_grad_ref, m)
        store_ungrouped(grad, own_ref if m == 0 else away_ref, blk, bit_order)


def total_main(values):
    rows, width = values.shape
    rounds = 2 + lax.axis_size("blk").bit_length() - 1

    def body(partners, ins, outs, scratch):
        (v_ref,), (o_ref,) = ins, outs
        out_buf, in_buf, send, recv = scratch
        blk, head = lax.axis_index("blk"), lax.axis_index("head")
        o_ref[...] = v_ref[...]
        yield
        for i in range(rounds):
            target = (blk, head ^ (1 << i)) if i < 2 else (blk ^ (1 << (i - 2)), head)
            out_buf[i] = o_ref[...]
            copy = remote(out_buf.at[i], in_buf.at[i], send.at[i], recv.at[i], target)
            copy.wait_recv()
            o_ref[...] += in_buf[i]
            copy.wait_send()
        yield

    vmem_spec = pl.BlockSpec(memory_space=pltpu.VMEM)
    return (
        [values],
        [vmem_spec],
        [jax.ShapeDtypeStruct(values.shape, F32)],
        [vmem_spec],
        [
            pltpu.VMEM((rounds, rows, width), F32),
            pltpu.VMEM((rounds, rows, width), F32),
            pltpu.SemaphoreType.DMA((rounds,)),
            pltpu.SemaphoreType.DMA((rounds,)),
        ],
        body,
        8 * MIB,
    )


class Moving:
    def __init__(self, copy, away):
        self.copy, self.away, self.here, self.gone = copy, away, False, not away

    def arrive(self):
        if not self.here:
            self.here = True
            (self.copy.wait_recv if self.away else self.copy.wait)()

    def sent(self):
        if not self.gone:
            self.gone = True
            self.copy.wait_send()


class Links:
    def __init__(self, send, recv, batch_mask):
        self.send, self.recv, self.all = send, recv, []
        blk, head = lax.axis_index("blk"), lax.axis_index("head")
        self.core, self.near, self.across = (blk, head ^ 1), (blk, head ^ 2), (blk ^ (1 << TENSOR_BIT), head)
        self.seq, self.batch = (blk ^ (1 << SEQ_BIT), head), (blk ^ batch_mask, head)
        self.both = (blk ^ (batch_mask | (1 << TENSOR_BIT)), head)
        self.place = bit_of(blk, TENSOR_BIT)
        self.blk = blk

    def greet(self):
        barrier = pltpu.get_barrier_semaphore()
        partners = (self.core, self.near, self.across, self.seq, self.batch, self.both)
        for target in partners:
            pl.semaphore_signal(barrier, inc=1, device_id=target, device_id_type=pl.DeviceIdType.MESH)
        pl.semaphore_wait(barrier, len(partners))

    def to(self, target, src, dst):
        i = len(self.all)
        self.all.append(Moving(remote(src, dst, self.send.at[i], self.recv.at[i], target), True))
        return self.all[-1]

    def load(self, src, dst):
        copy = pltpu.make_async_copy(src, dst, self.recv.at[len(self.all)])
        copy.start()
        self.all.append(Moving(copy, False))
        return self.all[-1]

    def finish(self):
        for moving in self.all:
            moving.arrive()
            moving.sent()

    def half(self, ref, other):
        n = ref.shape[1] // 2
        place = 1 - self.place if other else self.place
        return ref.at[:, pl.ds(pl.multiple_of(place * n, n), n)]


def nothing(stage):
    pass


def spread_in(links, s_ref, o_ref, chunk, between=nothing, in_vmem=True):
    pieces = s_ref.shape[-1] // chunk
    across = [
        links.to(
            links.across,
            s_ref.at[:, :, pl.ds(i * chunk, chunk)],
            o_ref.at[0, :, 1, 0, :, pl.ds((i ^ 1) * chunk, chunk)],
        )
        for i in range(pieces)
    ]
    near = links.to(links.near, s_ref, o_ref.at[0, :, 0, 1])
    core = [links.to(links.core, s_ref, o_ref.at[1, :, 0, 0])]
    if in_vmem:
        o_ref[0, :, 0, 0] = s_ref[...]
    else:
        links.load(s_ref, o_ref.at[0, :, 0, 0])
    between(0)
    for copy in across:
        copy.arrive()
    onward = links.to(links.near, o_ref.at[0, :, 1, 0], o_ref.at[0, :, 1, 1])
    core.append(links.to(links.core, o_ref.at[0, :, 1, 0], o_ref.at[1, :, 1, 0]))
    near.arrive()
    core.append(links.to(links.core, o_ref.at[0, :, 0, 1], o_ref.at[1, :, 0, 1]))
    between(1)
    onward.arrive()
    core.append(links.to(links.core, o_ref.at[0, :, 1, 1], o_ref.at[1, :, 1, 1]))
    between(2)
    for copy in core:
        copy.arrive()
    for copy in (*across, near, core[0]):
        copy.sent()


def sum_in(links, bufs, chunk, partial, between=nothing, far=None):
    p_ref, core_in, out_y, in_y, out_t, in_t, hold = bufs
    order = ((1, 1), (0, 1), (1, 0), (0, 0))
    if partial:
        partial(1)
        far = p_ref.at[1]
    core = [links.to(links.core, far.at[:, t, y], core_in.at[i]) for i, (t, y) in enumerate(order)]
    if partial:
        partial(0)
    near = []
    for i in range(2):
        t, y = order[i]
        core[i].arrive()
        out_y[i] = (p_ref[0, :, t, y].astype(F32) + core_in[i].astype(F32)).astype(BF16)
        near.append(links.to(links.near, out_y.at[i], in_y.at[i]))
    between(0)
    core[2].arrive()
    hold[...] = p_ref[0, :, 1, 0].astype(F32) + core_in[2].astype(F32)
    near[0].arrive()
    for i in range(p_ref.shape[-1] // chunk):
        a, b = slice(i * chunk, (i + 1) * chunk), slice((i ^ 1) * chunk, ((i ^ 1) + 1) * chunk)
        out_t[:, :, b] = (hold[:, :, a] + in_y[0, :, :, a].astype(F32)).astype(BF16)
    across = links.to(links.across, out_t, in_t)
    between(1)
    core[3].arrive()
    hold[...] = p_ref[0, :, 0, 0].astype(F32) + core_in[3].astype(F32)
    near[1].arrive()
    hold[...] += in_y[1].astype(F32)
    between(2)
    across.arrive()
    hold[...] += in_t[...].astype(F32)
    for copy in (*core, *near, across):
        copy.sent()


def loop(count, step):
    def one(i, carry):
        step(i)
        return carry

    lax.fori_loop(0, count, one, 0)


def rows_of(ref, i):
    value = ref[i // 2, i % 2]
    return value.reshape(-1, value.shape[-1])


def away_rows(a_cols, b_ref, away_ref):
    depth, tile = away_ref.shape[0], 512

    def step(i):
        product = tn(a_cols(pl.multiple_of(depth + i * tile, tile), tile), b_ref[...])
        away_ref[pl.ds(pl.multiple_of(i * tile, tile), tile), :] = product.astype(BF16)

    loop(depth // tile, step)


def keep_rows(a_cols, b_ref, fold_ref, own_ref, send_ref):
    f = own_ref.shape[0]
    own_ref[...] = tn(a_cols(0, f), b_ref[...]) + fold_ref[:f, :].astype(F32)

    def step(i):
        at = pl.multiple_of(i * f, f)
        product = tn(a_cols(pl.multiple_of(at + f, f), f), b_ref[...])
        send_ref[pl.ds(at, f), :] = (product + fold_ref[pl.ds(pl.multiple_of(at + f, f), f), :].astype(F32)).astype(BF16)

    loop(3, step)


def middle_kernel(
    low_ref, cot_ref, gain_ref, attn_ref, wo_ref, c_ref, wd_ref, wg_ref, gate_ref, up_ref,
    middle_ref, dmid_ref, gain_grad_ref, dall_ref, mixed_ref, own_d_ref, got_d_ref, own_g_ref, send_g_ref, keep_u_ref, away_u_ref,
    attn, wo, p, core_in, out_y, in_y, out_t, in_t, hold, xm_s, xm, c, wd, wg, wu, dact, gate, act, dg, du,
    away_d, fold_d, away_g, fold_g, own_d, send_d, own_g, send_g, up_tile, send, recv, *, batch_mask, chunk,
):
    links = Links(send, recv, batch_mask)
    f, ff = own_d.shape[0], act.shape[1]
    to, load = links.to, links.load
    loads = [load(attn_ref, attn), load(wo_ref, wo)]
    links.greet()

    def rows(ref, q):
        return ref.at[pl.ds(q * f, f), :]

    down = [to(links.seq, rows(wd_ref, q), rows(wd, q + 4)) for q in (1, 3)]
    gate_z = [to(links.batch, links.half(gate_ref, 0), rows(wg, 1)), to(links.both, links.half(gate_ref, 1), rows(wg, 3))]
    gates = [to(links.seq, rows(wg_ref, 2), rows(wg, 6))]
    up_t = to(links.across, links.half(up_ref, 1), rows(wu, 2))
    ups = []
    for copy in loads:
        copy.arrive()
    down += [load(rows(wd_ref, q), rows(wd, q)) for q in (0, 1, 2, 3, 4, 6)]
    gates += [load(rows(wg_ref, q), rows(wg, q)) for q in (0, 2, 4)]
    c_load = load(c_ref, c)
    up_own = load(links.half(up_ref, 0), rows(wu, 0))
    bufs = (p, core_in, out_y, in_y, out_t, in_t, hold)

    def out_partial(k):
        for m in range(2):
            at = (k * 2 + m) * attn.shape[0] // 4
            p[k, m] = nt(attn[at : at + attn.shape[0] // 4], wo[...]).astype(BF16).reshape(p.shape[2:])

    def while_out(stage):
        if stage == 0:
            ups.append(to(links.seq, links.half(up_ref, 0), rows(wu, 4)))
        if stage == 1:
            up_t.arrive()
            ups.append(to(links.seq, rows(wu, 2), rows(wu, 6)))

    sum_in(links, bufs, chunk, out_partial, while_out)
    for m in range(2):
        middle = low_ref[m].astype(F32) + hold[m]
        middle_ref[m] = middle
        xm_s[m] = (middle * inverse_rms(middle) * gain_ref[...]).astype(BF16)

    up_z = []

    def while_xm(stage):
        if stage == 0:
            for copy in gate_z:
                copy.arrive()
            up_z.append(to(links.batch, links.half(up_ref, 0), rows(wu, 1)))
            gates.extend(to(links.seq, rows(wg, q), rows(wg, q + 4)) for q in (1, 3))
            for copy in (*down, c_load):
                copy.arrive()

            def step(i):
                at = pl.ds(pl.multiple_of(i * 512, 512), 512)
                dact[at, :] = nn(c[at, :], wd[...])

            loop(c.shape[0] // 512, step)
        if stage == 2:
            up_z[0].arrive()
            up_z.append(to(links.both, links.half(up_ref, 1), rows(wu, 3)))
            ups.append(to(links.seq, rows(wu, 1), rows(wu, 5)))

    spread_in(links, xm_s, xm, chunk, while_xm)
    for copy in gates:
        copy.arrive()

    def gate_step(i):
        at = pl.ds(pl.multiple_of(i * 256, 256), 256)
        gate[at, :] = nn(rows_of(xm, i), wg[...])

    loop(4, gate_step)
    up_z[1].arrive()
    ups.append(to(links.seq, rows(wu, 3), rows(wu, 7)))
    up_own.arrive()
    for copy in ups:
        copy.arrive()

    def up_step(i):
        base = pl.multiple_of(i * 256, 256)
        up_tile[...] = nn(rows_of(xm, i), wu[...])

        def part(j):
            at, here = pl.ds(pl.multiple_of(base + j * 32, 32), 32), pl.ds(pl.multiple_of(j * 32, 32), 32)
            g, u, d = gate[at, :], up_tile[here, :], dact[at, :]
            sig = 1.0 / (1.0 + jnp.exp(-g))
            silu = g * sig
            act[at, :] = (silu * u).astype(BF16)
            dg[at, :] = (d * u * sig * (1.0 + g * (1.0 - sig))).astype(BF16)
            du[at, :] = (d * silu).astype(BF16)

        loop(8, part)

    loop(4, up_step)

    def c_cols(at, n):
        return c[:, pl.ds(at, n)]

    def xm_cols(at, n):
        return xm[:, :, :, :, :, pl.ds(at, n)].reshape(-1, n)

    away_rows(c_cols, act, away_d)
    fold = to(links.seq, away_d, fold_d)

    def back_partial(k):
        def step(m):
            at = pl.ds(pl.multiple_of((k * 2 + m) * 256, 256), 256)
            value = nt(dg[at, :], wg[...]) + nt(du[at, :], wu[...])
            p[k, m] = value.astype(BF16).reshape(p.shape[2:])

        loop(2, step)

    later = []

    def while_back(stage):
        if stage == 0:
            away_rows(xm_cols, dg, away_g)
            later.append(to(links.seq, away_g, fold_g))
        if stage == 1:
            def step(i):
                at = pl.ds(pl.multiple_of(i * 512, 512), 512)
                dact[at, :] = tn(xm_cols(pl.multiple_of(i * 512, 512), 512), du[...])

            loop(2, step)
            later.append(load(dact, keep_u_ref))

    sum_in(links, bufs, chunk, back_partial, while_back)
    for m in range(2):
        middle = middle_ref[m]
        grad = cot_ref[m].astype(F32) + norm_grad(hold[m], middle, gain_ref[...], gain_grad_ref, m)
        dmid_ref[m] = grad
        xm_s[m] = grad.astype(BF16)

    settles = []

    def while_mid(stage):
        if stage == 0:
            fold.arrive()
            fold.sent()
            keep_rows(c_cols, act, fold_d, own_d, send_d)
            for q, target in ((0, links.batch), (2, links.both), (1, links.across)):
                settles.append(to(target, rows(send_d, q), rows(got_d_ref, q)))
            settles.append(load(own_d, own_d_ref))
            away_rows(xm_cols, du, away_d)
            settles.append(load(away_d, away_u_ref))
        if stage == 1:

            def step(i):
                at = pl.ds(pl.multiple_of(i * 256, 256), 256)
                p[i // 2, i % 2] = nt(act[at, :], wd[...]).astype(BF16).reshape(p.shape[2:])

            loop(4, step)
            settles.append(load(p, mixed_ref))

    spread_in(links, xm_s, dall_ref, chunk, while_mid, in_vmem=False)
    later[0].arrive()
    keep_rows(xm_cols, dg, fold_g, own_g, send_g)
    load(own_g, own_g_ref)
    load(send_g, send_g_ref)
    links.finish()


def middle_call(batch_mask, low, cot, gain, attn, w_out, cot_all, w_down, w_gate, gate_weight, up_weight, collective_id):
    _, rows, width = low.shape
    tokens, columns = attn.shape
    ff = w_down.shape[1]
    f = w_down.shape[0] // 8
    share, full = (2, rows, width), (2, 2, 2, 2, rows, width)
    vmem, hbm = pl.BlockSpec(memory_space=pltpu.VMEM), pl.BlockSpec(memory_space=pltpu.HBM)
    like = jax.ShapeDtypeStruct
    return pl.pallas_call(
        functools.partial(middle_kernel, batch_mask=batch_mask, chunk=2 * width // 8),
        in_specs=[vmem] * 3 + [hbm] * 7,
        out_specs=[vmem] * 3 + [hbm] * 8,
        out_shape=[
            like(share, F32),
            like(share, F32),
            like((1, width), F32),
            like(full, BF16),
            like(full, BF16),
            like((f, ff), F32),
            like((3 * f, ff), BF16),
            like((f, ff), F32),
            like((3 * f, ff), BF16),
            like((4 * f, ff), F32),
            like((4 * f, ff), BF16),
        ],
        scratch_shapes=[
            pltpu.VMEM((tokens, columns), BF16),
            pltpu.VMEM((width, columns), BF16),
            pltpu.VMEM(full, BF16),
            pltpu.VMEM((4, *share), BF16),
            pltpu.VMEM((2, *share), BF16),
            pltpu.VMEM((2, *share), BF16),
            pltpu.VMEM(share, BF16),
            pltpu.VMEM(share, BF16),
            pltpu.VMEM(share, F32),
            pltpu.VMEM(share, BF16),
            pltpu.VMEM(full, BF16),
            pltpu.VMEM((tokens, width), BF16),
            *[pltpu.VMEM((width, ff), BF16)] * 3,
            *[pltpu.VMEM((tokens, ff), F32)] * 2,
            *[pltpu.VMEM((tokens, ff), BF16)] * 3,
            *[pltpu.VMEM((4 * f, ff), BF16)] * 4,
            pltpu.VMEM((f, ff), F32),
            pltpu.VMEM((3 * f, ff), BF16),
            pltpu.VMEM((f, ff), F32),
            pltpu.VMEM((3 * f, ff), BF16),
            pltpu.VMEM((256, ff), F32),
            pltpu.SemaphoreType.DMA((96,)),
            pltpu.SemaphoreType.DMA((96,)),
        ],
        compiler_params=pltpu.CompilerParams(
            collective_id=collective_id, has_side_effects=True, vmem_limit_bytes=60 * MIB
        ),
        cost_estimate=TINY_COST,
    )(low, cot, gain, attn, w_out, cot_all, w_down, w_gate, gate_weight, up_weight)


def block_of(n, batch_mask):
    blk = lax.axis_index("blk")
    return blk ^ ((n // 2) * batch_mask) ^ ((n % 2) << TENSOR_BIT)


def key_tokens(block, half):
    head = lax.axis_index("head")
    index = lax.broadcasted_iota(jnp.int32, (2 * half, 1), 0)
    return token_offset(head, index, half // 2) + block * (2 * half)


def query_tokens(block, half, lanes):
    head = lax.axis_index("head")
    index = lax.broadcasted_iota(jnp.int32, (1, lanes), 1) % (2 * half)
    return token_offset(head, index, half // 2) + block * (2 * half)


def head_rows(ref, i, heads, width):
    both = [ref[c, i] for c in range(2)]
    return jnp.concatenate([b[:, h * width : (h + 1) * width] for h in range(heads) for b in both], axis=0)


def attention_back(q, do, k, v, start, ot, l, dq, dk, dv, kt, acc, batch_mask, scaling):
    parts, _, blocks, half, width = k.shape
    heads = q.shape[-1] // width
    lanes = heads * 2 * half
    dk[...] = jnp.zeros_like(dk)
    dv[...] = jnp.zeros_like(dv)

    def turn(kb):
        kt[kb] = key_rows(k, kb // blocks, kb % blocks).T

    loop(parts * blocks, turn)

    def per_query(i):
        q_rows, do_rows = head_rows(q, i, heads, width), head_rows(do, i, heads, width)
        delta = jnp.sum(do_rows.astype(F32).T * ot[i], axis=0, keepdims=True)
        inverse, first = 1.0 / l[i], start[i]
        acc[...] = jnp.zeros_like(acc)
        q_block = block_of(i, batch_mask)

        def per_key(kb):
            part, block = kb // blocks, kb % blocks
            k_block = block_of(block, batch_mask) ^ (part << SEQ_BIT)

            def add(diagonal):
                tokens = key_tokens(k_block, half)
                allowed = tokens >= first
                if diagonal:
                    allowed = allowed & (tokens <= query_tokens(q_block, half, lanes))
                score = nt(key_rows(k, part, block), q_rows) * (scaling * LOG2E)
                prob = jnp.where(allowed, jnp.exp2(score), 0.0) * inverse
                d_prob = nt(key_rows(v, part, block), do_rows)
                d_score = (prob * (d_prob - delta)).astype(BF16)
                d_v, d_k = nn(prob.astype(BF16), do_rows), nn(d_score, q_rows) * scaling
                for c in range(2):
                    dv[part, c, block] += d_v[c * half : (c + 1) * half]
                    dk[part, c, block] += d_k[c * half : (c + 1) * half]
                acc[...] += nn(kt[kb], d_score)

            @pl.when(k_block < q_block)
            def _():
                add(False)

            @pl.when(k_block == q_block)
            def _():
                add(True)

        loop(parts * blocks, per_key)
        rows = acc[...].T * scaling
        for h in range(heads):
            for c in range(2):
                at = (h * 2 + c) * half
                dq[c, i, :, h * width : (h + 1) * width] = rows[at : at + half]

    loop(blocks, per_query)


def last_kernel(
    low_ref, middle_ref, dmid_ref, gain_ref, gain_m_grad_ref, gain_q_ref, gain_k_ref, start_ref, l_ref,
    dall_ref, wo_ref, attn_ref, q_ref, k_ref, v_ref, ot_ref, raw_ref, cos_ref, sin_ref, wa_ref, xa_ref, mixed_ref,
    send_g_ref, keep_u_ref, away_u_ref,
    mixed_own_ref, mixed_got_ref, input_own_ref, input_got_ref, sums_ref,
    got_g_ref, own_u_ref, got_u_ref, own_a_ref, got_a_ref, own_o_ref, got_o_ref,
    dall, wo, attn, q, do, k, v, ot, raw, cos, sin, wa, xa, dq, dk, dv, kt, acc, kv_out, kv_in, d_qkv,
    p, core_in, out_y, in_y, out_t, in_t, hold, m_near, m_core_in, m_out_y, m_in_y, m_out_t, m_in_t,
    swap_m, swap_i, keep_u, fold_u, own_u, send_u, away_o, fold_o, own_o, send_o, away_a, fold_a, own_a, send_a,
    gains_qk, gain_a_grad, ring_out, ring_in, send, recv, *, batch_mask, bit_order, scaling, chunk,
):
    links = Links(send, recv, batch_mask)
    to, load = links.to, links.load
    f = own_u.shape[0]
    heads = q.shape[-1] // k.shape[-1]
    width = k.shape[-1]

    def rows(ref, i):
        return ref.at[pl.ds(i * f, f), :]

    first = [load(dall_ref, dall), load(wo_ref, wo), load(attn_ref, attn)]
    second = [load(a, b) for a, b in ((q_ref, q), (k_ref, k), (v_ref, v), (ot_ref, ot))]
    third = [load(a, b) for a, b in ((raw_ref, raw), (cos_ref, cos), (sin_ref, sin), (wa_ref, wa), (xa_ref, xa))]
    mixed_near, keep_load = load(mixed_ref.at[0], m_near.at[0]), load(keep_u_ref, keep_u)
    links.greet()

    def settle(src, dst):
        for i, target in ((0, links.batch), (2, links.both), (1, links.across)):
            to(target, rows(src, i), rows(dst, i))

    settle(send_g_ref, got_g_ref)
    up_fold = to(links.seq, away_u_ref, fold_u)
    for copy in (*first, *second):
        copy.arrive()

    def d_attn(i):
        at = pl.ds(pl.multiple_of(i * 256, 256), 256)
        value = nn(dall[at, :], wo[...]).astype(BF16)
        do[i // 2, pl.ds((i % 2) * 2, 2)] = value.reshape(2, 128, value.shape[1])

    loop(4, d_attn)
    attention_back(q, do, k, v, start_ref, ot, l_ref, dq, dk, dv, kt, acc, batch_mask, scaling)
    kv_out[:, :width] = dk[1].reshape(-1, width).astype(BF16)
    kv_out[:, width:] = dv[1].reshape(-1, width).astype(BF16)
    kv = to(links.seq, kv_out, kv_in)

    def dall_cols(at, n):
        return dall[:, pl.ds(at, n)]

    def xa_cols(at, n):
        return xa[:, pl.ds(at, n)]

    folds = []

    def while_mixed(stage):
        if stage == 0:
            away_rows(dall_cols, attn, away_o)
        if stage == 1:
            kv.arrive()
            folds.append(to(links.seq, away_o, fold_o))
        if stage == 2:
            up_fold.arrive()
            keep_load.arrive()
            own_u[...] = keep_u[:f, :] + fold_u[:f, :].astype(F32)

            def step(i):
                at = pl.ds(pl.multiple_of(i * f, f), f)
                here = pl.ds(pl.multiple_of(i * f + f, f), f)
                send_u[at, :] = (keep_u[here, :] + fold_u[here, :].astype(F32)).astype(BF16)

            loop(3, step)
            settle(send_u, got_u_ref)
            load(own_u, own_u_ref)

    mixed_near.arrive()
    sum_in(links, (m_near, m_core_in, m_out_y, m_in_y, m_out_t, m_in_t, hold), chunk, None, while_mixed, mixed_ref.at[1])
    blk = lax.axis_index("blk")
    store_ungrouped(middle_ref[0] + hold[0], mixed_own_ref, blk, bit_order)
    store_ungrouped(middle_ref[1] + hold[1], swap_m, blk, bit_order)
    to(links.batch, swap_m, mixed_got_ref)

    for copy in third:
        copy.arrive()
    gains_qk[...] = jnp.zeros_like(gains_qk)

    def input_partial(c):
        def step(m):
            at = pl.ds(pl.multiple_of((c * 2 + m) * 256, 256), 256)
            pair = pl.ds(m * 2, 2)
            got = kv_in[at, :].astype(F32)
            for h in range(heads + 1):
                cut = slice(h * width, (h + 1) * width)
                if h < heads:
                    grad = dq[c, pair, :, cut].reshape(256, width)
                else:
                    grad = dk[0, c, pair].reshape(256, width) + got[:, :width]
                gain = (gain_q_ref if h < heads else gain_k_ref)[...]
                values = raw[at, cut]
                inverse = inverse_rms(values)
                normed = values * inverse
                turned = grad * cos[at, :] - pltpu.roll(grad, width // 2, 1) * sin[at, :]
                row = 0 if h < heads else 1
                gains_qk[row : row + 1, :] += jnp.sum(turned * normed, axis=0, keepdims=True)
                scaled = turned * gain
                mean = jnp.mean(scaled * normed, axis=-1, keepdims=True)
                d_qkv[at, cut] = (inverse * (scaled - normed * mean)).astype(BF16)
            d_qkv[at, (heads + 1) * width :] = (dv[0, c, pair].reshape(256, width) + got[:, width:]).astype(BF16)
            p[c, m] = nt(d_qkv[at, :], wa[...]).astype(BF16).reshape(p.shape[2:])

        loop(2, step)

    def while_input(stage):
        if stage == 0:
            away_rows(xa_cols, d_qkv, away_a)
            folds.append(to(links.seq, away_a, fold_a))
            folds[0].arrive()
            keep_rows(dall_cols, attn, fold_o, own_o, send_o)
            settle(send_o, got_o_ref)
            load(own_o, own_o_ref)
        if stage == 2:
            folds[1].arrive()
            keep_rows(xa_cols, d_qkv, fold_a, own_a, send_a)
            settle(send_a, got_a_ref)
            load(own_a, own_a_ref)

    sum_in(links, (p, core_in, out_y, in_y, out_t, in_t, hold), chunk, input_partial, while_input)
    for m in range(2):
        grad = dmid_ref[m] + norm_grad(hold[m], low_ref[m].astype(F32), gain_ref[...], gain_a_grad, m)
        store_ungrouped(grad, input_own_ref if m == 0 else swap_i, blk, bit_order)
    to(links.batch, swap_i, input_got_ref)
    n = gain_a_grad.shape[1]
    store_ungrouped(gain_a_grad[...], sums_ref.at[:, pl.ds(0, n)], blk, bit_order)
    sums_ref[:, n : n + width] = gains_qk[0:1, :]
    sums_ref[:, n + width : n + 2 * width] = gains_qk[1:2, :]
    store_ungrouped(gain_m_grad_ref[...], sums_ref.at[:, pl.ds(n + 2 * width, n)], blk, bit_order)
    for i, target in enumerate((links.core, links.near, links.seq, links.across, links.batch)):
        ring_out[i] = sums_ref[...]
        to(target, ring_out.at[i], ring_in.at[i]).arrive()
        sums_ref[...] += ring_in[i]
    links.finish()


def last_call(batch_mask, bit_order, scaling, arrays, collective_id):
    low, dall, attn, q, k, raw, wa, away_u = (arrays[n] for n in ("low", "dall", "attn", "q", "k", "raw", "wa", "away_u"))
    _, rows, width = low.shape
    tokens, columns = attn.shape
    head_size = k.shape[-1]
    ff, f = away_u.shape[1], away_u.shape[0] // 4
    n_a = wa.shape[1]
    share, full, half_full = (2, rows, width), (2, 2, 2, 2, rows, width), (1, 2, 2, 2, rows, width)
    vmem, hbm = pl.BlockSpec(memory_space=pltpu.VMEM), pl.BlockSpec(memory_space=pltpu.HBM)
    like, held = jax.ShapeDtypeStruct, pltpu.VMEM
    in_vmem = ("low", "middle", "d_middle", "gain", "gain_m_grad", "gain_q", "gain_k", "start", "l")
    in_hbm = (
        "dall", "w_out", "attn", "q", "k", "v", "ot", "raw", "cos", "sin", "wa", "xa", "mixed", "send_g", "keep_u", "away_u",
    )
    total = 2 * width + 2 * head_size
    lanes = 2 * 2 * 128
    sums = (1, total)
    own_and_send = lambda n: [held((f, n), F32), held((3 * f, n), BF16)]
    sum_bufs = [
        held((4, *share), BF16), held((2, *share), BF16), held((2, *share), BF16), held(share, BF16), held(share, BF16),
    ]
    return pl.pallas_call(
        functools.partial(last_kernel, batch_mask=batch_mask, bit_order=bit_order, scaling=scaling, chunk=2 * width // 8),
        in_specs=[vmem] * len(in_vmem) + [hbm] * len(in_hbm),
        out_specs=[vmem, hbm, vmem, hbm, vmem] + [hbm] * 7,
        out_shape=[
            like((rows, width), BF16),
            like((rows, width), BF16),
            like((rows, width), F32),
            like((rows, width), BF16),
            like(sums, F32),
            like((3 * f, ff), BF16),
            like((f, ff), F32),
            like((3 * f, ff), BF16),
            like((f, n_a), F32),
            like((3 * f, n_a), BF16),
            like((f, columns), F32),
            like((3 * f, columns), BF16),
        ],
        scratch_shapes=[
            held((tokens, width), BF16),
            held((width, columns), BF16),
            held((tokens, columns), BF16),
            held(q.shape, BF16),
            held(q.shape, BF16),
            held(k.shape, BF16),
            held(k.shape, BF16),
            held((4, head_size, lanes), F32),
            held(raw.shape, F32),
            held((tokens, head_size), F32),
            held((tokens, head_size), F32),
            held(wa.shape, BF16),
            held((tokens, width), BF16),
            held(q.shape, F32),
            held(k.shape, F32),
            held(k.shape, F32),
            held((8, head_size, 256), BF16),
            held((head_size, lanes), F32),
            held((tokens, 2 * head_size), BF16),
            held((tokens, 2 * head_size), BF16),
            held((tokens, n_a), BF16),
            held(full, BF16),
            *sum_bufs,
            held(share, F32),
            held(half_full, BF16),
            *sum_bufs,
            held((rows, width), BF16),
            held((rows, width), BF16),
            held((4 * f, ff), F32),
            held((4 * f, ff), BF16),
            *own_and_send(ff),
            held((4 * f, columns), BF16),
            held((4 * f, columns), BF16),
            *own_and_send(columns),
            held((4 * f, n_a), BF16),
            held((4 * f, n_a), BF16),
            *own_and_send(n_a),
            held((8, head_size), F32),
            held((1, width), F32),
            held((5, *sums), F32),
            held((5, *sums), F32),
            pltpu.SemaphoreType.DMA((96,)),
            pltpu.SemaphoreType.DMA((96,)),
        ],
        compiler_params=pltpu.CompilerParams(
            collective_id=collective_id, has_side_effects=True, vmem_limit_bytes=60 * MIB
        ),
        cost_estimate=TINY_COST,
    )(*[arrays[n] for n in (*in_vmem, *in_hbm)])


def local(
    hidden_in,
    lengths,
    query_weight,
    key_matrix,
    value_matrix,
    out_weight,
    gate_weight,
    up_weight,
    down_weight,
    attn_gain,
    query_gain,
    key_gain,
    mlp_gain,
    cotangent,
):
    ring = lax.axis_size("blk")
    bits = ring.bit_length() - 1
    batch_bit = bits - 1
    extra_bits = [i for i in range(bits) if i not in (TENSOR_BIT, SEQ_BIT, batch_bit)]
    seq_bits = [SEQ_BIT, *extra_bits]
    parts = 1 << len(seq_bits)
    bit_order = [batch_bit, TENSOR_BIT, SEQ_BIT, *extra_bits]
    b_mask, t_mask, x_mask = 1 << batch_bit, 1 << TENSOR_BIT, 1 << SEQ_BIT
    blk, head = lax.axis_index("blk"), lax.axis_index("head")
    batch, tensor = bit_of(blk, batch_bit), bit_of(blk, TENSOR_BIT)

    local_rows, width = hidden_in.shape[1:]
    block_rows = local_rows * lax.axis_size("head")
    half = block_rows // 2
    row_features = width // ring
    head_size = query_gain.shape[0]
    scaling = head_size ** (-0.5)
    tokens = 16 * local_rows
    heads = query_weight.shape[1] // (2 * head_size)
    ff = gate_weight.shape[1] // 2

    def moved(values, place_of):
        axis = values.ndim - 1
        return jnp.concatenate(
            [
                lax.dynamic_slice_in_dim(values, place_of(i) * row_features, row_features, axis)
                for i in range(ring)
            ],
            axis=axis,
        )

    def regroup(values):
        return moved(values, lambda p: blk ^ sum(((p >> i) & 1) << b for i, b in enumerate(bit_order)))

    def ungroup(values):
        return moved(values, lambda n: sum(bit_of(blk ^ n, b) << i for i, b in enumerate(bit_order)))

    def everything(ref):
        return ref

    def mask_of(p):
        return sum(((p >> i) & 1) << b for i, b in enumerate(bit_order))

    def rows_at(p):
        return lambda ref: ref.at[pl.ds(p * row_features, row_features), :]

    def half_cut(n, other):
        def cut(ref):
            place = bit_of(lax.axis_index("blk"), TENSOR_BIT)
            place = 1 - place if other else place
            return ref.at[:, pl.ds(pl.multiple_of(place * n, n), n)]

        return cut

    def send_over(plan, weight, buffer, p, point):
        mask, n = mask_of(p), weight.shape[1] // 2
        plan.copy((plan.read(weight), half_cut(n, mask & t_mask)), (buffer, rows_at(p)), mask, point=point)

    def keep_own(plan, weight, buffer, point, onward=True):
        here, n = plan.read(weight), weight.shape[1] // 2
        if onward:
            plan.copy((here, half_cut(n, 0)), (buffer, rows_at(4)), x_mask, point=point)
        plan.local((here, half_cut(n, 0)), (buffer, rows_at(0)), (row_features, n), point=point)

    def send_on(plan, buffer, places, point, after=None):
        for p in places:
            plan.copy((buffer, rows_at(p)), (buffer, rows_at(p + 4)), x_mask, after=after, point=point)

    def lay(plan, array, buffer, p, point=0, columns=None, onward=False):
        here = plan.read(array)
        cut = (lambda ref: ref.at[:, pl.ds(*columns)]) if columns else everything
        if onward:
            plan.copy((here, cut), (buffer, rows_at(p + 4)), x_mask, point=point)
        plan.local((here, cut), (buffer, rows_at(p)), (row_features, columns[1] if columns else array.shape[1]), point)

    def fresh_for(plan, weights):
        return plan.fresh(buffer_shape(weights), BF16)

    def buffer_shape(weights):
        return (8 * row_features, sum(w.shape[1] for w in weights) // 2)

    def whole_weight(buffer):
        pieces = [buffer]
        for b in extra_bits:
            pieces = pieces + [over_blk(c, 1 << b) for c in pieces]
        return jnp.concatenate(pieces, axis=0) if extra_bits else buffer

    def split_grad(grad):
        for b in reversed(extra_bits):
            n = grad.shape[0] // 2
            grad = grad[:n] + over_blk(grad[n:].astype(BF16), 1 << b).astype(F32)
        n = grad.shape[0] // 2
        return grad[:n], grad[n:].astype(BF16)

    def weight_sum(a, b):
        return split_grad(tn(a, b)) if extra_bits else weight_grad(a, b)

    def fold(plan, source, shape, point=0):
        plan.copy((source, everything), (plan.fresh(shape, BF16), everything), x_mask, point=point)

    def fold_part(plan, source, buffer, start, n, point=0):
        def part(ref):
            return ref.at[:, pl.ds(start, n)]

        plan.copy((source, part), (buffer, part), x_mask, point=point)

    def to_settle(keep, got):
        total = keep + got.astype(F32)
        return total[:row_features], total[row_features:].astype(BF16)

    def settle(plan, away, t_point=0):
        out, here = plan.fresh(away.shape, away.dtype), plan.read(away)
        for i, mask in ((0, b_mask), (2, b_mask | t_mask), (1, t_mask)):
            plan.copy((here, rows_at(i)), (out, rows_at(i)), mask, point=t_point if mask == t_mask else 0)

    def settled(sources, column_widths):
        if all(w % 128 == 0 for w in column_widths):
            return assemble(tensor, sources, column_widths)
        f, results = row_features, []
        widths = iter(column_widths)
        for own, got in sources:
            own = own + got[:f].astype(F32)
            other = got[f : 2 * f].astype(F32) + got[2 * f :].astype(F32)
            at = 0
            while at < own.shape[1]:
                w = next(widths)
                results.append(in_order(tensor, own[:, at : at + w], other[:, at : at + w], 1))
                at += w
        return results

    chunk = 2 * row_features
    ids = iter(range(100))

    def spread(flat, plan, fills=(), limit=None):
        (out,), rest = run(plan, spread_main(flat, chunk), next(ids), fills=fills, limit=limit)
        return out.reshape(tokens, width), rest

    share = (2, local_rows, width)

    def gather_sum(partial, plan, extra, outs_like, finish, fills=()):
        return run(plan, gather_main(partial, chunk, extra, outs_like, finish), next(ids), fills=fills)

    def like(shape, dtype):
        return jax.ShapeDtypeStruct(shape, dtype)

    aligned = row_features % 128 == 0
    local_order = bit_order if aligned else []

    def split_batch(rows):
        mine = lax.dynamic_index_in_dim(rows, batch, 0, keepdims=False)
        theirs = lax.dynamic_index_in_dim(rows, 1 - batch, 0, keepdims=False)
        return mine, theirs

    def natural(rows):
        return rows if aligned else ungroup(rows)

    length_row = lax.dynamic_index_in_dim(lengths, batch, 0, keepdims=False)
    doc_ends = jnp.cumsum(length_row)
    batch_flip = jnp.arange(2, dtype=jnp.int32)[:, None] << batch_bit
    tensor_flip = jnp.arange(2, dtype=jnp.int32)[None, :] << TENSOR_BIT
    q_blocks = (blk ^ batch_flip ^ tensor_flip).reshape(4)
    index = jnp.arange(2 * half, dtype=jnp.int32)
    in_block = token_offset(head, index, local_rows).reshape(2, 1, half)
    token_index = q_blocks[None, :, None] * block_rows + in_block
    passed = doc_ends <= token_index[..., None]
    doc_start = jnp.max(jnp.where(passed, doc_ends, 0), axis=-1).astype(jnp.int32)
    position = (token_index - doc_start).reshape(tokens)
    start_lanes = jnp.tile(jnp.transpose(doc_start, (1, 0, 2)).reshape(4, 1, 2 * half), (1, 1, heads))
    k_blocks = q_blocks
    for b in seq_bits:
        k_blocks = jnp.concatenate([k_blocks, k_blocks ^ (1 << b)])
    least_start = jnp.min(doc_start, axis=(0, 2))[:, None]
    last_start = jnp.max(doc_start, axis=(0, 2))[:, None]
    k_first = (k_blocks * block_rows)[None, :]
    none = (k_blocks[None, :] > q_blocks[:, None]) | (k_first + block_rows <= least_start)
    whole = (k_blocks[None, :] < q_blocks[:, None]) & (k_first >= last_start)
    flags = jnp.where(none, 0, jnp.where(whole, 1, 2))
    meta = jnp.concatenate([head[None], q_blocks, k_blocks, flags.reshape(-1)]).astype(jnp.int32)

    inverse_freq = THETA ** (-jnp.arange(head_size // 2, dtype=F32) / (head_size // 2))
    angles = position.astype(F32)[:, None] * inverse_freq[None, :]
    cosine, sine = jnp.cos(angles), jnp.sin(angles)
    cosine = jnp.concatenate([cosine, cosine], axis=1)
    sine = jnp.concatenate([-sine, sine], axis=1)

    def rms(values):
        return lax.rsqrt(jnp.mean(values * values, axis=-1, keepdims=True) + EPS)

    def norm_back(grad, normed, inverse, gain):
        scaled = grad * gain
        return inverse * (scaled - normed * jnp.mean(scaled * normed, axis=-1, keepdims=True))

    gains_in = jnp.stack([attn_gain, mlp_gain]).astype(F32)
    gain_q = query_gain.astype(F32)[None]
    gain_k = key_gain.astype(F32)[None]

    q_columns, k_columns = heads * head_size, head_size
    a_weights = (query_weight, key_matrix, value_matrix)

    def halves(weights, which):
        return jnp.concatenate(
            [lax.dynamic_slice_in_dim(w, which * (w.shape[1] // 2), w.shape[1] // 2, 1) for w in weights], axis=1
        )

    mine, theirs = split_batch(hidden_in)
    other = over_blk(theirs, b_mask)
    a_own, a_other = halves(a_weights, tensor), halves(a_weights, 1 - tensor)
    a_by_t = over_blk(a_other, t_mask)
    a_by_b = over_blk(a_own, b_mask)
    early = over_blk(jnp.concatenate([a_own, halves((down_weight,), tensor)], axis=1), x_mask)
    (mine, other, cosine, sine, start_lanes, meta) = pin((mine, other, cosine, sine, start_lanes, meta))
    if aligned:
        x_low, xa, gains_in = enter(blk, bit_order, mine, other, gains_in)
        gain_a, gain_m = gains_in[0], gains_in[1]
    else:
        gains_in = regroup(gains_in)
        gain_a, gain_m = gains_in[0], gains_in[1]
        x_low = regroup(jnp.concatenate([mine, other], axis=0))
        x_wide = x_low.astype(F32)
        xa = (x_wide * rms(x_wide) * gain_a).astype(BF16)

    plan = Plan()
    a_columns = a_own.shape[1]
    w_a = fresh_for(plan, a_weights)
    by_tb = plan.copy((plan.read(a_other), everything), (w_a, rows_at(3)), b_mask | t_mask)
    lay(plan, a_by_t, w_a, 2, onward=True)
    lay(plan, a_by_b, w_a, 1, onward=True)
    lay(plan, a_own, w_a, 0)
    lay(plan, early, w_a, 4, columns=(0, a_columns))
    here, cot_out = plan.read(cotangent), plan.fresh((2, local_rows, width), BF16)
    plan.copy(
        (here, lambda ref: ref.at[1 - bit_of(lax.axis_index("blk"), batch_bit)]),
        (cot_out, lambda ref: ref.at[1]),
        b_mask,
        point=1,
    )
    plan.local(
        (here, lambda ref: ref.at[bit_of(lax.axis_index("blk"), batch_bit)]),
        (cot_out, lambda ref: ref.at[0]),
        (local_rows, width),
    )
    w_out = fresh_for(plan, (out_weight,))
    send_over(plan, out_weight, w_out, 1, 1)
    send_over(plan, out_weight, w_out, 3, 1)
    send_over(plan, out_weight, w_out, 2, 1)
    keep_own(plan, out_weight, w_out, 0)
    w_down = fresh_for(plan, (down_weight,))
    send_over(plan, down_weight, w_down, 2, 1)
    keep_own(plan, down_weight, w_down, 0, onward=False)
    lay(plan, early, w_down, 4, columns=(a_columns, ff))
    w_gate = fresh_for(plan, (gate_weight,))
    keep_own(plan, gate_weight, w_gate, 1)
    send_on(plan, w_a, (3,), 2, after=by_tb)
    xa, (w_qkv, cot, w_out, w_down, w_gate) = spread(xa, plan, limit=56 * MIB)
    w_qkv = whole_weight(w_qkv)
    cot = cot.reshape(2 * local_rows, width)
    cot = enter(blk, bit_order, cot)[0] if aligned else regroup(cot)
    query, key_value, raw = prepare(xa, w_qkv, cosine, sine, gain_q, gain_k, heads)

    plan = Plan()
    kv_out = plan.fresh(key_value.shape, BF16)
    plan.copy((plan.read(key_value), everything), (kv_out, everything), x_mask)
    w_out = plan.through(w_out)
    send_on(plan, w_out, (1, 2, 3), 0)
    w_down = plan.through(w_down)
    send_over(plan, down_weight, w_down, 1, 0)
    send_over(plan, down_weight, w_down, 3, 0)
    send_on(plan, w_down, (2,), 1)
    w_gate = plan.through(w_gate)
    send_over(plan, gate_weight, w_gate, 2, 1)
    cot_all, (kv_x, w_out, w_down, w_gate) = spread(cot, plan)
    w_out = whole_weight(w_out)
    key_value = [key_value, kv_x]
    for b in extra_bits:
        key_value = key_value + [over_blk(c, 1 << b) for c in key_value]
    key_value = jnp.stack(key_value)
    keys = key_value[..., :head_size].reshape(parts, 2, 4, half, head_size)
    values = key_value[..., head_size:].reshape(parts, 2, 4, half, head_size)
    query = query.reshape(2, 4, half, q_columns)
    attn, attn_t, total_e = attend(meta, query, keys, values, start_lanes, scaling)
    attn = attn.reshape(tokens, q_columns)

    x_low = x_low.reshape(share)
    if extra_bits:
        plan = Plan()
        w_down = plan.through(w_down)
        send_on(plan, w_down, (1, 3), 0)
        w_gate = plan.through(w_gate)
        send_over(plan, gate_weight, w_gate, 1, 0)
        send_over(plan, gate_weight, w_gate, 3, 0)
        send_on(plan, w_gate, (2,), 0)
        w_up = fresh_for(plan, (up_weight,))
        send_over(plan, up_weight, w_up, 2, 0)
        keep_own(plan, up_weight, w_up, 1)
        (middle, xm), (w_down, w_gate, w_up) = gather_sum(
            nt(attn, w_out).astype(BF16),
            plan,
            [x_low, gain_m[None]],
            [like(share, F32), like(share, BF16)],
            finish_middle,
        )
        w_down = whole_weight(w_down)

        plan = Plan()
        w_gate = plan.through(w_gate)
        w_up = plan.through(w_up)
        by_b = len(plan.jobs)
        send_over(plan, up_weight, w_up, 1, 0)
        send_on(plan, w_gate, (1, 3), 0)
        send_on(plan, w_up, (2,), 1)
        by_tb = plan.copy(
            (plan.read(up_weight), half_cut(ff, True)), (w_up, rows_at(3)), b_mask | t_mask, after=by_b, point=2
        )
        send_on(plan, w_up, (1,), 2)
        send_on(plan, w_up, (3,), 3, after=by_tb)
        xm, (w_gate, w_up, d_active) = spread(
            xm.reshape(2 * local_rows, width), plan, [fill_product(cot_all, w_down, 0)]
        )
        w_gate, w_up = whole_weight(w_gate), whole_weight(w_up)
        gate = nn(xm, w_gate)
        up = nn(xm, w_up)
        sig = jax.nn.sigmoid(gate)
        silu = gate * sig
        active = (silu * up).astype(BF16)
        d_gate = (d_active * up * sig * (1.0 + gate * (1.0 - sig))).astype(BF16)
        d_up = (d_active * silu).astype(BF16)

        keep_down, away_down = weight_sum(cot_all, active)
        got_x = over_blk(away_down, x_mask)
        (d_gate, d_up, away_down) = pin((d_gate, d_up, away_down))
        ff_cut = ff // 2
        plan, fills = Plan(), []
        if extra_bits:
            keep_gate, away_gate = weight_sum(xm, d_gate)
            keep_up, away_up = weight_sum(xm, d_up)
            source, point = plan.read(away_gate), 0
        else:
            fills = [fill_weight_grad(xm, d_gate, 0), fill_weight_grad(xm, d_up, 1)]
            source, point = ("fill", (0, 1)), 1
        gate_x = plan.fresh((4 * row_features, ff), BF16)
        fold_part(plan, source, gate_x, 0, ff_cut, point)
        (d_middle, d_mid, gain_m_grad), (gate_x, *filled) = gather_sum(
            back_through((d_gate, d_up), (w_gate, w_up)),
            plan,
            [cot.reshape(share), middle, gain_m[None]],
            [like(share, F32), like(share, BF16), like((1, width), F32)],
            finish_mlp_norm,
            fills,
        )
        if filled:
            keep_gate, away_gate, keep_up, away_up = filled
        (d_mid, got_x) = pin((d_mid, got_x))
        own_down, away_down = to_settle(keep_down, got_x)

        plan = Plan()
        settle(plan, away_down, 1)
        gate_x = plan.through(gate_x)
        fold_part(plan, plan.read(away_gate), gate_x, ff_cut, ff - ff_cut)
        up_x = plan.fresh(away_up.shape, BF16)
        fold_part(plan, plan.read(away_up), up_x, 0, ff_cut)
        d_mid_all, (got_down, gate_x, up_x, mixed_partial) = spread(
            d_mid.reshape(2 * local_rows, width), plan, [fill_back(active, w_down, 0)]
        )
        (g_down,) = settled([(own_down, got_down)], (ff,))
        own_gate, away_gate = to_settle(keep_gate, gate_x)
    else:
        (
            middle, d_middle, gain_m_grad, d_mid_all, mixed_partial, own_down, got_down, own_gate, away_gate, keep_up, away_up,
        ) = middle_call(
            b_mask, x_low, cot.reshape(share), gain_m[None], attn, w_out, cot_all, w_down, w_gate, gate_weight, up_weight, next(ids)
        )
        d_mid_all = d_mid_all.reshape(tokens, width)
        mixed_partial = mixed_partial.reshape(tokens, width)
        (g_down,) = settled([(own_down, got_down)], (ff,))
        up_x = None
    if extra_bits:
        d_attn = nn(d_mid_all, w_out).astype(BF16).reshape(2, 4, half, q_columns)
        d_query, d_key, d_value = attend_back(
            meta, query, d_attn, keys, values, start_lanes, attn_t, total_e, scaling
        )
        d_key = d_key.reshape(parts, tokens, head_size)
        d_value = d_value.reshape(parts, tokens, head_size)
        for b in reversed(extra_bits):
            n = d_key.shape[0] // 2
            d_key = d_key[:n] + over_blk(d_key[n:].astype(BF16), 1 << b).astype(F32)
            d_value = d_value[:n] + over_blk(d_value[n:].astype(BF16), 1 << b).astype(F32)

        plan = Plan()
        away_kv = jnp.concatenate([d_key[1], d_value[1]], axis=1).astype(BF16)
        fold(plan, plan.read(away_kv), away_kv.shape)
        settle(plan, away_gate)
        if up_x is None:
            fold(plan, plan.read(away_up), away_up.shape)
        else:
            up_x = plan.through(up_x)
            fold_part(plan, plan.read(away_up), up_x, ff_cut, ff - ff_cut)
        (mixed,), (got_kv, got_gate, up_x, *filled) = gather_sum(
            mixed_partial,
            plan,
            [middle],
            [like(share, BF16)],
            functools.partial(finish_mixed, bit_order=local_order),
            [] if extra_bits else [fill_weight_grad(d_mid_all, attn, 0)],
        )
        keep_out, away_out = filled if filled else weight_sum(d_mid_all, attn)
        (g_gate,) = settled([(own_gate, got_gate)], (ff,))
        own_up, away_up = to_settle(keep_up, up_x)
        mixed = natural(mixed)
        mixed_got = over_blk(mixed[1], b_mask)
        d_qkv, d_xa_partial, gains_qk = prepare_back(
            d_query.reshape(tokens, q_columns), d_key, d_value, got_kv, raw, cosine, sine, gain_q, gain_k, w_qkv, heads
        )
        (d_xa_partial, mixed_got) = pin((d_xa_partial, mixed_got))

        plan, fills = Plan(), []
        settle(plan, away_up)
        fold(plan, plan.read(away_out), away_out.shape)
        if extra_bits:
            keep_qkv, away_qkv = weight_sum(xa, d_qkv)
            fold(plan, plan.read(away_qkv), away_qkv.shape)
        else:
            fills = [fill_weight_grad(xa, d_qkv, 0)]
            fold(plan, ("fill", (0, 1)), (4 * row_features, a_columns), 1)
        (input_own, input_away, gain_a_grad), (got_up, out_x, got, *filled) = gather_sum(
            d_xa_partial,
            plan,
            [x_low, d_middle, gain_a[None]],
            [like((local_rows, width), F32), like((local_rows, width), BF16), like((1, width), F32)],
            functools.partial(finish_input, bit_order=local_order),
            fills,
        )
        if filled:
            keep_qkv = filled[0]
        own_out, away_out = to_settle(keep_out, out_x)
        (g_up,) = settled([(own_up, got_up)], (ff,))
        own_qkv, away_qkv = to_settle(keep_qkv, got)

        plan = Plan()
        settle(plan, away_qkv)
        settle(plan, away_out)
        input_got = plan.fresh((local_rows, width), BF16)
        plan.copy((plan.read(natural(input_away)), everything), (input_got, everything), b_mask)
        sums = jnp.concatenate([ungroup(gain_a_grad[0]), gains_qk[0], gains_qk[1], ungroup(gain_m_grad[0])])
        (sums,), (got_a, got_o, input_got) = run(
            plan, total_main(sums.reshape(-1, 128)), next(ids), [1 << i for i in range(bits)]
        )
        g_query, g_key, g_value, g_out = settled(
            [(own_qkv, got_a), (own_out, got_o)], (q_columns, k_columns, k_columns, q_columns)
        )
        mixed = in_order(batch, mixed[:1], mixed_got[None], 0)
        input_grad = in_order(batch, natural(input_own)[None], input_got.astype(F32)[None], 0)
        gains = jnp.split(sums.reshape(-1), [width, width + head_size, width + 2 * head_size])
    else:
        (
            mixed_own, mixed_got, input_own, input_got, sums, got_gate, own_up, got_up, own_qkv, got_a, own_out, got_o,
        ) = last_call(
            b_mask,
            bit_order,
            scaling,
            dict(
                low=x_low,
                middle=middle,
                d_middle=d_middle,
                gain=gain_a[None],
                gain_m_grad=gain_m_grad,
                gain_q=gain_q,
                gain_k=gain_k,
                start=start_lanes,
                l=total_e,
                dall=d_mid_all,
                w_out=w_out,
                attn=attn,
                q=query,
                k=keys,
                v=values,
                ot=attn_t,
                raw=raw,
                cos=cosine,
                sin=sine,
                wa=w_qkv,
                xa=xa,
                mixed=mixed_partial.reshape(2, 2, 2, 2, local_rows, width),
                send_g=away_gate,
                keep_u=keep_up,
                away_u=away_up,
            ),
            next(ids),
        )
        g_gate, g_up, g_query, g_key, g_value, g_out = settled(
            [(own_gate, got_gate), (own_up, got_up), (own_qkv, got_a), (own_out, got_o)],
            (ff, ff, q_columns, k_columns, k_columns, q_columns),
        )
        mixed = in_order(batch, mixed_own[None], mixed_got[None], 0)
        input_grad = in_order(batch, input_own[None], input_got.astype(F32)[None], 0)
        gains = jnp.split(sums.reshape(-1), [width, width + head_size, width + 2 * head_size])
    return (
        mixed,
        input_grad,
        g_query,
        g_key,
        g_value,
        g_out,
        g_gate,
        g_up,
        g_down,
        *gains,
    )


def solution(mesh):
    rows = P(None, ("blk", "head"), None)
    weight = P("blk", "head")
    return jax.shard_map(
        local,
        mesh=mesh,
        in_specs=(rows, P(), *([weight] * 7), P(), P(), P(), P(), rows),
        out_specs=(rows, rows, *([weight] * 7), P(), P(), P(), P()),
        check_vma=False,
    )
```

```python
import functools
import math

import jax
import jax.numpy as jnp
from jax import lax
from jax.experimental import pallas as pl
from jax.experimental.pallas import tpu as pltpu
from jax.sharding import PartitionSpec as P

EPS = 1e-06
THETA = 1000000.0
LOG2E = 1.4426950408889634
F32 = jnp.float32
BF16 = jnp.bfloat16

MIB = 1024 * 1024
TINY_COST = pl.CostEstimate(flops=0, bytes_accessed=0, transcendentals=0)
VMEM_LIMIT = 32 * MIB
TENSOR_BIT = 1
SEQ_BIT = 0


def nt(a, b):
    return lax.dot_general(a, b, (((1,), (1,)), ((), ())), preferred_element_type=F32)


def tn(a, b):
    return lax.dot_general(a, b, (((0,), (0,)), ((), ())), preferred_element_type=F32)


def nn(a, b):
    return jnp.dot(a, b, preferred_element_type=F32)


def bit_of(value, bit):
    return (value >> bit) & 1


def over_blk(value, mask):
    count = lax.axis_size("blk")
    return lax.ppermute(value, "blk", [(i, i ^ mask) for i in range(count)])


def over_head(value, mask):
    count = lax.axis_size("head")
    return lax.ppermute(value, "head", [(i, i ^ mask) for i in range(count)])


def pin(values):
    return lax.optimization_barrier(values)


def in_order(flag, own, other, axis):
    return jnp.where(
        flag == 0,
        jnp.concatenate([own, other], axis=axis),
        jnp.concatenate([other, own], axis=axis),
    )


def token_offset(head_place, index, sub):
    core, upper, inner = index // (2 * sub), (index // sub) % 2, index % sub
    return (head_place ^ (upper * 2) ^ core) * sub + inner


def allowed_mask(meta_ref, start_row, q_block, k_block, rows, half, q_lanes):
    sub = half // 2
    head_place = meta_ref[0]
    k_index = lax.broadcasted_iota(jnp.int32, (2 * half, 1), 0)
    k_token = token_offset(head_place, k_index, sub) + k_block * (2 * half)
    q_index = lax.broadcasted_iota(jnp.int32, (1, q_lanes), 1) % (2 * half)
    q_token = token_offset(head_place, q_index, sub) + q_block * (2 * half)
    return (k_token <= q_token) & (k_token >= start_row)


def stacked(ref, heads, width):
    return jnp.concatenate(
        [ref[c, 0, :, h * width : (h + 1) * width] for h in range(heads) for c in range(2)], axis=0
    )


def key_rows(ref, part, block):
    return jnp.concatenate([ref[part, 0, block], ref[part, 1, block]], axis=0)


def attend_kernel(meta_ref, q_ref, k_ref, v_ref, start_ref, o_ref, ot_ref, l_ref, vt_ref, acc_ref, sum_ref, *, factor, heads):
    q_pos = pl.program_id(0)
    parts, _, blocks, half, width = k_ref.shape
    lanes = heads * 2 * half

    @pl.when(q_pos == 0)
    def _():
        for part in range(parts):
            for block in range(blocks):
                vt_ref[part * blocks + block] = key_rows(v_ref, part, block).T

    q_rows = stacked(q_ref, heads, width)
    acc_ref[...] = jnp.zeros_like(acc_ref)
    sum_ref[...] = jnp.zeros_like(sum_ref)
    start_row = start_ref[0]
    q_block = meta_ref[1 + q_pos]
    total = parts * blocks

    def add(kb, masked):
        e = jnp.exp2(nt(key_rows(k_ref, kb // blocks, kb % blocks), q_rows) * factor)
        if masked:
            k_block = meta_ref[1 + blocks + kb]
            e = jnp.where(allowed_mask(meta_ref, start_row, q_block, k_block, None, half, lanes), e, 0.0)
        sum_ref[...] += jnp.sum(e, axis=0, keepdims=True)
        acc_ref[...] += nn(vt_ref[kb], e.astype(BF16))

    def step(kb, carry):
        flag = meta_ref[1 + blocks + total + q_pos * total + kb]

        @pl.when(flag == 1)
        def _():
            add(kb, False)

        @pl.when(flag == 2)
        def _():
            add(kb, True)

        return carry

    lax.fori_loop(0, total, step, 0)
    out = acc_ref[...] / sum_ref[...]
    ot_ref[0] = out
    l_ref[0] = sum_ref[...]
    rows = out.T
    for h in range(heads):
        for c in range(2):
            at = (h * 2 + c) * half
            o_ref[c, 0, :, h * width : (h + 1) * width] = rows[at : at + half].astype(BF16)


def attend_back_kernel(
    meta_ref, q_ref, do_ref, k_ref, v_ref, start_ref, ot_ref, l_ref, dq_ref, dk_ref, dv_ref, kt_ref, acc_ref, *, factor, scaling, heads
):
    q_pos = pl.program_id(0)
    parts, _, blocks, half, width = k_ref.shape
    lanes = heads * 2 * half

    @pl.when(q_pos == 0)
    def _():
        dk_ref[...] = jnp.zeros_like(dk_ref)
        dv_ref[...] = jnp.zeros_like(dv_ref)
        for part in range(parts):
            for block in range(blocks):
                kt_ref[part * blocks + block] = key_rows(k_ref, part, block).T

    q_rows = stacked(q_ref, heads, width)
    do_rows = stacked(do_ref, heads, width)
    delta = jnp.sum(do_rows.astype(F32).T * ot_ref[0], axis=0, keepdims=True)
    inverse = 1.0 / l_ref[0]
    acc_ref[...] = jnp.zeros_like(acc_ref)
    start_row = start_ref[0]
    q_block = meta_ref[1 + q_pos]
    total = parts * blocks

    def add(kb, masked):
        part, block = kb // blocks, kb % blocks
        e = jnp.exp2(nt(key_rows(k_ref, part, block), q_rows) * factor)
        if masked:
            k_block = meta_ref[1 + blocks + kb]
            e = jnp.where(allowed_mask(meta_ref, start_row, q_block, k_block, None, half, lanes), e, 0.0)
        p = e * inverse
        dp = nt(key_rows(v_ref, part, block), do_rows)
        ds = (p * (dp - delta)).astype(BF16)
        dv = nn(p.astype(BF16), do_rows)
        dk = nn(ds, q_rows) * scaling
        for c in range(2):
            dv_ref[part, c, block] += dv[c * half : (c + 1) * half]
            dk_ref[part, c, block] += dk[c * half : (c + 1) * half]
        acc_ref[...] += nn(kt_ref[kb], ds)

    def step(kb, carry):
        flag = meta_ref[1 + blocks + total + q_pos * total + kb]

        @pl.when(flag == 1)
        def _():
            add(kb, False)

        @pl.when(flag == 2)
        def _():
            add(kb, True)

        return carry

    lax.fori_loop(0, total, step, 0)
    rows = acc_ref[...].T * scaling
    for h in range(heads):
        for c in range(2):
            at = (h * 2 + c) * half
            dq_ref[c, 0, :, h * width : (h + 1) * width] = rows[at : at + half]


def attend(meta, q, k, v, start, scaling):
    _, blocks, half, columns = q.shape
    parts, width = k.shape[0], k.shape[-1]
    heads = columns // width
    lanes = heads * 2 * half
    total = parts * blocks
    row_spec = pl.BlockSpec((2, 1, half, columns), lambda i: (0, i, 0, 0))
    key_spec = pl.BlockSpec(k.shape, lambda i: (0, 0, 0, 0, 0))
    lane_spec = pl.BlockSpec((1, 1, lanes), lambda i: (i, 0, 0))
    return pl.pallas_call(
        functools.partial(attend_kernel, factor=scaling * LOG2E, heads=heads),
        grid=(blocks,),
        in_specs=[pl.BlockSpec(memory_space=pltpu.SMEM), row_spec, key_spec, key_spec, lane_spec],
        out_specs=[row_spec, pl.BlockSpec((1, width, lanes), lambda i: (i, 0, 0)), lane_spec],
        out_shape=[
            jax.ShapeDtypeStruct(q.shape, BF16),
            jax.ShapeDtypeStruct((blocks, width, lanes), F32),
            jax.ShapeDtypeStruct((blocks, 1, lanes), F32),
        ],
        scratch_shapes=[
            pltpu.VMEM((total, width, 2 * half), BF16),
            pltpu.VMEM((width, lanes), F32),
            pltpu.VMEM((1, lanes), F32),
        ],
        compiler_params=pltpu.CompilerParams(vmem_limit_bytes=VMEM_LIMIT),
        cost_estimate=pl.CostEstimate(
            flops=2 * 2 * lanes * 2 * half * width * blocks * total,
            bytes_accessed=8 * q.size + 8 * k.size,
            transcendentals=lanes * 2 * half * blocks * total,
        ),
    )(meta, q, k, v, start)


def attend_back(meta, q, do, k, v, start, out_t, total_e, scaling):
    _, blocks, half, columns = q.shape
    parts, width = k.shape[0], k.shape[-1]
    heads = columns // width
    lanes = heads * 2 * half
    total = parts * blocks
    row_spec = pl.BlockSpec((2, 1, half, columns), lambda i: (0, i, 0, 0))
    key_spec = pl.BlockSpec(k.shape, lambda i: (0, 0, 0, 0, 0))
    lane_spec = pl.BlockSpec((1, 1, lanes), lambda i: (i, 0, 0))
    return pl.pallas_call(
        functools.partial(attend_back_kernel, factor=scaling * LOG2E, scaling=scaling, heads=heads),
        grid=(blocks,),
        in_specs=[
            pl.BlockSpec(memory_space=pltpu.SMEM),
            row_spec,
            row_spec,
            key_spec,
            key_spec,
            lane_spec,
            pl.BlockSpec((1, width, lanes), lambda i: (i, 0, 0)),
            lane_spec,
        ],
        out_specs=[row_spec, key_spec, key_spec],
        out_shape=[
            jax.ShapeDtypeStruct(q.shape, F32),
            jax.ShapeDtypeStruct(k.shape, F32),
            jax.ShapeDtypeStruct(k.shape, F32),
        ],
        scratch_shapes=[
            pltpu.VMEM((total, width, 2 * half), BF16),
            pltpu.VMEM((width, lanes), F32),
        ],
        compiler_params=pltpu.CompilerParams(vmem_limit_bytes=VMEM_LIMIT),
        cost_estimate=pl.CostEstimate(
            flops=5 * 2 * lanes * 2 * half * width * blocks * total,
            bytes_accessed=12 * q.size + 16 * k.size,
            transcendentals=lanes * 2 * half * blocks * total,
        ),
    )(meta, q, do, k, v, start, out_t, total_e)


def prepare_kernel(x_ref, w_ref, cos_ref, sin_ref, gq_ref, gk_ref, q_ref, kv_ref, raw_ref, *, heads, width):
    acc = jnp.dot(x_ref[...], w_ref[...], preferred_element_type=F32)
    raw_ref[...] = acc[:, : (heads + 1) * width]
    for h in range(heads + 1):
        part = acc[:, h * width : (h + 1) * width]
        normed = part * lax.rsqrt(jnp.mean(part * part, axis=-1, keepdims=True) + EPS)
        scaled = normed * (gq_ref if h < heads else gk_ref)[...]
        turned = (scaled * cos_ref[...] + pltpu.roll(scaled, width // 2, 1) * sin_ref[...]).astype(BF16)
        if h < heads:
            q_ref[:, h * width : (h + 1) * width] = turned
        else:
            kv_ref[:, :width] = turned
    kv_ref[:, width:] = acc[:, (heads + 1) * width :].astype(BF16)


def prepare(x, w, cos, sin, gain_q, gain_k, heads):
    tokens, depth = x.shape
    width, tile = gain_q.shape[1], 256
    row = lambda n: pl.BlockSpec((tile, n), lambda i: (i, 0))
    fixed = lambda a: pl.BlockSpec(a.shape, lambda i: (0, 0))
    return pl.pallas_call(
        functools.partial(prepare_kernel, heads=heads, width=width),
        grid=(tokens // tile,),
        in_specs=[row(depth), fixed(w), row(width), row(width), fixed(gain_q), fixed(gain_k)],
        out_specs=[row(heads * width), row(2 * width), row((heads + 1) * width)],
        out_shape=[
            jax.ShapeDtypeStruct((tokens, heads * width), BF16),
            jax.ShapeDtypeStruct((tokens, 2 * width), BF16),
            jax.ShapeDtypeStruct((tokens, (heads + 1) * width), F32),
        ],
        compiler_params=pltpu.CompilerParams(vmem_limit_bytes=VMEM_LIMIT),
        cost_estimate=TINY_COST,
    )(x, w, cos, sin, gain_q, gain_k)


def prepare_back_kernel(
    dq_ref, dk_ref, dv_ref, got_ref, raw_ref, cos_ref, sin_ref, gq_ref, gk_ref, w_ref, d_ref, p_ref, g_ref, *, heads, width
):
    @pl.when(pl.program_id(0) == 0)
    def _():
        g_ref[...] = jnp.zeros_like(g_ref)

    got = got_ref[...].astype(F32)
    for h in range(heads + 1):
        at = slice(h * width, (h + 1) * width)
        grad = dq_ref[:, at] if h < heads else dk_ref[0] + got[:, :width]
        gain = (gq_ref if h < heads else gk_ref)[...]
        raw = raw_ref[:, at]
        inverse = lax.rsqrt(jnp.mean(raw * raw, axis=-1, keepdims=True) + EPS)
        normed = raw * inverse
        turned = grad * cos_ref[...] - pltpu.roll(grad, width // 2, 1) * sin_ref[...]
        row = 0 if h < heads else 1
        g_ref[row : row + 1, :] += jnp.sum(turned * normed, axis=0, keepdims=True)
        scaled = turned * gain
        d_ref[:, at] = (inverse * (scaled - normed * jnp.mean(scaled * normed, axis=-1, keepdims=True))).astype(BF16)
    d_ref[:, (heads + 1) * width :] = (dv_ref[0] + got[:, width:]).astype(BF16)
    p_ref[...] = nt(d_ref[...], w_ref[...]).astype(BF16)


def prepare_back(dq, dk, dv, got, raw, cos, sin, gain_q, gain_k, w, heads):
    tokens, width, tile = dq.shape[0], gain_q.shape[1], 256
    row = lambda n: pl.BlockSpec((tile, n), lambda i: (i, 0))
    part = pl.BlockSpec((1, tile, width), lambda i: (0, i, 0))
    fixed = lambda a: pl.BlockSpec(a.shape, lambda i: (0, 0))
    return pl.pallas_call(
        functools.partial(prepare_back_kernel, heads=heads, width=width),
        grid=(tokens // tile,),
        in_specs=[
            row(heads * width),
            part,
            part,
            row(2 * width),
            row((heads + 1) * width),
            row(width),
            row(width),
            fixed(gain_q),
            fixed(gain_k),
            fixed(w),
        ],
        out_specs=[row(w.shape[1]), row(w.shape[0]), pl.BlockSpec((8, width), lambda i: (0, 0))],
        out_shape=[
            jax.ShapeDtypeStruct((tokens, w.shape[1]), BF16),
            jax.ShapeDtypeStruct((tokens, w.shape[0]), BF16),
            jax.ShapeDtypeStruct((8, width), F32),
        ],
        compiler_params=pltpu.CompilerParams(vmem_limit_bytes=VMEM_LIMIT),
        cost_estimate=TINY_COST,
    )(dq, dk, dv, got, raw, cos, sin, gain_q, gain_k, w)


def place_of_block(blk, bit_order, p):
    return blk ^ sum(((p >> i) & 1) << b for i, b in enumerate(bit_order))


def enter_kernel(blk_ref, *refs, bit_order, normed):
    if normed:
        mine_ref, other_ref, gain_ref, low_ref, out_ref, gains_ref = refs
    else:
        mine_ref, low_ref = refs
    rows, width = mine_ref.shape
    n = width >> len(bit_order)
    for p in range(1 << len(bit_order)):
        at = pl.ds(pl.multiple_of(place_of_block(blk_ref[0], bit_order, p) * n, n), n)
        low_ref[:rows, p * n : (p + 1) * n] = mine_ref[:, at]
        if normed:
            low_ref[rows:, p * n : (p + 1) * n] = other_ref[:, at]
            gains_ref[:, p * n : (p + 1) * n] = gain_ref[:, at]
    if normed:
        values = low_ref[...].astype(F32)
        inverse = lax.rsqrt(jnp.mean(values * values, axis=-1, keepdims=True) + EPS)
        out_ref[...] = (values * inverse * gains_ref[:1]).astype(BF16)


def enter(blk, bit_order, mine, other=None, gain=None):
    rows, width = mine.shape
    normed = gain is not None
    total = (2 * rows if normed else rows, width)
    vmem = pl.BlockSpec(memory_space=pltpu.VMEM)
    operands = [mine, other, gain] if normed else [mine]
    return pl.pallas_call(
        functools.partial(enter_kernel, bit_order=bit_order, normed=normed),
        in_specs=[pl.BlockSpec(memory_space=pltpu.SMEM), *[vmem] * len(operands)],
        out_specs=[vmem] * (3 if normed else 1),
        out_shape=[
            *[jax.ShapeDtypeStruct(total, BF16)] * (2 if normed else 1),
            *([jax.ShapeDtypeStruct(gain.shape, F32)] if normed else []),
        ],
        compiler_params=pltpu.CompilerParams(vmem_limit_bytes=VMEM_LIMIT),
        cost_estimate=TINY_COST,
    )(blk[None].astype(jnp.int32), *operands)


def assemble_kernel(place_ref, *refs, sources, widths):
    ins, outs = refs[: 2 * sources], refs[2 * sources :]
    place, k, at = place_ref[0], 0, 0
    for own_ref, got_ref in zip(ins[::2], ins[1::2]):
        f, at = own_ref.shape[0], 0
        while at < own_ref.shape[1]:
            w, cut = widths[k], slice(at, at + widths[k])
            mine = pl.ds(pl.multiple_of(place * w, w), w)
            theirs = pl.ds(pl.multiple_of((1 - place) * w, w), w)
            outs[k][:, mine] = own_ref[:, cut] + got_ref[:f, cut].astype(F32)
            outs[k][:, theirs] = got_ref[f : 2 * f, cut].astype(F32) + got_ref[2 * f :, cut].astype(F32)
            at += w
            k += 1


def assemble(place, sources, widths):
    vmem = pl.BlockSpec(memory_space=pltpu.VMEM)
    flat = [a for pair in sources for a in pair]
    return pl.pallas_call(
        functools.partial(assemble_kernel, sources=len(sources), widths=widths),
        in_specs=[pl.BlockSpec(memory_space=pltpu.SMEM), *[vmem] * len(flat)],
        out_specs=[vmem] * len(widths),
        out_shape=[jax.ShapeDtypeStruct((sources[0][0].shape[0], 2 * w), F32) for w in widths],
        compiler_params=pltpu.CompilerParams(vmem_limit_bytes=VMEM_LIMIT),
        cost_estimate=TINY_COST,
    )(place[None].astype(jnp.int32), *flat)


def back_kernel(*refs):
    *ins, out_ref = refs
    n = len(ins) // 2
    out_ref[...] = sum(nt(d[...], w[...]) for d, w in zip(ins[:n], ins[n:])).astype(BF16)


def back_through(grads, weights):
    tokens, depth, tile = grads[0].shape[0], weights[0].shape[0], 256
    return pl.pallas_call(
        back_kernel,
        grid=(depth // tile,),
        in_specs=[
            *[pl.BlockSpec(g.shape, lambda i: (0, 0)) for g in grads],
            *[pl.BlockSpec((tile, w.shape[1]), lambda i: (i, 0)) for w in weights],
        ],
        out_specs=pl.BlockSpec((tokens, tile), lambda i: (0, i)),
        out_shape=jax.ShapeDtypeStruct((tokens, depth), BF16),
        compiler_params=pltpu.CompilerParams(vmem_limit_bytes=VMEM_LIMIT),
        cost_estimate=TINY_COST,
    )(*grads, *weights)


def weight_grad_kernel(a_ref, b_ref, keep_ref, away_ref):
    product = tn(a_ref[...], b_ref[...])
    first = pl.program_id(0) < pl.num_programs(0) // 2

    @pl.when(first)
    def _():
        keep_ref[...] = product

    @pl.when(jnp.logical_not(first))
    def _():
        away_ref[...] = product.astype(BF16)


def weight_grad(a, b):
    tokens, depth = a.shape
    n, tile = b.shape[1], 256
    steps = depth // tile
    return pl.pallas_call(
        weight_grad_kernel,
        grid=(steps,),
        in_specs=[
            pl.BlockSpec((tokens, tile), lambda i: (0, i)),
            pl.BlockSpec((tokens, n), lambda i: (0, 0)),
        ],
        out_specs=[
            pl.BlockSpec((tile, n), lambda i: (jnp.minimum(i, steps // 2 - 1), 0)),
            pl.BlockSpec((tile, n), lambda i: (jnp.maximum(i - steps // 2, 0), 0)),
        ],
        out_shape=[
            jax.ShapeDtypeStruct((depth // 2, n), F32),
            jax.ShapeDtypeStruct((depth // 2, n), BF16),
        ],
        compiler_params=pltpu.CompilerParams(vmem_limit_bytes=VMEM_LIMIT),
        cost_estimate=TINY_COST,
    )(a, b)


def remote(src, dst, send, recv, target):
    copy = pltpu.make_async_remote_copy(
        src_ref=src, dst_ref=dst, send_sem=send, recv_sem=recv, device_id=target, device_id_type=pl.DeviceIdType.MESH
    )
    copy.start()
    return copy


class Plan:
    def __init__(self):
        self.inputs, self.shapes, self.aliases, self.jobs = [], [], {}, []

    def read(self, array):
        self.inputs.append(array)
        return ("in", len(self.inputs) - 1)

    def fresh(self, shape, dtype):
        self.shapes.append(jax.ShapeDtypeStruct(shape, dtype))
        return ("out", len(self.shapes) - 1)

    def through(self, array):
        self.inputs.append(array)
        self.aliases[len(self.inputs) - 1] = len(self.shapes)
        return self.fresh(array.shape, array.dtype)

    def copy(self, src, dst, mask, after=None, point=0):
        self.jobs.append((src, dst, mask, after, point, None))
        return len(self.jobs) - 1

    def local(self, src, dst, shape, point=0):
        self.jobs.append((src, dst, 0, None, point, shape))
        return len(self.jobs) - 1


class Fill:
    def __init__(self, inputs, outputs, step, point):
        self.inputs, self.outputs, self.step, self.point = inputs, outputs, step, point

    def scratch(self):
        shapes = [pltpu.VMEM(a.shape, a.dtype) for a in (*self.inputs, *self.outputs)]
        return [*shapes, pltpu.SemaphoreType.DMA((len(shapes),))]


def fill_weight_grad(a, b, point):
    depth, n, tile = a.shape[1], b.shape[1], 256
    half = depth // 2

    def step(ins, outs):
        (a_ref, b_ref), (keep_ref, away_ref) = ins, outs

        def one(i, carry):
            at = pl.ds(pl.multiple_of(i * tile, tile), tile)
            keep_ref[at, :] = tn(a_ref[:, at], b_ref[...])
            far = pl.ds(pl.multiple_of(half + i * tile, tile), tile)
            away_ref[at, :] = tn(a_ref[:, far], b_ref[...]).astype(BF16)
            return carry

        lax.fori_loop(0, half // tile, one, 0)

    outputs = [jax.ShapeDtypeStruct((half, n), F32), jax.ShapeDtypeStruct((half, n), BF16)]
    return Fill([a, b], outputs, step, point)


def fill_back(grad, weight, point):
    tokens, depth, tile = grad.shape[0], weight.shape[0], 256

    def step(ins, outs):
        (g_ref, w_ref), (out_ref,) = ins, outs

        def one(i, carry):
            at = pl.ds(pl.multiple_of(i * tile, tile), tile)
            out_ref[:, at] = nt(g_ref[...], w_ref[at, :]).astype(BF16)
            return carry

        lax.fori_loop(0, depth // tile, one, 0)

    return Fill([grad, weight], [jax.ShapeDtypeStruct((tokens, depth), BF16)], step, point)


def fill_product(left, right, point):
    tokens, n, tile = left.shape[0], right.shape[1], 256

    def step(ins, outs):
        (l_ref, r_ref), (out_ref,) = ins, outs

        def one(i, carry):
            at = pl.ds(pl.multiple_of(i * tile, tile), tile)
            out_ref[at, :] = nn(l_ref[at, :], r_ref[...])
            return carry

        lax.fori_loop(0, tokens // tile, one, 0)

    return Fill([left, right], [jax.ShapeDtypeStruct((tokens, n), F32)], step, point)


def run(plan, main, collective_id, greeted=(), fills=(), limit=None):
    inputs, in_specs, out_shapes, out_specs, scratch, body, own_limit = main
    limit = limit or own_limit + sum(math.prod(s.shape) * s.dtype.itemsize for f in fills for s in f.scratch()[:-1])
    f_in, f_out = [a for f in fills for a in f.inputs], [a for f in fills for a in f.outputs]
    n_in, n_out = len(inputs), len(out_shapes)
    m_in, m_out = len(plan.inputs), len(plan.shapes)
    jobs = plan.jobs
    local_jobs = [i for i, job in enumerate(jobs) if not job[2]]
    masks = sorted({*greeted, *[job[2] for job in jobs if job[2]]} - {1 << TENSOR_BIT})
    any_spec = pl.BlockSpec(memory_space=pltpu.HBM)

    def kernel(*refs):
        main_in, refs = refs[:n_in], refs[n_in:]
        plan_in, refs = refs[:m_in], refs[m_in:]
        fill_in, refs = refs[: len(f_in)], refs[len(f_in) :]
        main_out, refs = refs[:n_out], refs[n_out:]
        plan_out, refs = refs[:m_out], refs[m_out:]
        fill_out, refs = refs[: len(f_out)], refs[len(f_out) :]
        send, recv, *rest = refs
        bounce = dict(zip(local_jobs, rest))
        rest = rest[len(local_jobs) :]
        parts = []
        for f in fills:
            k, m = len(f.inputs), len(f.outputs)
            (*held, sems), rest = rest[: k + m + 1], rest[k + m + 1 :]
            loads = [pltpu.make_async_copy(fill_in[i], held[i], sems.at[i]) for i in range(k)]
            stores = [pltpu.make_async_copy(held[k + i], fill_out[i], sems.at[k + i]) for i in range(m)]
            fill_in, fill_out = fill_in[k:], fill_out[m:]
            for copy in loads:
                copy.start()
            parts.append((f, held[:k], held[k:], loads, stores))

        def compute(point):
            for f, ins, outs, loads, stores in parts:
                if f.point == point:
                    for copy in loads:
                        copy.wait()
                    f.step(ins, outs)
                    for copy in stores:
                        copy.start()

        blk, head = lax.axis_index("blk"), lax.axis_index("head")
        core, near, across = (blk, head ^ 1), (blk, head ^ 2), (blk ^ (1 << TENSOR_BIT), head)
        barrier = pltpu.get_barrier_semaphore()
        partners = [core, near, across, *[(blk ^ m, head) for m in masks]]
        for target in partners:
            pl.semaphore_signal(barrier, inc=1, device_id=target, device_id_type=pl.DeviceIdType.MESH)
        pl.semaphore_wait(barrier, len(partners))
        started, arrived, halfway = {}, set(), []

        def arrive(i):
            if i not in arrived:
                arrived.add(i)
                (started[i].wait_recv if jobs[i][2] else started[i].wait)()

        def part(side):
            (kind, index), cut = side
            if kind == "fill":
                return cut(parts[index[0]][2][index[1]])
            return cut((plan_in if kind == "in" else plan_out)[index])

        def issue(point):
            for i in list(halfway):
                started[i].wait()
                started[i] = pltpu.make_async_copy(bounce[i], part(jobs[i][1]), recv.at[i])
                started[i].start()
                halfway.remove(i)
            for i, (src, dst, mask, after, at, shape) in enumerate(jobs):
                if i in started or (at != point and point is not None):
                    continue
                if after is not None:
                    arrive(after)
                if mask:
                    started[i] = remote(part(src), part(dst), send.at[i], recv.at[i], (blk ^ mask, head))
                else:
                    started[i] = pltpu.make_async_copy(part(src), bounce[i], send.at[i])
                    started[i].start()
                    halfway.append(i)

        point = 0
        for _ in body((core, near, across), main_in, main_out, rest):
            issue(point)
            compute(point)
            point += 1
        issue(None)
        issue(None)
        for i in range(len(jobs)):
            arrive(i)
            if jobs[i][2]:
                started[i].wait_send()
        for *_, stores in parts:
            for copy in stores:
                copy.wait()

    results = pl.pallas_call(
        kernel,
        out_shape=[*out_shapes, *plan.shapes, *f_out],
        in_specs=[*in_specs, *[any_spec] * (m_in + len(f_in))],
        out_specs=[*out_specs, *[any_spec] * (m_out + len(f_out))],
        scratch_shapes=[
            pltpu.SemaphoreType.DMA((max(1, len(jobs)),)),
            pltpu.SemaphoreType.DMA((max(1, len(jobs)),)),
            *[pltpu.VMEM(jobs[i][5], BF16) for i in local_jobs],
            *[s for f in fills for s in f.scratch()],
            *scratch,
        ],
        input_output_aliases={n_in + i: n_out + o for i, o in plan.aliases.items()},
        compiler_params=pltpu.CompilerParams(
            collective_id=collective_id, has_side_effects=True, vmem_limit_bytes=limit
        ),
        cost_estimate=TINY_COST,
    )(*inputs, *plan.inputs, *f_in)
    return results[:n_out], results[n_out:]


def spread_main(flat, chunk):
    rows, width = flat.shape[0] // 2, flat.shape[1]
    pieces = width // chunk

    def body(partners, ins, outs, scratch):
        core, near, across = partners
        (s_ref,), (o_ref,), (hold, local_sem, send, recv) = ins, outs, scratch
        first = remote(s_ref, o_ref.at[0, :, 0, 1], send.at[0], recv.at[0], near)
        second = [
            remote(
                s_ref.at[:, :, pl.ds(i * chunk, chunk)],
                o_ref.at[0, :, 1, 0, :, pl.ds((i ^ 1) * chunk, chunk)],
                send.at[6 + i],
                recv.at[6 + i],
                across,
            )
            for i in range(pieces)
        ]
        third = remote(s_ref, o_ref.at[1, :, 0, 0], send.at[1], recv.at[1], core)
        held = pltpu.make_async_copy(s_ref, hold, local_sem.at[0])
        held.start()
        yield
        held.wait()
        own = pltpu.make_async_copy(hold, o_ref.at[0, :, 0, 0], local_sem.at[1])
        own.start()
        for copy in second:
            copy.wait_recv()
        fourth = remote(o_ref.at[0, :, 1, 0], o_ref.at[0, :, 1, 1], send.at[2], recv.at[2], near)
        fifth = remote(o_ref.at[0, :, 1, 0], o_ref.at[1, :, 1, 0], send.at[3], recv.at[3], core)
        yield
        first.wait_recv()
        sixth = remote(o_ref.at[0, :, 0, 1], o_ref.at[1, :, 0, 1], send.at[4], recv.at[4], core)
        yield
        fourth.wait_recv()
        seventh = remote(o_ref.at[0, :, 1, 1], o_ref.at[1, :, 1, 1], send.at[5], recv.at[5], core)
        yield
        own.wait()
        for copy in (first, *second, third, fourth, fifth, sixth, seventh):
            copy.wait_send()
        for copy in (third, fifth, sixth, seventh):
            copy.wait_recv()

    any_spec = pl.BlockSpec(memory_space=pltpu.HBM)
    return (
        [flat.reshape(2, rows, width)],
        [any_spec],
        [jax.ShapeDtypeStruct((2, 2, 2, 2, rows, width), flat.dtype)],
        [any_spec],
        [
            pltpu.VMEM((2, rows, width), flat.dtype),
            pltpu.SemaphoreType.DMA((2,)),
            pltpu.SemaphoreType.DMA((6 + pieces,)),
            pltpu.SemaphoreType.DMA((6 + pieces,)),
        ],
        body,
        8 * MIB,
    )


def gather_main(partial, chunk, extra, outs_like, finish):
    rows, width = partial.shape[0] // 16, partial.shape[1]
    share = (2, rows, width)
    pieces = width // chunk

    def body(partners, ins, outs, scratch):
        core, near, across = partners
        p_ref, *extra_refs = ins
        core_in, out_y, in_y, out_t, in_t, hold, send, recv = scratch
        order = ((1, 1), (0, 1), (1, 0), (0, 0))
        from_core = [
            remote(p_ref.at[1, :, t, y], core_in.at[i], send.at[i], recv.at[i], core) for i, (t, y) in enumerate(order)
        ]
        from_y = []
        for i in range(2):
            t, y = order[i]
            from_core[i].wait_recv()
            out_y[i] = (p_ref[0, :, t, y].astype(F32) + core_in[i].astype(F32)).astype(BF16)
            from_y.append(remote(out_y.at[i], in_y.at[i], send.at[4 + i], recv.at[4 + i], near))
        yield
        from_core[2].wait_recv()
        hold[...] = p_ref[0, :, 1, 0].astype(F32) + core_in[2].astype(F32)
        from_y[0].wait_recv()
        for i in range(pieces):
            a, b = slice(i * chunk, (i + 1) * chunk), slice((i ^ 1) * chunk, ((i ^ 1) + 1) * chunk)
            out_t[:, :, b] = (hold[:, :, a] + in_y[0, :, :, a].astype(F32)).astype(BF16)
        from_t = remote(out_t, in_t, send.at[6], recv.at[6], across)
        yield
        from_core[3].wait_recv()
        hold[...] = p_ref[0, :, 0, 0].astype(F32) + core_in[3].astype(F32)
        from_y[1].wait_recv()
        hold[...] += in_y[1].astype(F32)
        yield
        from_t.wait_recv()
        hold[...] += in_t[...].astype(F32)
        finish(hold, extra_refs, outs)
        for copy in (*from_core, *from_y, from_t):
            copy.wait_send()

    vmem_spec = pl.BlockSpec(memory_space=pltpu.VMEM)
    return (
        [partial.reshape(2, 2, 2, 2, rows, width), *extra],
        [vmem_spec] * (1 + len(extra)),
        outs_like,
        [vmem_spec] * len(outs_like),
        [
            pltpu.VMEM((4, *share), BF16),
            pltpu.VMEM((2, *share), BF16),
            pltpu.VMEM((2, *share), BF16),
            pltpu.VMEM(share, BF16),
            pltpu.VMEM(share, BF16),
            pltpu.VMEM(share, F32),
            pltpu.SemaphoreType.DMA((7,)),
            pltpu.SemaphoreType.DMA((7,)),
        ],
        body,
        24 * MIB,
    )


def inverse_rms(values):
    return lax.rsqrt(jnp.mean(values * values, axis=-1, keepdims=True) + EPS)


def finish_middle(total, extra, outs):
    (low_ref, gain_ref), (middle_ref, normed_ref) = extra, outs
    for m in range(2):
        middle = low_ref[m].astype(F32) + total[m]
        middle_ref[m] = middle
        normed_ref[m] = (middle * inverse_rms(middle) * gain_ref[...]).astype(BF16)


def norm_grad(total, values, gain, gain_grad_ref, m):
    inverse = inverse_rms(values)
    normal = values * inverse
    part = jnp.sum(total * normal, axis=0, keepdims=True)
    gain_grad_ref[...] = part if m == 0 else gain_grad_ref[...] + part
    scaled = total * gain
    return inverse * (scaled - normal * jnp.mean(scaled * normal, axis=-1, keepdims=True))


def finish_mlp_norm(total, extra, outs):
    (cot_ref, middle_ref, gain_ref), (grad_ref, low_ref, gain_grad_ref) = extra, outs
    for m in range(2):
        grad = cot_ref[m].astype(F32) + norm_grad(total[m], middle_ref[m], gain_ref[...], gain_grad_ref, m)
        grad_ref[m] = grad
        low_ref[m] = grad.astype(BF16)


def store_ungrouped(value, ref, blk, bit_order, lead=()):
    n = value.shape[-1] >> len(bit_order)
    for p in range(1 << len(bit_order)):
        block = value[:, p * n : (p + 1) * n]
        if bit_order and n % 128 == 0:
            at = pl.ds(pl.multiple_of(place_of_block(blk, bit_order, p) * n, n), n)
        else:
            at = pl.ds(p * n, n)
        ref[(*lead, slice(None), at)] = block.astype(ref.dtype)


def finish_mixed(total, extra, outs, *, bit_order):
    (middle_ref,), (mixed_ref,) = extra, outs
    blk = lax.axis_index("blk")
    for m in range(2):
        store_ungrouped(middle_ref[m] + total[m], mixed_ref, blk, bit_order, (m,))


def finish_input(total, extra, outs, *, bit_order):
    (low_ref, mid_ref, gain_ref), (own_ref, away_ref, gain_grad_ref) = extra, outs
    blk = lax.axis_index("blk")
    for m in range(2):
        grad = mid_ref[m] + norm_grad(total[m], low_ref[m].astype(F32), gain_ref[...], gain_grad_ref, m)
        store_ungrouped(grad, own_ref if m == 0 else away_ref, blk, bit_order)


def total_main(values):
    rows, width = values.shape
    rounds = 2 + lax.axis_size("blk").bit_length() - 1

    def body(partners, ins, outs, scratch):
        (v_ref,), (o_ref,) = ins, outs
        out_buf, in_buf, send, recv = scratch
        blk, head = lax.axis_index("blk"), lax.axis_index("head")
        o_ref[...] = v_ref[...]
        yield
        for i in range(rounds):
            target = (blk, head ^ (1 << i)) if i < 2 else (blk ^ (1 << (i - 2)), head)
            out_buf[i] = o_ref[...]
            copy = remote(out_buf.at[i], in_buf.at[i], send.at[i], recv.at[i], target)
            copy.wait_recv()
            o_ref[...] += in_buf[i]
            copy.wait_send()
        yield

    vmem_spec = pl.BlockSpec(memory_space=pltpu.VMEM)
    return (
        [values],
        [vmem_spec],
        [jax.ShapeDtypeStruct(values.shape, F32)],
        [vmem_spec],
        [
            pltpu.VMEM((rounds, rows, width), F32),
            pltpu.VMEM((rounds, rows, width), F32),
            pltpu.SemaphoreType.DMA((rounds,)),
            pltpu.SemaphoreType.DMA((rounds,)),
        ],
        body,
        8 * MIB,
    )


class Moving:
    def __init__(self, copy, away):
        self.copy, self.away, self.here, self.gone = copy, away, False, not away

    def arrive(self):
        if not self.here:
            self.here = True
            (self.copy.wait_recv if self.away else self.copy.wait)()

    def sent(self):
        if not self.gone:
            self.gone = True
            self.copy.wait_send()


class Links:
    def __init__(self, send, recv, batch_mask):
        self.send, self.recv, self.all = send, recv, []
        blk, head = lax.axis_index("blk"), lax.axis_index("head")
        self.core, self.near, self.across = (blk, head ^ 1), (blk, head ^ 2), (blk ^ (1 << TENSOR_BIT), head)
        self.seq, self.batch = (blk ^ (1 << SEQ_BIT), head), (blk ^ batch_mask, head)
        self.both = (blk ^ (batch_mask | (1 << TENSOR_BIT)), head)
        self.place = bit_of(blk, TENSOR_BIT)
        self.blk = blk

    def greet(self):
        barrier = pltpu.get_barrier_semaphore()
        partners = (self.core, self.near, self.across, self.seq, self.batch, self.both)
        for target in partners:
            pl.semaphore_signal(barrier, inc=1, device_id=target, device_id_type=pl.DeviceIdType.MESH)
        pl.semaphore_wait(barrier, len(partners))

    def to(self, target, src, dst):
        i = len(self.all)
        self.all.append(Moving(remote(src, dst, self.send.at[i], self.recv.at[i], target), True))
        return self.all[-1]

    def load(self, src, dst):
        copy = pltpu.make_async_copy(src, dst, self.recv.at[len(self.all)])
        copy.start()
        self.all.append(Moving(copy, False))
        return self.all[-1]

    def finish(self):
        for moving in self.all:
            moving.arrive()
            moving.sent()

    def half(self, ref, other):
        n = ref.shape[1] // 2
        place = 1 - self.place if other else self.place
        return ref.at[:, pl.ds(pl.multiple_of(place * n, n), n)]


def nothing(stage):
    pass


def spread_in(links, s_ref, o_ref, chunk, between=nothing, in_vmem=True):
    pieces = s_ref.shape[-1] // chunk
    across = [
        links.to(
            links.across,
            s_ref.at[:, :, pl.ds(i * chunk, chunk)],
            o_ref.at[0, :, 1, 0, :, pl.ds((i ^ 1) * chunk, chunk)],
        )
        for i in range(pieces)
    ]
    near = links.to(links.near, s_ref, o_ref.at[0, :, 0, 1])
    core = [links.to(links.core, s_ref, o_ref.at[1, :, 0, 0])]
    if in_vmem:
        o_ref[0, :, 0, 0] = s_ref[...]
    else:
        links.load(s_ref, o_ref.at[0, :, 0, 0])
    between(0)
    for copy in across:
        copy.arrive()
    onward = links.to(links.near, o_ref.at[0, :, 1, 0], o_ref.at[0, :, 1, 1])
    core.append(links.to(links.core, o_ref.at[0, :, 1, 0], o_ref.at[1, :, 1, 0]))
    near.arrive()
    core.append(links.to(links.core, o_ref.at[0, :, 0, 1], o_ref.at[1, :, 0, 1]))
    between(1)
    onward.arrive()
    core.append(links.to(links.core, o_ref.at[0, :, 1, 1], o_ref.at[1, :, 1, 1]))
    between(2)
    for copy in core:
        copy.arrive()
    for copy in (*across, near, core[0]):
        copy.sent()


def sum_in(links, bufs, chunk, partial, between=nothing, far=None):
    p_ref, core_in, out_y, in_y, out_t, in_t, hold = bufs
    order = ((1, 1), (1, 0), (0, 1), (0, 0))
    if partial:
        partial(1)
        far = p_ref.at[1]
    core = [links.to(links.core, far.at[:, t, y], core_in.at[i]) for i, (t, y) in enumerate(order)]
    if partial:
        partial(0)

    def both(i):
        t, y = order[i]
        core[i].arrive()
        return p_ref[0, :, t, y].astype(F32) + core_in[i].astype(F32)

    def near(i, m):
        return links.to(links.near, out_y.at[i, m], in_y.at[i, m])

    out_y[0] = both(0).astype(BF16)
    copies = [near(0, 0)]
    hold[...] = both(1)
    out_y[1] = both(2).astype(BF16)
    between(0)
    across = []
    for m in range(2):
        copies[m].arrive()
        copies += [near(0, 1)] if m == 0 else [near(1, 0), near(1, 1)]
        for i in range(p_ref.shape[-1] // chunk):
            a, b = slice(i * chunk, (i + 1) * chunk), slice((i ^ 1) * chunk, ((i ^ 1) + 1) * chunk)
            out_t[m, :, b] = (hold[m, :, a] + in_y[0, m, :, a].astype(F32)).astype(BF16)
        across.append(links.to(links.across, out_t.at[m], in_t.at[m]))
    hold[...] = both(3)
    between(1)
    for m in range(2):
        copies[2 + m].arrive()
        hold[m] += in_y[1, m].astype(F32)
    between(2)
    for m in range(2):
        across[m].arrive()
        hold[m] += in_t[m].astype(F32)
    for copy in (*core, *copies, *across):
        copy.sent()


def loop(count, step):
    def one(i, carry):
        step(i)
        return carry

    lax.fori_loop(0, count, one, 0)


def rows_of(ref, i):
    value = ref[i // 2, i % 2]
    return value.reshape(-1, value.shape[-1])


def away_rows(a_cols, b_ref, away_ref):
    depth, tile = away_ref.shape[0], 512

    def step(i):
        product = tn(a_cols(pl.multiple_of(depth + i * tile, tile), tile), b_ref[...])
        away_ref[pl.ds(pl.multiple_of(i * tile, tile), tile), :] = product.astype(BF16)

    loop(depth // tile, step)


def keep_rows(a_cols, b_ref, fold_ref, own_ref, send_ref):
    f = own_ref.shape[0]
    own_ref[...] = tn(a_cols(0, f), b_ref[...]) + fold_ref[:f, :].astype(F32)

    def step(i):
        at = pl.multiple_of(i * f, f)
        product = tn(a_cols(pl.multiple_of(at + f, f), f), b_ref[...])
        send_ref[pl.ds(at, f), :] = (product + fold_ref[pl.ds(pl.multiple_of(at + f, f), f), :].astype(F32)).astype(BF16)

    loop(3, step)


def middle_kernel(
    low_ref, cot_ref, gain_ref, attn_ref, wo_ref, c_ref, wd_ref, wg_ref, down_ref, gate_ref, up_ref,
    middle_ref, dmid_ref, gain_grad_ref, dall_ref, mixed_ref, own_d_ref, got_d_b_ref, got_d_o_ref, got_g_b_ref, send_g_ref, keep_g_ref, away_g_ref, keep_u_ref, away_u_ref,
    attn, wo, p, core_in, out_y, in_y, out_t, in_t, hold, xm_s, xm, c, wd, wg, wu, dact, gate, act, dg, du,
    away_d, fold_d, away_g, fold_g, own_d, send_d, keep_g, send_g, up_tile, send, recv, *, batch_mask, chunk,
):
    links = Links(send, recv, batch_mask)
    f, ff = own_d.shape[0], act.shape[1]
    to, load = links.to, links.load
    loads = [load(attn_ref, attn), load(wo_ref, wo)]
    links.greet()

    def rows(ref, q):
        return ref.at[pl.ds(q * f, f), :]

    down = [to(links.seq, rows(wd_ref, q), rows(wd, q + 4)) for q in (1, 3)]
    gate_z = [to(links.batch, links.half(gate_ref, 0), rows(wg, 1)), to(links.both, links.half(gate_ref, 1), rows(wg, 3))]
    gates = [to(links.seq, rows(wg_ref, 2), rows(wg, 6))]
    up_t = to(links.across, links.half(up_ref, 1), rows(wu, 2))
    ups = []
    for copy in loads:
        copy.arrive()
    down += [load(rows(wd_ref, q), rows(wd, q)) for q in (1, 2, 3, 4, 6)]
    gates += [load(rows(wg_ref, q), rows(wg, q)) for q in (2, 4)]
    down.append(load(links.half(down_ref, 0), rows(wd, 0)))
    gates.append(load(links.half(gate_ref, 0), rows(wg, 0)))
    c_load = load(c_ref, c)
    up_own = load(links.half(up_ref, 0), rows(wu, 0))
    bufs = (p, core_in, out_y, in_y, out_t, in_t, hold)

    def out_partial(k):
        for m in range(2):
            at = (k * 2 + m) * attn.shape[0] // 4
            p[k, m] = nt(attn[at : at + attn.shape[0] // 4], wo[...]).astype(BF16).reshape(p.shape[2:])

    def while_out(stage):
        if stage == 0:
            ups.append(to(links.seq, links.half(up_ref, 0), rows(wu, 4)))
        if stage == 1:
            up_t.arrive()
            ups.append(to(links.seq, rows(wu, 2), rows(wu, 6)))
            up_z.append(to(links.batch, links.half(up_ref, 0), rows(wu, 1)))

    up_z = []
    sum_in(links, bufs, chunk, out_partial, while_out)
    for m in range(2):
        middle = low_ref[m].astype(F32) + hold[m]
        middle_ref[m] = middle
        xm_s[m] = (middle * inverse_rms(middle) * gain_ref[...]).astype(BF16)

    def while_xm(stage):
        if stage == 0:
            up_z.append(to(links.both, links.half(up_ref, 1), rows(wu, 3)))
            for copy in (*down, c_load):
                copy.arrive()

            def step(i):
                at = pl.ds(pl.multiple_of(i * 512, 512), 512)
                dact[at, :] = nn(c[at, :], wd[...])

            loop(c.shape[0] // 512, step)
            for copy in gate_z:
                copy.arrive()
            gates.extend(to(links.seq, rows(wg, q), rows(wg, q + 4)) for q in (1, 3))
        if stage == 1:
            up_z[0].arrive()
            ups.append(to(links.seq, rows(wu, 1), rows(wu, 5)))
        if stage == 2:
            up_z[1].arrive()
            ups.append(to(links.seq, rows(wu, 3), rows(wu, 7)))

    spread_in(links, xm_s, xm, chunk, while_xm)
    for copy in gates:
        copy.arrive()

    def gate_step(i):
        at = pl.ds(pl.multiple_of(i * 256, 256), 256)
        gate[at, :] = nn(rows_of(xm, i), wg[...])

    loop(4, gate_step)
    up_own.arrive()
    for copy in ups:
        copy.arrive()

    def up_step(i):
        base = pl.multiple_of(i * 256, 256)
        up_tile[...] = nn(rows_of(xm, i), wu[...])

        def part(j):
            at, here = pl.ds(pl.multiple_of(base + j * 32, 32), 32), pl.ds(pl.multiple_of(j * 32, 32), 32)
            g, u, d = gate[at, :], up_tile[here, :], dact[at, :]
            sig = 1.0 / (1.0 + jnp.exp(-g))
            silu = g * sig
            act[at, :] = (silu * u).astype(BF16)
            dg[at, :] = (d * u * sig * (1.0 + g * (1.0 - sig))).astype(BF16)
            du[at, :] = (d * silu).astype(BF16)

        loop(8, part)

    loop(4, up_step)

    def c_cols(at, n):
        return c[:, pl.ds(at, n)]

    def xm_cols(at, n):
        return xm[:, :, :, :, :, pl.ds(at, n)].reshape(-1, n)

    def fold(away, into, *places):
        return {i: to(links.seq, rows(away, i), rows(into, i)) for i in places}

    def compute_away(a_cols, b_ref, away, *places):
        for i in places:
            away[pl.ds(i * f, f), :] = tn(a_cols((i + 4) * f, f), b_ref[...]).astype(BF16)

    def total(a_cols, b_ref, into, i):
        return tn(a_cols(i * f, f), b_ref[...]) + into[pl.ds(i * f, f), :].astype(F32)

    compute_away(c_cols, act, away_d, 1)
    folds_d = fold(away_d, fold_d, 1)
    folds_g = {}
    compute_away(c_cols, act, away_d, 3)

    def back_partial(k):
        def step(m):
            at = pl.ds(pl.multiple_of((k * 2 + m) * 256, 256), 256)
            value = nt(dg[at, :], wg[...]) + nt(du[at, :], wu[...])
            p[k, m] = value.astype(BF16).reshape(p.shape[2:])

        loop(2, step)
        if k == 1:
            folds_d.update(fold(away_d, fold_d, 3))

    def settle_d(i, target, dst):
        folds_d[i].arrive()
        send_d[pl.ds((i - 1) * f, f), :] = total(c_cols, act, fold_d, i).astype(BF16)
        to(target, rows(send_d, i - 1), dst)

    def while_back(stage):
        if stage == 0:
            compute_away(c_cols, act, away_d, 0, 2)
        if stage == 1:
            settle_d(1, links.batch, got_d_b_ref)
            folds_d.update(fold(away_d, fold_d, 2, 0))
            settle_d(3, links.both, rows(got_d_o_ref, 1))
            compute_away(xm_cols, dg, away_g, 1, 3)
            folds_g.update(fold(away_g, fold_g, 1))
        if stage == 2:
            compute_away(xm_cols, dg, away_g, 0, 2)
            folds_g.update(fold(away_g, fold_g, 3))
            load(away_g, away_g_ref)

    sum_in(links, bufs, chunk, back_partial, while_back)
    for m in range(2):
        middle = middle_ref[m]
        grad = cot_ref[m].astype(F32) + norm_grad(hold[m], middle, gain_ref[...], gain_grad_ref, m)
        dmid_ref[m] = grad
        xm_s[m] = grad.astype(BF16)

    def while_mid(stage):
        if stage == 0:
            folds_d[0].arrive()
            own_d[...] = total(c_cols, act, fold_d, 0)
            load(own_d, own_d_ref)
        if stage == 1:
            settle_d(2, links.across, rows(got_d_o_ref, 0))
            folds_g[1].arrive()
            send_g[pl.ds(0, f), :] = total(xm_cols, dg, fold_g, 1).astype(BF16)
            to(links.batch, rows(send_g, 0), got_g_b_ref)
            keep_g[pl.ds(0, f), :] = tn(xm_cols(0, f), dg[...])
            keep_g[pl.ds(f, f), :] = tn(xm_cols(2 * f, f), dg[...])
            load(keep_g, keep_g_ref)

            def step(i):
                at = pl.ds(pl.multiple_of(i * 512, 512), 512)
                dact[at, :] = tn(xm_cols(pl.multiple_of(i * 512, 512), 512), du[...])

            loop(2, step)
            load(dact, keep_u_ref)
            for copy in folds_d.values():
                copy.sent()
            compute_away(xm_cols, du, away_d, 0, 1, 2, 3)
            load(away_d, away_u_ref)

            def step(i):
                at = pl.ds(pl.multiple_of(i * 256, 256), 256)
                p[i // 2, i % 2] = nt(act[at, :], wd[...]).astype(BF16).reshape(p.shape[2:])

            loop(4, step)
            load(p, mixed_ref)
        if stage == 2:
            folds_g[3].arrive()
            send_g[pl.ds(f, f), :] = total(xm_cols, dg, fold_g, 3).astype(BF16)
            load(rows(send_g, 1), send_g_ref)

    spread_in(links, xm_s, dall_ref, chunk, while_mid, in_vmem=False)
    links.finish()


def middle_call(batch_mask, low, cot, gain, attn, w_out, cot_all, w_down, w_gate, params, collective_id):
    _, rows, width = low.shape
    tokens, columns = attn.shape
    ff = w_down.shape[1]
    f = w_down.shape[0] // 8
    share, full = (2, rows, width), (2, 2, 2, 2, rows, width)
    vmem, hbm = pl.BlockSpec(memory_space=pltpu.VMEM), pl.BlockSpec(memory_space=pltpu.HBM)
    like = jax.ShapeDtypeStruct
    return pl.pallas_call(
        functools.partial(middle_kernel, batch_mask=batch_mask, chunk=2 * width // 8),
        in_specs=[vmem] * 3 + [hbm] * 8,
        out_specs=[vmem] * 3 + [hbm] * 11,
        out_shape=[
            like(share, F32),
            like(share, F32),
            like((1, width), F32),
            like(full, BF16),
            like(full, BF16),
            like((f, ff), F32),
            like((f, ff), BF16),
            like((2 * f, ff), BF16),
            like((f, ff), BF16),
            like((f, ff), BF16),
            like((2 * f, ff), F32),
            like((4 * f, ff), BF16),
            like((4 * f, ff), F32),
            like((4 * f, ff), BF16),
        ],
        scratch_shapes=[
            pltpu.VMEM((tokens, columns), BF16),
            pltpu.VMEM((width, columns), BF16),
            pltpu.VMEM(full, BF16),
            pltpu.VMEM((4, *share), BF16),
            pltpu.VMEM((2, *share), BF16),
            pltpu.VMEM((2, *share), BF16),
            pltpu.VMEM(share, BF16),
            pltpu.VMEM(share, BF16),
            pltpu.VMEM(share, F32),
            pltpu.VMEM(share, BF16),
            pltpu.VMEM(full, BF16),
            pltpu.VMEM((tokens, width), BF16),
            *[pltpu.VMEM((width, ff), BF16)] * 3,
            *[pltpu.VMEM((tokens, ff), F32)] * 2,
            *[pltpu.VMEM((tokens, ff), BF16)] * 3,
            *[pltpu.VMEM((4 * f, ff), BF16)] * 4,
            pltpu.VMEM((f, ff), F32),
            pltpu.VMEM((3 * f, ff), BF16),
            pltpu.VMEM((2 * f, ff), F32),
            pltpu.VMEM((2 * f, ff), BF16),
            pltpu.VMEM((256, ff), F32),
            pltpu.SemaphoreType.DMA((96,)),
            pltpu.SemaphoreType.DMA((96,)),
        ],
        compiler_params=pltpu.CompilerParams(
            collective_id=collective_id, has_side_effects=True, vmem_limit_bytes=60 * MIB
        ),
        cost_estimate=TINY_COST,
    )(low, cot, gain, attn, w_out, cot_all, w_down, w_gate, *params)


def block_of(n, batch_mask):
    blk = lax.axis_index("blk")
    return blk ^ ((n // 2) * batch_mask) ^ ((n % 2) << TENSOR_BIT)


def key_tokens(block, half):
    head = lax.axis_index("head")
    index = lax.broadcasted_iota(jnp.int32, (2 * half, 1), 0)
    return token_offset(head, index, half // 2) + block * (2 * half)


def query_tokens(block, half, lanes):
    head = lax.axis_index("head")
    index = lax.broadcasted_iota(jnp.int32, (1, lanes), 1) % (2 * half)
    return token_offset(head, index, half // 2) + block * (2 * half)


def head_rows(ref, i, heads, width):
    both = [ref[c, i] for c in range(2)]
    return jnp.concatenate([b[:, h * width : (h + 1) * width] for h in range(heads) for b in both], axis=0)


def attention_back(q, do, k, v, start, ot, l, dq, dk, dv, kt, acc, batch_mask, scaling):
    parts, _, blocks, half, width = k.shape
    heads = q.shape[-1] // width
    lanes = heads * 2 * half
    dk[...] = jnp.zeros_like(dk)
    dv[...] = jnp.zeros_like(dv)

    def turn(kb):
        kt[kb] = key_rows(k, kb // blocks, kb % blocks).T

    loop(parts * blocks, turn)

    def per_query(i):
        q_rows, do_rows = head_rows(q, i, heads, width), head_rows(do, i, heads, width)
        delta = jnp.sum(do_rows.astype(F32).T * ot[i], axis=0, keepdims=True)
        inverse, first = 1.0 / l[i], start[i]
        acc[...] = jnp.zeros_like(acc)
        q_block = block_of(i, batch_mask)

        def per_key(kb):
            part, block = kb // blocks, kb % blocks
            k_block = block_of(block, batch_mask) ^ (part << SEQ_BIT)

            def add(diagonal):
                tokens = key_tokens(k_block, half)
                allowed = tokens >= first
                if diagonal:
                    allowed = allowed & (tokens <= query_tokens(q_block, half, lanes))
                score = nt(key_rows(k, part, block), q_rows) * (scaling * LOG2E)
                prob = jnp.where(allowed, jnp.exp2(score), 0.0) * inverse
                d_prob = nt(key_rows(v, part, block), do_rows)
                d_score = (prob * (d_prob - delta)).astype(BF16)
                d_v, d_k = nn(prob.astype(BF16), do_rows), nn(d_score, q_rows) * scaling
                for c in range(2):
                    dv[part, c, block] += d_v[c * half : (c + 1) * half]
                    dk[part, c, block] += d_k[c * half : (c + 1) * half]
                acc[...] += nn(kt[kb], d_score)

            @pl.when(k_block < q_block)
            def _():
                add(False)

            @pl.when(k_block == q_block)
            def _():
                add(True)

        loop(parts * blocks, per_key)
        rows = acc[...].T * scaling
        for h in range(heads):
            for c in range(2):
                at = (h * 2 + c) * half
                dq[c, i, :, h * width : (h + 1) * width] = rows[at : at + half]

    loop(blocks, per_query)


def last_kernel(
    low_ref, middle_ref, dmid_ref, gain_ref, gain_m_grad_ref, gain_q_ref, gain_k_ref, start_ref, l_ref,
    dall_ref, wo_ref, attn_ref, q_ref, k_ref, v_ref, ot_ref, raw_ref, table_ref, wa_ref, xa_ref, mixed_ref,
    send_g_ref, keep_g_ref, away_g_ref, keep_u_ref, away_u_ref,
    mixed_own_ref, mixed_got_ref, input_own_ref, input_got_ref, sums_ref,
    own_g_ref, got_g_o_ref, own_u_ref, got_u_b_ref, got_u_o_ref, own_a_ref, got_a_b_ref, got_a_o_ref, own_o_ref, got_o_b_ref, got_o_o_ref,
    dall, wo, attn, q, do, k, v, ot, raw, table, wa, xa, dq, dk, dv, kt, acc, kv_out, kv_in, d_qkv,
    p, core_in, out_y, in_y, out_t, in_t, hold, m_near, m_core_in, m_in_y, m_in_t,
    swap_m, swap_i, keep_g, fold_g, own_g, send_g, keep_u, fold_u, own_u, send_u, away_o, fold_o, own_o, send_o, away_a, fold_a, own_a, send_a,
    gains_qk, gain_a_grad, ring_out, ring_in, send, recv, *, batch_mask, bit_order, scaling, chunk,
):
    links = Links(send, recv, batch_mask)
    to, load = links.to, links.load
    f = own_u.shape[0]
    heads = q.shape[-1] // k.shape[-1]
    width = k.shape[-1]

    def rows(ref, i):
        return ref.at[pl.ds(i * f, f), :]

    first = [load(dall_ref, dall), load(wo_ref, wo), load(attn_ref, attn)]
    second = [load(a, b) for a, b in ((q_ref, q), (k_ref, k), (v_ref, v), (ot_ref, ot))]
    third = [load(a, b) for a, b in ((raw_ref, raw), (table_ref, table), (wa_ref, wa), (xa_ref, xa))]
    mixed_near, keep_load, keep_g_load = load(mixed_ref.at[0], m_near.at[0]), load(keep_u_ref, keep_u), load(keep_g_ref, keep_g)
    links.greet()

    def settle(src, dst_b, dst_o):
        to(links.batch, rows(src, 0), dst_b)
        to(links.both, rows(src, 2), rows(dst_o, 1))
        to(links.across, rows(src, 1), rows(dst_o, 0))

    to(links.both, send_g_ref, rows(got_g_o_ref, 1))
    folds_u = {i: to(links.seq, rows(away_u_ref, i), rows(fold_u, i)) for i in (1, 3)}
    folds_g = {i: to(links.seq, rows(away_g_ref, i), rows(fold_g, i // 2)) for i in (0, 2)}
    for copy in (*first, *second):
        copy.arrive()

    def total_u(i):
        return keep_u[pl.ds(i * f, f), :] + fold_u[pl.ds(i * f, f), :].astype(F32)

    def settle_u(i, target, dst):
        folds_u[i].arrive()
        send_u[pl.ds((i - 1) * f, f), :] = total_u(i).astype(BF16)
        to(target, rows(send_u, i - 1), dst)

    def d_attn(i):
        at = pl.ds(pl.multiple_of(i * 256, 256), 256)
        value = nn(dall[at, :], wo[...]).astype(BF16)
        do[i // 2, pl.ds((i % 2) * 2, 2)] = value.reshape(2, 128, value.shape[1])

    def dall_cols(at, n):
        return dall[:, pl.ds(at, n)]

    def xa_cols(at, n):
        return xa[:, pl.ds(at, n)]

    folds = []

    def while_mixed(stage):
        if stage == 0:
            loop(4, d_attn)
            attention_back(q, do, k, v, start_ref, ot, l_ref, dq, dk, dv, kt, acc, batch_mask, scaling)
            kv_out[:, :width] = dk[1].reshape(-1, width).astype(BF16)
            kv_out[:, width:] = dv[1].reshape(-1, width).astype(BF16)
            folds.extend(to(links.seq, kv_out.at[pl.ds(i, 128), :], kv_in.at[pl.ds(i, 128), :]) for i in range(0, kv_out.shape[0], 128))
            keep_load.arrive()
            settle_u(1, links.batch, got_u_b_ref)
            settle_u(3, links.both, rows(got_u_o_ref, 1))
            away_rows(dall_cols, attn, away_o)
        if stage == 1:
            for copy in folds:
                copy.arrive()
            folds[:] = [to(links.seq, away_o, fold_o)]

    mixed_near.arrive()
    sum_in(links, (m_near, m_core_in, out_y, m_in_y, out_t, m_in_t, hold), chunk, None, while_mixed, mixed_ref.at[1])
    blk = lax.axis_index("blk")
    store_ungrouped(middle_ref[0] + hold[0], mixed_own_ref, blk, bit_order)
    store_ungrouped(middle_ref[1] + hold[1], swap_m, blk, bit_order)
    to(links.batch, swap_m, mixed_got_ref)

    for copy in third:
        copy.arrive()
    gains_qk[...] = jnp.zeros_like(gains_qk)

    def input_partial(c):
        def step(m):
            at = pl.ds(pl.multiple_of((c * 2 + m) * 256, 256), 256)
            pair = pl.ds(m * 2, 2)
            got = kv_in[at, :].astype(F32)
            cos, sin = table[at, : width // 2], table[at, width // 2 :]
            cos, sin = jnp.concatenate([cos, cos], axis=1), jnp.concatenate([-sin, sin], axis=1)
            for h in range(heads + 1):
                cut = slice(h * width, (h + 1) * width)
                if h < heads:
                    grad = dq[c, pair, :, cut].reshape(256, width)
                else:
                    grad = dk[0, c, pair].reshape(256, width) + got[:, :width]
                gain = (gain_q_ref if h < heads else gain_k_ref)[...]
                values = raw[at, cut]
                inverse = inverse_rms(values)
                normed = values * inverse
                turned = grad * cos - pltpu.roll(grad, width // 2, 1) * sin
                row = 0 if h < heads else 1
                gains_qk[row : row + 1, :] += jnp.sum(turned * normed, axis=0, keepdims=True)
                scaled = turned * gain
                mean = jnp.mean(scaled * normed, axis=-1, keepdims=True)
                d_qkv[at, cut] = (inverse * (scaled - normed * mean)).astype(BF16)
            d_qkv[at, (heads + 1) * width :] = (dv[0, c, pair].reshape(256, width) + got[:, width:]).astype(BF16)
            p[c, m] = nt(d_qkv[at, :], wa[...]).astype(BF16).reshape(p.shape[2:])

        loop(2, step)

    def while_input(stage):
        if stage == 0:
            away_rows(xa_cols, d_qkv, away_a)
            folds.extend(to(links.seq, rows(away_a, i), rows(fold_a, i)) for i in (1, 3, 0, 2))
            folds[0].arrive()
            keep_rows(dall_cols, attn, fold_o, own_o, send_o)
            settle(send_o, got_o_b_ref, got_o_o_ref)
            load(own_o, own_o_ref)
        if stage == 1:
            folds_u.update({i: to(links.seq, rows(away_u_ref, i), rows(fold_u, i)) for i in (2, 0)})
            for copy in (*folds_g.values(), keep_g_load):
                copy.arrive()
            for i, ref in ((0, own_g), (1, send_g)):
                here = pl.ds(i * f, f)
                ref[...] = (keep_g[here, :] + fold_g[here, :].astype(F32)).astype(ref.dtype)
            load(own_g, own_g_ref)
            to(links.across, send_g, rows(got_g_o_ref, 0))
        if stage == 2:
            for copy in folds:
                copy.arrive()
            keep_rows(xa_cols, d_qkv, fold_a, own_a, send_a)
            settle(send_a, got_a_b_ref, got_a_o_ref)
            load(own_a, own_a_ref)
            settle_u(2, links.across, rows(got_u_o_ref, 0))
            folds_u[0].arrive()
            own_u[...] = total_u(0)
            load(own_u, own_u_ref)

    sum_in(links, (p, core_in, out_y, in_y, out_t, in_t, hold), chunk, input_partial, while_input)
    for m in range(2):
        grad = dmid_ref[m] + norm_grad(hold[m], low_ref[m].astype(F32), gain_ref[...], gain_a_grad, m)
        store_ungrouped(grad, input_own_ref if m == 0 else swap_i, blk, bit_order)
    to(links.batch, swap_i, input_got_ref)
    n = gain_a_grad.shape[1]
    store_ungrouped(gain_a_grad[...], sums_ref.at[:, pl.ds(0, n)], blk, bit_order)
    sums_ref[:, n : n + width] = gains_qk[0:1, :]
    sums_ref[:, n + width : n + 2 * width] = gains_qk[1:2, :]
    store_ungrouped(gain_m_grad_ref[...], sums_ref.at[:, pl.ds(n + 2 * width, n)], blk, bit_order)
    for i, target in enumerate((links.core, links.near, links.seq, links.across, links.batch)):
        ring_out[i] = sums_ref[...]
        to(target, ring_out.at[i], ring_in.at[i]).arrive()
        sums_ref[...] += ring_in[i]
    links.finish()


def last_call(batch_mask, bit_order, scaling, arrays, collective_id):
    low, dall, attn, q, k, raw, wa, away_u = (arrays[n] for n in ("low", "dall", "attn", "q", "k", "raw", "wa", "away_u"))
    _, rows, width = low.shape
    tokens, columns = attn.shape
    head_size = k.shape[-1]
    ff, f = away_u.shape[1], away_u.shape[0] // 4
    n_a = wa.shape[1]
    share, full, half_full = (2, rows, width), (2, 2, 2, 2, rows, width), (1, 2, 2, 2, rows, width)
    vmem, hbm = pl.BlockSpec(memory_space=pltpu.VMEM), pl.BlockSpec(memory_space=pltpu.HBM)
    like, held = jax.ShapeDtypeStruct, pltpu.VMEM
    in_vmem = ("low", "middle", "d_middle", "gain", "gain_m_grad", "gain_q", "gain_k", "start", "l")
    in_hbm = (
        "dall", "w_out", "attn", "q", "k", "v", "ot", "raw", "table", "wa", "xa", "mixed", "send_g", "keep_g", "away_g", "keep_u",
        "away_u",
    )
    total = 2 * width + 2 * head_size
    lanes = 2 * 2 * 128
    sums = (1, total)
    own_and_send = lambda n: [held((f, n), F32), held((3 * f, n), BF16)]
    sum_bufs = [
        held((4, *share), BF16), held((2, *share), BF16), held((2, *share), BF16), held(share, BF16), held(share, BF16),
    ]
    return pl.pallas_call(
        functools.partial(last_kernel, batch_mask=batch_mask, bit_order=bit_order, scaling=scaling, chunk=2 * width // 8),
        in_specs=[vmem] * len(in_vmem) + [hbm] * len(in_hbm),
        out_specs=[vmem, hbm, vmem, hbm, vmem] + [hbm] * 11,
        out_shape=[
            like((rows, width), BF16),
            like((rows, width), BF16),
            like((rows, width), F32),
            like((rows, width), BF16),
            like(sums, F32),
            like((f, ff), F32),
            like((2 * f, ff), BF16),
            *[
                like((m * f, n), dtype)
                for n in (ff, n_a, columns)
                for m, dtype in ((1, F32), (1, BF16), (2, BF16))
            ],
        ],
        scratch_shapes=[
            held((tokens, width), BF16),
            held((width, columns), BF16),
            held((tokens, columns), BF16),
            held(q.shape, BF16),
            held(q.shape, BF16),
            held(k.shape, BF16),
            held(k.shape, BF16),
            held((4, head_size, lanes), F32),
            held(raw.shape, F32),
            held((tokens, head_size), F32),
            held(wa.shape, BF16),
            held((tokens, width), BF16),
            held(q.shape, F32),
            held(k.shape, F32),
            held(k.shape, F32),
            held((8, head_size, 256), BF16),
            held((head_size, lanes), F32),
            held((tokens, 2 * head_size), BF16),
            held((tokens, 2 * head_size), BF16),
            held((tokens, n_a), BF16),
            held(full, BF16),
            *sum_bufs,
            held(share, F32),
            held(half_full, BF16),
            *[sum_bufs[i] for i in (0, 2, 4)],
            held((rows, width), BF16),
            held((rows, width), BF16),
            held((2 * f, ff), F32),
            held((2 * f, ff), BF16),
            held((f, ff), F32),
            held((f, ff), BF16),
            held((4 * f, ff), F32),
            held((4 * f, ff), BF16),
            *own_and_send(ff),
            held((4 * f, columns), BF16),
            held((4 * f, columns), BF16),
            *own_and_send(columns),
            held((4 * f, n_a), BF16),
            held((4 * f, n_a), BF16),
            *own_and_send(n_a),
            held((8, head_size), F32),
            held((1, width), F32),
            held((5, *sums), F32),
            held((5, *sums), F32),
            pltpu.SemaphoreType.DMA((96,)),
            pltpu.SemaphoreType.DMA((96,)),
        ],
        compiler_params=pltpu.CompilerParams(
            collective_id=collective_id, has_side_effects=True, vmem_limit_bytes=60 * MIB
        ),
        cost_estimate=TINY_COST,
    )(*[arrays[n] for n in (*in_vmem, *in_hbm)])


def attention(q, k, v, start, out, ot, total_ref, vt, acc, total, batch_mask, scaling):
    parts, _, blocks, half, width = k.shape
    heads = q.shape[-1] // width
    lanes = heads * 2 * half

    def turn(kb):
        vt[kb] = key_rows(v, kb // blocks, kb % blocks).T

    loop(parts * blocks, turn)

    def per_query(i):
        q_rows = head_rows(q, i, heads, width)
        first = start[i]
        acc[...] = jnp.zeros_like(acc)
        total[...] = jnp.zeros_like(total)
        q_block = block_of(i, batch_mask)

        def per_key(kb):
            part, block = kb // blocks, kb % blocks
            k_block = block_of(block, batch_mask) ^ (part << SEQ_BIT)

            def add(diagonal):
                tokens = key_tokens(k_block, half)
                allowed = tokens >= first
                if diagonal:
                    allowed = allowed & (tokens <= query_tokens(q_block, half, lanes))
                score = nt(key_rows(k, part, block), q_rows) * (scaling * LOG2E)
                e = jnp.where(allowed, jnp.exp2(score), 0.0)
                total[...] += jnp.sum(e, axis=0, keepdims=True)
                acc[...] += nn(vt[kb], e.astype(BF16))

            @pl.when(k_block < q_block)
            def _():
                add(False)

            @pl.when(k_block == q_block)
            def _():
                add(True)

        loop(parts * blocks, per_key)
        value = acc[...] / total[...]
        ot[i] = value
        total_ref[i] = total[...]
        rows = value.T
        for h in range(heads):
            for c in range(2):
                at = (h * 2 + c) * half
                out[c, i, :, h * width : (h + 1) * width] = rows[at : at + half].astype(BF16)

    loop(blocks, per_query)


def first_kernel(
    gains_ref, gain_q_ref, gain_k_ref, table_ref, start_ref,
    hid_ref, cot_ref, wq_ref, wk_ref, wv_ref, wo_ref, wd_ref, wg_ref,
    low_ref, cot_low_ref, gains_out_ref, l_ref,
    xa_ref, call_ref, wa_out, wo_out, wd_out, wg_out, q_ref, k_ref, v_ref, raw_ref, attn_ref, ot_ref,
    x_in, c_in, xa_s, xa, wa, wb, q, k, v, raw, out, ot, vt, acc, total, send, recv, *, batch_mask, bit_order, scaling, chunk,
):
    links = Links(send, recv, batch_mask)
    to, load = links.to, links.load
    blk = lax.axis_index("blk")
    batch = bit_of(blk, bit_order[0])
    width = k.shape[-1]
    heads = q.shape[-1] // width
    f = wa.shape[0] // 8
    a_params, at = [], 0
    for ref in (wq_ref, wk_ref, wv_ref):
        n = ref.shape[1] // 2
        a_params.append((ref, at, n))
        at += n

    def rows(ref, i):
        return ref.at[pl.ds(i * f, f), :]

    x_own = load(hid_ref.at[batch], x_in.at[0])
    c_own = load(cot_ref.at[batch], c_in.at[0])
    a_own = [load(links.half(ref, 0), wa.at[pl.ds(0, f), pl.ds(start, n)]) for ref, start, n in a_params]
    a_other = [load(links.half(ref, 1), wb.at[:, pl.ds(start, n)]) for ref, start, n in a_params]
    links.greet()
    x_far = to(links.batch, hid_ref.at[1 - batch], x_in.at[1])
    for copy in (*a_own, *a_other):
        copy.arrive()
    a_t = to(links.across, wb, rows(wa, 2))
    a_rest = [to(links.seq, rows(wa, 0), rows(wa, 4))]
    to(links.seq, links.half(wo_ref, 0), rows(wo_out, 4))
    load(links.half(wo_ref, 0), rows(wo_out, 0))
    to(links.seq, links.half(wd_ref, 0), rows(wd_out, 4))
    to(links.seq, links.half(wg_ref, 0), rows(wg_out, 4))
    down_t = to(links.across, links.half(wd_ref, 1), rows(wd_out, 2))
    out_rows = [to(links.across, links.half(wo_ref, 1), rows(wo_out, 2))]
    n_blocks = 1 << len(bit_order)
    n = x_in.shape[-1] // n_blocks

    def regroup(src, dst, lead):
        for p in range(n_blocks):
            cut = pl.ds(pl.multiple_of(place_of_block(blk, bit_order, p) * n, n), n)
            dst[(*lead, pl.ds(p * n, n))] = src[(*lead, cut)]

    all_rows = (slice(None), slice(None))
    regroup(gains_ref, gains_out_ref, (slice(None),))
    x_own.arrive()
    x_far.arrive()
    a_far = {1: to(links.batch, rows(wa, 0), rows(wa, 1)), 3: to(links.both, wb, rows(wa, 3))}
    c_far = to(links.batch, cot_ref.at[1 - batch], c_in.at[1])
    to(links.batch, links.half(wd_ref, 0), rows(wd_out, 1))
    regroup(x_in, low_ref, all_rows)
    for m in range(2):
        value = low_ref[m].astype(F32)
        xa_s[m] = (value * inverse_rms(value) * gains_out_ref[0:1, :]).astype(BF16)

    def while_xa(stage):
        if stage == 0:
            a_t.arrive()
            a_rest.append(to(links.seq, rows(wa, 2), rows(wa, 6)))
        if stage == 1:
            for i, copy in a_far.items():
                copy.arrive()
                a_rest.append(to(links.seq, rows(wa, i), rows(wa, i + 4)))
            out_rows.append(to(links.batch, links.half(wo_ref, 0), rows(wo_out, 1)))
            out_rows.append(to(links.both, links.half(wo_ref, 1), rows(wo_out, 3)))
            to(links.both, links.half(wd_ref, 1), rows(wd_out, 3))
            c_own.arrive()
            c_far.arrive()
            regroup(c_in, cot_low_ref, all_rows)

    spread_in(links, xa_s, xa, chunk, while_xa)
    load(xa, xa_ref)

    def prepare_rows(i):
        c, m = i // 2, i % 2
        pair = pl.ds(m * 2, 2)
        at = pl.ds(pl.multiple_of(i * 256, 256), 256)
        acc_rows = nn(rows_of(xa, i), wa[...])
        raw[at, :] = acc_rows[:, : (heads + 1) * width]
        cos, sin = table_ref[at, : width // 2], table_ref[at, width // 2 :]
        cos, sin = jnp.concatenate([cos, cos], axis=1), jnp.concatenate([-sin, sin], axis=1)
        for h in range(heads + 1):
            part = acc_rows[:, h * width : (h + 1) * width]
            scaled = part * inverse_rms(part) * (gain_q_ref if h < heads else gain_k_ref)[...]
            turned = (scaled * cos + pltpu.roll(scaled, width // 2, 1) * sin).astype(BF16).reshape(2, 128, width)
            if h < heads:
                q[c, pair, :, h * width : (h + 1) * width] = turned
            else:
                k[0, c, pair] = turned
        v[0, c, pair] = acc_rows[:, (heads + 1) * width :].astype(BF16).reshape(2, 128, width)

    kv = []

    def while_cot(stage):
        if stage == 0:
            for copy in a_rest:
                copy.arrive()
            loop(4, prepare_rows)
            kv.extend(
                to(links.seq, ref.at[0, c, i], ref.at[1, c, i]) for ref in (k, v) for c in range(2) for i in range(4)
            )
            load(wa, wa_out)
            load(raw, raw_ref)
            load(q, q_ref)
            down_t.arrive()
            to(links.seq, rows(wd_out, 2), rows(wd_out, 6))
        if stage == 1:
            to(links.across, links.half(wg_ref, 1), rows(wg_out, 2))
            for i, copy in zip((2, 1, 3), out_rows):
                copy.arrive()
                to(links.seq, rows(wo_out, i), rows(wo_out, i + 4))
            for copy in kv:
                copy.arrive()
            load(k, k_ref)
            load(v, v_ref)
            attention(q, k, v, start_ref, out, ot, l_ref, vt, acc, total, batch_mask, scaling)
            load(out, attn_ref)
            load(ot, ot_ref)

    spread_in(links, cot_low_ref, call_ref, chunk, while_cot, in_vmem=False)
    links.finish()


def first_call(batch_mask, bit_order, scaling, arrays, collective_id):
    hid, wq, wk, wv, wo, wd, wg = (arrays[n] for n in ("hidden", "wq", "wk", "wv", "wo", "wd", "wg"))
    _, rows, width = hid.shape
    tokens, head_size = 16 * rows, arrays["gain_q"].shape[1]
    columns, n_a = wq.shape[1] // 2, (wq.shape[1] + wk.shape[1] + wv.shape[1]) // 2
    heads = columns // head_size
    half, lanes = tokens // 8, heads * tokens // 4
    share, full = (2, rows, width), (2, 2, 2, 2, rows, width)
    vmem, hbm = pl.BlockSpec(memory_space=pltpu.VMEM), pl.BlockSpec(memory_space=pltpu.HBM)
    like, held = jax.ShapeDtypeStruct, pltpu.VMEM
    in_vmem = ("gains", "gain_q", "gain_k", "table", "start")
    in_hbm = ("hidden", "cotangent", "wq", "wk", "wv", "wo", "wd", "wg")
    q_shape, k_shape = (2, 4, half, columns), (2, 2, 4, half, head_size)
    ot_shape, raw_shape = (4, head_size, lanes), (tokens, (heads + 1) * head_size)
    return pl.pallas_call(
        functools.partial(first_kernel, batch_mask=batch_mask, bit_order=bit_order, scaling=scaling, chunk=2 * width // 8),
        in_specs=[vmem] * len(in_vmem) + [hbm] * len(in_hbm),
        out_specs=[vmem] * 4 + [hbm] * 12,
        out_shape=[
            like(share, BF16),
            like(share, BF16),
            like((2, width), F32),
            like((4, 1, lanes), F32),
            like(full, BF16),
            like(full, BF16),
            like((width, n_a), BF16),
            like((width, columns), BF16),
            like((width, wd.shape[1] // 2), BF16),
            like((width, wg.shape[1] // 2), BF16),
            like(q_shape, BF16),
            like(k_shape, BF16),
            like(k_shape, BF16),
            like(raw_shape, F32),
            like(q_shape, BF16),
            like(ot_shape, F32),
        ],
        scratch_shapes=[
            held(share, BF16),
            held(share, BF16),
            held(share, BF16),
            held(full, BF16),
            held((width, n_a), BF16),
            held((width // 8, n_a), BF16),
            held(q_shape, BF16),
            held(k_shape, BF16),
            held(k_shape, BF16),
            held(raw_shape, F32),
            held(q_shape, BF16),
            held(ot_shape, F32),
            held((8, head_size, 2 * half), BF16),
            held((head_size, lanes), F32),
            held((1, lanes), F32),
            pltpu.SemaphoreType.DMA((96,)),
            pltpu.SemaphoreType.DMA((96,)),
        ],
        compiler_params=pltpu.CompilerParams(
            collective_id=collective_id, has_side_effects=True, vmem_limit_bytes=56 * MIB
        ),
        cost_estimate=TINY_COST,
    )(*[arrays[n] for n in (*in_vmem, *in_hbm)])


def finish_kernel(place_ref, mixed_own, mixed_got, input_own, input_got, *refs, sources, widths):
    ins, (mixed_ref, input_ref, *outs) = refs[: 3 * sources], refs[3 * sources :]
    place, batch, k = place_ref[0], place_ref[1], 0
    mixed_ref[batch] = mixed_own[...]
    mixed_ref[1 - batch] = mixed_got[...]
    input_ref[batch] = input_own[...]
    input_ref[1 - batch] = input_got[...].astype(F32)
    for own, by_batch, by_other in zip(ins[::3], ins[1::3], ins[2::3]):
        at = 0
        while at < own.shape[1]:
            w, cut = widths[k], slice(at, at + widths[k])
            mine = pl.ds(pl.multiple_of(place * w, w), w)
            theirs = pl.ds(pl.multiple_of((1 - place) * w, w), w)
            outs[k][:, mine] = own[:, cut] + by_batch[:, cut].astype(F32)
            outs[k][:, theirs] = by_other[0, :, cut].astype(F32) + by_other[1, :, cut].astype(F32)
            at += w
            k += 1


def finish_call(places, rows, sources, widths):
    steps = 4
    f, (n_rows, width) = sources[0][0].shape[0], rows[0].shape
    tile, row_tile = f // steps, n_rows // steps
    by_rows = lambda t, n: pl.BlockSpec((t, n), lambda i: (i, 0))
    by_pairs = lambda t, n: pl.BlockSpec((2, t, n), lambda i: (0, i, 0))
    flat, specs = [], []
    for own, by_batch, by_other in sources:
        n = own.shape[1]
        flat += [own, by_batch, by_other.reshape(2, f, n)]
        specs += [by_rows(tile, n), by_rows(tile, n), by_pairs(tile, n)]
    like = jax.ShapeDtypeStruct
    return pl.pallas_call(
        functools.partial(finish_kernel, sources=len(sources), widths=widths),
        grid=(steps,),
        in_specs=[pl.BlockSpec(memory_space=pltpu.SMEM), *[by_rows(row_tile, width)] * 4, *specs],
        out_specs=[*[by_pairs(row_tile, width)] * 2, *[by_rows(tile, 2 * w) for w in widths]],
        out_shape=[
            like((2, n_rows, width), BF16),
            like((2, n_rows, width), F32),
            *[like((f, 2 * w), F32) for w in widths],
        ],
        compiler_params=pltpu.CompilerParams(vmem_limit_bytes=60 * MIB),
        cost_estimate=TINY_COST,
    )(places.astype(jnp.int32), *rows, *flat)


def local(
    hidden_in,
    lengths,
    query_weight,
    key_matrix,
    value_matrix,
    out_weight,
    gate_weight,
    up_weight,
    down_weight,
    attn_gain,
    query_gain,
    key_gain,
    mlp_gain,
    cotangent,
):
    ring = lax.axis_size("blk")
    bits = ring.bit_length() - 1
    batch_bit = bits - 1
    extra_bits = [i for i in range(bits) if i not in (TENSOR_BIT, SEQ_BIT, batch_bit)]
    seq_bits = [SEQ_BIT, *extra_bits]
    parts = 1 << len(seq_bits)
    bit_order = [batch_bit, TENSOR_BIT, SEQ_BIT, *extra_bits]
    b_mask, t_mask, x_mask = 1 << batch_bit, 1 << TENSOR_BIT, 1 << SEQ_BIT
    blk, head = lax.axis_index("blk"), lax.axis_index("head")
    batch, tensor = bit_of(blk, batch_bit), bit_of(blk, TENSOR_BIT)

    local_rows, width = hidden_in.shape[1:]
    block_rows = local_rows * lax.axis_size("head")
    half = block_rows // 2
    row_features = width // ring
    head_size = query_gain.shape[0]
    scaling = head_size ** (-0.5)
    tokens = 16 * local_rows
    heads = query_weight.shape[1] // (2 * head_size)
    ff = gate_weight.shape[1] // 2

    def moved(values, place_of):
        axis = values.ndim - 1
        return jnp.concatenate(
            [
                lax.dynamic_slice_in_dim(values, place_of(i) * row_features, row_features, axis)
                for i in range(ring)
            ],
            axis=axis,
        )

    def regroup(values):
        return moved(values, lambda p: blk ^ sum(((p >> i) & 1) << b for i, b in enumerate(bit_order)))

    def ungroup(values):
        return moved(values, lambda n: sum(bit_of(blk ^ n, b) << i for i, b in enumerate(bit_order)))

    def everything(ref):
        return ref

    def mask_of(p):
        return sum(((p >> i) & 1) << b for i, b in enumerate(bit_order))

    def rows_at(p):
        return lambda ref: ref.at[pl.ds(p * row_features, row_features), :]

    def half_cut(n, other):
        def cut(ref):
            place = bit_of(lax.axis_index("blk"), TENSOR_BIT)
            place = 1 - place if other else place
            return ref.at[:, pl.ds(pl.multiple_of(place * n, n), n)]

        return cut

    def send_over(plan, weight, buffer, p, point):
        mask, n = mask_of(p), weight.shape[1] // 2
        plan.copy((plan.read(weight), half_cut(n, mask & t_mask)), (buffer, rows_at(p)), mask, point=point)

    def keep_own(plan, weight, buffer, point, onward=True):
        here, n = plan.read(weight), weight.shape[1] // 2
        if onward:
            plan.copy((here, half_cut(n, 0)), (buffer, rows_at(4)), x_mask, point=point)
        plan.local((here, half_cut(n, 0)), (buffer, rows_at(0)), (row_features, n), point=point)

    def send_on(plan, buffer, places, point, after=None):
        for p in places:
            plan.copy((buffer, rows_at(p)), (buffer, rows_at(p + 4)), x_mask, after=after, point=point)

    def lay(plan, array, buffer, p, point=0, columns=None, onward=False):
        here = plan.read(array)
        cut = (lambda ref: ref.at[:, pl.ds(*columns)]) if columns else everything
        if onward:
            plan.copy((here, cut), (buffer, rows_at(p + 4)), x_mask, point=point)
        plan.local((here, cut), (buffer, rows_at(p)), (row_features, columns[1] if columns else array.shape[1]), point)

    def fresh_for(plan, weights):
        return plan.fresh(buffer_shape(weights), BF16)

    def buffer_shape(weights):
        return (8 * row_features, sum(w.shape[1] for w in weights) // 2)

    def whole_weight(buffer):
        pieces = [buffer]
        for b in extra_bits:
            pieces = pieces + [over_blk(c, 1 << b) for c in pieces]
        return jnp.concatenate(pieces, axis=0) if extra_bits else buffer

    def split_grad(grad):
        for b in reversed(extra_bits):
            n = grad.shape[0] // 2
            grad = grad[:n] + over_blk(grad[n:].astype(BF16), 1 << b).astype(F32)
        n = grad.shape[0] // 2
        return grad[:n], grad[n:].astype(BF16)

    def weight_sum(a, b):
        return split_grad(tn(a, b)) if extra_bits else weight_grad(a, b)

    def fold(plan, source, shape, point=0):
        plan.copy((source, everything), (plan.fresh(shape, BF16), everything), x_mask, point=point)

    def fold_part(plan, source, buffer, start, n, point=0):
        def part(ref):
            return ref.at[:, pl.ds(start, n)]

        plan.copy((source, part), (buffer, part), x_mask, point=point)

    def to_settle(keep, got):
        total = keep + got.astype(F32)
        return total[:row_features], total[row_features:].astype(BF16)

    def settle(plan, away, t_point=0):
        out, here = plan.fresh(away.shape, away.dtype), plan.read(away)
        for i, mask in ((0, b_mask), (2, b_mask | t_mask), (1, t_mask)):
            plan.copy((here, rows_at(i)), (out, rows_at(i)), mask, point=t_point if mask == t_mask else 0)

    def settled(sources, column_widths):
        if all(w % 128 == 0 for w in column_widths):
            return assemble(tensor, sources, column_widths)
        f, results = row_features, []
        widths = iter(column_widths)
        for own, got in sources:
            own = own + got[:f].astype(F32)
            other = got[f : 2 * f].astype(F32) + got[2 * f :].astype(F32)
            at = 0
            while at < own.shape[1]:
                w = next(widths)
                results.append(in_order(tensor, own[:, at : at + w], other[:, at : at + w], 1))
                at += w
        return results

    chunk = 2 * row_features
    ids = iter(range(100))

    def spread(flat, plan, fills=(), limit=None):
        (out,), rest = run(plan, spread_main(flat, chunk), next(ids), fills=fills, limit=limit)
        return out.reshape(tokens, width), rest

    share = (2, local_rows, width)

    def gather_sum(partial, plan, extra, outs_like, finish, fills=()):
        return run(plan, gather_main(partial, chunk, extra, outs_like, finish), next(ids), fills=fills)

    def like(shape, dtype):
        return jax.ShapeDtypeStruct(shape, dtype)

    aligned = row_features % 128 == 0
    local_order = bit_order if aligned else []

    def split_batch(rows):
        mine = lax.dynamic_index_in_dim(rows, batch, 0, keepdims=False)
        theirs = lax.dynamic_index_in_dim(rows, 1 - batch, 0, keepdims=False)
        return mine, theirs

    def natural(rows):
        return rows if aligned else ungroup(rows)

    length_row = lax.dynamic_index_in_dim(lengths, batch, 0, keepdims=False)
    doc_ends = jnp.cumsum(length_row)
    batch_flip = jnp.arange(2, dtype=jnp.int32)[:, None] << batch_bit
    tensor_flip = jnp.arange(2, dtype=jnp.int32)[None, :] << TENSOR_BIT
    q_blocks = (blk ^ batch_flip ^ tensor_flip).reshape(4)
    index = jnp.arange(2 * half, dtype=jnp.int32)
    in_block = token_offset(head, index, local_rows).reshape(2, 1, half)
    token_index = q_blocks[None, :, None] * block_rows + in_block
    passed = doc_ends <= token_index[..., None]
    doc_start = jnp.max(jnp.where(passed, doc_ends, 0), axis=-1).astype(jnp.int32)
    position = (token_index - doc_start).reshape(tokens)
    start_lanes = jnp.tile(jnp.transpose(doc_start, (1, 0, 2)).reshape(4, 1, 2 * half), (1, 1, heads))
    k_blocks = q_blocks
    for b in seq_bits:
        k_blocks = jnp.concatenate([k_blocks, k_blocks ^ (1 << b)])
    least_start = jnp.min(doc_start, axis=(0, 2))[:, None]
    last_start = jnp.max(doc_start, axis=(0, 2))[:, None]
    k_first = (k_blocks * block_rows)[None, :]
    none = (k_blocks[None, :] > q_blocks[:, None]) | (k_first + block_rows <= least_start)
    whole = (k_blocks[None, :] < q_blocks[:, None]) & (k_first >= last_start)
    flags = jnp.where(none, 0, jnp.where(whole, 1, 2))
    meta = jnp.concatenate([head[None], q_blocks, k_blocks, flags.reshape(-1)]).astype(jnp.int32)

    inverse_freq = THETA ** (-jnp.arange(head_size // 2, dtype=F32) / (head_size // 2))
    angles = position.astype(F32)[:, None] * inverse_freq[None, :]
    cosine, sine = jnp.cos(angles), jnp.sin(angles)
    table = jnp.concatenate([cosine, sine], axis=1)
    cosine = jnp.concatenate([cosine, cosine], axis=1)
    sine = jnp.concatenate([-sine, sine], axis=1)

    def rms(values):
        return lax.rsqrt(jnp.mean(values * values, axis=-1, keepdims=True) + EPS)

    def norm_back(grad, normed, inverse, gain):
        scaled = grad * gain
        return inverse * (scaled - normed * jnp.mean(scaled * normed, axis=-1, keepdims=True))

    gains_in = jnp.stack([attn_gain, mlp_gain]).astype(F32)
    gain_q = query_gain.astype(F32)[None]
    gain_k = key_gain.astype(F32)[None]

    q_columns, k_columns = heads * head_size, head_size
    a_weights = (query_weight, key_matrix, value_matrix)

    def halves(weights, which):
        return jnp.concatenate(
            [lax.dynamic_slice_in_dim(w, which * (w.shape[1] // 2), w.shape[1] // 2, 1) for w in weights], axis=1
        )

    if extra_bits:
        mine, theirs = split_batch(hidden_in)
        other = over_blk(theirs, b_mask)
        a_own, a_other = halves(a_weights, tensor), halves(a_weights, 1 - tensor)
        a_by_t = over_blk(a_other, t_mask)
        a_by_b = over_blk(a_own, b_mask)
        early = over_blk(jnp.concatenate([a_own, halves((down_weight,), tensor)], axis=1), x_mask)
        (mine, other, cosine, sine, start_lanes, meta) = pin((mine, other, cosine, sine, start_lanes, meta))
        if aligned:
            x_low, xa, gains_in = enter(blk, bit_order, mine, other, gains_in)
            gain_a, gain_m = gains_in[0], gains_in[1]
        else:
            gains_in = regroup(gains_in)
            gain_a, gain_m = gains_in[0], gains_in[1]
            x_low = regroup(jnp.concatenate([mine, other], axis=0))
            x_wide = x_low.astype(F32)
            xa = (x_wide * rms(x_wide) * gain_a).astype(BF16)

        plan = Plan()
        a_columns = a_own.shape[1]
        w_a = fresh_for(plan, a_weights)
        by_tb = plan.copy((plan.read(a_other), everything), (w_a, rows_at(3)), b_mask | t_mask)
        lay(plan, a_by_t, w_a, 2, onward=True)
        lay(plan, a_by_b, w_a, 1, onward=True)
        lay(plan, a_own, w_a, 0)
        lay(plan, early, w_a, 4, columns=(0, a_columns))
        here, cot_out = plan.read(cotangent), plan.fresh((2, local_rows, width), BF16)
        plan.copy(
            (here, lambda ref: ref.at[1 - bit_of(lax.axis_index("blk"), batch_bit)]),
            (cot_out, lambda ref: ref.at[1]),
            b_mask,
            point=1,
        )
        plan.local(
            (here, lambda ref: ref.at[bit_of(lax.axis_index("blk"), batch_bit)]),
            (cot_out, lambda ref: ref.at[0]),
            (local_rows, width),
        )
        w_out = fresh_for(plan, (out_weight,))
        send_over(plan, out_weight, w_out, 1, 1)
        send_over(plan, out_weight, w_out, 3, 1)
        send_over(plan, out_weight, w_out, 2, 1)
        keep_own(plan, out_weight, w_out, 0)
        w_down = fresh_for(plan, (down_weight,))
        send_over(plan, down_weight, w_down, 2, 1)
        keep_own(plan, down_weight, w_down, 0, onward=False)
        lay(plan, early, w_down, 4, columns=(a_columns, ff))
        w_gate = fresh_for(plan, (gate_weight,))
        keep_own(plan, gate_weight, w_gate, 1)
        send_on(plan, w_a, (3,), 2, after=by_tb)
        xa, (w_qkv, cot, w_out, w_down, w_gate) = spread(xa, plan, limit=56 * MIB)
        w_qkv = whole_weight(w_qkv)
        cot = cot.reshape(2 * local_rows, width)
        cot = enter(blk, bit_order, cot)[0] if aligned else regroup(cot)
        query, key_value, raw = prepare(xa, w_qkv, cosine, sine, gain_q, gain_k, heads)

        plan = Plan()
        kv_out = plan.fresh(key_value.shape, BF16)
        plan.copy((plan.read(key_value), everything), (kv_out, everything), x_mask)
        w_out = plan.through(w_out)
        send_on(plan, w_out, (1, 2, 3), 0)
        w_down = plan.through(w_down)
        send_over(plan, down_weight, w_down, 1, 0)
        send_over(plan, down_weight, w_down, 3, 0)
        send_on(plan, w_down, (2,), 1)
        w_gate = plan.through(w_gate)
        send_over(plan, gate_weight, w_gate, 2, 1)
        cot_all, (kv_x, w_out, w_down, w_gate) = spread(cot, plan)
        w_out = whole_weight(w_out)
        key_value = [key_value, kv_x]
        for b in extra_bits:
            key_value = key_value + [over_blk(c, 1 << b) for c in key_value]
        key_value = jnp.stack(key_value)
        keys = key_value[..., :head_size].reshape(parts, 2, 4, half, head_size)
        values = key_value[..., head_size:].reshape(parts, 2, 4, half, head_size)
        query = query.reshape(2, 4, half, q_columns)
        attn, attn_t, total_e = attend(meta, query, keys, values, start_lanes, scaling)
        attn = attn.reshape(tokens, q_columns)

        x_low = x_low.reshape(share)
    else:
        (
            x_low, cot, gains_group, total_e, xa, cot_all, w_qkv, w_out, w_down, w_gate, query, keys, values, raw, attn, attn_t,
        ) = first_call(
            b_mask,
            bit_order,
            scaling,
            dict(
                gains=gains_in,
                gain_q=gain_q,
                gain_k=gain_k,
                table=table,
                start=start_lanes,
                hidden=hidden_in,
                cotangent=cotangent,
                wq=query_weight,
                wk=key_matrix,
                wv=value_matrix,
                wo=out_weight,
                wd=down_weight,
                wg=gate_weight,
            ),
            next(ids),
        )
        gain_a, gain_m = gains_group[0], gains_group[1]
        xa, cot_all = xa.reshape(tokens, width), cot_all.reshape(tokens, width)
        attn = attn.reshape(tokens, q_columns)

    if extra_bits:
        plan = Plan()
        w_down = plan.through(w_down)
        send_on(plan, w_down, (1, 3), 0)
        w_gate = plan.through(w_gate)
        send_over(plan, gate_weight, w_gate, 1, 0)
        send_over(plan, gate_weight, w_gate, 3, 0)
        send_on(plan, w_gate, (2,), 0)
        w_up = fresh_for(plan, (up_weight,))
        send_over(plan, up_weight, w_up, 2, 0)
        keep_own(plan, up_weight, w_up, 1)
        (middle, xm), (w_down, w_gate, w_up) = gather_sum(
            nt(attn, w_out).astype(BF16),
            plan,
            [x_low, gain_m[None]],
            [like(share, F32), like(share, BF16)],
            finish_middle,
        )
        w_down = whole_weight(w_down)

        plan = Plan()
        w_gate = plan.through(w_gate)
        w_up = plan.through(w_up)
        by_b = len(plan.jobs)
        send_over(plan, up_weight, w_up, 1, 0)
        send_on(plan, w_gate, (1, 3), 0)
        send_on(plan, w_up, (2,), 1)
        by_tb = plan.copy(
            (plan.read(up_weight), half_cut(ff, True)), (w_up, rows_at(3)), b_mask | t_mask, after=by_b, point=2
        )
        send_on(plan, w_up, (1,), 2)
        send_on(plan, w_up, (3,), 3, after=by_tb)
        xm, (w_gate, w_up, d_active) = spread(
            xm.reshape(2 * local_rows, width), plan, [fill_product(cot_all, w_down, 0)]
        )
        w_gate, w_up = whole_weight(w_gate), whole_weight(w_up)
        gate = nn(xm, w_gate)
        up = nn(xm, w_up)
        sig = jax.nn.sigmoid(gate)
        silu = gate * sig
        active = (silu * up).astype(BF16)
        d_gate = (d_active * up * sig * (1.0 + gate * (1.0 - sig))).astype(BF16)
        d_up = (d_active * silu).astype(BF16)

        keep_down, away_down = weight_sum(cot_all, active)
        got_x = over_blk(away_down, x_mask)
        (d_gate, d_up, away_down) = pin((d_gate, d_up, away_down))
        ff_cut = ff // 2
        plan, fills = Plan(), []
        if extra_bits:
            keep_gate, away_gate = weight_sum(xm, d_gate)
            keep_up, away_up = weight_sum(xm, d_up)
            source, point = plan.read(away_gate), 0
        else:
            fills = [fill_weight_grad(xm, d_gate, 0), fill_weight_grad(xm, d_up, 1)]
            source, point = ("fill", (0, 1)), 1
        gate_x = plan.fresh((4 * row_features, ff), BF16)
        fold_part(plan, source, gate_x, 0, ff_cut, point)
        (d_middle, d_mid, gain_m_grad), (gate_x, *filled) = gather_sum(
            back_through((d_gate, d_up), (w_gate, w_up)),
            plan,
            [cot.reshape(share), middle, gain_m[None]],
            [like(share, F32), like(share, BF16), like((1, width), F32)],
            finish_mlp_norm,
            fills,
        )
        if filled:
            keep_gate, away_gate, keep_up, away_up = filled
        (d_mid, got_x) = pin((d_mid, got_x))
        own_down, away_down = to_settle(keep_down, got_x)

        plan = Plan()
        settle(plan, away_down, 1)
        gate_x = plan.through(gate_x)
        fold_part(plan, plan.read(away_gate), gate_x, ff_cut, ff - ff_cut)
        up_x = plan.fresh(away_up.shape, BF16)
        fold_part(plan, plan.read(away_up), up_x, 0, ff_cut)
        d_mid_all, (got_down, gate_x, up_x, mixed_partial) = spread(
            d_mid.reshape(2 * local_rows, width), plan, [fill_back(active, w_down, 0)]
        )
        (g_down,) = settled([(own_down, got_down)], (ff,))
        own_gate, away_gate = to_settle(keep_gate, gate_x)
    else:
        (
            middle, d_middle, gain_m_grad, d_mid_all, mixed_partial, own_down, down_b, down_o, gate_b, send_gate, keep_gate, away_gate, keep_up, away_up,
        ) = middle_call(
            b_mask, x_low, cot.reshape(share), gain_m[None], attn, w_out, cot_all, w_down, w_gate, (down_weight, gate_weight, up_weight), next(ids)
        )
        d_mid_all = d_mid_all.reshape(tokens, width)
        mixed_partial = mixed_partial.reshape(tokens, width)
        up_x = None
    if extra_bits:
        d_attn = nn(d_mid_all, w_out).astype(BF16).reshape(2, 4, half, q_columns)
        d_query, d_key, d_value = attend_back(
            meta, query, d_attn, keys, values, start_lanes, attn_t, total_e, scaling
        )
        d_key = d_key.reshape(parts, tokens, head_size)
        d_value = d_value.reshape(parts, tokens, head_size)
        for b in reversed(extra_bits):
            n = d_key.shape[0] // 2
            d_key = d_key[:n] + over_blk(d_key[n:].astype(BF16), 1 << b).astype(F32)
            d_value = d_value[:n] + over_blk(d_value[n:].astype(BF16), 1 << b).astype(F32)

        plan = Plan()
        away_kv = jnp.concatenate([d_key[1], d_value[1]], axis=1).astype(BF16)
        fold(plan, plan.read(away_kv), away_kv.shape)
        settle(plan, away_gate)
        if up_x is None:
            fold(plan, plan.read(away_up), away_up.shape)
        else:
            up_x = plan.through(up_x)
            fold_part(plan, plan.read(away_up), up_x, ff_cut, ff - ff_cut)
        (mixed,), (got_kv, got_gate, up_x, *filled) = gather_sum(
            mixed_partial,
            plan,
            [middle],
            [like(share, BF16)],
            functools.partial(finish_mixed, bit_order=local_order),
            [] if extra_bits else [fill_weight_grad(d_mid_all, attn, 0)],
        )
        keep_out, away_out = filled if filled else weight_sum(d_mid_all, attn)
        (g_gate,) = settled([(own_gate, got_gate)], (ff,))
        own_up, away_up = to_settle(keep_up, up_x)
        mixed = natural(mixed)
        mixed_got = over_blk(mixed[1], b_mask)
        d_qkv, d_xa_partial, gains_qk = prepare_back(
            d_query.reshape(tokens, q_columns), d_key, d_value, got_kv, raw, cosine, sine, gain_q, gain_k, w_qkv, heads
        )
        (d_xa_partial, mixed_got) = pin((d_xa_partial, mixed_got))

        plan, fills = Plan(), []
        settle(plan, away_up)
        fold(plan, plan.read(away_out), away_out.shape)
        if extra_bits:
            keep_qkv, away_qkv = weight_sum(xa, d_qkv)
            fold(plan, plan.read(away_qkv), away_qkv.shape)
        else:
            fills = [fill_weight_grad(xa, d_qkv, 0)]
            fold(plan, ("fill", (0, 1)), (4 * row_features, a_columns), 1)
        (input_own, input_away, gain_a_grad), (got_up, out_x, got, *filled) = gather_sum(
            d_xa_partial,
            plan,
            [x_low, d_middle, gain_a[None]],
            [like((local_rows, width), F32), like((local_rows, width), BF16), like((1, width), F32)],
            functools.partial(finish_input, bit_order=local_order),
            fills,
        )
        if filled:
            keep_qkv = filled[0]
        own_out, away_out = to_settle(keep_out, out_x)
        (g_up,) = settled([(own_up, got_up)], (ff,))
        own_qkv, away_qkv = to_settle(keep_qkv, got)

        plan = Plan()
        settle(plan, away_qkv)
        settle(plan, away_out)
        input_got = plan.fresh((local_rows, width), BF16)
        plan.copy((plan.read(natural(input_away)), everything), (input_got, everything), b_mask)
        sums = jnp.concatenate([ungroup(gain_a_grad[0]), gains_qk[0], gains_qk[1], ungroup(gain_m_grad[0])])
        (sums,), (got_a, got_o, input_got) = run(
            plan, total_main(sums.reshape(-1, 128)), next(ids), [1 << i for i in range(bits)]
        )
        g_query, g_key, g_value, g_out = settled(
            [(own_qkv, got_a), (own_out, got_o)], (q_columns, k_columns, k_columns, q_columns)
        )
        mixed = in_order(batch, mixed[:1], mixed_got[None], 0)
        input_grad = in_order(batch, natural(input_own)[None], input_got.astype(F32)[None], 0)
        gains = jnp.split(sums.reshape(-1), [width, width + head_size, width + 2 * head_size])
    else:
        (
            mixed_own, mixed_got, input_own, input_got, sums, own_gate, gate_o, own_up, up_b, up_o, own_qkv, a_b, a_o, own_out, out_b, out_o,
        ) = last_call(
            b_mask,
            bit_order,
            scaling,
            dict(
                low=x_low,
                middle=middle,
                d_middle=d_middle,
                gain=gain_a[None],
                gain_m_grad=gain_m_grad,
                gain_q=gain_q,
                gain_k=gain_k,
                start=start_lanes,
                l=total_e,
                dall=d_mid_all,
                w_out=w_out,
                attn=attn,
                q=query,
                k=keys,
                v=values,
                ot=attn_t,
                raw=raw,
                table=table,
                wa=w_qkv,
                xa=xa,
                mixed=mixed_partial.reshape(2, 2, 2, 2, local_rows, width),
                send_g=send_gate,
                keep_g=keep_gate,
                away_g=away_gate,
                keep_u=keep_up,
                away_u=away_up,
            ),
            next(ids),
        )
        mixed, input_grad, g_down, g_gate, g_up, g_query, g_key, g_value, g_out = finish_call(
            jnp.stack([tensor, batch]),
            (mixed_own, mixed_got, input_own, input_got),
            [
                (own_down, down_b, down_o),
                (own_gate, gate_b, gate_o),
                (own_up, up_b, up_o),
                (own_qkv, a_b, a_o),
                (own_out, out_b, out_o),
            ],
            (ff, ff, ff, q_columns, k_columns, k_columns, q_columns),
        )
        gains = jnp.split(sums.reshape(-1), [width, width + head_size, width + 2 * head_size])
    return (
        mixed,
        input_grad,
        g_query,
        g_key,
        g_value,
        g_out,
        g_gate,
        g_up,
        g_down,
        *gains,
    )


def solution(mesh):
    rows = P(None, ("blk", "head"), None)
    weight = P("blk", "head")
    return jax.shard_map(
        local,
        mesh=mesh,
        in_specs=(rows, P(), *([weight] * 7), P(), P(), P(), P(), rows),
        out_specs=(rows, rows, *([weight] * 7), P(), P(), P(), P()),
        check_vma=False,
    )
```

```python
import functools
import math

import jax
import jax.numpy as jnp
from jax import lax
from jax.experimental import pallas as pl
from jax.experimental.pallas import tpu as pltpu
from jax.sharding import PartitionSpec as P

EPS = 1e-06
THETA = 1000000.0
LOG2E = 1.4426950408889634
F32 = jnp.float32
BF16 = jnp.bfloat16

MIB = 1024 * 1024
TINY_COST = pl.CostEstimate(flops=0, bytes_accessed=0, transcendentals=0)
VMEM_LIMIT = 32 * MIB
TENSOR_BIT = 1
SEQ_BIT = 0


def nt(a, b):
    return lax.dot_general(a, b, (((1,), (1,)), ((), ())), preferred_element_type=F32)


def tn(a, b):
    return lax.dot_general(a, b, (((0,), (0,)), ((), ())), preferred_element_type=F32)


def nn(a, b):
    return jnp.dot(a, b, preferred_element_type=F32)


def bit_of(value, bit):
    return (value >> bit) & 1


def over_blk(value, mask):
    count = lax.axis_size("blk")
    return lax.ppermute(value, "blk", [(i, i ^ mask) for i in range(count)])


def over_head(value, mask):
    count = lax.axis_size("head")
    return lax.ppermute(value, "head", [(i, i ^ mask) for i in range(count)])


def pin(values):
    return lax.optimization_barrier(values)


def in_order(flag, own, other, axis):
    return jnp.where(
        flag == 0,
        jnp.concatenate([own, other], axis=axis),
        jnp.concatenate([other, own], axis=axis),
    )


def token_offset(head_place, index, sub):
    core, upper, inner = index // (2 * sub), (index // sub) % 2, index % sub
    return (head_place ^ (upper * 2) ^ core) * sub + inner


def allowed_mask(meta_ref, start_row, q_block, k_block, rows, half, q_lanes):
    sub = half // 2
    head_place = meta_ref[0]
    k_index = lax.broadcasted_iota(jnp.int32, (2 * half, 1), 0)
    k_token = token_offset(head_place, k_index, sub) + k_block * (2 * half)
    q_index = lax.broadcasted_iota(jnp.int32, (1, q_lanes), 1) % (2 * half)
    q_token = token_offset(head_place, q_index, sub) + q_block * (2 * half)
    return (k_token <= q_token) & (k_token >= start_row)


def stacked(ref, heads, width):
    return jnp.concatenate(
        [ref[c, 0, :, h * width : (h + 1) * width] for h in range(heads) for c in range(2)], axis=0
    )


def key_rows(ref, part, block):
    return jnp.concatenate([ref[part, 0, block], ref[part, 1, block]], axis=0)


def attend_kernel(meta_ref, q_ref, k_ref, v_ref, start_ref, o_ref, ot_ref, l_ref, vt_ref, acc_ref, sum_ref, *, factor, heads):
    q_pos = pl.program_id(0)
    parts, _, blocks, half, width = k_ref.shape
    lanes = heads * 2 * half

    @pl.when(q_pos == 0)
    def _():
        for part in range(parts):
            for block in range(blocks):
                vt_ref[part * blocks + block] = key_rows(v_ref, part, block).T

    q_rows = stacked(q_ref, heads, width)
    acc_ref[...] = jnp.zeros_like(acc_ref)
    sum_ref[...] = jnp.zeros_like(sum_ref)
    start_row = start_ref[0]
    q_block = meta_ref[1 + q_pos]
    total = parts * blocks

    def add(kb, masked):
        e = jnp.exp2(nt(key_rows(k_ref, kb // blocks, kb % blocks), q_rows) * factor)
        if masked:
            k_block = meta_ref[1 + blocks + kb]
            e = jnp.where(allowed_mask(meta_ref, start_row, q_block, k_block, None, half, lanes), e, 0.0)
        sum_ref[...] += jnp.sum(e, axis=0, keepdims=True)
        acc_ref[...] += nn(vt_ref[kb], e.astype(BF16))

    def step(kb, carry):
        flag = meta_ref[1 + blocks + total + q_pos * total + kb]

        @pl.when(flag == 1)
        def _():
            add(kb, False)

        @pl.when(flag == 2)
        def _():
            add(kb, True)

        return carry

    lax.fori_loop(0, total, step, 0)
    out = acc_ref[...] / sum_ref[...]
    ot_ref[0] = out
    l_ref[0] = sum_ref[...]
    rows = out.T
    for h in range(heads):
        for c in range(2):
            at = (h * 2 + c) * half
            o_ref[c, 0, :, h * width : (h + 1) * width] = rows[at : at + half].astype(BF16)


def attend_back_kernel(
    meta_ref, q_ref, do_ref, k_ref, v_ref, start_ref, ot_ref, l_ref, dq_ref, dk_ref, dv_ref, kt_ref, acc_ref, *, factor, scaling, heads
):
    q_pos = pl.program_id(0)
    parts, _, blocks, half, width = k_ref.shape
    lanes = heads * 2 * half

    @pl.when(q_pos == 0)
    def _():
        dk_ref[...] = jnp.zeros_like(dk_ref)
        dv_ref[...] = jnp.zeros_like(dv_ref)
        for part in range(parts):
            for block in range(blocks):
                kt_ref[part * blocks + block] = key_rows(k_ref, part, block).T

    q_rows = stacked(q_ref, heads, width)
    do_rows = stacked(do_ref, heads, width)
    delta = jnp.sum(do_rows.astype(F32).T * ot_ref[0], axis=0, keepdims=True)
    inverse = 1.0 / l_ref[0]
    acc_ref[...] = jnp.zeros_like(acc_ref)
    start_row = start_ref[0]
    q_block = meta_ref[1 + q_pos]
    total = parts * blocks

    def add(kb, masked):
        part, block = kb // blocks, kb % blocks
        e = jnp.exp2(nt(key_rows(k_ref, part, block), q_rows) * factor)
        if masked:
            k_block = meta_ref[1 + blocks + kb]
            e = jnp.where(allowed_mask(meta_ref, start_row, q_block, k_block, None, half, lanes), e, 0.0)
        p = e * inverse
        dp = nt(key_rows(v_ref, part, block), do_rows)
        ds = (p * (dp - delta)).astype(BF16)
        dv = nn(p.astype(BF16), do_rows)
        dk = nn(ds, q_rows) * scaling
        for c in range(2):
            dv_ref[part, c, block] += dv[c * half : (c + 1) * half]
            dk_ref[part, c, block] += dk[c * half : (c + 1) * half]
        acc_ref[...] += nn(kt_ref[kb], ds)

    def step(kb, carry):
        flag = meta_ref[1 + blocks + total + q_pos * total + kb]

        @pl.when(flag == 1)
        def _():
            add(kb, False)

        @pl.when(flag == 2)
        def _():
            add(kb, True)

        return carry

    lax.fori_loop(0, total, step, 0)
    rows = acc_ref[...].T * scaling
    for h in range(heads):
        for c in range(2):
            at = (h * 2 + c) * half
            dq_ref[c, 0, :, h * width : (h + 1) * width] = rows[at : at + half]


def attend(meta, q, k, v, start, scaling):
    _, blocks, half, columns = q.shape
    parts, width = k.shape[0], k.shape[-1]
    heads = columns // width
    lanes = heads * 2 * half
    total = parts * blocks
    row_spec = pl.BlockSpec((2, 1, half, columns), lambda i: (0, i, 0, 0))
    key_spec = pl.BlockSpec(k.shape, lambda i: (0, 0, 0, 0, 0))
    lane_spec = pl.BlockSpec((1, 1, lanes), lambda i: (i, 0, 0))
    return pl.pallas_call(
        functools.partial(attend_kernel, factor=scaling * LOG2E, heads=heads),
        grid=(blocks,),
        in_specs=[pl.BlockSpec(memory_space=pltpu.SMEM), row_spec, key_spec, key_spec, lane_spec],
        out_specs=[row_spec, pl.BlockSpec((1, width, lanes), lambda i: (i, 0, 0)), lane_spec],
        out_shape=[
            jax.ShapeDtypeStruct(q.shape, BF16),
            jax.ShapeDtypeStruct((blocks, width, lanes), F32),
            jax.ShapeDtypeStruct((blocks, 1, lanes), F32),
        ],
        scratch_shapes=[
            pltpu.VMEM((total, width, 2 * half), BF16),
            pltpu.VMEM((width, lanes), F32),
            pltpu.VMEM((1, lanes), F32),
        ],
        compiler_params=pltpu.CompilerParams(vmem_limit_bytes=VMEM_LIMIT),
        cost_estimate=pl.CostEstimate(
            flops=2 * 2 * lanes * 2 * half * width * blocks * total,
            bytes_accessed=8 * q.size + 8 * k.size,
            transcendentals=lanes * 2 * half * blocks * total,
        ),
    )(meta, q, k, v, start)


def attend_back(meta, q, do, k, v, start, out_t, total_e, scaling):
    _, blocks, half, columns = q.shape
    parts, width = k.shape[0], k.shape[-1]
    heads = columns // width
    lanes = heads * 2 * half
    total = parts * blocks
    row_spec = pl.BlockSpec((2, 1, half, columns), lambda i: (0, i, 0, 0))
    key_spec = pl.BlockSpec(k.shape, lambda i: (0, 0, 0, 0, 0))
    lane_spec = pl.BlockSpec((1, 1, lanes), lambda i: (i, 0, 0))
    return pl.pallas_call(
        functools.partial(attend_back_kernel, factor=scaling * LOG2E, scaling=scaling, heads=heads),
        grid=(blocks,),
        in_specs=[
            pl.BlockSpec(memory_space=pltpu.SMEM),
            row_spec,
            row_spec,
            key_spec,
            key_spec,
            lane_spec,
            pl.BlockSpec((1, width, lanes), lambda i: (i, 0, 0)),
            lane_spec,
        ],
        out_specs=[row_spec, key_spec, key_spec],
        out_shape=[
            jax.ShapeDtypeStruct(q.shape, F32),
            jax.ShapeDtypeStruct(k.shape, F32),
            jax.ShapeDtypeStruct(k.shape, F32),
        ],
        scratch_shapes=[
            pltpu.VMEM((total, width, 2 * half), BF16),
            pltpu.VMEM((width, lanes), F32),
        ],
        compiler_params=pltpu.CompilerParams(vmem_limit_bytes=VMEM_LIMIT),
        cost_estimate=pl.CostEstimate(
            flops=5 * 2 * lanes * 2 * half * width * blocks * total,
            bytes_accessed=12 * q.size + 16 * k.size,
            transcendentals=lanes * 2 * half * blocks * total,
        ),
    )(meta, q, do, k, v, start, out_t, total_e)


def prepare_kernel(x_ref, w_ref, cos_ref, sin_ref, gq_ref, gk_ref, q_ref, kv_ref, raw_ref, *, heads, width):
    acc = jnp.dot(x_ref[...], w_ref[...], preferred_element_type=F32)
    raw_ref[...] = acc[:, : (heads + 1) * width]
    for h in range(heads + 1):
        part = acc[:, h * width : (h + 1) * width]
        normed = part * lax.rsqrt(jnp.mean(part * part, axis=-1, keepdims=True) + EPS)
        scaled = normed * (gq_ref if h < heads else gk_ref)[...]
        turned = (scaled * cos_ref[...] + pltpu.roll(scaled, width // 2, 1) * sin_ref[...]).astype(BF16)
        if h < heads:
            q_ref[:, h * width : (h + 1) * width] = turned
        else:
            kv_ref[:, :width] = turned
    kv_ref[:, width:] = acc[:, (heads + 1) * width :].astype(BF16)


def prepare(x, w, cos, sin, gain_q, gain_k, heads):
    tokens, depth = x.shape
    width, tile = gain_q.shape[1], 256
    row = lambda n: pl.BlockSpec((tile, n), lambda i: (i, 0))
    fixed = lambda a: pl.BlockSpec(a.shape, lambda i: (0, 0))
    return pl.pallas_call(
        functools.partial(prepare_kernel, heads=heads, width=width),
        grid=(tokens // tile,),
        in_specs=[row(depth), fixed(w), row(width), row(width), fixed(gain_q), fixed(gain_k)],
        out_specs=[row(heads * width), row(2 * width), row((heads + 1) * width)],
        out_shape=[
            jax.ShapeDtypeStruct((tokens, heads * width), BF16),
            jax.ShapeDtypeStruct((tokens, 2 * width), BF16),
            jax.ShapeDtypeStruct((tokens, (heads + 1) * width), F32),
        ],
        compiler_params=pltpu.CompilerParams(vmem_limit_bytes=VMEM_LIMIT),
        cost_estimate=TINY_COST,
    )(x, w, cos, sin, gain_q, gain_k)


def prepare_back_kernel(
    dq_ref, dk_ref, dv_ref, got_ref, raw_ref, cos_ref, sin_ref, gq_ref, gk_ref, w_ref, d_ref, p_ref, g_ref, *, heads, width
):
    @pl.when(pl.program_id(0) == 0)
    def _():
        g_ref[...] = jnp.zeros_like(g_ref)

    got = got_ref[...].astype(F32)
    for h in range(heads + 1):
        at = slice(h * width, (h + 1) * width)
        grad = dq_ref[:, at] if h < heads else dk_ref[0] + got[:, :width]
        gain = (gq_ref if h < heads else gk_ref)[...]
        raw = raw_ref[:, at]
        inverse = lax.rsqrt(jnp.mean(raw * raw, axis=-1, keepdims=True) + EPS)
        normed = raw * inverse
        turned = grad * cos_ref[...] - pltpu.roll(grad, width // 2, 1) * sin_ref[...]
        row = 0 if h < heads else 1
        g_ref[row : row + 1, :] += jnp.sum(turned * normed, axis=0, keepdims=True)
        scaled = turned * gain
        d_ref[:, at] = (inverse * (scaled - normed * jnp.mean(scaled * normed, axis=-1, keepdims=True))).astype(BF16)
    d_ref[:, (heads + 1) * width :] = (dv_ref[0] + got[:, width:]).astype(BF16)
    p_ref[...] = nt(d_ref[...], w_ref[...]).astype(BF16)


def prepare_back(dq, dk, dv, got, raw, cos, sin, gain_q, gain_k, w, heads):
    tokens, width, tile = dq.shape[0], gain_q.shape[1], 256
    row = lambda n: pl.BlockSpec((tile, n), lambda i: (i, 0))
    part = pl.BlockSpec((1, tile, width), lambda i: (0, i, 0))
    fixed = lambda a: pl.BlockSpec(a.shape, lambda i: (0, 0))
    return pl.pallas_call(
        functools.partial(prepare_back_kernel, heads=heads, width=width),
        grid=(tokens // tile,),
        in_specs=[
            row(heads * width),
            part,
            part,
            row(2 * width),
            row((heads + 1) * width),
            row(width),
            row(width),
            fixed(gain_q),
            fixed(gain_k),
            fixed(w),
        ],
        out_specs=[row(w.shape[1]), row(w.shape[0]), pl.BlockSpec((8, width), lambda i: (0, 0))],
        out_shape=[
            jax.ShapeDtypeStruct((tokens, w.shape[1]), BF16),
            jax.ShapeDtypeStruct((tokens, w.shape[0]), BF16),
            jax.ShapeDtypeStruct((8, width), F32),
        ],
        compiler_params=pltpu.CompilerParams(vmem_limit_bytes=VMEM_LIMIT),
        cost_estimate=TINY_COST,
    )(dq, dk, dv, got, raw, cos, sin, gain_q, gain_k, w)


def place_of_block(blk, bit_order, p):
    return blk ^ sum(((p >> i) & 1) << b for i, b in enumerate(bit_order))


def enter_kernel(blk_ref, *refs, bit_order, normed):
    if normed:
        mine_ref, other_ref, gain_ref, low_ref, out_ref, gains_ref = refs
    else:
        mine_ref, low_ref = refs
    rows, width = mine_ref.shape
    n = width >> len(bit_order)
    for p in range(1 << len(bit_order)):
        at = pl.ds(pl.multiple_of(place_of_block(blk_ref[0], bit_order, p) * n, n), n)
        low_ref[:rows, p * n : (p + 1) * n] = mine_ref[:, at]
        if normed:
            low_ref[rows:, p * n : (p + 1) * n] = other_ref[:, at]
            gains_ref[:, p * n : (p + 1) * n] = gain_ref[:, at]
    if normed:
        values = low_ref[...].astype(F32)
        inverse = lax.rsqrt(jnp.mean(values * values, axis=-1, keepdims=True) + EPS)
        out_ref[...] = (values * inverse * gains_ref[:1]).astype(BF16)


def enter(blk, bit_order, mine, other=None, gain=None):
    rows, width = mine.shape
    normed = gain is not None
    total = (2 * rows if normed else rows, width)
    vmem = pl.BlockSpec(memory_space=pltpu.VMEM)
    operands = [mine, other, gain] if normed else [mine]
    return pl.pallas_call(
        functools.partial(enter_kernel, bit_order=bit_order, normed=normed),
        in_specs=[pl.BlockSpec(memory_space=pltpu.SMEM), *[vmem] * len(operands)],
        out_specs=[vmem] * (3 if normed else 1),
        out_shape=[
            *[jax.ShapeDtypeStruct(total, BF16)] * (2 if normed else 1),
            *([jax.ShapeDtypeStruct(gain.shape, F32)] if normed else []),
        ],
        compiler_params=pltpu.CompilerParams(vmem_limit_bytes=VMEM_LIMIT),
        cost_estimate=TINY_COST,
    )(blk[None].astype(jnp.int32), *operands)


def assemble_kernel(place_ref, *refs, sources, widths):
    ins, outs = refs[: 2 * sources], refs[2 * sources :]
    place, k, at = place_ref[0], 0, 0
    for own_ref, got_ref in zip(ins[::2], ins[1::2]):
        f, at = own_ref.shape[0], 0
        while at < own_ref.shape[1]:
            w, cut = widths[k], slice(at, at + widths[k])
            mine = pl.ds(pl.multiple_of(place * w, w), w)
            theirs = pl.ds(pl.multiple_of((1 - place) * w, w), w)
            outs[k][:, mine] = own_ref[:, cut] + got_ref[:f, cut].astype(F32)
            outs[k][:, theirs] = got_ref[f : 2 * f, cut].astype(F32) + got_ref[2 * f :, cut].astype(F32)
            at += w
            k += 1


def assemble(place, sources, widths):
    vmem = pl.BlockSpec(memory_space=pltpu.VMEM)
    flat = [a for pair in sources for a in pair]
    return pl.pallas_call(
        functools.partial(assemble_kernel, sources=len(sources), widths=widths),
        in_specs=[pl.BlockSpec(memory_space=pltpu.SMEM), *[vmem] * len(flat)],
        out_specs=[vmem] * len(widths),
        out_shape=[jax.ShapeDtypeStruct((sources[0][0].shape[0], 2 * w), F32) for w in widths],
        compiler_params=pltpu.CompilerParams(vmem_limit_bytes=VMEM_LIMIT),
        cost_estimate=TINY_COST,
    )(place[None].astype(jnp.int32), *flat)


def back_kernel(*refs):
    *ins, out_ref = refs
    n = len(ins) // 2
    out_ref[...] = sum(nt(d[...], w[...]) for d, w in zip(ins[:n], ins[n:])).astype(BF16)


def back_through(grads, weights):
    tokens, depth, tile = grads[0].shape[0], weights[0].shape[0], 256
    return pl.pallas_call(
        back_kernel,
        grid=(depth // tile,),
        in_specs=[
            *[pl.BlockSpec(g.shape, lambda i: (0, 0)) for g in grads],
            *[pl.BlockSpec((tile, w.shape[1]), lambda i: (i, 0)) for w in weights],
        ],
        out_specs=pl.BlockSpec((tokens, tile), lambda i: (0, i)),
        out_shape=jax.ShapeDtypeStruct((tokens, depth), BF16),
        compiler_params=pltpu.CompilerParams(vmem_limit_bytes=VMEM_LIMIT),
        cost_estimate=TINY_COST,
    )(*grads, *weights)


def weight_grad_kernel(a_ref, b_ref, keep_ref, away_ref):
    product = tn(a_ref[...], b_ref[...])
    first = pl.program_id(0) < pl.num_programs(0) // 2

    @pl.when(first)
    def _():
        keep_ref[...] = product

    @pl.when(jnp.logical_not(first))
    def _():
        away_ref[...] = product.astype(BF16)


def weight_grad(a, b):
    tokens, depth = a.shape
    n, tile = b.shape[1], 256
    steps = depth // tile
    return pl.pallas_call(
        weight_grad_kernel,
        grid=(steps,),
        in_specs=[
            pl.BlockSpec((tokens, tile), lambda i: (0, i)),
            pl.BlockSpec((tokens, n), lambda i: (0, 0)),
        ],
        out_specs=[
            pl.BlockSpec((tile, n), lambda i: (jnp.minimum(i, steps // 2 - 1), 0)),
            pl.BlockSpec((tile, n), lambda i: (jnp.maximum(i - steps // 2, 0), 0)),
        ],
        out_shape=[
            jax.ShapeDtypeStruct((depth // 2, n), F32),
            jax.ShapeDtypeStruct((depth // 2, n), BF16),
        ],
        compiler_params=pltpu.CompilerParams(vmem_limit_bytes=VMEM_LIMIT),
        cost_estimate=TINY_COST,
    )(a, b)


def remote(src, dst, send, recv, target):
    copy = pltpu.make_async_remote_copy(
        src_ref=src, dst_ref=dst, send_sem=send, recv_sem=recv, device_id=target, device_id_type=pl.DeviceIdType.MESH
    )
    copy.start()
    return copy


class Plan:
    def __init__(self):
        self.inputs, self.shapes, self.aliases, self.jobs = [], [], {}, []

    def read(self, array):
        self.inputs.append(array)
        return ("in", len(self.inputs) - 1)

    def fresh(self, shape, dtype):
        self.shapes.append(jax.ShapeDtypeStruct(shape, dtype))
        return ("out", len(self.shapes) - 1)

    def through(self, array):
        self.inputs.append(array)
        self.aliases[len(self.inputs) - 1] = len(self.shapes)
        return self.fresh(array.shape, array.dtype)

    def copy(self, src, dst, mask, after=None, point=0):
        self.jobs.append((src, dst, mask, after, point, None))
        return len(self.jobs) - 1

    def local(self, src, dst, shape, point=0):
        self.jobs.append((src, dst, 0, None, point, shape))
        return len(self.jobs) - 1


class Fill:
    def __init__(self, inputs, outputs, step, point):
        self.inputs, self.outputs, self.step, self.point = inputs, outputs, step, point

    def scratch(self):
        shapes = [pltpu.VMEM(a.shape, a.dtype) for a in (*self.inputs, *self.outputs)]
        return [*shapes, pltpu.SemaphoreType.DMA((len(shapes),))]


def fill_weight_grad(a, b, point):
    depth, n, tile = a.shape[1], b.shape[1], 256
    half = depth // 2

    def step(ins, outs):
        (a_ref, b_ref), (keep_ref, away_ref) = ins, outs

        def one(i, carry):
            at = pl.ds(pl.multiple_of(i * tile, tile), tile)
            keep_ref[at, :] = tn(a_ref[:, at], b_ref[...])
            far = pl.ds(pl.multiple_of(half + i * tile, tile), tile)
            away_ref[at, :] = tn(a_ref[:, far], b_ref[...]).astype(BF16)
            return carry

        lax.fori_loop(0, half // tile, one, 0)

    outputs = [jax.ShapeDtypeStruct((half, n), F32), jax.ShapeDtypeStruct((half, n), BF16)]
    return Fill([a, b], outputs, step, point)


def fill_back(grad, weight, point):
    tokens, depth, tile = grad.shape[0], weight.shape[0], 256

    def step(ins, outs):
        (g_ref, w_ref), (out_ref,) = ins, outs

        def one(i, carry):
            at = pl.ds(pl.multiple_of(i * tile, tile), tile)
            out_ref[:, at] = nt(g_ref[...], w_ref[at, :]).astype(BF16)
            return carry

        lax.fori_loop(0, depth // tile, one, 0)

    return Fill([grad, weight], [jax.ShapeDtypeStruct((tokens, depth), BF16)], step, point)


def fill_product(left, right, point):
    tokens, n, tile = left.shape[0], right.shape[1], 256

    def step(ins, outs):
        (l_ref, r_ref), (out_ref,) = ins, outs

        def one(i, carry):
            at = pl.ds(pl.multiple_of(i * tile, tile), tile)
            out_ref[at, :] = nn(l_ref[at, :], r_ref[...])
            return carry

        lax.fori_loop(0, tokens // tile, one, 0)

    return Fill([left, right], [jax.ShapeDtypeStruct((tokens, n), F32)], step, point)


def run(plan, main, collective_id, greeted=(), fills=(), limit=None):
    inputs, in_specs, out_shapes, out_specs, scratch, body, own_limit = main
    limit = limit or own_limit + sum(math.prod(s.shape) * s.dtype.itemsize for f in fills for s in f.scratch()[:-1])
    f_in, f_out = [a for f in fills for a in f.inputs], [a for f in fills for a in f.outputs]
    n_in, n_out = len(inputs), len(out_shapes)
    m_in, m_out = len(plan.inputs), len(plan.shapes)
    jobs = plan.jobs
    local_jobs = [i for i, job in enumerate(jobs) if not job[2]]
    masks = sorted({*greeted, *[job[2] for job in jobs if job[2]]} - {1 << TENSOR_BIT})
    any_spec = pl.BlockSpec(memory_space=pltpu.HBM)

    def kernel(*refs):
        main_in, refs = refs[:n_in], refs[n_in:]
        plan_in, refs = refs[:m_in], refs[m_in:]
        fill_in, refs = refs[: len(f_in)], refs[len(f_in) :]
        main_out, refs = refs[:n_out], refs[n_out:]
        plan_out, refs = refs[:m_out], refs[m_out:]
        fill_out, refs = refs[: len(f_out)], refs[len(f_out) :]
        send, recv, *rest = refs
        bounce = dict(zip(local_jobs, rest))
        rest = rest[len(local_jobs) :]
        parts = []
        for f in fills:
            k, m = len(f.inputs), len(f.outputs)
            (*held, sems), rest = rest[: k + m + 1], rest[k + m + 1 :]
            loads = [pltpu.make_async_copy(fill_in[i], held[i], sems.at[i]) for i in range(k)]
            stores = [pltpu.make_async_copy(held[k + i], fill_out[i], sems.at[k + i]) for i in range(m)]
            fill_in, fill_out = fill_in[k:], fill_out[m:]
            for copy in loads:
                copy.start()
            parts.append((f, held[:k], held[k:], loads, stores))

        def compute(point):
            for f, ins, outs, loads, stores in parts:
                if f.point == point:
                    for copy in loads:
                        copy.wait()
                    f.step(ins, outs)
                    for copy in stores:
                        copy.start()

        blk, head = lax.axis_index("blk"), lax.axis_index("head")
        core, near, across = (blk, head ^ 1), (blk, head ^ 2), (blk ^ (1 << TENSOR_BIT), head)
        barrier = pltpu.get_barrier_semaphore()
        partners = [core, near, across, *[(blk ^ m, head) for m in masks]]
        for target in partners:
            pl.semaphore_signal(barrier, inc=1, device_id=target, device_id_type=pl.DeviceIdType.MESH)
        pl.semaphore_wait(barrier, len(partners))
        started, arrived, halfway = {}, set(), []

        def arrive(i):
            if i not in arrived:
                arrived.add(i)
                (started[i].wait_recv if jobs[i][2] else started[i].wait)()

        def part(side):
            (kind, index), cut = side
            if kind == "fill":
                return cut(parts[index[0]][2][index[1]])
            return cut((plan_in if kind == "in" else plan_out)[index])

        def issue(point):
            for i in list(halfway):
                started[i].wait()
                started[i] = pltpu.make_async_copy(bounce[i], part(jobs[i][1]), recv.at[i])
                started[i].start()
                halfway.remove(i)
            for i, (src, dst, mask, after, at, shape) in enumerate(jobs):
                if i in started or (at != point and point is not None):
                    continue
                if after is not None:
                    arrive(after)
                if mask:
                    started[i] = remote(part(src), part(dst), send.at[i], recv.at[i], (blk ^ mask, head))
                else:
                    started[i] = pltpu.make_async_copy(part(src), bounce[i], send.at[i])
                    started[i].start()
                    halfway.append(i)

        point = 0
        for _ in body((core, near, across), main_in, main_out, rest):
            issue(point)
            compute(point)
            point += 1
        issue(None)
        issue(None)
        for i in range(len(jobs)):
            arrive(i)
            if jobs[i][2]:
                started[i].wait_send()
        for *_, stores in parts:
            for copy in stores:
                copy.wait()

    results = pl.pallas_call(
        kernel,
        out_shape=[*out_shapes, *plan.shapes, *f_out],
        in_specs=[*in_specs, *[any_spec] * (m_in + len(f_in))],
        out_specs=[*out_specs, *[any_spec] * (m_out + len(f_out))],
        scratch_shapes=[
            pltpu.SemaphoreType.DMA((max(1, len(jobs)),)),
            pltpu.SemaphoreType.DMA((max(1, len(jobs)),)),
            *[pltpu.VMEM(jobs[i][5], BF16) for i in local_jobs],
            *[s for f in fills for s in f.scratch()],
            *scratch,
        ],
        input_output_aliases={n_in + i: n_out + o for i, o in plan.aliases.items()},
        compiler_params=pltpu.CompilerParams(
            collective_id=collective_id, has_side_effects=True, vmem_limit_bytes=limit
        ),
        cost_estimate=TINY_COST,
    )(*inputs, *plan.inputs, *f_in)
    return results[:n_out], results[n_out:]


def spread_main(flat, chunk):
    rows, width = flat.shape[0] // 2, flat.shape[1]
    pieces = width // chunk

    def body(partners, ins, outs, scratch):
        core, near, across = partners
        (s_ref,), (o_ref,), (hold, local_sem, send, recv) = ins, outs, scratch
        first = remote(s_ref, o_ref.at[0, :, 0, 1], send.at[0], recv.at[0], near)
        second = [
            remote(
                s_ref.at[:, :, pl.ds(i * chunk, chunk)],
                o_ref.at[0, :, 1, 0, :, pl.ds((i ^ 1) * chunk, chunk)],
                send.at[6 + i],
                recv.at[6 + i],
                across,
            )
            for i in range(pieces)
        ]
        third = remote(s_ref, o_ref.at[1, :, 0, 0], send.at[1], recv.at[1], core)
        held = pltpu.make_async_copy(s_ref, hold, local_sem.at[0])
        held.start()
        yield
        held.wait()
        own = pltpu.make_async_copy(hold, o_ref.at[0, :, 0, 0], local_sem.at[1])
        own.start()
        for copy in second:
            copy.wait_recv()
        fourth = remote(o_ref.at[0, :, 1, 0], o_ref.at[0, :, 1, 1], send.at[2], recv.at[2], near)
        fifth = remote(o_ref.at[0, :, 1, 0], o_ref.at[1, :, 1, 0], send.at[3], recv.at[3], core)
        yield
        first.wait_recv()
        sixth = remote(o_ref.at[0, :, 0, 1], o_ref.at[1, :, 0, 1], send.at[4], recv.at[4], core)
        yield
        fourth.wait_recv()
        seventh = remote(o_ref.at[0, :, 1, 1], o_ref.at[1, :, 1, 1], send.at[5], recv.at[5], core)
        yield
        own.wait()
        for copy in (first, *second, third, fourth, fifth, sixth, seventh):
            copy.wait_send()
        for copy in (third, fifth, sixth, seventh):
            copy.wait_recv()

    any_spec = pl.BlockSpec(memory_space=pltpu.HBM)
    return (
        [flat.reshape(2, rows, width)],
        [any_spec],
        [jax.ShapeDtypeStruct((2, 2, 2, 2, rows, width), flat.dtype)],
        [any_spec],
        [
            pltpu.VMEM((2, rows, width), flat.dtype),
            pltpu.SemaphoreType.DMA((2,)),
            pltpu.SemaphoreType.DMA((6 + pieces,)),
            pltpu.SemaphoreType.DMA((6 + pieces,)),
        ],
        body,
        8 * MIB,
    )


def gather_main(partial, chunk, extra, outs_like, finish):
    rows, width = partial.shape[0] // 16, partial.shape[1]
    share = (2, rows, width)
    pieces = width // chunk

    def body(partners, ins, outs, scratch):
        core, near, across = partners
        p_ref, *extra_refs = ins
        core_in, out_y, in_y, out_t, in_t, hold, send, recv = scratch
        order = ((1, 1), (0, 1), (1, 0), (0, 0))
        from_core = [
            remote(p_ref.at[1, :, t, y], core_in.at[i], send.at[i], recv.at[i], core) for i, (t, y) in enumerate(order)
        ]
        from_y = []
        for i in range(2):
            t, y = order[i]
            from_core[i].wait_recv()
            out_y[i] = (p_ref[0, :, t, y].astype(F32) + core_in[i].astype(F32)).astype(BF16)
            from_y.append(remote(out_y.at[i], in_y.at[i], send.at[4 + i], recv.at[4 + i], near))
        yield
        from_core[2].wait_recv()
        hold[...] = p_ref[0, :, 1, 0].astype(F32) + core_in[2].astype(F32)
        from_y[0].wait_recv()
        for i in range(pieces):
            a, b = slice(i * chunk, (i + 1) * chunk), slice((i ^ 1) * chunk, ((i ^ 1) + 1) * chunk)
            out_t[:, :, b] = (hold[:, :, a] + in_y[0, :, :, a].astype(F32)).astype(BF16)
        from_t = remote(out_t, in_t, send.at[6], recv.at[6], across)
        yield
        from_core[3].wait_recv()
        hold[...] = p_ref[0, :, 0, 0].astype(F32) + core_in[3].astype(F32)
        from_y[1].wait_recv()
        hold[...] += in_y[1].astype(F32)
        yield
        from_t.wait_recv()
        hold[...] += in_t[...].astype(F32)
        finish(hold, extra_refs, outs)
        for copy in (*from_core, *from_y, from_t):
            copy.wait_send()

    vmem_spec = pl.BlockSpec(memory_space=pltpu.VMEM)
    return (
        [partial.reshape(2, 2, 2, 2, rows, width), *extra],
        [vmem_spec] * (1 + len(extra)),
        outs_like,
        [vmem_spec] * len(outs_like),
        [
            pltpu.VMEM((4, *share), BF16),
            pltpu.VMEM((2, *share), BF16),
            pltpu.VMEM((2, *share), BF16),
            pltpu.VMEM(share, BF16),
            pltpu.VMEM(share, BF16),
            pltpu.VMEM(share, F32),
            pltpu.SemaphoreType.DMA((7,)),
            pltpu.SemaphoreType.DMA((7,)),
        ],
        body,
        24 * MIB,
    )


def inverse_rms(values):
    return lax.rsqrt(jnp.mean(values * values, axis=-1, keepdims=True) + EPS)


def finish_middle(total, extra, outs):
    (low_ref, gain_ref), (middle_ref, normed_ref) = extra, outs
    for m in range(2):
        middle = low_ref[m].astype(F32) + total[m]
        middle_ref[m] = middle
        normed_ref[m] = (middle * inverse_rms(middle) * gain_ref[...]).astype(BF16)


def norm_grad(total, values, gain, gain_grad_ref, m):
    inverse = inverse_rms(values)
    normal = values * inverse
    part = jnp.sum(total * normal, axis=0, keepdims=True)
    gain_grad_ref[...] = part if m == 0 else gain_grad_ref[...] + part
    scaled = total * gain
    return inverse * (scaled - normal * jnp.mean(scaled * normal, axis=-1, keepdims=True))


def finish_mlp_norm(total, extra, outs):
    (cot_ref, middle_ref, gain_ref), (grad_ref, low_ref, gain_grad_ref) = extra, outs
    for m in range(2):
        grad = cot_ref[m].astype(F32) + norm_grad(total[m], middle_ref[m], gain_ref[...], gain_grad_ref, m)
        grad_ref[m] = grad
        low_ref[m] = grad.astype(BF16)


def store_ungrouped(value, ref, blk, bit_order, lead=()):
    n = value.shape[-1] >> len(bit_order)
    for p in range(1 << len(bit_order)):
        block = value[:, p * n : (p + 1) * n]
        if bit_order and n % 128 == 0:
            at = pl.ds(pl.multiple_of(place_of_block(blk, bit_order, p) * n, n), n)
        else:
            at = pl.ds(p * n, n)
        ref[(*lead, slice(None), at)] = block.astype(ref.dtype)


def finish_mixed(total, extra, outs, *, bit_order):
    (middle_ref,), (mixed_ref,) = extra, outs
    blk = lax.axis_index("blk")
    for m in range(2):
        store_ungrouped(middle_ref[m] + total[m], mixed_ref, blk, bit_order, (m,))


def finish_input(total, extra, outs, *, bit_order):
    (low_ref, mid_ref, gain_ref), (own_ref, away_ref, gain_grad_ref) = extra, outs
    blk = lax.axis_index("blk")
    for m in range(2):
        grad = mid_ref[m] + norm_grad(total[m], low_ref[m].astype(F32), gain_ref[...], gain_grad_ref, m)
        store_ungrouped(grad, own_ref if m == 0 else away_ref, blk, bit_order)


def total_main(values):
    rows, width = values.shape
    rounds = 2 + lax.axis_size("blk").bit_length() - 1

    def body(partners, ins, outs, scratch):
        (v_ref,), (o_ref,) = ins, outs
        out_buf, in_buf, send, recv = scratch
        blk, head = lax.axis_index("blk"), lax.axis_index("head")
        o_ref[...] = v_ref[...]
        yield
        for i in range(rounds):
            target = (blk, head ^ (1 << i)) if i < 2 else (blk ^ (1 << (i - 2)), head)
            out_buf[i] = o_ref[...]
            copy = remote(out_buf.at[i], in_buf.at[i], send.at[i], recv.at[i], target)
            copy.wait_recv()
            o_ref[...] += in_buf[i]
            copy.wait_send()
        yield

    vmem_spec = pl.BlockSpec(memory_space=pltpu.VMEM)
    return (
        [values],
        [vmem_spec],
        [jax.ShapeDtypeStruct(values.shape, F32)],
        [vmem_spec],
        [
            pltpu.VMEM((rounds, rows, width), F32),
            pltpu.VMEM((rounds, rows, width), F32),
            pltpu.SemaphoreType.DMA((rounds,)),
            pltpu.SemaphoreType.DMA((rounds,)),
        ],
        body,
        8 * MIB,
    )


class Moving:
    def __init__(self, copy, away):
        self.copy, self.away, self.here, self.gone = copy, away, False, not away

    def arrive(self):
        if not self.here:
            self.here = True
            (self.copy.wait_recv if self.away else self.copy.wait)()

    def sent(self):
        if not self.gone:
            self.gone = True
            self.copy.wait_send()


class Links:
    def __init__(self, send, recv, batch_mask):
        self.send, self.recv, self.all = send, recv, []
        blk, head = lax.axis_index("blk"), lax.axis_index("head")
        self.core, self.near, self.across = (blk, head ^ 1), (blk, head ^ 2), (blk ^ (1 << TENSOR_BIT), head)
        self.seq, self.batch = (blk ^ (1 << SEQ_BIT), head), (blk ^ batch_mask, head)
        self.both = (blk ^ (batch_mask | (1 << TENSOR_BIT)), head)
        self.place = bit_of(blk, TENSOR_BIT)
        self.blk = blk

    def greet(self):
        barrier = pltpu.get_barrier_semaphore()
        partners = (self.core, self.near, self.across, self.seq, self.batch, self.both)
        for target in partners:
            pl.semaphore_signal(barrier, inc=1, device_id=target, device_id_type=pl.DeviceIdType.MESH)
        pl.semaphore_wait(barrier, len(partners))

    def to(self, target, src, dst):
        i = len(self.all)
        self.all.append(Moving(remote(src, dst, self.send.at[i], self.recv.at[i], target), True))
        return self.all[-1]

    def load(self, src, dst):
        copy = pltpu.make_async_copy(src, dst, self.recv.at[len(self.all)])
        copy.start()
        self.all.append(Moving(copy, False))
        return self.all[-1]

    def finish(self):
        for moving in self.all:
            moving.arrive()
            moving.sent()

    def half(self, ref, other):
        n = ref.shape[1] // 2
        place = 1 - self.place if other else self.place
        return ref.at[:, pl.ds(pl.multiple_of(place * n, n), n)]


def nothing(stage):
    pass


def spread_in(links, s_ref, o_ref, chunk, between=nothing, in_vmem=True):
    pieces = s_ref.shape[-1] // chunk
    across = [
        links.to(
            links.across,
            s_ref.at[:, :, pl.ds(i * chunk, chunk)],
            o_ref.at[0, :, 1, 0, :, pl.ds((i ^ 1) * chunk, chunk)],
        )
        for i in range(pieces)
    ]
    near = links.to(links.near, s_ref, o_ref.at[0, :, 0, 1])
    core = [links.to(links.core, s_ref, o_ref.at[1, :, 0, 0])]
    if in_vmem:
        o_ref[0, :, 0, 0] = s_ref[...]
    else:
        links.load(s_ref, o_ref.at[0, :, 0, 0])
    between(0)
    for copy in across:
        copy.arrive()
    onward = links.to(links.near, o_ref.at[0, :, 1, 0], o_ref.at[0, :, 1, 1])
    core.append(links.to(links.core, o_ref.at[0, :, 1, 0], o_ref.at[1, :, 1, 0]))
    near.arrive()
    core.append(links.to(links.core, o_ref.at[0, :, 0, 1], o_ref.at[1, :, 0, 1]))
    between(1)
    onward.arrive()
    core.append(links.to(links.core, o_ref.at[0, :, 1, 1], o_ref.at[1, :, 1, 1]))
    between(2)
    for copy in core:
        copy.arrive()
    for copy in (*across, near, core[0]):
        copy.sent()


def sum_in(links, bufs, chunk, partial, between=nothing, far=None):
    p_ref, core_in, out_y, in_y, out_t, in_t, hold = bufs
    order = ((1, 1), (1, 0), (0, 1), (0, 0))
    if partial:
        partial(1)
        far = p_ref.at[1]
    core = [links.to(links.core, far.at[:, t, y], core_in.at[i]) for i, (t, y) in enumerate(order)]
    if partial:
        partial(0)

    def both(i):
        t, y = order[i]
        core[i].arrive()
        return p_ref[0, :, t, y].astype(F32) + core_in[i].astype(F32)

    def near(i, m):
        return links.to(links.near, out_y.at[i, m], in_y.at[i, m])

    out_y[0] = both(0).astype(BF16)
    copies = [near(0, 0)]
    hold[...] = both(1)
    out_y[1] = both(2).astype(BF16)
    between(0)
    across = []
    for m in range(2):
        copies[m].arrive()
        copies += [near(0, 1)] if m == 0 else [near(1, 0), near(1, 1)]
        for i in range(p_ref.shape[-1] // chunk):
            a, b = slice(i * chunk, (i + 1) * chunk), slice((i ^ 1) * chunk, ((i ^ 1) + 1) * chunk)
            out_t[m, :, b] = (hold[m, :, a] + in_y[0, m, :, a].astype(F32)).astype(BF16)
        across.append(links.to(links.across, out_t.at[m], in_t.at[m]))
    hold[...] = both(3)
    between(1)
    for m in range(2):
        copies[2 + m].arrive()
        hold[m] += in_y[1, m].astype(F32)
    between(2)
    for m in range(2):
        across[m].arrive()
        hold[m] += in_t[m].astype(F32)
    for copy in (*core, *copies, *across):
        copy.sent()


def loop(count, step):
    def one(i, carry):
        step(i)
        return carry

    lax.fori_loop(0, count, one, 0)


def rows_of(ref, i):
    value = ref[i // 2, i % 2]
    return value.reshape(-1, value.shape[-1])


def away_rows(a_cols, b_ref, away_ref):
    depth, tile = away_ref.shape[0], 512

    def step(i):
        product = tn(a_cols(pl.multiple_of(depth + i * tile, tile), tile), b_ref[...])
        away_ref[pl.ds(pl.multiple_of(i * tile, tile), tile), :] = product.astype(BF16)

    loop(depth // tile, step)


def keep_rows(a_cols, b_ref, fold_ref, own_ref, send_ref):
    f = own_ref.shape[0]
    own_ref[...] = tn(a_cols(0, f), b_ref[...]) + fold_ref[:f, :].astype(F32)

    def step(i):
        at = pl.multiple_of(i * f, f)
        product = tn(a_cols(pl.multiple_of(at + f, f), f), b_ref[...])
        send_ref[pl.ds(at, f), :] = (product + fold_ref[pl.ds(pl.multiple_of(at + f, f), f), :].astype(F32)).astype(BF16)

    loop(3, step)


def middle_kernel(
    low_ref, cot_ref, gain_ref, attn_ref, wo_ref, c_ref, wd_ref, wg_ref, down_ref, gate_ref, up_ref,
    middle_ref, dmid_ref, gain_grad_ref, dall_ref, mixed_ref, own_d_ref, got_d_b_ref, got_d_o_ref, got_g_b_ref, send_g_ref, own_g_ref, keep_u_ref, away_u_ref,
    attn, wo, p, core_in, out_y, in_y, out_t, in_t, hold, xm_s, xm, c, wd, wg, wu, dact, gate, act, dg, du,
    away_d, fold_d, away_g, fold_g, own_d, send_d, send_g, up_tile, send, recv, *, batch_mask, chunk,
):
    links = Links(send, recv, batch_mask)
    f, ff = own_d.shape[0], act.shape[1]
    to, load = links.to, links.load
    loads = [load(attn_ref, attn), load(wo_ref, wo)]
    links.greet()

    def rows(ref, q):
        return ref.at[pl.ds(q * f, f), :]

    down = [to(links.seq, rows(wd_ref, q), rows(wd, q + 4)) for q in (1, 3)]
    gate_z = [to(links.batch, links.half(gate_ref, 0), rows(wg, 1)), to(links.both, links.half(gate_ref, 1), rows(wg, 3))]
    gates = [to(links.seq, rows(wg_ref, 2), rows(wg, 6))]
    up_t = to(links.across, links.half(up_ref, 1), rows(wu, 2))
    ups = []
    for copy in loads:
        copy.arrive()
    down += [load(rows(wd_ref, q), rows(wd, q)) for q in (1, 2, 3, 4, 6)]
    gates += [load(rows(wg_ref, q), rows(wg, q)) for q in (2, 4)]
    down.append(load(links.half(down_ref, 0), rows(wd, 0)))
    gates.append(load(links.half(gate_ref, 0), rows(wg, 0)))
    c_load = load(c_ref, c)
    up_own = load(links.half(up_ref, 0), rows(wu, 0))
    bufs = (p, core_in, out_y, in_y, out_t, in_t, hold)

    def out_partial(k):
        for m in range(2):
            at = (k * 2 + m) * attn.shape[0] // 4
            p[k, m] = nt(attn[at : at + attn.shape[0] // 4], wo[...]).astype(BF16).reshape(p.shape[2:])

    def while_out(stage):
        if stage == 0:
            ups.append(to(links.seq, links.half(up_ref, 0), rows(wu, 4)))
        if stage == 1:
            up_t.arrive()
            ups.append(to(links.seq, rows(wu, 2), rows(wu, 6)))
            up_z.append(to(links.batch, links.half(up_ref, 0), rows(wu, 1)))

    up_z = []
    sum_in(links, bufs, chunk, out_partial, while_out)
    for m in range(2):
        middle = low_ref[m].astype(F32) + hold[m]
        middle_ref[m] = middle
        xm_s[m] = (middle * inverse_rms(middle) * gain_ref[...]).astype(BF16)

    def while_xm(stage):
        if stage == 0:
            up_z.append(to(links.both, links.half(up_ref, 1), rows(wu, 3)))
            for copy in (*down, c_load):
                copy.arrive()

            def step(i):
                at = pl.ds(pl.multiple_of(i * 512, 512), 512)
                dact[at, :] = nn(c[at, :], wd[...])

            loop(c.shape[0] // 512, step)
            for copy in gate_z:
                copy.arrive()
            gates.extend(to(links.seq, rows(wg, q), rows(wg, q + 4)) for q in (1, 3))
        if stage == 1:
            up_z[0].arrive()
            ups.append(to(links.seq, rows(wu, 1), rows(wu, 5)))
        if stage == 2:
            up_z[1].arrive()
            ups.append(to(links.seq, rows(wu, 3), rows(wu, 7)))

    spread_in(links, xm_s, xm, chunk, while_xm)
    for copy in gates:
        copy.arrive()

    def gate_step(i):
        at = pl.ds(pl.multiple_of(i * 256, 256), 256)
        gate[at, :] = nn(rows_of(xm, i), wg[...])

    loop(4, gate_step)
    up_own.arrive()
    for copy in ups:
        copy.arrive()

    def up_step(i):
        base = pl.multiple_of(i * 256, 256)
        up_tile[...] = nn(rows_of(xm, i), wu[...])

        def part(j):
            at, here = pl.ds(pl.multiple_of(base + j * 32, 32), 32), pl.ds(pl.multiple_of(j * 32, 32), 32)
            g, u, d = gate[at, :], up_tile[here, :], dact[at, :]
            sig = 1.0 / (1.0 + jnp.exp(-g))
            silu = g * sig
            act[at, :] = (silu * u).astype(BF16)
            dg[at, :] = (d * u * sig * (1.0 + g * (1.0 - sig))).astype(BF16)
            du[at, :] = (d * silu).astype(BF16)

        loop(8, part)

    loop(4, up_step)

    def c_cols(at, n):
        return c[:, pl.ds(at, n)]

    def xm_cols(at, n):
        return xm[:, :, :, :, :, pl.ds(at, n)].reshape(-1, n)

    def fold(away, into, *places):
        return {i: to(links.seq, rows(away, i), rows(into, i)) for i in places}

    def compute_away(a_cols, b_ref, away, *places):
        for i in places:
            away[pl.ds(i * f, f), :] = tn(a_cols((i + 4) * f, f), b_ref[...]).astype(BF16)

    def total(a_cols, b_ref, into, i):
        return tn(a_cols(i * f, f), b_ref[...]) + into[pl.ds(i * f, f), :].astype(F32)

    compute_away(c_cols, act, away_d, 1)
    folds_d = fold(away_d, fold_d, 1)
    folds_g = {}
    compute_away(c_cols, act, away_d, 3)

    def back_partial(k):
        def step(m):
            at = pl.ds(pl.multiple_of((k * 2 + m) * 256, 256), 256)
            value = nt(dg[at, :], wg[...]) + nt(du[at, :], wu[...])
            p[k, m] = value.astype(BF16).reshape(p.shape[2:])

        loop(2, step)
        if k == 1:
            folds_d.update(fold(away_d, fold_d, 3))

    def settle_d(i, target, dst):
        folds_d[i].arrive()
        send_d[pl.ds((i - 1) * f, f), :] = total(c_cols, act, fold_d, i).astype(BF16)
        to(target, rows(send_d, i - 1), dst)

    def while_back(stage):
        if stage == 0:
            compute_away(c_cols, act, away_d, 0, 2)
        if stage == 1:
            settle_d(1, links.batch, got_d_b_ref)
            folds_d.update(fold(away_d, fold_d, 2, 0))
            settle_d(3, links.both, rows(got_d_o_ref, 1))
            compute_away(xm_cols, dg, away_g, 1, 3)
            folds_g.update(fold(away_g, fold_g, 1))
        if stage == 2:
            folds_g.update(fold(away_g, fold_g, 3))
            compute_away(xm_cols, dg, away_g, 0, 2)

    sum_in(links, bufs, chunk, back_partial, while_back)
    for m in range(2):
        middle = middle_ref[m]
        grad = cot_ref[m].astype(F32) + norm_grad(hold[m], middle, gain_ref[...], gain_grad_ref, m)
        dmid_ref[m] = grad
        xm_s[m] = grad.astype(BF16)

    later = []

    def while_mid(stage):
        if stage == 0:
            folds_d[0].arrive()
            own_d[...] = total(c_cols, act, fold_d, 0)
            own_load = load(own_d, own_d_ref)
            later.append(own_load)
        if stage == 1:
            settle_d(2, links.across, rows(got_d_o_ref, 0))
            folds_g[1].arrive()
            send_g[pl.ds(0, f), :] = total(xm_cols, dg, fold_g, 1).astype(BF16)
            to(links.batch, rows(send_g, 0), got_g_b_ref)
            folds_g.update(fold(away_g, fold_g, 2, 0))

            def step(i):
                at = pl.ds(pl.multiple_of(i * 512, 512), 512)
                dact[at, :] = tn(xm_cols(pl.multiple_of(i * 512, 512), 512), du[...])

            loop(2, step)
            load(dact, keep_u_ref)
            for copy in folds_d.values():
                copy.sent()
            compute_away(xm_cols, du, away_d, 0, 1, 2, 3)
            load(away_d, away_u_ref)

            def step(i):
                at = pl.ds(pl.multiple_of(i * 256, 256), 256)
                p[i // 2, i % 2] = nt(act[at, :], wd[...]).astype(BF16).reshape(p.shape[2:])

            loop(4, step)
            load(p, mixed_ref)
        if stage == 2:
            folds_g[3].arrive()
            send_g[pl.ds(2 * f, f), :] = total(xm_cols, dg, fold_g, 3).astype(BF16)

    spread_in(links, xm_s, dall_ref, chunk, while_mid, in_vmem=False)
    folds_g[2].arrive()
    send_g[pl.ds(f, f), :] = total(xm_cols, dg, fold_g, 2).astype(BF16)
    load(send_g.at[pl.ds(f, 2 * f), :], send_g_ref)
    folds_g[0].arrive()
    later[0].arrive()
    own_d[...] = total(xm_cols, dg, fold_g, 0)
    load(own_d, own_g_ref)
    links.finish()


def middle_call(batch_mask, low, cot, gain, attn, w_out, cot_all, w_down, w_gate, params, collective_id):
    _, rows, width = low.shape
    tokens, columns = attn.shape
    ff = w_down.shape[1]
    f = w_down.shape[0] // 8
    share, full = (2, rows, width), (2, 2, 2, 2, rows, width)
    vmem, hbm = pl.BlockSpec(memory_space=pltpu.VMEM), pl.BlockSpec(memory_space=pltpu.HBM)
    like = jax.ShapeDtypeStruct
    return pl.pallas_call(
        functools.partial(middle_kernel, batch_mask=batch_mask, chunk=2 * width // 8),
        in_specs=[vmem] * 3 + [hbm] * 8,
        out_specs=[vmem] * 3 + [hbm] * 10,
        out_shape=[
            like(share, F32),
            like(share, F32),
            like((1, width), F32),
            like(full, BF16),
            like(full, BF16),
            like((f, ff), F32),
            like((f, ff), BF16),
            like((2 * f, ff), BF16),
            like((f, ff), BF16),
            like((2 * f, ff), BF16),
            like((f, ff), F32),
            like((4 * f, ff), F32),
            like((4 * f, ff), BF16),
        ],
        scratch_shapes=[
            pltpu.VMEM((tokens, columns), BF16),
            pltpu.VMEM((width, columns), BF16),
            pltpu.VMEM(full, BF16),
            pltpu.VMEM((4, *share), BF16),
            pltpu.VMEM((2, *share), BF16),
            pltpu.VMEM((2, *share), BF16),
            pltpu.VMEM(share, BF16),
            pltpu.VMEM(share, BF16),
            pltpu.VMEM(share, F32),
            pltpu.VMEM(share, BF16),
            pltpu.VMEM(full, BF16),
            pltpu.VMEM((tokens, width), BF16),
            *[pltpu.VMEM((width, ff), BF16)] * 3,
            *[pltpu.VMEM((tokens, ff), F32)] * 2,
            *[pltpu.VMEM((tokens, ff), BF16)] * 3,
            *[pltpu.VMEM((4 * f, ff), BF16)] * 4,
            pltpu.VMEM((f, ff), F32),
            pltpu.VMEM((3 * f, ff), BF16),
            pltpu.VMEM((3 * f, ff), BF16),
            pltpu.VMEM((256, ff), F32),
            pltpu.SemaphoreType.DMA((96,)),
            pltpu.SemaphoreType.DMA((96,)),
        ],
        compiler_params=pltpu.CompilerParams(
            collective_id=collective_id, has_side_effects=True, vmem_limit_bytes=60 * MIB
        ),
        cost_estimate=TINY_COST,
    )(low, cot, gain, attn, w_out, cot_all, w_down, w_gate, *params)


def block_of(n, batch_mask):
    blk = lax.axis_index("blk")
    return blk ^ ((n // 2) * batch_mask) ^ ((n % 2) << TENSOR_BIT)


def key_tokens(block, half):
    head = lax.axis_index("head")
    index = lax.broadcasted_iota(jnp.int32, (2 * half, 1), 0)
    return token_offset(head, index, half // 2) + block * (2 * half)


def query_tokens(block, half, lanes):
    head = lax.axis_index("head")
    index = lax.broadcasted_iota(jnp.int32, (1, lanes), 1) % (2 * half)
    return token_offset(head, index, half // 2) + block * (2 * half)


def head_rows(ref, i, heads, width):
    both = [ref[c, i] for c in range(2)]
    return jnp.concatenate([b[:, h * width : (h + 1) * width] for h in range(heads) for b in both], axis=0)


def attention_back(q, do, k, v, start, ot, l, dq, dk, dv, kt, acc, batch_mask, scaling):
    parts, _, blocks, half, width = k.shape
    heads = q.shape[-1] // width
    lanes = heads * 2 * half
    dk[...] = jnp.zeros_like(dk)
    dv[...] = jnp.zeros_like(dv)

    def turn(kb):
        kt[kb] = key_rows(k, kb // blocks, kb % blocks).T

    loop(parts * blocks, turn)

    def per_query(i):
        q_rows, do_rows = head_rows(q, i, heads, width), head_rows(do, i, heads, width)
        delta = jnp.sum(do_rows.astype(F32).T * ot[i], axis=0, keepdims=True)
        inverse, first = 1.0 / l[i], start[i]
        acc[...] = jnp.zeros_like(acc)
        q_block = block_of(i, batch_mask)

        def per_key(kb):
            part, block = kb // blocks, kb % blocks
            k_block = block_of(block, batch_mask) ^ (part << SEQ_BIT)

            def add(diagonal):
                tokens = key_tokens(k_block, half)
                allowed = tokens >= first
                if diagonal:
                    allowed = allowed & (tokens <= query_tokens(q_block, half, lanes))
                score = nt(key_rows(k, part, block), q_rows) * (scaling * LOG2E)
                prob = jnp.where(allowed, jnp.exp2(score), 0.0) * inverse
                d_prob = nt(key_rows(v, part, block), do_rows)
                d_score = (prob * (d_prob - delta)).astype(BF16)
                d_v, d_k = nn(prob.astype(BF16), do_rows), nn(d_score, q_rows) * scaling
                for c in range(2):
                    dv[part, c, block] += d_v[c * half : (c + 1) * half]
                    dk[part, c, block] += d_k[c * half : (c + 1) * half]
                acc[...] += nn(kt[kb], d_score)

            @pl.when(k_block < q_block)
            def _():
                add(False)

            @pl.when(k_block == q_block)
            def _():
                add(True)

        loop(parts * blocks, per_key)
        rows = acc[...].T * scaling
        for h in range(heads):
            for c in range(2):
                at = (h * 2 + c) * half
                dq[c, i, :, h * width : (h + 1) * width] = rows[at : at + half]

    loop(blocks, per_query)


def last_kernel(
    low_ref, middle_ref, dmid_ref, gain_ref, gain_m_grad_ref, gain_q_ref, gain_k_ref, start_ref, l_ref,
    dall_ref, wo_ref, attn_ref, q_ref, k_ref, v_ref, ot_ref, raw_ref, table_ref, wa_ref, xa_ref, mixed_ref,
    send_g_ref, keep_u_ref, away_u_ref,
    mixed_own_ref, mixed_got_ref, input_own_ref, input_got_ref, sums_ref,
    got_g_o_ref, own_u_ref, got_u_b_ref, got_u_o_ref, own_a_ref, got_a_b_ref, got_a_o_ref, own_o_ref, got_o_b_ref, got_o_o_ref,
    dall, wo, attn, q, do, k, v, ot, raw, table, wa, xa, dq, dk, dv, kt, acc, kv_out, kv_in, d_qkv,
    p, core_in, out_y, in_y, out_t, in_t, hold, m_near, m_core_in, m_out_y, m_in_y, m_out_t, m_in_t, m_hold,
    swap_m, swap_i, keep_u, fold_u, own_u, send_u, away_o, fold_o, own_o, send_o, away_a, fold_a, own_a, send_a,
    gains_qk, gain_a_grad, ring_out, ring_in, send, recv, *, batch_mask, bit_order, scaling, chunk,
):
    links = Links(send, recv, batch_mask)
    to, load = links.to, links.load
    f = own_u.shape[0]
    heads = q.shape[-1] // k.shape[-1]
    width = k.shape[-1]

    def rows(ref, i):
        return ref.at[pl.ds(i * f, f), :]

    first = [load(dall_ref, dall), load(wo_ref, wo), load(attn_ref, attn)]
    second = [load(a, b) for a, b in ((q_ref, q), (k_ref, k), (v_ref, v), (ot_ref, ot))]
    third = [load(a, b) for a, b in ((raw_ref, raw), (table_ref, table), (wa_ref, wa), (xa_ref, xa))]
    mixed_near, keep_load = load(mixed_ref.at[0], m_near.at[0]), load(keep_u_ref, keep_u)
    links.greet()

    def settle(src, dst_b, dst_o):
        to(links.batch, rows(src, 0), dst_b)
        to(links.both, rows(src, 2), rows(dst_o, 1))
        to(links.across, rows(src, 1), rows(dst_o, 0))

    to(links.both, rows(send_g_ref, 1), rows(got_g_o_ref, 1))
    to(links.across, rows(send_g_ref, 0), rows(got_g_o_ref, 0))
    folds_u = {i: to(links.seq, rows(away_u_ref, i), rows(fold_u, i)) for i in (1, 3)}
    for copy in (*first, *second):
        copy.arrive()

    def total_u(i):
        return keep_u[pl.ds(i * f, f), :] + fold_u[pl.ds(i * f, f), :].astype(F32)

    def settle_u(i, target, dst):
        folds_u[i].arrive()
        send_u[pl.ds((i - 1) * f, f), :] = total_u(i).astype(BF16)
        to(target, rows(send_u, i - 1), dst)

    def d_attn(i):
        at = pl.ds(pl.multiple_of(i * 256, 256), 256)
        value = nn(dall[at, :], wo[...]).astype(BF16)
        do[i // 2, pl.ds((i % 2) * 2, 2)] = value.reshape(2, 128, value.shape[1])

    def dall_cols(at, n):
        return dall[:, pl.ds(at, n)]

    def xa_cols(at, n):
        return xa[:, pl.ds(at, n)]

    def input_partial(c):
        def step(m):
            at = pl.ds(pl.multiple_of((c * 2 + m) * 256, 256), 256)
            pair = pl.ds(m * 2, 2)
            got = kv_in[at, :].astype(F32)
            cos, sin = table[at, : width // 2], table[at, width // 2 :]
            cos, sin = jnp.concatenate([cos, cos], axis=1), jnp.concatenate([-sin, sin], axis=1)
            for h in range(heads + 1):
                cut = slice(h * width, (h + 1) * width)
                if h < heads:
                    grad = dq[c, pair, :, cut].reshape(256, width)
                else:
                    grad = dk[0, c, pair].reshape(256, width) + got[:, :width]
                gain = (gain_q_ref if h < heads else gain_k_ref)[...]
                values = raw[at, cut]
                inverse = inverse_rms(values)
                normed = values * inverse
                turned = grad * cos - pltpu.roll(grad, width // 2, 1) * sin
                row = 0 if h < heads else 1
                gains_qk[row : row + 1, :] += jnp.sum(turned * normed, axis=0, keepdims=True)
                scaled = turned * gain
                mean = jnp.mean(scaled * normed, axis=-1, keepdims=True)
                d_qkv[at, cut] = (inverse * (scaled - normed * mean)).astype(BF16)
            d_qkv[at, (heads + 1) * width :] = (dv[0, c, pair].reshape(256, width) + got[:, width:]).astype(BF16)
            p[c, m] = nt(d_qkv[at, :], wa[...]).astype(BF16).reshape(p.shape[2:])

        loop(2, step)

    def while_input(stage):
        if stage == 0:
            away_rows(xa_cols, d_qkv, away_a)
            folds.extend(to(links.seq, rows(away_a, i), rows(fold_a, i)) for i in (1, 3, 0, 2))
        if stage == 1:
            folds[0].arrive()
            keep_rows(dall_cols, attn, fold_o, own_o, send_o)
            settle(send_o, got_o_b_ref, got_o_o_ref)
            load(own_o, own_o_ref)
            folds_u.update({i: to(links.seq, rows(away_u_ref, i), rows(fold_u, i)) for i in (2, 0)})

    folds = []

    def while_mixed(stage):
        if stage == 0:
            loop(4, d_attn)
            attention_back(q, do, k, v, start_ref, ot, l_ref, dq, dk, dv, kt, acc, batch_mask, scaling)
            kv_out[:, :width] = dk[1].reshape(-1, width).astype(BF16)
            kv_out[:, width:] = dv[1].reshape(-1, width).astype(BF16)
            folds.extend(
                to(links.seq, kv_out.at[pl.ds(i, 128), :], kv_in.at[pl.ds(i, 128), :])
                for i in range(0, kv_out.shape[0], 128)
            )
            keep_load.arrive()
            settle_u(1, links.batch, got_u_b_ref)
            settle_u(3, links.both, rows(got_u_o_ref, 1))
        if stage == 1:
            away_rows(dall_cols, attn, away_o)
            out_fold = to(links.seq, away_o, fold_o)
            for copy in (*folds, *third):
                copy.arrive()
            folds[:] = [out_fold]
            gains_qk[...] = jnp.zeros_like(gains_qk)
            sum_in(links, (p, core_in, out_y, in_y, out_t, in_t, hold), chunk, input_partial, while_input)
            for m in range(2):
                grad = dmid_ref[m] + norm_grad(hold[m], low_ref[m].astype(F32), gain_ref[...], gain_a_grad, m)
                store_ungrouped(grad, input_own_ref if m == 0 else swap_i, blk, bit_order)
            to(links.batch, swap_i, input_got_ref)
            for copy in folds:
                copy.arrive()
            keep_rows(xa_cols, d_qkv, fold_a, own_a, send_a)
            settle(send_a, got_a_b_ref, got_a_o_ref)
            load(own_a, own_a_ref)

    mixed_near.arrive()
    blk = lax.axis_index("blk")
    sum_in(links, (m_near, m_core_in, m_out_y, m_in_y, m_out_t, m_in_t, m_hold), chunk, None, while_mixed, mixed_ref.at[1])
    store_ungrouped(middle_ref[0] + m_hold[0], mixed_own_ref, blk, bit_order)
    store_ungrouped(middle_ref[1] + m_hold[1], swap_m, blk, bit_order)
    to(links.batch, swap_m, mixed_got_ref)
    settle_u(2, links.across, rows(got_u_o_ref, 0))
    folds_u[0].arrive()
    own_u[...] = total_u(0)
    load(own_u, own_u_ref)
    n = gain_a_grad.shape[1]
    store_ungrouped(gain_a_grad[...], sums_ref.at[:, pl.ds(0, n)], blk, bit_order)
    sums_ref[:, n : n + width] = gains_qk[0:1, :]
    sums_ref[:, n + width : n + 2 * width] = gains_qk[1:2, :]
    store_ungrouped(gain_m_grad_ref[...], sums_ref.at[:, pl.ds(n + 2 * width, n)], blk, bit_order)
    for i, target in enumerate((links.core, links.near, links.seq, links.across, links.batch)):
        ring_out[i] = sums_ref[...]
        to(target, ring_out.at[i], ring_in.at[i]).arrive()
        sums_ref[...] += ring_in[i]
    links.finish()


def last_call(batch_mask, bit_order, scaling, arrays, collective_id):
    low, dall, attn, q, k, raw, wa, away_u = (arrays[n] for n in ("low", "dall", "attn", "q", "k", "raw", "wa", "away_u"))
    _, rows, width = low.shape
    tokens, columns = attn.shape
    head_size = k.shape[-1]
    ff, f = away_u.shape[1], away_u.shape[0] // 4
    n_a = wa.shape[1]
    share, full, half_full = (2, rows, width), (2, 2, 2, 2, rows, width), (1, 2, 2, 2, rows, width)
    vmem, hbm = pl.BlockSpec(memory_space=pltpu.VMEM), pl.BlockSpec(memory_space=pltpu.HBM)
    like, held = jax.ShapeDtypeStruct, pltpu.VMEM
    in_vmem = ("low", "middle", "d_middle", "gain", "gain_m_grad", "gain_q", "gain_k", "start", "l")
    in_hbm = (
        "dall", "w_out", "attn", "q", "k", "v", "ot", "raw", "table", "wa", "xa", "mixed", "send_g", "keep_u", "away_u",
    )
    total = 2 * width + 2 * head_size
    lanes = 2 * 2 * 128
    sums = (1, total)
    own_and_send = lambda n: [held((f, n), F32), held((3 * f, n), BF16)]
    sum_bufs = [
        held((4, *share), BF16), held((2, *share), BF16), held((2, *share), BF16), held(share, BF16), held(share, BF16),
    ]
    return pl.pallas_call(
        functools.partial(last_kernel, batch_mask=batch_mask, bit_order=bit_order, scaling=scaling, chunk=2 * width // 8),
        in_specs=[vmem] * len(in_vmem) + [hbm] * len(in_hbm),
        out_specs=[vmem, hbm, vmem, hbm, vmem] + [hbm] * 10,
        out_shape=[
            like((rows, width), BF16),
            like((rows, width), BF16),
            like((rows, width), F32),
            like((rows, width), BF16),
            like(sums, F32),
            like((2 * f, ff), BF16),
            *[
                like((m * f, n), dtype)
                for n in (ff, n_a, columns)
                for m, dtype in ((1, F32), (1, BF16), (2, BF16))
            ],
        ],
        scratch_shapes=[
            held((tokens, width), BF16),
            held((width, columns), BF16),
            held((tokens, columns), BF16),
            held(q.shape, BF16),
            held(q.shape, BF16),
            held(k.shape, BF16),
            held(k.shape, BF16),
            held((4, head_size, lanes), F32),
            held(raw.shape, F32),
            held((tokens, head_size), F32),
            held(wa.shape, BF16),
            held((tokens, width), BF16),
            held(q.shape, F32),
            held(k.shape, F32),
            held(k.shape, F32),
            held((8, head_size, 256), BF16),
            held((head_size, lanes), F32),
            held((tokens, 2 * head_size), BF16),
            held((tokens, 2 * head_size), BF16),
            held((tokens, n_a), BF16),
            held(full, BF16),
            *sum_bufs,
            held(share, F32),
            held(half_full, BF16),
            *sum_bufs,
            held(share, F32),
            held((rows, width), BF16),
            held((rows, width), BF16),
            held((4 * f, ff), F32),
            held((4 * f, ff), BF16),
            *own_and_send(ff),
            held((4 * f, columns), BF16),
            held((4 * f, columns), BF16),
            *own_and_send(columns),
            held((4 * f, n_a), BF16),
            held((4 * f, n_a), BF16),
            *own_and_send(n_a),
            held((8, head_size), F32),
            held((1, width), F32),
            held((5, *sums), F32),
            held((5, *sums), F32),
            pltpu.SemaphoreType.DMA((96,)),
            pltpu.SemaphoreType.DMA((96,)),
        ],
        compiler_params=pltpu.CompilerParams(
            collective_id=collective_id, has_side_effects=True, vmem_limit_bytes=60 * MIB
        ),
        cost_estimate=TINY_COST,
    )(*[arrays[n] for n in (*in_vmem, *in_hbm)])


def attention(q, k, v, start, out, ot, total_ref, vt, acc, total, batch_mask, scaling):
    parts, _, blocks, half, width = k.shape
    heads = q.shape[-1] // width
    lanes = heads * 2 * half

    def turn(kb):
        vt[kb] = key_rows(v, kb // blocks, kb % blocks).T

    loop(parts * blocks, turn)

    def per_query(i):
        q_rows = head_rows(q, i, heads, width)
        first = start[i]
        acc[...] = jnp.zeros_like(acc)
        total[...] = jnp.zeros_like(total)
        q_block = block_of(i, batch_mask)

        def per_key(kb):
            part, block = kb // blocks, kb % blocks
            k_block = block_of(block, batch_mask) ^ (part << SEQ_BIT)

            def add(diagonal):
                tokens = key_tokens(k_block, half)
                allowed = tokens >= first
                if diagonal:
                    allowed = allowed & (tokens <= query_tokens(q_block, half, lanes))
                score = nt(key_rows(k, part, block), q_rows) * (scaling * LOG2E)
                e = jnp.where(allowed, jnp.exp2(score), 0.0)
                total[...] += jnp.sum(e, axis=0, keepdims=True)
                acc[...] += nn(vt[kb], e.astype(BF16))

            @pl.when(k_block < q_block)
            def _():
                add(False)

            @pl.when(k_block == q_block)
            def _():
                add(True)

        loop(parts * blocks, per_key)
        value = acc[...] / total[...]
        ot[i] = value
        total_ref[i] = total[...]
        rows = value.T
        for h in range(heads):
            for c in range(2):
                at = (h * 2 + c) * half
                out[c, i, :, h * width : (h + 1) * width] = rows[at : at + half].astype(BF16)

    loop(blocks, per_query)


def first_kernel(
    gains_ref, gain_q_ref, gain_k_ref, table_ref, start_ref,
    hid_ref, cot_ref, wq_ref, wk_ref, wv_ref, wo_ref, wd_ref, wg_ref,
    low_ref, cot_low_ref, gains_out_ref, l_ref,
    xa_ref, call_ref, wa_out, wo_out, wd_out, wg_out, q_ref, k_ref, v_ref, raw_ref, attn_ref, ot_ref,
    x_in, c_in, xa_s, xa, wa, wb, q, k, v, raw, out, ot, vt, acc, total, send, recv, *, batch_mask, bit_order, scaling, chunk,
):
    links = Links(send, recv, batch_mask)
    to, load = links.to, links.load
    blk = lax.axis_index("blk")
    batch = bit_of(blk, bit_order[0])
    width = k.shape[-1]
    heads = q.shape[-1] // width
    f = wa.shape[0] // 8
    a_params, at = [], 0
    for ref in (wq_ref, wk_ref, wv_ref):
        n = ref.shape[1] // 2
        a_params.append((ref, at, n))
        at += n

    def rows(ref, i):
        return ref.at[pl.ds(i * f, f), :]

    x_own = load(hid_ref.at[batch], x_in.at[0])
    c_own = load(cot_ref.at[batch], c_in.at[0])
    a_own = [load(links.half(ref, 0), wa.at[pl.ds(0, f), pl.ds(start, n)]) for ref, start, n in a_params]
    a_other = [load(links.half(ref, 1), wb.at[:, pl.ds(start, n)]) for ref, start, n in a_params]
    links.greet()
    x_far = to(links.batch, hid_ref.at[1 - batch], x_in.at[1])
    for copy in (*a_own, *a_other):
        copy.arrive()
    a_t = to(links.across, wb, rows(wa, 2))
    a_rest = [to(links.seq, rows(wa, 0), rows(wa, 4))]
    to(links.seq, links.half(wo_ref, 0), rows(wo_out, 4))
    load(links.half(wo_ref, 0), rows(wo_out, 0))
    to(links.seq, links.half(wd_ref, 0), rows(wd_out, 4))
    to(links.seq, links.half(wg_ref, 0), rows(wg_out, 4))
    down_t, out_rows = [], []
    n_blocks = 1 << len(bit_order)
    n = x_in.shape[-1] // n_blocks

    def regroup(src, dst, lead):
        for p in range(n_blocks):
            cut = pl.ds(pl.multiple_of(place_of_block(blk, bit_order, p) * n, n), n)
            dst[(*lead, pl.ds(p * n, n))] = src[(*lead, cut)]

    all_rows = (slice(None), slice(None))
    regroup(gains_ref, gains_out_ref, (slice(None),))
    x_own.arrive()
    x_far.arrive()
    a_far = {1: to(links.batch, rows(wa, 0), rows(wa, 1)), 3: to(links.both, wb, rows(wa, 3))}
    c_far = to(links.batch, cot_ref.at[1 - batch], c_in.at[1])
    regroup(x_in, low_ref, all_rows)
    for m in range(2):
        value = low_ref[m].astype(F32)
        xa_s[m] = (value * inverse_rms(value) * gains_out_ref[0:1, :]).astype(BF16)

    def while_xa(stage):
        if stage == 0:
            a_t.arrive()
            a_rest.append(to(links.seq, rows(wa, 2), rows(wa, 6)))
        if stage == 1:
            down_t.append(to(links.across, links.half(wd_ref, 1), rows(wd_out, 2)))
            out_rows.append(to(links.across, links.half(wo_ref, 1), rows(wo_out, 2)))
            for i, copy in a_far.items():
                copy.arrive()
                a_rest.append(to(links.seq, rows(wa, i), rows(wa, i + 4)))
            out_rows.append(to(links.batch, links.half(wo_ref, 0), rows(wo_out, 1)))
            out_rows.append(to(links.both, links.half(wo_ref, 1), rows(wo_out, 3)))
            to(links.both, links.half(wd_ref, 1), rows(wd_out, 3))
            to(links.batch, links.half(wd_ref, 0), rows(wd_out, 1))
            c_own.arrive()
            c_far.arrive()
            regroup(c_in, cot_low_ref, all_rows)

    spread_in(links, xa_s, xa, chunk, while_xa)
    load(xa, xa_ref)

    def prepare_rows(i):
        c, m = i // 2, i % 2
        pair = pl.ds(m * 2, 2)
        at = pl.ds(pl.multiple_of(i * 256, 256), 256)
        acc_rows = nn(rows_of(xa, i), wa[...])
        raw[at, :] = acc_rows[:, : (heads + 1) * width]
        cos, sin = table_ref[at, : width // 2], table_ref[at, width // 2 :]
        cos, sin = jnp.concatenate([cos, cos], axis=1), jnp.concatenate([-sin, sin], axis=1)
        for h in range(heads + 1):
            part = acc_rows[:, h * width : (h + 1) * width]
            scaled = part * inverse_rms(part) * (gain_q_ref if h < heads else gain_k_ref)[...]
            turned = (scaled * cos + pltpu.roll(scaled, width // 2, 1) * sin).astype(BF16).reshape(2, 128, width)
            if h < heads:
                q[c, pair, :, h * width : (h + 1) * width] = turned
            else:
                k[0, c, pair] = turned
        v[0, c, pair] = acc_rows[:, (heads + 1) * width :].astype(BF16).reshape(2, 128, width)

    kv = []

    def while_cot(stage):
        if stage == 0:
            for copy in a_rest:
                copy.arrive()
            loop(4, prepare_rows)
            kv.extend(
                to(links.seq, ref.at[0, c, i], ref.at[1, c, i]) for ref in (k, v) for c in range(2) for i in range(4)
            )
            load(wa, wa_out)
            load(raw, raw_ref)
            load(q, q_ref)
            down_t[0].arrive()
            to(links.seq, rows(wd_out, 2), rows(wd_out, 6))
        if stage == 1:
            to(links.across, links.half(wg_ref, 1), rows(wg_out, 2))
            for i, copy in zip((2, 1, 3), out_rows):
                copy.arrive()
                to(links.seq, rows(wo_out, i), rows(wo_out, i + 4))
            for copy in kv:
                copy.arrive()
            load(k, k_ref)
            load(v, v_ref)
            attention(q, k, v, start_ref, out, ot, l_ref, vt, acc, total, batch_mask, scaling)
            load(out, attn_ref)
            load(ot, ot_ref)

    spread_in(links, cot_low_ref, call_ref, chunk, while_cot, in_vmem=False)
    links.finish()


def first_call(batch_mask, bit_order, scaling, arrays, collective_id):
    hid, wq, wk, wv, wo, wd, wg = (arrays[n] for n in ("hidden", "wq", "wk", "wv", "wo", "wd", "wg"))
    _, rows, width = hid.shape
    tokens, head_size = 16 * rows, arrays["gain_q"].shape[1]
    columns, n_a = wq.shape[1] // 2, (wq.shape[1] + wk.shape[1] + wv.shape[1]) // 2
    heads = columns // head_size
    half, lanes = tokens // 8, heads * tokens // 4
    share, full = (2, rows, width), (2, 2, 2, 2, rows, width)
    vmem, hbm = pl.BlockSpec(memory_space=pltpu.VMEM), pl.BlockSpec(memory_space=pltpu.HBM)
    like, held = jax.ShapeDtypeStruct, pltpu.VMEM
    in_vmem = ("gains", "gain_q", "gain_k", "table", "start")
    in_hbm = ("hidden", "cotangent", "wq", "wk", "wv", "wo", "wd", "wg")
    q_shape, k_shape = (2, 4, half, columns), (2, 2, 4, half, head_size)
    ot_shape, raw_shape = (4, head_size, lanes), (tokens, (heads + 1) * head_size)
    return pl.pallas_call(
        functools.partial(first_kernel, batch_mask=batch_mask, bit_order=bit_order, scaling=scaling, chunk=2 * width // 8),
        in_specs=[vmem] * len(in_vmem) + [hbm] * len(in_hbm),
        out_specs=[vmem] * 4 + [hbm] * 12,
        out_shape=[
            like(share, BF16),
            like(share, BF16),
            like((2, width), F32),
            like((4, 1, lanes), F32),
            like(full, BF16),
            like(full, BF16),
            like((width, n_a), BF16),
            like((width, columns), BF16),
            like((width, wd.shape[1] // 2), BF16),
            like((width, wg.shape[1] // 2), BF16),
            like(q_shape, BF16),
            like(k_shape, BF16),
            like(k_shape, BF16),
            like(raw_shape, F32),
            like(q_shape, BF16),
            like(ot_shape, F32),
        ],
        scratch_shapes=[
            held(share, BF16),
            held(share, BF16),
            held(share, BF16),
            held(full, BF16),
            held((width, n_a), BF16),
            held((width // 8, n_a), BF16),
            held(q_shape, BF16),
            held(k_shape, BF16),
            held(k_shape, BF16),
            held(raw_shape, F32),
            held(q_shape, BF16),
            held(ot_shape, F32),
            held((8, head_size, 2 * half), BF16),
            held((head_size, lanes), F32),
            held((1, lanes), F32),
            pltpu.SemaphoreType.DMA((96,)),
            pltpu.SemaphoreType.DMA((96,)),
        ],
        compiler_params=pltpu.CompilerParams(
            collective_id=collective_id, has_side_effects=True, vmem_limit_bytes=56 * MIB
        ),
        cost_estimate=TINY_COST,
    )(*[arrays[n] for n in (*in_vmem, *in_hbm)])


def finish_kernel(place_ref, mixed_own, mixed_got, input_own, input_got, *refs, sources, widths):
    ins, (mixed_ref, input_ref, *outs) = refs[: 3 * sources], refs[3 * sources :]
    place, batch, k = place_ref[0], place_ref[1], 0
    mixed_ref[batch] = mixed_own[...]
    mixed_ref[1 - batch] = mixed_got[...]
    input_ref[batch] = input_own[...]
    input_ref[1 - batch] = input_got[...].astype(F32)
    for own, by_batch, by_other in zip(ins[::3], ins[1::3], ins[2::3]):
        at = 0
        while at < own.shape[1]:
            w, cut = widths[k], slice(at, at + widths[k])
            mine = pl.ds(pl.multiple_of(place * w, w), w)
            theirs = pl.ds(pl.multiple_of((1 - place) * w, w), w)
            outs[k][:, mine] = own[:, cut] + by_batch[:, cut].astype(F32)
            outs[k][:, theirs] = by_other[0, :, cut].astype(F32) + by_other[1, :, cut].astype(F32)
            at += w
            k += 1


def finish_call(places, rows, sources, widths):
    steps = 4
    f, (n_rows, width) = sources[0][0].shape[0], rows[0].shape
    tile, row_tile = f // steps, n_rows // steps
    by_rows = lambda t, n: pl.BlockSpec((t, n), lambda i: (i, 0))
    by_pairs = lambda t, n: pl.BlockSpec((2, t, n), lambda i: (0, i, 0))
    flat, specs = [], []
    for own, by_batch, by_other in sources:
        n = own.shape[1]
        flat += [own, by_batch, by_other.reshape(2, f, n)]
        specs += [by_rows(tile, n), by_rows(tile, n), by_pairs(tile, n)]
    like = jax.ShapeDtypeStruct
    return pl.pallas_call(
        functools.partial(finish_kernel, sources=len(sources), widths=widths),
        grid=(steps,),
        in_specs=[pl.BlockSpec(memory_space=pltpu.SMEM), *[by_rows(row_tile, width)] * 4, *specs],
        out_specs=[*[by_pairs(row_tile, width)] * 2, *[by_rows(tile, 2 * w) for w in widths]],
        out_shape=[
            like((2, n_rows, width), BF16),
            like((2, n_rows, width), F32),
            *[like((f, 2 * w), F32) for w in widths],
        ],
        compiler_params=pltpu.CompilerParams(vmem_limit_bytes=60 * MIB),
        cost_estimate=TINY_COST,
    )(places.astype(jnp.int32), *rows, *flat)


def local(
    hidden_in,
    lengths,
    query_weight,
    key_matrix,
    value_matrix,
    out_weight,
    gate_weight,
    up_weight,
    down_weight,
    attn_gain,
    query_gain,
    key_gain,
    mlp_gain,
    cotangent,
):
    ring = lax.axis_size("blk")
    bits = ring.bit_length() - 1
    batch_bit = bits - 1
    extra_bits = [i for i in range(bits) if i not in (TENSOR_BIT, SEQ_BIT, batch_bit)]
    seq_bits = [SEQ_BIT, *extra_bits]
    parts = 1 << len(seq_bits)
    bit_order = [batch_bit, TENSOR_BIT, SEQ_BIT, *extra_bits]
    b_mask, t_mask, x_mask = 1 << batch_bit, 1 << TENSOR_BIT, 1 << SEQ_BIT
    blk, head = lax.axis_index("blk"), lax.axis_index("head")
    batch, tensor = bit_of(blk, batch_bit), bit_of(blk, TENSOR_BIT)

    local_rows, width = hidden_in.shape[1:]
    block_rows = local_rows * lax.axis_size("head")
    half = block_rows // 2
    row_features = width // ring
    head_size = query_gain.shape[0]
    scaling = head_size ** (-0.5)
    tokens = 16 * local_rows
    heads = query_weight.shape[1] // (2 * head_size)
    ff = gate_weight.shape[1] // 2

    def moved(values, place_of):
        axis = values.ndim - 1
        return jnp.concatenate(
            [
                lax.dynamic_slice_in_dim(values, place_of(i) * row_features, row_features, axis)
                for i in range(ring)
            ],
            axis=axis,
        )

    def regroup(values):
        return moved(values, lambda p: blk ^ sum(((p >> i) & 1) << b for i, b in enumerate(bit_order)))

    def ungroup(values):
        return moved(values, lambda n: sum(bit_of(blk ^ n, b) << i for i, b in enumerate(bit_order)))

    def everything(ref):
        return ref

    def mask_of(p):
        return sum(((p >> i) & 1) << b for i, b in enumerate(bit_order))

    def rows_at(p):
        return lambda ref: ref.at[pl.ds(p * row_features, row_features), :]

    def half_cut(n, other):
        def cut(ref):
            place = bit_of(lax.axis_index("blk"), TENSOR_BIT)
            place = 1 - place if other else place
            return ref.at[:, pl.ds(pl.multiple_of(place * n, n), n)]

        return cut

    def send_over(plan, weight, buffer, p, point):
        mask, n = mask_of(p), weight.shape[1] // 2
        plan.copy((plan.read(weight), half_cut(n, mask & t_mask)), (buffer, rows_at(p)), mask, point=point)

    def keep_own(plan, weight, buffer, point, onward=True):
        here, n = plan.read(weight), weight.shape[1] // 2
        if onward:
            plan.copy((here, half_cut(n, 0)), (buffer, rows_at(4)), x_mask, point=point)
        plan.local((here, half_cut(n, 0)), (buffer, rows_at(0)), (row_features, n), point=point)

    def send_on(plan, buffer, places, point, after=None):
        for p in places:
            plan.copy((buffer, rows_at(p)), (buffer, rows_at(p + 4)), x_mask, after=after, point=point)

    def lay(plan, array, buffer, p, point=0, columns=None, onward=False):
        here = plan.read(array)
        cut = (lambda ref: ref.at[:, pl.ds(*columns)]) if columns else everything
        if onward:
            plan.copy((here, cut), (buffer, rows_at(p + 4)), x_mask, point=point)
        plan.local((here, cut), (buffer, rows_at(p)), (row_features, columns[1] if columns else array.shape[1]), point)

    def fresh_for(plan, weights):
        return plan.fresh(buffer_shape(weights), BF16)

    def buffer_shape(weights):
        return (8 * row_features, sum(w.shape[1] for w in weights) // 2)

    def whole_weight(buffer):
        pieces = [buffer]
        for b in extra_bits:
            pieces = pieces + [over_blk(c, 1 << b) for c in pieces]
        return jnp.concatenate(pieces, axis=0) if extra_bits else buffer

    def split_grad(grad):
        for b in reversed(extra_bits):
            n = grad.shape[0] // 2
            grad = grad[:n] + over_blk(grad[n:].astype(BF16), 1 << b).astype(F32)
        n = grad.shape[0] // 2
        return grad[:n], grad[n:].astype(BF16)

    def weight_sum(a, b):
        return split_grad(tn(a, b)) if extra_bits else weight_grad(a, b)

    def fold(plan, source, shape, point=0):
        plan.copy((source, everything), (plan.fresh(shape, BF16), everything), x_mask, point=point)

    def fold_part(plan, source, buffer, start, n, point=0):
        def part(ref):
            return ref.at[:, pl.ds(start, n)]

        plan.copy((source, part), (buffer, part), x_mask, point=point)

    def to_settle(keep, got):
        total = keep + got.astype(F32)
        return total[:row_features], total[row_features:].astype(BF16)

    def settle(plan, away, t_point=0):
        out, here = plan.fresh(away.shape, away.dtype), plan.read(away)
        for i, mask in ((0, b_mask), (2, b_mask | t_mask), (1, t_mask)):
            plan.copy((here, rows_at(i)), (out, rows_at(i)), mask, point=t_point if mask == t_mask else 0)

    def settled(sources, column_widths):
        if all(w % 128 == 0 for w in column_widths):
            return assemble(tensor, sources, column_widths)
        f, results = row_features, []
        widths = iter(column_widths)
        for own, got in sources:
            own = own + got[:f].astype(F32)
            other = got[f : 2 * f].astype(F32) + got[2 * f :].astype(F32)
            at = 0
            while at < own.shape[1]:
                w = next(widths)
                results.append(in_order(tensor, own[:, at : at + w], other[:, at : at + w], 1))
                at += w
        return results

    chunk = 2 * row_features
    ids = iter(range(100))

    def spread(flat, plan, fills=(), limit=None):
        (out,), rest = run(plan, spread_main(flat, chunk), next(ids), fills=fills, limit=limit)
        return out.reshape(tokens, width), rest

    share = (2, local_rows, width)

    def gather_sum(partial, plan, extra, outs_like, finish, fills=()):
        return run(plan, gather_main(partial, chunk, extra, outs_like, finish), next(ids), fills=fills)

    def like(shape, dtype):
        return jax.ShapeDtypeStruct(shape, dtype)

    aligned = row_features % 128 == 0
    local_order = bit_order if aligned else []

    def split_batch(rows):
        mine = lax.dynamic_index_in_dim(rows, batch, 0, keepdims=False)
        theirs = lax.dynamic_index_in_dim(rows, 1 - batch, 0, keepdims=False)
        return mine, theirs

    def natural(rows):
        return rows if aligned else ungroup(rows)

    length_row = lax.dynamic_index_in_dim(lengths, batch, 0, keepdims=False)
    doc_ends = jnp.cumsum(length_row)
    batch_flip = jnp.arange(2, dtype=jnp.int32)[:, None] << batch_bit
    tensor_flip = jnp.arange(2, dtype=jnp.int32)[None, :] << TENSOR_BIT
    q_blocks = (blk ^ batch_flip ^ tensor_flip).reshape(4)
    index = jnp.arange(2 * half, dtype=jnp.int32)
    in_block = token_offset(head, index, local_rows).reshape(2, 1, half)
    token_index = q_blocks[None, :, None] * block_rows + in_block
    passed = doc_ends <= token_index[..., None]
    doc_start = jnp.max(jnp.where(passed, doc_ends, 0), axis=-1).astype(jnp.int32)
    position = (token_index - doc_start).reshape(tokens)
    start_lanes = jnp.tile(jnp.transpose(doc_start, (1, 0, 2)).reshape(4, 1, 2 * half), (1, 1, heads))
    k_blocks = q_blocks
    for b in seq_bits:
        k_blocks = jnp.concatenate([k_blocks, k_blocks ^ (1 << b)])
    least_start = jnp.min(doc_start, axis=(0, 2))[:, None]
    last_start = jnp.max(doc_start, axis=(0, 2))[:, None]
    k_first = (k_blocks * block_rows)[None, :]
    none = (k_blocks[None, :] > q_blocks[:, None]) | (k_first + block_rows <= least_start)
    whole = (k_blocks[None, :] < q_blocks[:, None]) & (k_first >= last_start)
    flags = jnp.where(none, 0, jnp.where(whole, 1, 2))
    meta = jnp.concatenate([head[None], q_blocks, k_blocks, flags.reshape(-1)]).astype(jnp.int32)

    inverse_freq = THETA ** (-jnp.arange(head_size // 2, dtype=F32) / (head_size // 2))
    angles = position.astype(F32)[:, None] * inverse_freq[None, :]
    cosine, sine = jnp.cos(angles), jnp.sin(angles)
    table = jnp.concatenate([cosine, sine], axis=1)
    cosine = jnp.concatenate([cosine, cosine], axis=1)
    sine = jnp.concatenate([-sine, sine], axis=1)

    def rms(values):
        return lax.rsqrt(jnp.mean(values * values, axis=-1, keepdims=True) + EPS)

    def norm_back(grad, normed, inverse, gain):
        scaled = grad * gain
        return inverse * (scaled - normed * jnp.mean(scaled * normed, axis=-1, keepdims=True))

    gains_in = jnp.stack([attn_gain, mlp_gain]).astype(F32)
    gain_q = query_gain.astype(F32)[None]
    gain_k = key_gain.astype(F32)[None]

    q_columns, k_columns = heads * head_size, head_size
    a_weights = (query_weight, key_matrix, value_matrix)

    def halves(weights, which):
        return jnp.concatenate(
            [lax.dynamic_slice_in_dim(w, which * (w.shape[1] // 2), w.shape[1] // 2, 1) for w in weights], axis=1
        )

    if extra_bits:
        mine, theirs = split_batch(hidden_in)
        other = over_blk(theirs, b_mask)
        a_own, a_other = halves(a_weights, tensor), halves(a_weights, 1 - tensor)
        a_by_t = over_blk(a_other, t_mask)
        a_by_b = over_blk(a_own, b_mask)
        early = over_blk(jnp.concatenate([a_own, halves((down_weight,), tensor)], axis=1), x_mask)
        (mine, other, cosine, sine, start_lanes, meta) = pin((mine, other, cosine, sine, start_lanes, meta))
        if aligned:
            x_low, xa, gains_in = enter(blk, bit_order, mine, other, gains_in)
            gain_a, gain_m = gains_in[0], gains_in[1]
        else:
            gains_in = regroup(gains_in)
            gain_a, gain_m = gains_in[0], gains_in[1]
            x_low = regroup(jnp.concatenate([mine, other], axis=0))
            x_wide = x_low.astype(F32)
            xa = (x_wide * rms(x_wide) * gain_a).astype(BF16)

        plan = Plan()
        a_columns = a_own.shape[1]
        w_a = fresh_for(plan, a_weights)
        by_tb = plan.copy((plan.read(a_other), everything), (w_a, rows_at(3)), b_mask | t_mask)
        lay(plan, a_by_t, w_a, 2, onward=True)
        lay(plan, a_by_b, w_a, 1, onward=True)
        lay(plan, a_own, w_a, 0)
        lay(plan, early, w_a, 4, columns=(0, a_columns))
        here, cot_out = plan.read(cotangent), plan.fresh((2, local_rows, width), BF16)
        plan.copy(
            (here, lambda ref: ref.at[1 - bit_of(lax.axis_index("blk"), batch_bit)]),
            (cot_out, lambda ref: ref.at[1]),
            b_mask,
            point=1,
        )
        plan.local(
            (here, lambda ref: ref.at[bit_of(lax.axis_index("blk"), batch_bit)]),
            (cot_out, lambda ref: ref.at[0]),
            (local_rows, width),
        )
        w_out = fresh_for(plan, (out_weight,))
        send_over(plan, out_weight, w_out, 1, 1)
        send_over(plan, out_weight, w_out, 3, 1)
        send_over(plan, out_weight, w_out, 2, 1)
        keep_own(plan, out_weight, w_out, 0)
        w_down = fresh_for(plan, (down_weight,))
        send_over(plan, down_weight, w_down, 2, 1)
        keep_own(plan, down_weight, w_down, 0, onward=False)
        lay(plan, early, w_down, 4, columns=(a_columns, ff))
        w_gate = fresh_for(plan, (gate_weight,))
        keep_own(plan, gate_weight, w_gate, 1)
        send_on(plan, w_a, (3,), 2, after=by_tb)
        xa, (w_qkv, cot, w_out, w_down, w_gate) = spread(xa, plan, limit=56 * MIB)
        w_qkv = whole_weight(w_qkv)
        cot = cot.reshape(2 * local_rows, width)
        cot = enter(blk, bit_order, cot)[0] if aligned else regroup(cot)
        query, key_value, raw = prepare(xa, w_qkv, cosine, sine, gain_q, gain_k, heads)

        plan = Plan()
        kv_out = plan.fresh(key_value.shape, BF16)
        plan.copy((plan.read(key_value), everything), (kv_out, everything), x_mask)
        w_out = plan.through(w_out)
        send_on(plan, w_out, (1, 2, 3), 0)
        w_down = plan.through(w_down)
        send_over(plan, down_weight, w_down, 1, 0)
        send_over(plan, down_weight, w_down, 3, 0)
        send_on(plan, w_down, (2,), 1)
        w_gate = plan.through(w_gate)
        send_over(plan, gate_weight, w_gate, 2, 1)
        cot_all, (kv_x, w_out, w_down, w_gate) = spread(cot, plan)
        w_out = whole_weight(w_out)
        key_value = [key_value, kv_x]
        for b in extra_bits:
            key_value = key_value + [over_blk(c, 1 << b) for c in key_value]
        key_value = jnp.stack(key_value)
        keys = key_value[..., :head_size].reshape(parts, 2, 4, half, head_size)
        values = key_value[..., head_size:].reshape(parts, 2, 4, half, head_size)
        query = query.reshape(2, 4, half, q_columns)
        attn, attn_t, total_e = attend(meta, query, keys, values, start_lanes, scaling)
        attn = attn.reshape(tokens, q_columns)

        x_low = x_low.reshape(share)
    else:
        (
            x_low, cot, gains_group, total_e, xa, cot_all, w_qkv, w_out, w_down, w_gate, query, keys, values, raw, attn, attn_t,
        ) = first_call(
            b_mask,
            bit_order,
            scaling,
            dict(
                gains=gains_in,
                gain_q=gain_q,
                gain_k=gain_k,
                table=table,
                start=start_lanes,
                hidden=hidden_in,
                cotangent=cotangent,
                wq=query_weight,
                wk=key_matrix,
                wv=value_matrix,
                wo=out_weight,
                wd=down_weight,
                wg=gate_weight,
            ),
            next(ids),
        )
        gain_a, gain_m = gains_group[0], gains_group[1]
        xa, cot_all = xa.reshape(tokens, width), cot_all.reshape(tokens, width)
        attn = attn.reshape(tokens, q_columns)

    if extra_bits:
        plan = Plan()
        w_down = plan.through(w_down)
        send_on(plan, w_down, (1, 3), 0)
        w_gate = plan.through(w_gate)
        send_over(plan, gate_weight, w_gate, 1, 0)
        send_over(plan, gate_weight, w_gate, 3, 0)
        send_on(plan, w_gate, (2,), 0)
        w_up = fresh_for(plan, (up_weight,))
        send_over(plan, up_weight, w_up, 2, 0)
        keep_own(plan, up_weight, w_up, 1)
        (middle, xm), (w_down, w_gate, w_up) = gather_sum(
            nt(attn, w_out).astype(BF16),
            plan,
            [x_low, gain_m[None]],
            [like(share, F32), like(share, BF16)],
            finish_middle,
        )
        w_down = whole_weight(w_down)

        plan = Plan()
        w_gate = plan.through(w_gate)
        w_up = plan.through(w_up)
        by_b = len(plan.jobs)
        send_over(plan, up_weight, w_up, 1, 0)
        send_on(plan, w_gate, (1, 3), 0)
        send_on(plan, w_up, (2,), 1)
        by_tb = plan.copy(
            (plan.read(up_weight), half_cut(ff, True)), (w_up, rows_at(3)), b_mask | t_mask, after=by_b, point=2
        )
        send_on(plan, w_up, (1,), 2)
        send_on(plan, w_up, (3,), 3, after=by_tb)
        xm, (w_gate, w_up, d_active) = spread(
            xm.reshape(2 * local_rows, width), plan, [fill_product(cot_all, w_down, 0)]
        )
        w_gate, w_up = whole_weight(w_gate), whole_weight(w_up)
        gate = nn(xm, w_gate)
        up = nn(xm, w_up)
        sig = jax.nn.sigmoid(gate)
        silu = gate * sig
        active = (silu * up).astype(BF16)
        d_gate = (d_active * up * sig * (1.0 + gate * (1.0 - sig))).astype(BF16)
        d_up = (d_active * silu).astype(BF16)

        keep_down, away_down = weight_sum(cot_all, active)
        got_x = over_blk(away_down, x_mask)
        (d_gate, d_up, away_down) = pin((d_gate, d_up, away_down))
        ff_cut = ff // 2
        plan, fills = Plan(), []
        if extra_bits:
            keep_gate, away_gate = weight_sum(xm, d_gate)
            keep_up, away_up = weight_sum(xm, d_up)
            source, point = plan.read(away_gate), 0
        else:
            fills = [fill_weight_grad(xm, d_gate, 0), fill_weight_grad(xm, d_up, 1)]
            source, point = ("fill", (0, 1)), 1
        gate_x = plan.fresh((4 * row_features, ff), BF16)
        fold_part(plan, source, gate_x, 0, ff_cut, point)
        (d_middle, d_mid, gain_m_grad), (gate_x, *filled) = gather_sum(
            back_through((d_gate, d_up), (w_gate, w_up)),
            plan,
            [cot.reshape(share), middle, gain_m[None]],
            [like(share, F32), like(share, BF16), like((1, width), F32)],
            finish_mlp_norm,
            fills,
        )
        if filled:
            keep_gate, away_gate, keep_up, away_up = filled
        (d_mid, got_x) = pin((d_mid, got_x))
        own_down, away_down = to_settle(keep_down, got_x)

        plan = Plan()
        settle(plan, away_down, 1)
        gate_x = plan.through(gate_x)
        fold_part(plan, plan.read(away_gate), gate_x, ff_cut, ff - ff_cut)
        up_x = plan.fresh(away_up.shape, BF16)
        fold_part(plan, plan.read(away_up), up_x, 0, ff_cut)
        d_mid_all, (got_down, gate_x, up_x, mixed_partial) = spread(
            d_mid.reshape(2 * local_rows, width), plan, [fill_back(active, w_down, 0)]
        )
        (g_down,) = settled([(own_down, got_down)], (ff,))
        own_gate, away_gate = to_settle(keep_gate, gate_x)
    else:
        (
            middle, d_middle, gain_m_grad, d_mid_all, mixed_partial, own_down, down_b, down_o, gate_b, send_gate, own_gate, keep_up, away_up,
        ) = middle_call(
            b_mask, x_low, cot.reshape(share), gain_m[None], attn, w_out, cot_all, w_down, w_gate, (down_weight, gate_weight, up_weight), next(ids)
        )
        d_mid_all = d_mid_all.reshape(tokens, width)
        mixed_partial = mixed_partial.reshape(tokens, width)
        up_x = None
    if extra_bits:
        d_attn = nn(d_mid_all, w_out).astype(BF16).reshape(2, 4, half, q_columns)
        d_query, d_key, d_value = attend_back(
            meta, query, d_attn, keys, values, start_lanes, attn_t, total_e, scaling
        )
        d_key = d_key.reshape(parts, tokens, head_size)
        d_value = d_value.reshape(parts, tokens, head_size)
        for b in reversed(extra_bits):
            n = d_key.shape[0] // 2
            d_key = d_key[:n] + over_blk(d_key[n:].astype(BF16), 1 << b).astype(F32)
            d_value = d_value[:n] + over_blk(d_value[n:].astype(BF16), 1 << b).astype(F32)

        plan = Plan()
        away_kv = jnp.concatenate([d_key[1], d_value[1]], axis=1).astype(BF16)
        fold(plan, plan.read(away_kv), away_kv.shape)
        settle(plan, away_gate)
        if up_x is None:
            fold(plan, plan.read(away_up), away_up.shape)
        else:
            up_x = plan.through(up_x)
            fold_part(plan, plan.read(away_up), up_x, ff_cut, ff - ff_cut)
        (mixed,), (got_kv, got_gate, up_x, *filled) = gather_sum(
            mixed_partial,
            plan,
            [middle],
            [like(share, BF16)],
            functools.partial(finish_mixed, bit_order=local_order),
            [] if extra_bits else [fill_weight_grad(d_mid_all, attn, 0)],
        )
        keep_out, away_out = filled if filled else weight_sum(d_mid_all, attn)
        (g_gate,) = settled([(own_gate, got_gate)], (ff,))
        own_up, away_up = to_settle(keep_up, up_x)
        mixed = natural(mixed)
        mixed_got = over_blk(mixed[1], b_mask)
        d_qkv, d_xa_partial, gains_qk = prepare_back(
            d_query.reshape(tokens, q_columns), d_key, d_value, got_kv, raw, cosine, sine, gain_q, gain_k, w_qkv, heads
        )
        (d_xa_partial, mixed_got) = pin((d_xa_partial, mixed_got))

        plan, fills = Plan(), []
        settle(plan, away_up)
        fold(plan, plan.read(away_out), away_out.shape)
        if extra_bits:
            keep_qkv, away_qkv = weight_sum(xa, d_qkv)
            fold(plan, plan.read(away_qkv), away_qkv.shape)
        else:
            fills = [fill_weight_grad(xa, d_qkv, 0)]
            fold(plan, ("fill", (0, 1)), (4 * row_features, a_columns), 1)
        (input_own, input_away, gain_a_grad), (got_up, out_x, got, *filled) = gather_sum(
            d_xa_partial,
            plan,
            [x_low, d_middle, gain_a[None]],
            [like((local_rows, width), F32), like((local_rows, width), BF16), like((1, width), F32)],
            functools.partial(finish_input, bit_order=local_order),
            fills,
        )
        if filled:
            keep_qkv = filled[0]
        own_out, away_out = to_settle(keep_out, out_x)
        (g_up,) = settled([(own_up, got_up)], (ff,))
        own_qkv, away_qkv = to_settle(keep_qkv, got)

        plan = Plan()
        settle(plan, away_qkv)
        settle(plan, away_out)
        input_got = plan.fresh((local_rows, width), BF16)
        plan.copy((plan.read(natural(input_away)), everything), (input_got, everything), b_mask)
        sums = jnp.concatenate([ungroup(gain_a_grad[0]), gains_qk[0], gains_qk[1], ungroup(gain_m_grad[0])])
        (sums,), (got_a, got_o, input_got) = run(
            plan, total_main(sums.reshape(-1, 128)), next(ids), [1 << i for i in range(bits)]
        )
        g_query, g_key, g_value, g_out = settled(
            [(own_qkv, got_a), (own_out, got_o)], (q_columns, k_columns, k_columns, q_columns)
        )
        mixed = in_order(batch, mixed[:1], mixed_got[None], 0)
        input_grad = in_order(batch, natural(input_own)[None], input_got.astype(F32)[None], 0)
        gains = jnp.split(sums.reshape(-1), [width, width + head_size, width + 2 * head_size])
    else:
        (
            mixed_own, mixed_got, input_own, input_got, sums, gate_o, own_up, up_b, up_o, own_qkv, a_b, a_o, own_out, out_b, out_o,
        ) = last_call(
            b_mask,
            bit_order,
            scaling,
            dict(
                low=x_low,
                middle=middle,
                d_middle=d_middle,
                gain=gain_a[None],
                gain_m_grad=gain_m_grad,
                gain_q=gain_q,
                gain_k=gain_k,
                start=start_lanes,
                l=total_e,
                dall=d_mid_all,
                w_out=w_out,
                attn=attn,
                q=query,
                k=keys,
                v=values,
                ot=attn_t,
                raw=raw,
                table=table,
                wa=w_qkv,
                xa=xa,
                mixed=mixed_partial.reshape(2, 2, 2, 2, local_rows, width),
                send_g=send_gate,
                keep_u=keep_up,
                away_u=away_up,
            ),
            next(ids),
        )
        mixed, input_grad, g_down, g_gate, g_up, g_query, g_key, g_value, g_out = finish_call(
            jnp.stack([tensor, batch]),
            (mixed_own, mixed_got, input_own, input_got),
            [
                (own_down, down_b, down_o),
                (own_gate, gate_b, gate_o),
                (own_up, up_b, up_o),
                (own_qkv, a_b, a_o),
                (own_out, out_b, out_o),
            ],
            (ff, ff, ff, q_columns, k_columns, k_columns, q_columns),
        )
        gains = jnp.split(sums.reshape(-1), [width, width + head_size, width + 2 * head_size])
    return (
        mixed,
        input_grad,
        g_query,
        g_key,
        g_value,
        g_out,
        g_gate,
        g_up,
        g_down,
        *gains,
    )


def solution(mesh):
    rows = P(None, ("blk", "head"), None)
    weight = P("blk", "head")
    return jax.shard_map(
        local,
        mesh=mesh,
        in_specs=(rows, P(), *([weight] * 7), P(), P(), P(), P(), rows),
        out_specs=(rows, rows, *([weight] * 7), P(), P(), P(), P()),
        check_vma=False,
    )
```

```python
import functools
import math

import jax
import jax.numpy as jnp
from jax import lax
from jax.experimental import pallas as pl
from jax.experimental.pallas import tpu as pltpu
from jax.sharding import PartitionSpec as P

EPS = 1e-06
THETA = 1000000.0
LOG2E = 1.4426950408889634
F32 = jnp.float32
BF16 = jnp.bfloat16

MIB = 1024 * 1024
TINY_COST = pl.CostEstimate(flops=0, bytes_accessed=0, transcendentals=0)
VMEM_LIMIT = 32 * MIB
TENSOR_BIT = 1
SEQ_BIT = 0


def nt(a, b):
    return lax.dot_general(a, b, (((1,), (1,)), ((), ())), preferred_element_type=F32)


def tn(a, b):
    return lax.dot_general(a, b, (((0,), (0,)), ((), ())), preferred_element_type=F32)


def nn(a, b):
    return jnp.dot(a, b, preferred_element_type=F32)


def bit_of(value, bit):
    return (value >> bit) & 1


def over_blk(value, mask):
    count = lax.axis_size("blk")
    return lax.ppermute(value, "blk", [(i, i ^ mask) for i in range(count)])


def over_head(value, mask):
    count = lax.axis_size("head")
    return lax.ppermute(value, "head", [(i, i ^ mask) for i in range(count)])


def pin(values):
    return lax.optimization_barrier(values)


def in_order(flag, own, other, axis):
    return jnp.where(
        flag == 0,
        jnp.concatenate([own, other], axis=axis),
        jnp.concatenate([other, own], axis=axis),
    )


def token_offset(head_place, index, sub):
    core, upper, inner = index // (2 * sub), (index // sub) % 2, index % sub
    return (head_place ^ (upper * 2) ^ core) * sub + inner


def allowed_mask(meta_ref, start_row, q_block, k_block, rows, half, q_lanes):
    sub = half // 2
    head_place = meta_ref[0]
    k_index = lax.broadcasted_iota(jnp.int32, (2 * half, 1), 0)
    k_token = token_offset(head_place, k_index, sub) + k_block * (2 * half)
    q_index = lax.broadcasted_iota(jnp.int32, (1, q_lanes), 1) % (2 * half)
    q_token = token_offset(head_place, q_index, sub) + q_block * (2 * half)
    return (k_token <= q_token) & (k_token >= start_row)


def stacked(ref, heads, width):
    return jnp.concatenate(
        [ref[c, 0, :, h * width : (h + 1) * width] for h in range(heads) for c in range(2)], axis=0
    )


def key_rows(ref, part, block):
    return jnp.concatenate([ref[part, 0, block], ref[part, 1, block]], axis=0)


def attend_kernel(meta_ref, q_ref, k_ref, v_ref, start_ref, o_ref, ot_ref, l_ref, vt_ref, acc_ref, sum_ref, *, factor, heads):
    q_pos = pl.program_id(0)
    parts, _, blocks, half, width = k_ref.shape
    lanes = heads * 2 * half

    @pl.when(q_pos == 0)
    def _():
        for part in range(parts):
            for block in range(blocks):
                vt_ref[part * blocks + block] = key_rows(v_ref, part, block).T

    q_rows = stacked(q_ref, heads, width)
    acc_ref[...] = jnp.zeros_like(acc_ref)
    sum_ref[...] = jnp.zeros_like(sum_ref)
    start_row = start_ref[0]
    q_block = meta_ref[1 + q_pos]
    total = parts * blocks

    def add(kb, masked):
        e = jnp.exp2(nt(key_rows(k_ref, kb // blocks, kb % blocks), q_rows) * factor)
        if masked:
            k_block = meta_ref[1 + blocks + kb]
            e = jnp.where(allowed_mask(meta_ref, start_row, q_block, k_block, None, half, lanes), e, 0.0)
        sum_ref[...] += jnp.sum(e, axis=0, keepdims=True)
        acc_ref[...] += nn(vt_ref[kb], e.astype(BF16))

    def step(kb, carry):
        flag = meta_ref[1 + blocks + total + q_pos * total + kb]

        @pl.when(flag == 1)
        def _():
            add(kb, False)

        @pl.when(flag == 2)
        def _():
            add(kb, True)

        return carry

    lax.fori_loop(0, total, step, 0)
    out = acc_ref[...] / sum_ref[...]
    ot_ref[0] = out
    l_ref[0] = sum_ref[...]
    rows = out.T
    for h in range(heads):
        for c in range(2):
            at = (h * 2 + c) * half
            o_ref[c, 0, :, h * width : (h + 1) * width] = rows[at : at + half].astype(BF16)


def attend_back_kernel(
    meta_ref, q_ref, do_ref, k_ref, v_ref, start_ref, ot_ref, l_ref, dq_ref, dk_ref, dv_ref, kt_ref, acc_ref, *, factor, scaling, heads
):
    q_pos = pl.program_id(0)
    parts, _, blocks, half, width = k_ref.shape
    lanes = heads * 2 * half

    @pl.when(q_pos == 0)
    def _():
        dk_ref[...] = jnp.zeros_like(dk_ref)
        dv_ref[...] = jnp.zeros_like(dv_ref)
        for part in range(parts):
            for block in range(blocks):
                kt_ref[part * blocks + block] = key_rows(k_ref, part, block).T

    q_rows = stacked(q_ref, heads, width)
    do_rows = stacked(do_ref, heads, width)
    delta = jnp.sum(do_rows.astype(F32).T * ot_ref[0], axis=0, keepdims=True)
    inverse = 1.0 / l_ref[0]
    acc_ref[...] = jnp.zeros_like(acc_ref)
    start_row = start_ref[0]
    q_block = meta_ref[1 + q_pos]
    total = parts * blocks

    def add(kb, masked):
        part, block = kb // blocks, kb % blocks
        e = jnp.exp2(nt(key_rows(k_ref, part, block), q_rows) * factor)
        if masked:
            k_block = meta_ref[1 + blocks + kb]
            e = jnp.where(allowed_mask(meta_ref, start_row, q_block, k_block, None, half, lanes), e, 0.0)
        p = e * inverse
        dp = nt(key_rows(v_ref, part, block), do_rows)
        ds = (p * (dp - delta)).astype(BF16)
        dv = nn(p.astype(BF16), do_rows)
        dk = nn(ds, q_rows) * scaling
        for c in range(2):
            dv_ref[part, c, block] += dv[c * half : (c + 1) * half]
            dk_ref[part, c, block] += dk[c * half : (c + 1) * half]
        acc_ref[...] += nn(kt_ref[kb], ds)

    def step(kb, carry):
        flag = meta_ref[1 + blocks + total + q_pos * total + kb]

        @pl.when(flag == 1)
        def _():
            add(kb, False)

        @pl.when(flag == 2)
        def _():
            add(kb, True)

        return carry

    lax.fori_loop(0, total, step, 0)
    rows = acc_ref[...].T * scaling
    for h in range(heads):
        for c in range(2):
            at = (h * 2 + c) * half
            dq_ref[c, 0, :, h * width : (h + 1) * width] = rows[at : at + half]


def attend(meta, q, k, v, start, scaling):
    _, blocks, half, columns = q.shape
    parts, width = k.shape[0], k.shape[-1]
    heads = columns // width
    lanes = heads * 2 * half
    total = parts * blocks
    row_spec = pl.BlockSpec((2, 1, half, columns), lambda i: (0, i, 0, 0))
    key_spec = pl.BlockSpec(k.shape, lambda i: (0, 0, 0, 0, 0))
    lane_spec = pl.BlockSpec((1, 1, lanes), lambda i: (i, 0, 0))
    return pl.pallas_call(
        functools.partial(attend_kernel, factor=scaling * LOG2E, heads=heads),
        grid=(blocks,),
        in_specs=[pl.BlockSpec(memory_space=pltpu.SMEM), row_spec, key_spec, key_spec, lane_spec],
        out_specs=[row_spec, pl.BlockSpec((1, width, lanes), lambda i: (i, 0, 0)), lane_spec],
        out_shape=[
            jax.ShapeDtypeStruct(q.shape, BF16),
            jax.ShapeDtypeStruct((blocks, width, lanes), F32),
            jax.ShapeDtypeStruct((blocks, 1, lanes), F32),
        ],
        scratch_shapes=[
            pltpu.VMEM((total, width, 2 * half), BF16),
            pltpu.VMEM((width, lanes), F32),
            pltpu.VMEM((1, lanes), F32),
        ],
        compiler_params=pltpu.CompilerParams(vmem_limit_bytes=VMEM_LIMIT),
        cost_estimate=pl.CostEstimate(
            flops=2 * 2 * lanes * 2 * half * width * blocks * total,
            bytes_accessed=8 * q.size + 8 * k.size,
            transcendentals=lanes * 2 * half * blocks * total,
        ),
    )(meta, q, k, v, start)


def attend_back(meta, q, do, k, v, start, out_t, total_e, scaling):
    _, blocks, half, columns = q.shape
    parts, width = k.shape[0], k.shape[-1]
    heads = columns // width
    lanes = heads * 2 * half
    total = parts * blocks
    row_spec = pl.BlockSpec((2, 1, half, columns), lambda i: (0, i, 0, 0))
    key_spec = pl.BlockSpec(k.shape, lambda i: (0, 0, 0, 0, 0))
    lane_spec = pl.BlockSpec((1, 1, lanes), lambda i: (i, 0, 0))
    return pl.pallas_call(
        functools.partial(attend_back_kernel, factor=scaling * LOG2E, scaling=scaling, heads=heads),
        grid=(blocks,),
        in_specs=[
            pl.BlockSpec(memory_space=pltpu.SMEM),
            row_spec,
            row_spec,
            key_spec,
            key_spec,
            lane_spec,
            pl.BlockSpec((1, width, lanes), lambda i: (i, 0, 0)),
            lane_spec,
        ],
        out_specs=[row_spec, key_spec, key_spec],
        out_shape=[
            jax.ShapeDtypeStruct(q.shape, F32),
            jax.ShapeDtypeStruct(k.shape, F32),
            jax.ShapeDtypeStruct(k.shape, F32),
        ],
        scratch_shapes=[
            pltpu.VMEM((total, width, 2 * half), BF16),
            pltpu.VMEM((width, lanes), F32),
        ],
        compiler_params=pltpu.CompilerParams(vmem_limit_bytes=VMEM_LIMIT),
        cost_estimate=pl.CostEstimate(
            flops=5 * 2 * lanes * 2 * half * width * blocks * total,
            bytes_accessed=12 * q.size + 16 * k.size,
            transcendentals=lanes * 2 * half * blocks * total,
        ),
    )(meta, q, do, k, v, start, out_t, total_e)


def prepare_kernel(x_ref, w_ref, cos_ref, sin_ref, gq_ref, gk_ref, q_ref, kv_ref, raw_ref, *, heads, width):
    acc = jnp.dot(x_ref[...], w_ref[...], preferred_element_type=F32)
    raw_ref[...] = acc[:, : (heads + 1) * width]
    for h in range(heads + 1):
        part = acc[:, h * width : (h + 1) * width]
        normed = part * lax.rsqrt(jnp.mean(part * part, axis=-1, keepdims=True) + EPS)
        scaled = normed * (gq_ref if h < heads else gk_ref)[...]
        turned = (scaled * cos_ref[...] + pltpu.roll(scaled, width // 2, 1) * sin_ref[...]).astype(BF16)
        if h < heads:
            q_ref[:, h * width : (h + 1) * width] = turned
        else:
            kv_ref[:, :width] = turned
    kv_ref[:, width:] = acc[:, (heads + 1) * width :].astype(BF16)


def prepare(x, w, cos, sin, gain_q, gain_k, heads):
    tokens, depth = x.shape
    width, tile = gain_q.shape[1], 256
    row = lambda n: pl.BlockSpec((tile, n), lambda i: (i, 0))
    fixed = lambda a: pl.BlockSpec(a.shape, lambda i: (0, 0))
    return pl.pallas_call(
        functools.partial(prepare_kernel, heads=heads, width=width),
        grid=(tokens // tile,),
        in_specs=[row(depth), fixed(w), row(width), row(width), fixed(gain_q), fixed(gain_k)],
        out_specs=[row(heads * width), row(2 * width), row((heads + 1) * width)],
        out_shape=[
            jax.ShapeDtypeStruct((tokens, heads * width), BF16),
            jax.ShapeDtypeStruct((tokens, 2 * width), BF16),
            jax.ShapeDtypeStruct((tokens, (heads + 1) * width), F32),
        ],
        compiler_params=pltpu.CompilerParams(vmem_limit_bytes=VMEM_LIMIT),
        cost_estimate=TINY_COST,
    )(x, w, cos, sin, gain_q, gain_k)


def prepare_back_kernel(
    dq_ref, dk_ref, dv_ref, got_ref, raw_ref, cos_ref, sin_ref, gq_ref, gk_ref, w_ref, d_ref, p_ref, g_ref, *, heads, width
):
    @pl.when(pl.program_id(0) == 0)
    def _():
        g_ref[...] = jnp.zeros_like(g_ref)

    got = got_ref[...].astype(F32)
    for h in range(heads + 1):
        at = slice(h * width, (h + 1) * width)
        grad = dq_ref[:, at] if h < heads else dk_ref[0] + got[:, :width]
        gain = (gq_ref if h < heads else gk_ref)[...]
        raw = raw_ref[:, at]
        inverse = lax.rsqrt(jnp.mean(raw * raw, axis=-1, keepdims=True) + EPS)
        normed = raw * inverse
        turned = grad * cos_ref[...] - pltpu.roll(grad, width // 2, 1) * sin_ref[...]
        row = 0 if h < heads else 1
        g_ref[row : row + 1, :] += jnp.sum(turned * normed, axis=0, keepdims=True)
        scaled = turned * gain
        d_ref[:, at] = (inverse * (scaled - normed * jnp.mean(scaled * normed, axis=-1, keepdims=True))).astype(BF16)
    d_ref[:, (heads + 1) * width :] = (dv_ref[0] + got[:, width:]).astype(BF16)
    p_ref[...] = nt(d_ref[...], w_ref[...]).astype(BF16)


def prepare_back(dq, dk, dv, got, raw, cos, sin, gain_q, gain_k, w, heads):
    tokens, width, tile = dq.shape[0], gain_q.shape[1], 256
    row = lambda n: pl.BlockSpec((tile, n), lambda i: (i, 0))
    part = pl.BlockSpec((1, tile, width), lambda i: (0, i, 0))
    fixed = lambda a: pl.BlockSpec(a.shape, lambda i: (0, 0))
    return pl.pallas_call(
        functools.partial(prepare_back_kernel, heads=heads, width=width),
        grid=(tokens // tile,),
        in_specs=[
            row(heads * width),
            part,
            part,
            row(2 * width),
            row((heads + 1) * width),
            row(width),
            row(width),
            fixed(gain_q),
            fixed(gain_k),
            fixed(w),
        ],
        out_specs=[row(w.shape[1]), row(w.shape[0]), pl.BlockSpec((8, width), lambda i: (0, 0))],
        out_shape=[
            jax.ShapeDtypeStruct((tokens, w.shape[1]), BF16),
            jax.ShapeDtypeStruct((tokens, w.shape[0]), BF16),
            jax.ShapeDtypeStruct((8, width), F32),
        ],
        compiler_params=pltpu.CompilerParams(vmem_limit_bytes=VMEM_LIMIT),
        cost_estimate=TINY_COST,
    )(dq, dk, dv, got, raw, cos, sin, gain_q, gain_k, w)


def place_of_block(blk, bit_order, p):
    return blk ^ sum(((p >> i) & 1) << b for i, b in enumerate(bit_order))


def enter_kernel(blk_ref, *refs, bit_order, normed):
    if normed:
        mine_ref, other_ref, gain_ref, low_ref, out_ref, gains_ref = refs
    else:
        mine_ref, low_ref = refs
    rows, width = mine_ref.shape
    n = width >> len(bit_order)
    for p in range(1 << len(bit_order)):
        at = pl.ds(pl.multiple_of(place_of_block(blk_ref[0], bit_order, p) * n, n), n)
        low_ref[:rows, p * n : (p + 1) * n] = mine_ref[:, at]
        if normed:
            low_ref[rows:, p * n : (p + 1) * n] = other_ref[:, at]
            gains_ref[:, p * n : (p + 1) * n] = gain_ref[:, at]
    if normed:
        values = low_ref[...].astype(F32)
        inverse = lax.rsqrt(jnp.mean(values * values, axis=-1, keepdims=True) + EPS)
        out_ref[...] = (values * inverse * gains_ref[:1]).astype(BF16)


def enter(blk, bit_order, mine, other=None, gain=None):
    rows, width = mine.shape
    normed = gain is not None
    total = (2 * rows if normed else rows, width)
    vmem = pl.BlockSpec(memory_space=pltpu.VMEM)
    operands = [mine, other, gain] if normed else [mine]
    return pl.pallas_call(
        functools.partial(enter_kernel, bit_order=bit_order, normed=normed),
        in_specs=[pl.BlockSpec(memory_space=pltpu.SMEM), *[vmem] * len(operands)],
        out_specs=[vmem] * (3 if normed else 1),
        out_shape=[
            *[jax.ShapeDtypeStruct(total, BF16)] * (2 if normed else 1),
            *([jax.ShapeDtypeStruct(gain.shape, F32)] if normed else []),
        ],
        compiler_params=pltpu.CompilerParams(vmem_limit_bytes=VMEM_LIMIT),
        cost_estimate=TINY_COST,
    )(blk[None].astype(jnp.int32), *operands)


def assemble_kernel(place_ref, *refs, sources, widths):
    ins, outs = refs[: 2 * sources], refs[2 * sources :]
    place, k, at = place_ref[0], 0, 0
    for own_ref, got_ref in zip(ins[::2], ins[1::2]):
        f, at = own_ref.shape[0], 0
        while at < own_ref.shape[1]:
            w, cut = widths[k], slice(at, at + widths[k])
            mine = pl.ds(pl.multiple_of(place * w, w), w)
            theirs = pl.ds(pl.multiple_of((1 - place) * w, w), w)
            outs[k][:, mine] = own_ref[:, cut] + got_ref[:f, cut].astype(F32)
            outs[k][:, theirs] = got_ref[f : 2 * f, cut].astype(F32) + got_ref[2 * f :, cut].astype(F32)
            at += w
            k += 1


def assemble(place, sources, widths):
    vmem = pl.BlockSpec(memory_space=pltpu.VMEM)
    flat = [a for pair in sources for a in pair]
    return pl.pallas_call(
        functools.partial(assemble_kernel, sources=len(sources), widths=widths),
        in_specs=[pl.BlockSpec(memory_space=pltpu.SMEM), *[vmem] * len(flat)],
        out_specs=[vmem] * len(widths),
        out_shape=[jax.ShapeDtypeStruct((sources[0][0].shape[0], 2 * w), F32) for w in widths],
        compiler_params=pltpu.CompilerParams(vmem_limit_bytes=VMEM_LIMIT),
        cost_estimate=TINY_COST,
    )(place[None].astype(jnp.int32), *flat)


def back_kernel(*refs):
    *ins, out_ref = refs
    n = len(ins) // 2
    out_ref[...] = sum(nt(d[...], w[...]) for d, w in zip(ins[:n], ins[n:])).astype(BF16)


def back_through(grads, weights):
    tokens, depth, tile = grads[0].shape[0], weights[0].shape[0], 256
    return pl.pallas_call(
        back_kernel,
        grid=(depth // tile,),
        in_specs=[
            *[pl.BlockSpec(g.shape, lambda i: (0, 0)) for g in grads],
            *[pl.BlockSpec((tile, w.shape[1]), lambda i: (i, 0)) for w in weights],
        ],
        out_specs=pl.BlockSpec((tokens, tile), lambda i: (0, i)),
        out_shape=jax.ShapeDtypeStruct((tokens, depth), BF16),
        compiler_params=pltpu.CompilerParams(vmem_limit_bytes=VMEM_LIMIT),
        cost_estimate=TINY_COST,
    )(*grads, *weights)


def weight_grad_kernel(a_ref, b_ref, keep_ref, away_ref):
    product = tn(a_ref[...], b_ref[...])
    first = pl.program_id(0) < pl.num_programs(0) // 2

    @pl.when(first)
    def _():
        keep_ref[...] = product

    @pl.when(jnp.logical_not(first))
    def _():
        away_ref[...] = product.astype(BF16)


def weight_grad(a, b):
    tokens, depth = a.shape
    n, tile = b.shape[1], 256
    steps = depth // tile
    return pl.pallas_call(
        weight_grad_kernel,
        grid=(steps,),
        in_specs=[
            pl.BlockSpec((tokens, tile), lambda i: (0, i)),
            pl.BlockSpec((tokens, n), lambda i: (0, 0)),
        ],
        out_specs=[
            pl.BlockSpec((tile, n), lambda i: (jnp.minimum(i, steps // 2 - 1), 0)),
            pl.BlockSpec((tile, n), lambda i: (jnp.maximum(i - steps // 2, 0), 0)),
        ],
        out_shape=[
            jax.ShapeDtypeStruct((depth // 2, n), F32),
            jax.ShapeDtypeStruct((depth // 2, n), BF16),
        ],
        compiler_params=pltpu.CompilerParams(vmem_limit_bytes=VMEM_LIMIT),
        cost_estimate=TINY_COST,
    )(a, b)


def remote(src, dst, send, recv, target):
    copy = pltpu.make_async_remote_copy(
        src_ref=src, dst_ref=dst, send_sem=send, recv_sem=recv, device_id=target, device_id_type=pl.DeviceIdType.MESH
    )
    copy.start()
    return copy


class Plan:
    def __init__(self):
        self.inputs, self.shapes, self.aliases, self.jobs = [], [], {}, []

    def read(self, array):
        self.inputs.append(array)
        return ("in", len(self.inputs) - 1)

    def fresh(self, shape, dtype):
        self.shapes.append(jax.ShapeDtypeStruct(shape, dtype))
        return ("out", len(self.shapes) - 1)

    def through(self, array):
        self.inputs.append(array)
        self.aliases[len(self.inputs) - 1] = len(self.shapes)
        return self.fresh(array.shape, array.dtype)

    def copy(self, src, dst, mask, after=None, point=0):
        self.jobs.append((src, dst, mask, after, point, None))
        return len(self.jobs) - 1

    def local(self, src, dst, shape, point=0):
        self.jobs.append((src, dst, 0, None, point, shape))
        return len(self.jobs) - 1


class Fill:
    def __init__(self, inputs, outputs, step, point):
        self.inputs, self.outputs, self.step, self.point = inputs, outputs, step, point

    def scratch(self):
        shapes = [pltpu.VMEM(a.shape, a.dtype) for a in (*self.inputs, *self.outputs)]
        return [*shapes, pltpu.SemaphoreType.DMA((len(shapes),))]


def fill_weight_grad(a, b, point):
    depth, n, tile = a.shape[1], b.shape[1], 256
    half = depth // 2

    def step(ins, outs):
        (a_ref, b_ref), (keep_ref, away_ref) = ins, outs

        def one(i, carry):
            at = pl.ds(pl.multiple_of(i * tile, tile), tile)
            keep_ref[at, :] = tn(a_ref[:, at], b_ref[...])
            far = pl.ds(pl.multiple_of(half + i * tile, tile), tile)
            away_ref[at, :] = tn(a_ref[:, far], b_ref[...]).astype(BF16)
            return carry

        lax.fori_loop(0, half // tile, one, 0)

    outputs = [jax.ShapeDtypeStruct((half, n), F32), jax.ShapeDtypeStruct((half, n), BF16)]
    return Fill([a, b], outputs, step, point)


def fill_back(grad, weight, point):
    tokens, depth, tile = grad.shape[0], weight.shape[0], 256

    def step(ins, outs):
        (g_ref, w_ref), (out_ref,) = ins, outs

        def one(i, carry):
            at = pl.ds(pl.multiple_of(i * tile, tile), tile)
            out_ref[:, at] = nt(g_ref[...], w_ref[at, :]).astype(BF16)
            return carry

        lax.fori_loop(0, depth // tile, one, 0)

    return Fill([grad, weight], [jax.ShapeDtypeStruct((tokens, depth), BF16)], step, point)


def fill_product(left, right, point):
    tokens, n, tile = left.shape[0], right.shape[1], 256

    def step(ins, outs):
        (l_ref, r_ref), (out_ref,) = ins, outs

        def one(i, carry):
            at = pl.ds(pl.multiple_of(i * tile, tile), tile)
            out_ref[at, :] = nn(l_ref[at, :], r_ref[...])
            return carry

        lax.fori_loop(0, tokens // tile, one, 0)

    return Fill([left, right], [jax.ShapeDtypeStruct((tokens, n), F32)], step, point)


def run(plan, main, collective_id, greeted=(), fills=(), limit=None):
    inputs, in_specs, out_shapes, out_specs, scratch, body, own_limit = main
    limit = limit or own_limit + sum(math.prod(s.shape) * s.dtype.itemsize for f in fills for s in f.scratch()[:-1])
    f_in, f_out = [a for f in fills for a in f.inputs], [a for f in fills for a in f.outputs]
    n_in, n_out = len(inputs), len(out_shapes)
    m_in, m_out = len(plan.inputs), len(plan.shapes)
    jobs = plan.jobs
    local_jobs = [i for i, job in enumerate(jobs) if not job[2]]
    masks = sorted({*greeted, *[job[2] for job in jobs if job[2]]} - {1 << TENSOR_BIT})
    any_spec = pl.BlockSpec(memory_space=pltpu.HBM)

    def kernel(*refs):
        main_in, refs = refs[:n_in], refs[n_in:]
        plan_in, refs = refs[:m_in], refs[m_in:]
        fill_in, refs = refs[: len(f_in)], refs[len(f_in) :]
        main_out, refs = refs[:n_out], refs[n_out:]
        plan_out, refs = refs[:m_out], refs[m_out:]
        fill_out, refs = refs[: len(f_out)], refs[len(f_out) :]
        send, recv, *rest = refs
        bounce = dict(zip(local_jobs, rest))
        rest = rest[len(local_jobs) :]
        parts = []
        for f in fills:
            k, m = len(f.inputs), len(f.outputs)
            (*held, sems), rest = rest[: k + m + 1], rest[k + m + 1 :]
            loads = [pltpu.make_async_copy(fill_in[i], held[i], sems.at[i]) for i in range(k)]
            stores = [pltpu.make_async_copy(held[k + i], fill_out[i], sems.at[k + i]) for i in range(m)]
            fill_in, fill_out = fill_in[k:], fill_out[m:]
            for copy in loads:
                copy.start()
            parts.append((f, held[:k], held[k:], loads, stores))

        def compute(point):
            for f, ins, outs, loads, stores in parts:
                if f.point == point:
                    for copy in loads:
                        copy.wait()
                    f.step(ins, outs)
                    for copy in stores:
                        copy.start()

        blk, head = lax.axis_index("blk"), lax.axis_index("head")
        core, near, across = (blk, head ^ 1), (blk, head ^ 2), (blk ^ (1 << TENSOR_BIT), head)
        barrier = pltpu.get_barrier_semaphore()
        partners = [core, near, across, *[(blk ^ m, head) for m in masks]]
        for target in partners:
            pl.semaphore_signal(barrier, inc=1, device_id=target, device_id_type=pl.DeviceIdType.MESH)
        pl.semaphore_wait(barrier, len(partners))
        started, arrived, halfway = {}, set(), []

        def arrive(i):
            if i not in arrived:
                arrived.add(i)
                (started[i].wait_recv if jobs[i][2] else started[i].wait)()

        def part(side):
            (kind, index), cut = side
            if kind == "fill":
                return cut(parts[index[0]][2][index[1]])
            return cut((plan_in if kind == "in" else plan_out)[index])

        def issue(point):
            for i in list(halfway):
                started[i].wait()
                started[i] = pltpu.make_async_copy(bounce[i], part(jobs[i][1]), recv.at[i])
                started[i].start()
                halfway.remove(i)
            for i, (src, dst, mask, after, at, shape) in enumerate(jobs):
                if i in started or (at != point and point is not None):
                    continue
                if after is not None:
                    arrive(after)
                if mask:
                    started[i] = remote(part(src), part(dst), send.at[i], recv.at[i], (blk ^ mask, head))
                else:
                    started[i] = pltpu.make_async_copy(part(src), bounce[i], send.at[i])
                    started[i].start()
                    halfway.append(i)

        point = 0
        for _ in body((core, near, across), main_in, main_out, rest):
            issue(point)
            compute(point)
            point += 1
        issue(None)
        issue(None)
        for i in range(len(jobs)):
            arrive(i)
            if jobs[i][2]:
                started[i].wait_send()
        for *_, stores in parts:
            for copy in stores:
                copy.wait()

    results = pl.pallas_call(
        kernel,
        out_shape=[*out_shapes, *plan.shapes, *f_out],
        in_specs=[*in_specs, *[any_spec] * (m_in + len(f_in))],
        out_specs=[*out_specs, *[any_spec] * (m_out + len(f_out))],
        scratch_shapes=[
            pltpu.SemaphoreType.DMA((max(1, len(jobs)),)),
            pltpu.SemaphoreType.DMA((max(1, len(jobs)),)),
            *[pltpu.VMEM(jobs[i][5], BF16) for i in local_jobs],
            *[s for f in fills for s in f.scratch()],
            *scratch,
        ],
        input_output_aliases={n_in + i: n_out + o for i, o in plan.aliases.items()},
        compiler_params=pltpu.CompilerParams(
            collective_id=collective_id, has_side_effects=True, vmem_limit_bytes=limit
        ),
        cost_estimate=TINY_COST,
    )(*inputs, *plan.inputs, *f_in)
    return results[:n_out], results[n_out:]


def spread_main(flat, chunk):
    rows, width = flat.shape[0] // 2, flat.shape[1]
    pieces = width // chunk

    def body(partners, ins, outs, scratch):
        core, near, across = partners
        (s_ref,), (o_ref,), (hold, local_sem, send, recv) = ins, outs, scratch
        first = remote(s_ref, o_ref.at[0, :, 0, 1], send.at[0], recv.at[0], near)
        second = [
            remote(
                s_ref.at[:, :, pl.ds(i * chunk, chunk)],
                o_ref.at[0, :, 1, 0, :, pl.ds((i ^ 1) * chunk, chunk)],
                send.at[6 + i],
                recv.at[6 + i],
                across,
            )
            for i in range(pieces)
        ]
        third = remote(s_ref, o_ref.at[1, :, 0, 0], send.at[1], recv.at[1], core)
        held = pltpu.make_async_copy(s_ref, hold, local_sem.at[0])
        held.start()
        yield
        held.wait()
        own = pltpu.make_async_copy(hold, o_ref.at[0, :, 0, 0], local_sem.at[1])
        own.start()
        for copy in second:
            copy.wait_recv()
        fourth = remote(o_ref.at[0, :, 1, 0], o_ref.at[0, :, 1, 1], send.at[2], recv.at[2], near)
        fifth = remote(o_ref.at[0, :, 1, 0], o_ref.at[1, :, 1, 0], send.at[3], recv.at[3], core)
        yield
        first.wait_recv()
        sixth = remote(o_ref.at[0, :, 0, 1], o_ref.at[1, :, 0, 1], send.at[4], recv.at[4], core)
        yield
        fourth.wait_recv()
        seventh = remote(o_ref.at[0, :, 1, 1], o_ref.at[1, :, 1, 1], send.at[5], recv.at[5], core)
        yield
        own.wait()
        for copy in (first, *second, third, fourth, fifth, sixth, seventh):
            copy.wait_send()
        for copy in (third, fifth, sixth, seventh):
            copy.wait_recv()

    any_spec = pl.BlockSpec(memory_space=pltpu.HBM)
    return (
        [flat.reshape(2, rows, width)],
        [any_spec],
        [jax.ShapeDtypeStruct((2, 2, 2, 2, rows, width), flat.dtype)],
        [any_spec],
        [
            pltpu.VMEM((2, rows, width), flat.dtype),
            pltpu.SemaphoreType.DMA((2,)),
            pltpu.SemaphoreType.DMA((6 + pieces,)),
            pltpu.SemaphoreType.DMA((6 + pieces,)),
        ],
        body,
        8 * MIB,
    )


def gather_main(partial, chunk, extra, outs_like, finish):
    rows, width = partial.shape[0] // 16, partial.shape[1]
    share = (2, rows, width)
    pieces = width // chunk

    def body(partners, ins, outs, scratch):
        core, near, across = partners
        p_ref, *extra_refs = ins
        core_in, out_y, in_y, out_t, in_t, hold, send, recv = scratch
        order = ((1, 1), (0, 1), (1, 0), (0, 0))
        from_core = [
            remote(p_ref.at[1, :, t, y], core_in.at[i], send.at[i], recv.at[i], core) for i, (t, y) in enumerate(order)
        ]
        from_y = []
        for i in range(2):
            t, y = order[i]
            from_core[i].wait_recv()
            out_y[i] = (p_ref[0, :, t, y].astype(F32) + core_in[i].astype(F32)).astype(BF16)
            from_y.append(remote(out_y.at[i], in_y.at[i], send.at[4 + i], recv.at[4 + i], near))
        yield
        from_core[2].wait_recv()
        hold[...] = p_ref[0, :, 1, 0].astype(F32) + core_in[2].astype(F32)
        from_y[0].wait_recv()
        for i in range(pieces):
            a, b = slice(i * chunk, (i + 1) * chunk), slice((i ^ 1) * chunk, ((i ^ 1) + 1) * chunk)
            out_t[:, :, b] = (hold[:, :, a] + in_y[0, :, :, a].astype(F32)).astype(BF16)
        from_t = remote(out_t, in_t, send.at[6], recv.at[6], across)
        yield
        from_core[3].wait_recv()
        hold[...] = p_ref[0, :, 0, 0].astype(F32) + core_in[3].astype(F32)
        from_y[1].wait_recv()
        hold[...] += in_y[1].astype(F32)
        yield
        from_t.wait_recv()
        hold[...] += in_t[...].astype(F32)
        finish(hold, extra_refs, outs)
        for copy in (*from_core, *from_y, from_t):
            copy.wait_send()

    vmem_spec = pl.BlockSpec(memory_space=pltpu.VMEM)
    return (
        [partial.reshape(2, 2, 2, 2, rows, width), *extra],
        [vmem_spec] * (1 + len(extra)),
        outs_like,
        [vmem_spec] * len(outs_like),
        [
            pltpu.VMEM((4, *share), BF16),
            pltpu.VMEM((2, *share), BF16),
            pltpu.VMEM((2, *share), BF16),
            pltpu.VMEM(share, BF16),
            pltpu.VMEM(share, BF16),
            pltpu.VMEM(share, F32),
            pltpu.SemaphoreType.DMA((7,)),
            pltpu.SemaphoreType.DMA((7,)),
        ],
        body,
        24 * MIB,
    )


def inverse_rms(values):
    return lax.rsqrt(jnp.mean(values * values, axis=-1, keepdims=True) + EPS)


def finish_middle(total, extra, outs):
    (low_ref, gain_ref), (middle_ref, normed_ref) = extra, outs
    for m in range(2):
        middle = low_ref[m].astype(F32) + total[m]
        middle_ref[m] = middle
        normed_ref[m] = (middle * inverse_rms(middle) * gain_ref[...]).astype(BF16)


def norm_grad(total, values, gain, gain_grad_ref, m):
    inverse = inverse_rms(values)
    normal = values * inverse
    part = jnp.sum(total * normal, axis=0, keepdims=True)
    gain_grad_ref[...] = part if m == 0 else gain_grad_ref[...] + part
    scaled = total * gain
    return inverse * (scaled - normal * jnp.mean(scaled * normal, axis=-1, keepdims=True))


def finish_mlp_norm(total, extra, outs):
    (cot_ref, middle_ref, gain_ref), (grad_ref, low_ref, gain_grad_ref) = extra, outs
    for m in range(2):
        grad = cot_ref[m].astype(F32) + norm_grad(total[m], middle_ref[m], gain_ref[...], gain_grad_ref, m)
        grad_ref[m] = grad
        low_ref[m] = grad.astype(BF16)


def store_ungrouped(value, ref, blk, bit_order, lead=()):
    n = value.shape[-1] >> len(bit_order)
    for p in range(1 << len(bit_order)):
        block = value[:, p * n : (p + 1) * n]
        if bit_order and n % 128 == 0:
            at = pl.ds(pl.multiple_of(place_of_block(blk, bit_order, p) * n, n), n)
        else:
            at = pl.ds(p * n, n)
        ref[(*lead, slice(None), at)] = block.astype(ref.dtype)


def finish_mixed(total, extra, outs, *, bit_order):
    (middle_ref,), (mixed_ref,) = extra, outs
    blk = lax.axis_index("blk")
    for m in range(2):
        store_ungrouped(middle_ref[m] + total[m], mixed_ref, blk, bit_order, (m,))


def finish_input(total, extra, outs, *, bit_order):
    (low_ref, mid_ref, gain_ref), (own_ref, away_ref, gain_grad_ref) = extra, outs
    blk = lax.axis_index("blk")
    for m in range(2):
        grad = mid_ref[m] + norm_grad(total[m], low_ref[m].astype(F32), gain_ref[...], gain_grad_ref, m)
        store_ungrouped(grad, own_ref if m == 0 else away_ref, blk, bit_order)


def total_main(values):
    rows, width = values.shape
    rounds = 2 + lax.axis_size("blk").bit_length() - 1

    def body(partners, ins, outs, scratch):
        (v_ref,), (o_ref,) = ins, outs
        out_buf, in_buf, send, recv = scratch
        blk, head = lax.axis_index("blk"), lax.axis_index("head")
        o_ref[...] = v_ref[...]
        yield
        for i in range(rounds):
            target = (blk, head ^ (1 << i)) if i < 2 else (blk ^ (1 << (i - 2)), head)
            out_buf[i] = o_ref[...]
            copy = remote(out_buf.at[i], in_buf.at[i], send.at[i], recv.at[i], target)
            copy.wait_recv()
            o_ref[...] += in_buf[i]
            copy.wait_send()
        yield

    vmem_spec = pl.BlockSpec(memory_space=pltpu.VMEM)
    return (
        [values],
        [vmem_spec],
        [jax.ShapeDtypeStruct(values.shape, F32)],
        [vmem_spec],
        [
            pltpu.VMEM((rounds, rows, width), F32),
            pltpu.VMEM((rounds, rows, width), F32),
            pltpu.SemaphoreType.DMA((rounds,)),
            pltpu.SemaphoreType.DMA((rounds,)),
        ],
        body,
        8 * MIB,
    )


class Moving:
    def __init__(self, copy, away):
        self.copy, self.away, self.here, self.gone = copy, away, False, not away

    def arrive(self):
        if not self.here:
            self.here = True
            (self.copy.wait_recv if self.away else self.copy.wait)()

    def sent(self):
        if not self.gone:
            self.gone = True
            self.copy.wait_send()


class Links:
    def __init__(self, send, recv, batch_mask):
        self.send, self.recv, self.all = send, recv, []
        blk, head = lax.axis_index("blk"), lax.axis_index("head")
        self.core, self.near, self.across = (blk, head ^ 1), (blk, head ^ 2), (blk ^ (1 << TENSOR_BIT), head)
        self.seq, self.batch = (blk ^ (1 << SEQ_BIT), head), (blk ^ batch_mask, head)
        self.both = (blk ^ (batch_mask | (1 << TENSOR_BIT)), head)
        self.place = bit_of(blk, TENSOR_BIT)
        self.blk = blk

    def greet(self):
        barrier = pltpu.get_barrier_semaphore()
        partners = (self.core, self.near, self.across, self.seq, self.batch, self.both)
        for target in partners:
            pl.semaphore_signal(barrier, inc=1, device_id=target, device_id_type=pl.DeviceIdType.MESH)
        pl.semaphore_wait(barrier, len(partners))

    def to(self, target, src, dst):
        i = len(self.all)
        self.all.append(Moving(remote(src, dst, self.send.at[i], self.recv.at[i], target), True))
        return self.all[-1]

    def load(self, src, dst):
        copy = pltpu.make_async_copy(src, dst, self.recv.at[len(self.all)])
        copy.start()
        self.all.append(Moving(copy, False))
        return self.all[-1]

    def finish(self):
        for moving in self.all:
            moving.arrive()
            moving.sent()

    def half(self, ref, other):
        n = ref.shape[1] // 2
        place = 1 - self.place if other else self.place
        return ref.at[:, pl.ds(pl.multiple_of(place * n, n), n)]


def nothing(stage):
    pass


class Spread:
    def __init__(self, links, s_ref, o_ref, chunk, in_vmem=True):
        self.links, self.s_ref, self.o_ref, self.chunk, self.in_vmem = links, s_ref, o_ref, chunk, in_vmem

    def begin(self):
        links, s_ref, o_ref, chunk = self.links, self.s_ref, self.o_ref, self.chunk
        self.across = [
            links.to(
                links.across,
                s_ref.at[:, :, pl.ds(i * chunk, chunk)],
                o_ref.at[0, :, 1, 0, :, pl.ds((i ^ 1) * chunk, chunk)],
            )
            for i in range(s_ref.shape[-1] // chunk)
        ]
        self.near = links.to(links.near, s_ref, o_ref.at[0, :, 0, 1])
        self.core = [links.to(links.core, s_ref, o_ref.at[1, :, 0, 0])]
        if self.in_vmem:
            o_ref[0, :, 0, 0] = s_ref[...]
        else:
            links.load(s_ref, o_ref.at[0, :, 0, 0])

    def pass_on(self):
        links, o_ref = self.links, self.o_ref
        for copy in self.across:
            copy.arrive()
        self.onward = links.to(links.near, o_ref.at[0, :, 1, 0], o_ref.at[0, :, 1, 1])
        self.core.append(links.to(links.core, o_ref.at[0, :, 1, 0], o_ref.at[1, :, 1, 0]))
        self.near.arrive()
        self.core.append(links.to(links.core, o_ref.at[0, :, 0, 1], o_ref.at[1, :, 0, 1]))

    def end(self, between=nothing):
        links, o_ref = self.links, self.o_ref
        self.onward.arrive()
        self.core.append(links.to(links.core, o_ref.at[0, :, 1, 1], o_ref.at[1, :, 1, 1]))
        between(2)
        for copy in self.core:
            copy.arrive()
        for copy in (*self.across, self.near, self.core[0]):
            copy.sent()


def spread_in(links, s_ref, o_ref, chunk, between=nothing, in_vmem=True):
    spread = Spread(links, s_ref, o_ref, chunk, in_vmem)
    spread.begin()
    between(0)
    spread.pass_on()
    between(1)
    spread.end(between)


def sum_in(links, bufs, chunk, partial, between=nothing, far=None):
    p_ref, core_in, out_y, in_y, out_t, in_t, hold = bufs
    order = ((1, 1), (1, 0), (0, 1), (0, 0))
    if partial:
        partial(1)
        far = p_ref.at[1]
    core = [links.to(links.core, far.at[:, t, y], core_in.at[i]) for i, (t, y) in enumerate(order)]
    if partial:
        partial(0)

    def both(i):
        t, y = order[i]
        core[i].arrive()
        return p_ref[0, :, t, y].astype(F32) + core_in[i].astype(F32)

    def near(i, m):
        return links.to(links.near, out_y.at[i, m], in_y.at[i, m])

    out_y[0] = both(0).astype(BF16)
    copies = [near(0, 0)]
    hold[...] = both(1)
    out_y[1] = both(2).astype(BF16)
    between(0)
    across = []
    for m in range(2):
        copies[m].arrive()
        copies += [near(0, 1)] if m == 0 else [near(1, 0), near(1, 1)]
        for i in range(p_ref.shape[-1] // chunk):
            a, b = slice(i * chunk, (i + 1) * chunk), slice((i ^ 1) * chunk, ((i ^ 1) + 1) * chunk)
            out_t[m, :, b] = (hold[m, :, a] + in_y[0, m, :, a].astype(F32)).astype(BF16)
        across.append(links.to(links.across, out_t.at[m], in_t.at[m]))
    hold[...] = both(3)
    between(1)
    for m in range(2):
        copies[2 + m].arrive()
        hold[m] += in_y[1, m].astype(F32)
    between(2)
    for m in range(2):
        across[m].arrive()
        hold[m] += in_t[m].astype(F32)
    for copy in (*core, *copies, *across):
        copy.sent()


def loop(count, step):
    def one(i, carry):
        step(i)
        return carry

    lax.fori_loop(0, count, one, 0)


def rows_of(ref, i):
    value = ref[i // 2, i % 2]
    return value.reshape(-1, value.shape[-1])


def away_rows(a_cols, b_ref, away_ref):
    depth, tile = away_ref.shape[0], 512

    def step(i):
        product = tn(a_cols(pl.multiple_of(depth + i * tile, tile), tile), b_ref[...])
        away_ref[pl.ds(pl.multiple_of(i * tile, tile), tile), :] = product.astype(BF16)

    loop(depth // tile, step)


def keep_rows(a_cols, b_ref, fold_ref, own_ref, send_ref):
    f = own_ref.shape[0]
    own_ref[...] = tn(a_cols(0, f), b_ref[...]) + fold_ref[:f, :].astype(F32)

    def step(i):
        at = pl.multiple_of(i * f, f)
        product = tn(a_cols(pl.multiple_of(at + f, f), f), b_ref[...])
        send_ref[pl.ds(at, f), :] = (product + fold_ref[pl.ds(pl.multiple_of(at + f, f), f), :].astype(F32)).astype(BF16)

    loop(3, step)


def middle_kernel(
    low_ref, cot_ref, gain_ref, attn_ref, wo_ref, c_ref, wd_ref, wg_ref, down_ref, gate_ref, up_ref,
    middle_ref, dmid_ref, gain_grad_ref, dall_ref, mixed_ref, own_d_ref, got_d_b_ref, got_d_o_ref, got_g_b_ref, send_g_ref, own_g_ref, keep_u_ref, away_u_ref,
    attn, wo, p, core_in, out_y, in_y, out_t, in_t, hold, xm_s, xm, c, wd, wg, wu, dact, gate, act, dg, du,
    away_d, fold_d, away_g, fold_g, own_d, send_d, send_g, up_tile, send, recv, *, batch_mask, chunk,
):
    links = Links(send, recv, batch_mask)
    f, ff = own_d.shape[0], act.shape[1]
    to, load = links.to, links.load
    loads = [load(attn_ref, attn), load(wo_ref, wo)]
    links.greet()

    def rows(ref, q):
        return ref.at[pl.ds(q * f, f), :]

    down = [to(links.seq, rows(wd_ref, q), rows(wd, q + 4)) for q in (1, 3)]
    gate_z = [to(links.batch, links.half(gate_ref, 0), rows(wg, 1)), to(links.both, links.half(gate_ref, 1), rows(wg, 3))]
    gates = [to(links.seq, rows(wg_ref, 2), rows(wg, 6))]
    up_t = to(links.across, links.half(up_ref, 1), rows(wu, 2))
    ups = []
    for copy in loads:
        copy.arrive()
    down += [load(rows(wd_ref, q), rows(wd, q)) for q in (1, 2, 3, 4, 6)]
    gates += [load(rows(wg_ref, q), rows(wg, q)) for q in (2, 4)]
    down.append(load(links.half(down_ref, 0), rows(wd, 0)))
    gates.append(load(links.half(gate_ref, 0), rows(wg, 0)))
    c_load = load(c_ref, c)
    up_own = load(links.half(up_ref, 0), rows(wu, 0))
    bufs = (p, core_in, out_y, in_y, out_t, in_t, hold)

    def out_partial(k):
        for m in range(2):
            at = (k * 2 + m) * attn.shape[0] // 4
            p[k, m] = nt(attn[at : at + attn.shape[0] // 4], wo[...]).astype(BF16).reshape(p.shape[2:])

    def while_out(stage):
        if stage == 0:
            ups.append(to(links.seq, links.half(up_ref, 0), rows(wu, 4)))
        if stage == 1:
            up_t.arrive()
            ups.append(to(links.seq, rows(wu, 2), rows(wu, 6)))
            up_z.append(to(links.batch, links.half(up_ref, 0), rows(wu, 1)))

    up_z = []
    sum_in(links, bufs, chunk, out_partial, while_out)
    for m in range(2):
        middle = low_ref[m].astype(F32) + hold[m]
        middle_ref[m] = middle
        xm_s[m] = (middle * inverse_rms(middle) * gain_ref[1:2, :]).astype(BF16)

    def while_xm(stage):
        if stage == 0:
            up_z.append(to(links.both, links.half(up_ref, 1), rows(wu, 3)))
            for copy in (*down, c_load):
                copy.arrive()

            def step(i):
                at = pl.ds(pl.multiple_of(i * 512, 512), 512)
                dact[at, :] = nn(c[at, :], wd[...])

            loop(c.shape[0] // 512, step)
            for copy in gate_z:
                copy.arrive()
            gates.extend(to(links.seq, rows(wg, q), rows(wg, q + 4)) for q in (1, 3))
        if stage == 1:
            up_z[0].arrive()
            ups.append(to(links.seq, rows(wu, 1), rows(wu, 5)))
        if stage == 2:
            up_z[1].arrive()
            ups.append(to(links.seq, rows(wu, 3), rows(wu, 7)))

    spread_in(links, xm_s, xm, chunk, while_xm)
    for copy in gates:
        copy.arrive()

    def gate_step(i):
        at = pl.ds(pl.multiple_of(i * 256, 256), 256)
        gate[at, :] = nn(rows_of(xm, i), wg[...])

    loop(4, gate_step)
    up_own.arrive()
    for copy in ups:
        copy.arrive()

    def up_step(i):
        base = pl.multiple_of(i * 256, 256)
        up_tile[...] = nn(rows_of(xm, i), wu[...])

        def part(j):
            at, here = pl.ds(pl.multiple_of(base + j * 32, 32), 32), pl.ds(pl.multiple_of(j * 32, 32), 32)
            g, u, d = gate[at, :], up_tile[here, :], dact[at, :]
            sig = 1.0 / (1.0 + jnp.exp(-g))
            silu = g * sig
            act[at, :] = (silu * u).astype(BF16)
            dg[at, :] = (d * u * sig * (1.0 + g * (1.0 - sig))).astype(BF16)
            du[at, :] = (d * silu).astype(BF16)

        loop(8, part)

    loop(4, up_step)

    def c_cols(at, n):
        return c[:, pl.ds(at, n)]

    def xm_cols(at, n):
        return xm[:, :, :, :, :, pl.ds(at, n)].reshape(-1, n)

    def fold(away, into, *places):
        return {i: to(links.seq, rows(away, i), rows(into, i)) for i in places}

    def compute_away(a_cols, b_ref, away, *places):
        for i in places:
            away[pl.ds(i * f, f), :] = tn(a_cols((i + 4) * f, f), b_ref[...]).astype(BF16)

    def total(a_cols, b_ref, into, i):
        return tn(a_cols(i * f, f), b_ref[...]) + into[pl.ds(i * f, f), :].astype(F32)

    compute_away(c_cols, act, away_d, 1)
    folds_d = fold(away_d, fold_d, 1)
    folds_g = {}
    compute_away(c_cols, act, away_d, 3)

    def back_partial(k):
        def step(m):
            at = pl.ds(pl.multiple_of((k * 2 + m) * 256, 256), 256)
            value = nt(dg[at, :], wg[...]) + nt(du[at, :], wu[...])
            p[k, m] = value.astype(BF16).reshape(p.shape[2:])

        loop(2, step)
        if k == 1:
            folds_d.update(fold(away_d, fold_d, 3))

    def settle_d(i, target, dst):
        folds_d[i].arrive()
        send_d[pl.ds((i - 1) * f, f), :] = total(c_cols, act, fold_d, i).astype(BF16)
        to(target, rows(send_d, i - 1), dst)

    def while_back(stage):
        if stage == 0:
            compute_away(c_cols, act, away_d, 0, 2)
        if stage == 1:
            settle_d(1, links.batch, got_d_b_ref)
            folds_d.update(fold(away_d, fold_d, 2, 0))
            settle_d(3, links.both, rows(got_d_o_ref, 1))
            compute_away(xm_cols, dg, away_g, 1, 3)
            folds_g.update(fold(away_g, fold_g, 1))
        if stage == 2:
            folds_g.update(fold(away_g, fold_g, 3))
            compute_away(xm_cols, dg, away_g, 0, 2)

    sum_in(links, bufs, chunk, back_partial, while_back)
    for m in range(2):
        middle = middle_ref[m]
        grad = cot_ref[m].astype(F32) + norm_grad(hold[m], middle, gain_ref[1:2, :], gain_grad_ref, m)
        dmid_ref[m] = grad
        xm_s[m] = grad.astype(BF16)

    later = []

    def while_mid(stage):
        if stage == 0:
            folds_d[0].arrive()
            own_d[...] = total(c_cols, act, fold_d, 0)
            own_load = load(own_d, own_d_ref)
            later.append(own_load)
        if stage == 1:
            settle_d(2, links.across, rows(got_d_o_ref, 0))
            folds_g[1].arrive()
            send_g[pl.ds(0, f), :] = total(xm_cols, dg, fold_g, 1).astype(BF16)
            to(links.batch, rows(send_g, 0), got_g_b_ref)
            folds_g.update(fold(away_g, fold_g, 2, 0))

            def step(i):
                at = pl.ds(pl.multiple_of(i * 512, 512), 512)
                dact[at, :] = tn(xm_cols(pl.multiple_of(i * 512, 512), 512), du[...])

            loop(2, step)
            load(dact, keep_u_ref)
            for copy in folds_d.values():
                copy.sent()
            compute_away(xm_cols, du, away_d, 0, 1, 2, 3)
            load(away_d, away_u_ref)

            def step(i):
                at = pl.ds(pl.multiple_of(i * 256, 256), 256)
                p[i // 2, i % 2] = nt(act[at, :], wd[...]).astype(BF16).reshape(p.shape[2:])

            loop(4, step)
            load(p, mixed_ref)
        if stage == 2:
            folds_g[3].arrive()
            send_g[pl.ds(2 * f, f), :] = total(xm_cols, dg, fold_g, 3).astype(BF16)

    spread_in(links, xm_s, dall_ref, chunk, while_mid, in_vmem=False)
    folds_g[2].arrive()
    send_g[pl.ds(f, f), :] = total(xm_cols, dg, fold_g, 2).astype(BF16)
    load(send_g.at[pl.ds(f, 2 * f), :], send_g_ref)
    folds_g[0].arrive()
    later[0].arrive()
    own_d[...] = total(xm_cols, dg, fold_g, 0)
    load(own_d, own_g_ref)
    links.finish()


def middle_call(batch_mask, low, cot, gain, attn, w_out, cot_all, w_down, w_gate, params, collective_id):
    _, rows, width = low.shape
    tokens, columns = attn.shape
    ff = w_down.shape[1]
    f = w_down.shape[0] // 8
    share, full = (2, rows, width), (2, 2, 2, 2, rows, width)
    vmem, hbm = pl.BlockSpec(memory_space=pltpu.VMEM), pl.BlockSpec(memory_space=pltpu.HBM)
    like = jax.ShapeDtypeStruct
    return pl.pallas_call(
        functools.partial(middle_kernel, batch_mask=batch_mask, chunk=2 * width // 8),
        in_specs=[vmem] * 3 + [hbm] * 8,
        out_specs=[vmem] * 3 + [hbm] * 10,
        out_shape=[
            like(share, F32),
            like(share, F32),
            like((1, width), F32),
            like(full, BF16),
            like(full, BF16),
            like((f, ff), F32),
            like((f, ff), BF16),
            like((2 * f, ff), BF16),
            like((f, ff), BF16),
            like((2 * f, ff), BF16),
            like((f, ff), F32),
            like((4 * f, ff), F32),
            like((4 * f, ff), BF16),
        ],
        scratch_shapes=[
            pltpu.VMEM((tokens, columns), BF16),
            pltpu.VMEM((width, columns), BF16),
            pltpu.VMEM(full, BF16),
            pltpu.VMEM((4, *share), BF16),
            pltpu.VMEM((2, *share), BF16),
            pltpu.VMEM((2, *share), BF16),
            pltpu.VMEM(share, BF16),
            pltpu.VMEM(share, BF16),
            pltpu.VMEM(share, F32),
            pltpu.VMEM(share, BF16),
            pltpu.VMEM(full, BF16),
            pltpu.VMEM((tokens, width), BF16),
            *[pltpu.VMEM((width, ff), BF16)] * 3,
            *[pltpu.VMEM((tokens, ff), F32)] * 2,
            *[pltpu.VMEM((tokens, ff), BF16)] * 3,
            *[pltpu.VMEM((4 * f, ff), BF16)] * 4,
            pltpu.VMEM((f, ff), F32),
            pltpu.VMEM((3 * f, ff), BF16),
            pltpu.VMEM((3 * f, ff), BF16),
            pltpu.VMEM((256, ff), F32),
            pltpu.SemaphoreType.DMA((96,)),
            pltpu.SemaphoreType.DMA((96,)),
        ],
        compiler_params=pltpu.CompilerParams(
            collective_id=collective_id, has_side_effects=True, vmem_limit_bytes=60 * MIB
        ),
        cost_estimate=TINY_COST,
    )(low, cot, gain, attn, w_out, cot_all, w_down, w_gate, *params)


def block_of(n, batch_mask):
    blk = lax.axis_index("blk")
    return blk ^ ((n // 2) * batch_mask) ^ ((n % 2) << TENSOR_BIT)


def key_tokens(block, half):
    head = lax.axis_index("head")
    index = lax.broadcasted_iota(jnp.int32, (2 * half, 1), 0)
    return token_offset(head, index, half // 2) + block * (2 * half)


def query_tokens(block, half, lanes):
    head = lax.axis_index("head")
    index = lax.broadcasted_iota(jnp.int32, (1, lanes), 1) % (2 * half)
    return token_offset(head, index, half // 2) + block * (2 * half)


def head_rows(ref, i, heads, width):
    both = [ref[c, i] for c in range(2)]
    return jnp.concatenate([b[:, h * width : (h + 1) * width] for h in range(heads) for b in both], axis=0)


def attention_back(q, do, k, v, start, ot, l, dq, dk, dv, kt, acc, batch_mask, scaling):
    parts, _, blocks, half, width = k.shape
    heads = q.shape[-1] // width
    lanes = heads * 2 * half
    dk[...] = jnp.zeros_like(dk)
    dv[...] = jnp.zeros_like(dv)

    def turn(kb):
        kt[kb] = key_rows(k, kb // blocks, kb % blocks).T

    loop(parts * blocks, turn)

    def per_query(i):
        q_rows, do_rows = head_rows(q, i, heads, width), head_rows(do, i, heads, width)
        delta = jnp.sum(do_rows.astype(F32).T * ot[i], axis=0, keepdims=True)
        inverse, first = 1.0 / l[i], start[i]
        acc[...] = jnp.zeros_like(acc)
        q_block = block_of(i, batch_mask)

        def per_key(kb):
            part, block = kb // blocks, kb % blocks
            k_block = block_of(block, batch_mask) ^ (part << SEQ_BIT)

            def add(diagonal):
                tokens = key_tokens(k_block, half)
                allowed = tokens >= first
                if diagonal:
                    allowed = allowed & (tokens <= query_tokens(q_block, half, lanes))
                score = nt(key_rows(k, part, block), q_rows) * (scaling * LOG2E)
                prob = jnp.where(allowed, jnp.exp2(score), 0.0) * inverse
                d_prob = nt(key_rows(v, part, block), do_rows)
                d_score = (prob * (d_prob - delta)).astype(BF16)
                d_v, d_k = nn(prob.astype(BF16), do_rows), nn(d_score, q_rows) * scaling
                for c in range(2):
                    dv[part, c, block] += d_v[c * half : (c + 1) * half]
                    dk[part, c, block] += d_k[c * half : (c + 1) * half]
                acc[...] += nn(kt[kb], d_score)

            @pl.when(k_block < q_block)
            def _():
                add(False)

            @pl.when(k_block == q_block)
            def _():
                add(True)

        loop(parts * blocks, per_key)
        rows = acc[...].T * scaling
        for h in range(heads):
            for c in range(2):
                at = (h * 2 + c) * half
                dq[c, i, :, h * width : (h + 1) * width] = rows[at : at + half]

    loop(blocks, per_query)


def last_kernel(
    low_ref, middle_ref, dmid_ref, gain_ref, gain_m_grad_ref, gain_q_ref, gain_k_ref, start_ref, l_ref,
    dall_ref, wo_ref, attn_ref, q_ref, k_ref, v_ref, ot_ref, raw_ref, table_ref, wa_ref, xa_ref, mixed_ref,
    send_g_ref, keep_u_ref, away_u_ref,
    mixed_own_ref, mixed_got_ref, input_own_ref, input_got_ref, sums_ref,
    got_g_o_ref, own_u_ref, got_u_b_ref, got_u_o_ref, own_a_ref, got_a_b_ref, got_a_o_ref, own_o_ref, got_o_b_ref, got_o_o_ref,
    dall, wo, attn, q, do, k, v, ot, raw, table, wa, xa, dq, dk, dv, kt, acc, kv_out, kv_in, d_qkv,
    p, core_in, out_y, in_y, out_t, in_t, hold, m_near, m_core_in, m_out_y, m_in_y, m_out_t, m_in_t, m_hold,
    swap_m, swap_i, keep_u, fold_u, own_u, send_u, away_o, fold_o, own_o, send_o, away_a, fold_a, own_a, send_a,
    gains_qk, gain_a_grad, ring_out, ring_in, send, recv, *, batch_mask, bit_order, scaling, chunk,
):
    links = Links(send, recv, batch_mask)
    to, load = links.to, links.load
    f = own_u.shape[0]
    heads = q.shape[-1] // k.shape[-1]
    width = k.shape[-1]

    def rows(ref, i):
        return ref.at[pl.ds(i * f, f), :]

    first = [load(dall_ref, dall), load(wo_ref, wo), load(attn_ref, attn)]
    second = [load(a, b) for a, b in ((q_ref, q), (k_ref, k), (v_ref, v), (ot_ref, ot))]
    third = [load(a, b) for a, b in ((raw_ref, raw), (table_ref, table), (wa_ref, wa), (xa_ref, xa))]
    mixed_near, keep_load = load(mixed_ref.at[0], m_near.at[0]), load(keep_u_ref, keep_u)
    links.greet()

    def settle(src, dst_b, dst_o):
        to(links.batch, rows(src, 0), dst_b)
        to(links.both, rows(src, 2), rows(dst_o, 1))
        to(links.across, rows(src, 1), rows(dst_o, 0))

    to(links.both, rows(send_g_ref, 1), rows(got_g_o_ref, 1))
    to(links.across, rows(send_g_ref, 0), rows(got_g_o_ref, 0))
    folds_u = {i: to(links.seq, rows(away_u_ref, i), rows(fold_u, i)) for i in (1, 3)}
    for copy in (*first, *second):
        copy.arrive()

    def total_u(i):
        return keep_u[pl.ds(i * f, f), :] + fold_u[pl.ds(i * f, f), :].astype(F32)

    def settle_u(i, target, dst):
        folds_u[i].arrive()
        send_u[pl.ds((i - 1) * f, f), :] = total_u(i).astype(BF16)
        to(target, rows(send_u, i - 1), dst)

    def d_attn(i):
        at = pl.ds(pl.multiple_of(i * 256, 256), 256)
        value = nn(dall[at, :], wo[...]).astype(BF16)
        do[i // 2, pl.ds((i % 2) * 2, 2)] = value.reshape(2, 128, value.shape[1])

    def dall_cols(at, n):
        return dall[:, pl.ds(at, n)]

    def xa_cols(at, n):
        return xa[:, pl.ds(at, n)]

    def input_partial(c):
        def step(m):
            at = pl.ds(pl.multiple_of((c * 2 + m) * 256, 256), 256)
            pair = pl.ds(m * 2, 2)
            got = kv_in[at, :].astype(F32)
            cos, sin = table[at, : width // 2], table[at, width // 2 :]
            cos, sin = jnp.concatenate([cos, cos], axis=1), jnp.concatenate([-sin, sin], axis=1)
            for h in range(heads + 1):
                cut = slice(h * width, (h + 1) * width)
                if h < heads:
                    grad = dq[c, pair, :, cut].reshape(256, width)
                else:
                    grad = dk[0, c, pair].reshape(256, width) + got[:, :width]
                gain = (gain_q_ref if h < heads else gain_k_ref)[...].astype(F32)
                values = raw[at, cut]
                inverse = inverse_rms(values)
                normed = values * inverse
                turned = grad * cos - pltpu.roll(grad, width // 2, 1) * sin
                row = 0 if h < heads else 1
                gains_qk[row : row + 1, :] += jnp.sum(turned * normed, axis=0, keepdims=True)
                scaled = turned * gain
                mean = jnp.mean(scaled * normed, axis=-1, keepdims=True)
                d_qkv[at, cut] = (inverse * (scaled - normed * mean)).astype(BF16)
            d_qkv[at, (heads + 1) * width :] = (dv[0, c, pair].reshape(256, width) + got[:, width:]).astype(BF16)
            p[c, m] = nt(d_qkv[at, :], wa[...]).astype(BF16).reshape(p.shape[2:])

        loop(2, step)

    def while_input(stage):
        if stage == 0:
            away_rows(xa_cols, d_qkv, away_a)
            folds.extend(to(links.seq, rows(away_a, i), rows(fold_a, i)) for i in (1, 3, 0, 2))
        if stage == 1:
            folds[0].arrive()
            keep_rows(dall_cols, attn, fold_o, own_o, send_o)
            settle(send_o, got_o_b_ref, got_o_o_ref)
            load(own_o, own_o_ref)
            folds_u.update({i: to(links.seq, rows(away_u_ref, i), rows(fold_u, i)) for i in (2, 0)})

    folds = []

    def while_mixed(stage):
        if stage == 0:
            loop(4, d_attn)
            attention_back(q, do, k, v, start_ref, ot, l_ref, dq, dk, dv, kt, acc, batch_mask, scaling)
            kv_out[:, :width] = dk[1].reshape(-1, width).astype(BF16)
            kv_out[:, width:] = dv[1].reshape(-1, width).astype(BF16)
            folds.extend(
                to(links.seq, kv_out.at[pl.ds(i, 128), :], kv_in.at[pl.ds(i, 128), :])
                for i in range(0, kv_out.shape[0], 128)
            )
            keep_load.arrive()
            settle_u(1, links.batch, got_u_b_ref)
            settle_u(3, links.both, rows(got_u_o_ref, 1))
        if stage == 1:
            away_rows(dall_cols, attn, away_o)
            out_fold = to(links.seq, away_o, fold_o)
            for copy in (*folds, *third):
                copy.arrive()
            folds[:] = [out_fold]
            gains_qk[...] = jnp.zeros_like(gains_qk)
            sum_in(links, (p, core_in, out_y, in_y, out_t, in_t, hold), chunk, input_partial, while_input)
            for m in range(2):
                grad = dmid_ref[m] + norm_grad(hold[m], low_ref[m].astype(F32), gain_ref[0:1, :], gain_a_grad, m)
                store_ungrouped(grad, input_own_ref if m == 0 else swap_i, blk, bit_order)
            to(links.batch, swap_i, input_got_ref)
            for copy in folds:
                copy.arrive()
            keep_rows(xa_cols, d_qkv, fold_a, own_a, send_a)
            settle(send_a, got_a_b_ref, got_a_o_ref)
            load(own_a, own_a_ref)

    mixed_near.arrive()
    blk = lax.axis_index("blk")
    sum_in(links, (m_near, m_core_in, m_out_y, m_in_y, m_out_t, m_in_t, m_hold), chunk, None, while_mixed, mixed_ref.at[1])
    store_ungrouped(middle_ref[0] + m_hold[0], mixed_own_ref, blk, bit_order)
    store_ungrouped(middle_ref[1] + m_hold[1], swap_m, blk, bit_order)
    to(links.batch, swap_m, mixed_got_ref)
    settle_u(2, links.across, rows(got_u_o_ref, 0))
    folds_u[0].arrive()
    own_u[...] = total_u(0)
    load(own_u, own_u_ref)
    n = gain_a_grad.shape[1]
    store_ungrouped(gain_a_grad[...], sums_ref.at[:, pl.ds(0, n)], blk, bit_order)
    sums_ref[:, n : n + width] = gains_qk[0:1, :]
    sums_ref[:, n + width : n + 2 * width] = gains_qk[1:2, :]
    store_ungrouped(gain_m_grad_ref[...], sums_ref.at[:, pl.ds(n + 2 * width, n)], blk, bit_order)
    for i, target in enumerate((links.core, links.near, links.seq, links.across, links.batch)):
        ring_out[i] = sums_ref[...]
        to(target, ring_out.at[i], ring_in.at[i]).arrive()
        sums_ref[...] += ring_in[i]
    links.finish()


def last_call(batch_mask, bit_order, scaling, arrays, collective_id):
    low, dall, attn, q, k, raw, wa, away_u = (arrays[n] for n in ("low", "dall", "attn", "q", "k", "raw", "wa", "away_u"))
    _, rows, width = low.shape
    tokens, columns = attn.shape
    head_size = k.shape[-1]
    ff, f = away_u.shape[1], away_u.shape[0] // 4
    n_a = wa.shape[1]
    share, full, half_full = (2, rows, width), (2, 2, 2, 2, rows, width), (1, 2, 2, 2, rows, width)
    vmem, hbm = pl.BlockSpec(memory_space=pltpu.VMEM), pl.BlockSpec(memory_space=pltpu.HBM)
    like, held = jax.ShapeDtypeStruct, pltpu.VMEM
    in_vmem = ("low", "middle", "d_middle", "gain", "gain_m_grad", "gain_q", "gain_k", "start", "l")
    in_hbm = (
        "dall", "w_out", "attn", "q", "k", "v", "ot", "raw", "table", "wa", "xa", "mixed", "send_g", "keep_u", "away_u",
    )
    total = 2 * width + 2 * head_size
    lanes = 2 * 2 * 128
    sums = (1, total)
    own_and_send = lambda n: [held((f, n), F32), held((3 * f, n), BF16)]
    sum_bufs = [
        held((4, *share), BF16), held((2, *share), BF16), held((2, *share), BF16), held(share, BF16), held(share, BF16),
    ]
    return pl.pallas_call(
        functools.partial(last_kernel, batch_mask=batch_mask, bit_order=bit_order, scaling=scaling, chunk=2 * width // 8),
        in_specs=[vmem] * len(in_vmem) + [hbm] * len(in_hbm),
        out_specs=[vmem, hbm, vmem, hbm, vmem] + [hbm] * 10,
        out_shape=[
            like((rows, width), BF16),
            like((rows, width), BF16),
            like((rows, width), F32),
            like((rows, width), BF16),
            like(sums, F32),
            like((2 * f, ff), BF16),
            *[
                like((m * f, n), dtype)
                for n in (ff, n_a, columns)
                for m, dtype in ((1, F32), (1, BF16), (2, BF16))
            ],
        ],
        scratch_shapes=[
            held((tokens, width), BF16),
            held((width, columns), BF16),
            held((tokens, columns), BF16),
            held(q.shape, BF16),
            held(q.shape, BF16),
            held(k.shape, BF16),
            held(k.shape, BF16),
            held((4, head_size, lanes), F32),
            held(raw.shape, F32),
            held((tokens, head_size), F32),
            held(wa.shape, BF16),
            held((tokens, width), BF16),
            held(q.shape, F32),
            held(k.shape, F32),
            held(k.shape, F32),
            held((8, head_size, 256), BF16),
            held((head_size, lanes), F32),
            held((tokens, 2 * head_size), BF16),
            held((tokens, 2 * head_size), BF16),
            held((tokens, n_a), BF16),
            held(full, BF16),
            *sum_bufs,
            held(share, F32),
            held(half_full, BF16),
            *sum_bufs,
            held(share, F32),
            held((rows, width), BF16),
            held((rows, width), BF16),
            held((4 * f, ff), F32),
            held((4 * f, ff), BF16),
            *own_and_send(ff),
            held((4 * f, columns), BF16),
            held((4 * f, columns), BF16),
            *own_and_send(columns),
            held((4 * f, n_a), BF16),
            held((4 * f, n_a), BF16),
            *own_and_send(n_a),
            held((8, head_size), F32),
            held((1, width), F32),
            held((5, *sums), F32),
            held((5, *sums), F32),
            pltpu.SemaphoreType.DMA((96,)),
            pltpu.SemaphoreType.DMA((96,)),
        ],
        compiler_params=pltpu.CompilerParams(
            collective_id=collective_id, has_side_effects=True, vmem_limit_bytes=60 * MIB
        ),
        cost_estimate=TINY_COST,
    )(*[arrays[n] for n in (*in_vmem, *in_hbm)])


def attention(q, k, v, start, out, ot, total_ref, vt, acc, total, batch_mask, scaling):
    parts, _, blocks, half, width = k.shape
    heads = q.shape[-1] // width
    lanes = heads * 2 * half

    def turn(kb):
        vt[kb] = key_rows(v, kb // blocks, kb % blocks).T

    loop(parts * blocks, turn)

    def per_query(i):
        q_rows = head_rows(q, i, heads, width)
        first = start[i]
        acc[...] = jnp.zeros_like(acc)
        total[...] = jnp.zeros_like(total)
        q_block = block_of(i, batch_mask)

        def per_key(kb):
            part, block = kb // blocks, kb % blocks
            k_block = block_of(block, batch_mask) ^ (part << SEQ_BIT)

            def add(diagonal):
                tokens = key_tokens(k_block, half)
                allowed = tokens >= first
                if diagonal:
                    allowed = allowed & (tokens <= query_tokens(q_block, half, lanes))
                score = nt(key_rows(k, part, block), q_rows) * (scaling * LOG2E)
                e = jnp.where(allowed, jnp.exp2(score), 0.0)
                total[...] += jnp.sum(e, axis=0, keepdims=True)
                acc[...] += nn(vt[kb], e.astype(BF16))

            @pl.when(k_block < q_block)
            def _():
                add(False)

            @pl.when(k_block == q_block)
            def _():
                add(True)

        loop(parts * blocks, per_key)
        value = acc[...] / total[...]
        ot[i] = value
        total_ref[i] = total[...]
        rows = value.T
        for h in range(heads):
            for c in range(2):
                at = (h * 2 + c) * half
                out[c, i, :, h * width : (h + 1) * width] = rows[at : at + half].astype(BF16)

    loop(blocks, per_query)


def first_kernel(
    gain_a_ref, gain_m_ref, gain_q_ref, gain_k_ref, table_ref, start_ref,
    hid_ref, far_ref, cot_ref, wq_ref, wk_ref, wv_ref, wo_ref, wd_ref, wg_ref,
    low_ref, cot_low_ref, gains_out_ref, l_ref,
    xa_ref, call_ref, wa_out, wo_out, wd_out, wg_out, q_ref, k_ref, v_ref, raw_ref, attn_ref, ot_ref,
    x_in, c_in, xa_s, xa, wa, wb, q, k, v, raw, out, ot, vt, acc, total, send, recv, *, batch_mask, bit_order, scaling, chunk,
):
    links = Links(send, recv, batch_mask)
    to, load = links.to, links.load
    blk = lax.axis_index("blk")
    batch = bit_of(blk, bit_order[0])
    width = k.shape[-1]
    heads = q.shape[-1] // width
    f = wa.shape[0] // 8
    a_params, at = [], 0
    for ref in (wq_ref, wk_ref, wv_ref):
        n = ref.shape[1] // 2
        a_params.append((ref, at, n))
        at += n

    def rows(ref, i):
        return ref.at[pl.ds(i * f, f), :]

    x_own, x_far = load(hid_ref.at[batch], x_in.at[0]), load(far_ref, x_in.at[1])
    c_own = load(cot_ref.at[batch], c_in.at[0])
    a_own = [load(links.half(ref, 0), wa.at[pl.ds(0, f), pl.ds(start, n)]) for ref, start, n in a_params]
    a_other = [load(links.half(ref, 1), wb.at[:, pl.ds(start, n)]) for ref, start, n in a_params]
    links.greet()
    for copy in (*a_own, *a_other):
        copy.arrive()
    a_t = to(links.across, wb, rows(wa, 2))
    a_rest = [to(links.seq, rows(wa, 0), rows(wa, 4))]
    to(links.seq, links.half(wo_ref, 0), rows(wo_out, 4))
    load(links.half(wo_ref, 0), rows(wo_out, 0))
    to(links.seq, links.half(wd_ref, 0), rows(wd_out, 4))
    to(links.seq, links.half(wg_ref, 0), rows(wg_out, 4))
    n_blocks = 1 << len(bit_order)
    n = x_in.shape[-1] // n_blocks

    def regroup(src, dst, lead):
        for p in range(n_blocks):
            cut = pl.ds(pl.multiple_of(place_of_block(blk, bit_order, p) * n, n), n)
            dst[(*lead, pl.ds(p * n, n))] = src[(*lead, cut)]

    all_rows = (slice(None), slice(None))
    for p in range(n_blocks):
        cut = pl.ds(pl.multiple_of(place_of_block(blk, bit_order, p) * n, n), n)
        gains_out_ref[0:1, p * n : (p + 1) * n] = gain_a_ref[:, cut].astype(F32)
        gains_out_ref[1:2, p * n : (p + 1) * n] = gain_m_ref[:, cut].astype(F32)
    x_own.arrive()
    x_far.arrive()
    a_far = {1: to(links.batch, rows(wa, 0), rows(wa, 1)), 3: to(links.both, wb, rows(wa, 3))}
    c_far = to(links.batch, cot_ref.at[1 - batch], c_in.at[1])
    regroup(x_in, low_ref, all_rows)
    for m in range(2):
        value = low_ref[m].astype(F32)
        xa_s[m] = (value * inverse_rms(value) * gains_out_ref[0:1, :]).astype(BF16)

    by_rows = Spread(links, xa_s, xa, chunk)
    by_rows.begin()
    a_t.arrive()
    a_rest.append(to(links.seq, rows(wa, 2), rows(wa, 6)))
    by_rows.pass_on()
    down_t = to(links.across, links.half(wd_ref, 1), rows(wd_out, 2))
    out_rows = [to(links.across, links.half(wo_ref, 1), rows(wo_out, 2))]
    for i, copy in a_far.items():
        copy.arrive()
        a_rest.append(to(links.seq, rows(wa, i), rows(wa, i + 4)))
    c_own.arrive()
    c_far.arrive()
    regroup(c_in, cot_low_ref, all_rows)
    by_cot = Spread(links, cot_low_ref, call_ref, chunk, in_vmem=False)
    by_cot.begin()
    out_rows.append(to(links.batch, links.half(wo_ref, 0), rows(wo_out, 1)))
    out_rows.append(to(links.both, links.half(wo_ref, 1), rows(wo_out, 3)))
    to(links.both, links.half(wd_ref, 1), rows(wd_out, 3))
    by_rows.end()
    load(xa, xa_ref)

    def prepare_rows(i):
        c, m = i // 2, i % 2
        pair = pl.ds(m * 2, 2)
        at = pl.ds(pl.multiple_of(i * 256, 256), 256)
        acc_rows = nn(rows_of(xa, i), wa[...])
        raw[at, :] = acc_rows[:, : (heads + 1) * width]
        cos, sin = table_ref[at, : width // 2], table_ref[at, width // 2 :]
        cos, sin = jnp.concatenate([cos, cos], axis=1), jnp.concatenate([-sin, sin], axis=1)
        for h in range(heads + 1):
            part = acc_rows[:, h * width : (h + 1) * width]
            scaled = part * inverse_rms(part) * (gain_q_ref if h < heads else gain_k_ref)[...].astype(F32)
            turned = (scaled * cos + pltpu.roll(scaled, width // 2, 1) * sin).astype(BF16).reshape(2, 128, width)
            if h < heads:
                q[c, pair, :, h * width : (h + 1) * width] = turned
            else:
                k[0, c, pair] = turned
        v[0, c, pair] = acc_rows[:, (heads + 1) * width :].astype(BF16).reshape(2, 128, width)

    for copy in a_rest:
        copy.arrive()
    loop(4, prepare_rows)
    kv = [to(links.seq, ref.at[0, c, i], ref.at[1, c, i]) for ref in (k, v) for c in range(2) for i in range(4)]
    to(links.batch, links.half(wd_ref, 0), rows(wd_out, 1))
    load(wa, wa_out)
    load(raw, raw_ref)
    load(q, q_ref)
    down_t.arrive()
    to(links.seq, rows(wd_out, 2), rows(wd_out, 6))
    by_cot.pass_on()
    to(links.across, links.half(wg_ref, 1), rows(wg_out, 2))
    for i, copy in zip((2, 1, 3), out_rows):
        copy.arrive()
        to(links.seq, rows(wo_out, i), rows(wo_out, i + 4))
    for copy in kv:
        copy.arrive()
    load(k, k_ref)
    load(v, v_ref)
    attention(q, k, v, start_ref, out, ot, l_ref, vt, acc, total, batch_mask, scaling)
    load(out, attn_ref)
    load(ot, ot_ref)
    by_cot.end()
    links.finish()


def first_call(batch_mask, bit_order, scaling, arrays, collective_id):
    hid, wq, wk, wv, wo, wd, wg = (arrays[n] for n in ("hidden", "wq", "wk", "wv", "wo", "wd", "wg"))
    _, rows, width = hid.shape
    tokens, head_size = 16 * rows, arrays["gain_q"].shape[1]
    columns, n_a = wq.shape[1] // 2, (wq.shape[1] + wk.shape[1] + wv.shape[1]) // 2
    heads = columns // head_size
    half, lanes = tokens // 8, heads * tokens // 4
    share, full = (2, rows, width), (2, 2, 2, 2, rows, width)
    vmem, hbm = pl.BlockSpec(memory_space=pltpu.VMEM), pl.BlockSpec(memory_space=pltpu.HBM)
    like, held = jax.ShapeDtypeStruct, pltpu.VMEM
    in_vmem = ("gain_a", "gain_m", "gain_q", "gain_k", "table", "start")
    in_hbm = ("hidden", "far", "cotangent", "wq", "wk", "wv", "wo", "wd", "wg")
    q_shape, k_shape = (2, 4, half, columns), (2, 2, 4, half, head_size)
    ot_shape, raw_shape = (4, head_size, lanes), (tokens, (heads + 1) * head_size)
    return pl.pallas_call(
        functools.partial(first_kernel, batch_mask=batch_mask, bit_order=bit_order, scaling=scaling, chunk=2 * width // 8),
        in_specs=[vmem] * len(in_vmem) + [hbm] * len(in_hbm),
        out_specs=[vmem] * 4 + [hbm] * 12,
        out_shape=[
            like(share, BF16),
            like(share, BF16),
            like((2, width), F32),
            like((4, 1, lanes), F32),
            like(full, BF16),
            like(full, BF16),
            like((width, n_a), BF16),
            like((width, columns), BF16),
            like((width, wd.shape[1] // 2), BF16),
            like((width, wg.shape[1] // 2), BF16),
            like(q_shape, BF16),
            like(k_shape, BF16),
            like(k_shape, BF16),
            like(raw_shape, F32),
            like(q_shape, BF16),
            like(ot_shape, F32),
        ],
        scratch_shapes=[
            held(share, BF16),
            held(share, BF16),
            held(share, BF16),
            held(full, BF16),
            held((width, n_a), BF16),
            held((width // 8, n_a), BF16),
            held(q_shape, BF16),
            held(k_shape, BF16),
            held(k_shape, BF16),
            held(raw_shape, F32),
            held(q_shape, BF16),
            held(ot_shape, F32),
            held((8, head_size, 2 * half), BF16),
            held((head_size, lanes), F32),
            held((1, lanes), F32),
            pltpu.SemaphoreType.DMA((96,)),
            pltpu.SemaphoreType.DMA((96,)),
        ],
        compiler_params=pltpu.CompilerParams(
            collective_id=collective_id, has_side_effects=True, vmem_limit_bytes=56 * MIB
        ),
        cost_estimate=TINY_COST,
    )(*[arrays[n] for n in (*in_vmem, *in_hbm)])


def finish_kernel(mixed_own, mixed_got, input_own, input_got, *refs, sources, widths, batch_bit):
    ins, (mixed_ref, input_ref, *outs) = refs[: 3 * sources], refs[3 * sources :]
    blk = lax.axis_index("blk")
    place, batch, k = bit_of(blk, TENSOR_BIT), bit_of(blk, batch_bit), 0
    mixed_ref[batch] = mixed_own[...]
    mixed_ref[1 - batch] = mixed_got[...]
    input_ref[batch] = input_own[...]
    input_ref[1 - batch] = input_got[...].astype(F32)
    for own, by_batch, by_other in zip(ins[::3], ins[1::3], ins[2::3]):
        at = 0
        while at < own.shape[1]:
            w, cut = widths[k], slice(at, at + widths[k])
            mine = pl.ds(pl.multiple_of(place * w, w), w)
            theirs = pl.ds(pl.multiple_of((1 - place) * w, w), w)
            outs[k][:, mine] = own[:, cut] + by_batch[:, cut].astype(F32)
            outs[k][:, theirs] = by_other[0, :, cut].astype(F32) + by_other[1, :, cut].astype(F32)
            at += w
            k += 1


def finish_call(batch_bit, rows, sources, widths):
    steps = 4
    f, (n_rows, width) = sources[0][0].shape[0], rows[0].shape
    tile, row_tile = f // steps, n_rows // steps
    by_rows = lambda t, n: pl.BlockSpec((t, n), lambda i: (i, 0))
    by_pairs = lambda t, n: pl.BlockSpec((2, t, n), lambda i: (0, i, 0))
    flat, specs = [], []
    for own, by_batch, by_other in sources:
        n = own.shape[1]
        flat += [own, by_batch, by_other.reshape(2, f, n)]
        specs += [by_rows(tile, n), by_rows(tile, n), by_pairs(tile, n)]
    like = jax.ShapeDtypeStruct
    return pl.pallas_call(
        functools.partial(finish_kernel, sources=len(sources), widths=widths, batch_bit=batch_bit),
        grid=(steps,),
        in_specs=[*[by_rows(row_tile, width)] * 4, *specs],
        out_specs=[*[by_pairs(row_tile, width)] * 2, *[by_rows(tile, 2 * w) for w in widths]],
        out_shape=[
            like((2, n_rows, width), BF16),
            like((2, n_rows, width), F32),
            *[like((f, 2 * w), F32) for w in widths],
        ],
        compiler_params=pltpu.CompilerParams(vmem_limit_bytes=60 * MIB),
        cost_estimate=TINY_COST,
    )(*rows, *flat)


def local(
    hidden_in,
    lengths,
    query_weight,
    key_matrix,
    value_matrix,
    out_weight,
    gate_weight,
    up_weight,
    down_weight,
    attn_gain,
    query_gain,
    key_gain,
    mlp_gain,
    cotangent,
):
    ring = lax.axis_size("blk")
    bits = ring.bit_length() - 1
    batch_bit = bits - 1
    extra_bits = [i for i in range(bits) if i not in (TENSOR_BIT, SEQ_BIT, batch_bit)]
    seq_bits = [SEQ_BIT, *extra_bits]
    parts = 1 << len(seq_bits)
    bit_order = [batch_bit, TENSOR_BIT, SEQ_BIT, *extra_bits]
    b_mask, t_mask, x_mask = 1 << batch_bit, 1 << TENSOR_BIT, 1 << SEQ_BIT
    blk, head = lax.axis_index("blk"), lax.axis_index("head")
    batch, tensor = bit_of(blk, batch_bit), bit_of(blk, TENSOR_BIT)

    local_rows, width = hidden_in.shape[1:]
    block_rows = local_rows * lax.axis_size("head")
    half = block_rows // 2
    row_features = width // ring
    head_size = query_gain.shape[0]
    scaling = head_size ** (-0.5)
    tokens = 16 * local_rows
    heads = query_weight.shape[1] // (2 * head_size)
    ff = gate_weight.shape[1] // 2

    def moved(values, place_of):
        axis = values.ndim - 1
        return jnp.concatenate(
            [
                lax.dynamic_slice_in_dim(values, place_of(i) * row_features, row_features, axis)
                for i in range(ring)
            ],
            axis=axis,
        )

    def regroup(values):
        return moved(values, lambda p: blk ^ sum(((p >> i) & 1) << b for i, b in enumerate(bit_order)))

    def ungroup(values):
        return moved(values, lambda n: sum(bit_of(blk ^ n, b) << i for i, b in enumerate(bit_order)))

    def everything(ref):
        return ref

    def mask_of(p):
        return sum(((p >> i) & 1) << b for i, b in enumerate(bit_order))

    def rows_at(p):
        return lambda ref: ref.at[pl.ds(p * row_features, row_features), :]

    def half_cut(n, other):
        def cut(ref):
            place = bit_of(lax.axis_index("blk"), TENSOR_BIT)
            place = 1 - place if other else place
            return ref.at[:, pl.ds(pl.multiple_of(place * n, n), n)]

        return cut

    def send_over(plan, weight, buffer, p, point):
        mask, n = mask_of(p), weight.shape[1] // 2
        plan.copy((plan.read(weight), half_cut(n, mask & t_mask)), (buffer, rows_at(p)), mask, point=point)

    def keep_own(plan, weight, buffer, point, onward=True):
        here, n = plan.read(weight), weight.shape[1] // 2
        if onward:
            plan.copy((here, half_cut(n, 0)), (buffer, rows_at(4)), x_mask, point=point)
        plan.local((here, half_cut(n, 0)), (buffer, rows_at(0)), (row_features, n), point=point)

    def send_on(plan, buffer, places, point, after=None):
        for p in places:
            plan.copy((buffer, rows_at(p)), (buffer, rows_at(p + 4)), x_mask, after=after, point=point)

    def lay(plan, array, buffer, p, point=0, columns=None, onward=False):
        here = plan.read(array)
        cut = (lambda ref: ref.at[:, pl.ds(*columns)]) if columns else everything
        if onward:
            plan.copy((here, cut), (buffer, rows_at(p + 4)), x_mask, point=point)
        plan.local((here, cut), (buffer, rows_at(p)), (row_features, columns[1] if columns else array.shape[1]), point)

    def fresh_for(plan, weights):
        return plan.fresh(buffer_shape(weights), BF16)

    def buffer_shape(weights):
        return (8 * row_features, sum(w.shape[1] for w in weights) // 2)

    def whole_weight(buffer):
        pieces = [buffer]
        for b in extra_bits:
            pieces = pieces + [over_blk(c, 1 << b) for c in pieces]
        return jnp.concatenate(pieces, axis=0) if extra_bits else buffer

    def split_grad(grad):
        for b in reversed(extra_bits):
            n = grad.shape[0] // 2
            grad = grad[:n] + over_blk(grad[n:].astype(BF16), 1 << b).astype(F32)
        n = grad.shape[0] // 2
        return grad[:n], grad[n:].astype(BF16)

    def weight_sum(a, b):
        return split_grad(tn(a, b)) if extra_bits else weight_grad(a, b)

    def fold(plan, source, shape, point=0):
        plan.copy((source, everything), (plan.fresh(shape, BF16), everything), x_mask, point=point)

    def fold_part(plan, source, buffer, start, n, point=0):
        def part(ref):
            return ref.at[:, pl.ds(start, n)]

        plan.copy((source, part), (buffer, part), x_mask, point=point)

    def to_settle(keep, got):
        total = keep + got.astype(F32)
        return total[:row_features], total[row_features:].astype(BF16)

    def settle(plan, away, t_point=0):
        out, here = plan.fresh(away.shape, away.dtype), plan.read(away)
        for i, mask in ((0, b_mask), (2, b_mask | t_mask), (1, t_mask)):
            plan.copy((here, rows_at(i)), (out, rows_at(i)), mask, point=t_point if mask == t_mask else 0)

    def settled(sources, column_widths):
        if all(w % 128 == 0 for w in column_widths):
            return assemble(tensor, sources, column_widths)
        f, results = row_features, []
        widths = iter(column_widths)
        for own, got in sources:
            own = own + got[:f].astype(F32)
            other = got[f : 2 * f].astype(F32) + got[2 * f :].astype(F32)
            at = 0
            while at < own.shape[1]:
                w = next(widths)
                results.append(in_order(tensor, own[:, at : at + w], other[:, at : at + w], 1))
                at += w
        return results

    chunk = 2 * row_features
    ids = iter(range(100))

    def spread(flat, plan, fills=(), limit=None):
        (out,), rest = run(plan, spread_main(flat, chunk), next(ids), fills=fills, limit=limit)
        return out.reshape(tokens, width), rest

    share = (2, local_rows, width)

    def gather_sum(partial, plan, extra, outs_like, finish, fills=()):
        return run(plan, gather_main(partial, chunk, extra, outs_like, finish), next(ids), fills=fills)

    def like(shape, dtype):
        return jax.ShapeDtypeStruct(shape, dtype)

    aligned = row_features % 128 == 0
    local_order = bit_order if aligned else []

    def split_batch(rows):
        mine = lax.dynamic_index_in_dim(rows, batch, 0, keepdims=False)
        theirs = lax.dynamic_index_in_dim(rows, 1 - batch, 0, keepdims=False)
        return mine, theirs

    def natural(rows):
        return rows if aligned else ungroup(rows)

    length_row = lax.dynamic_index_in_dim(lengths, batch, 0, keepdims=False)
    doc_ends = jnp.cumsum(length_row)
    batch_flip = jnp.arange(2, dtype=jnp.int32)[:, None] << batch_bit
    tensor_flip = jnp.arange(2, dtype=jnp.int32)[None, :] << TENSOR_BIT
    q_blocks = (blk ^ batch_flip ^ tensor_flip).reshape(4)
    index = jnp.arange(2 * half, dtype=jnp.int32)
    in_block = token_offset(head, index, local_rows).reshape(2, 1, half)
    token_index = q_blocks[None, :, None] * block_rows + in_block
    passed = doc_ends <= token_index[..., None]
    doc_start = jnp.max(jnp.where(passed, doc_ends, 0), axis=-1).astype(jnp.int32)
    position = (token_index - doc_start).reshape(tokens)
    start_lanes = jnp.tile(jnp.transpose(doc_start, (1, 0, 2)).reshape(4, 1, 2 * half), (1, 1, heads))
    k_blocks = q_blocks
    for b in seq_bits:
        k_blocks = jnp.concatenate([k_blocks, k_blocks ^ (1 << b)])
    least_start = jnp.min(doc_start, axis=(0, 2))[:, None]
    last_start = jnp.max(doc_start, axis=(0, 2))[:, None]
    k_first = (k_blocks * block_rows)[None, :]
    none = (k_blocks[None, :] > q_blocks[:, None]) | (k_first + block_rows <= least_start)
    whole = (k_blocks[None, :] < q_blocks[:, None]) & (k_first >= last_start)
    flags = jnp.where(none, 0, jnp.where(whole, 1, 2))
    meta = jnp.concatenate([head[None], q_blocks, k_blocks, flags.reshape(-1)]).astype(jnp.int32)

    inverse_freq = THETA ** (-jnp.arange(head_size // 2, dtype=F32) / (head_size // 2))
    angles = position.astype(F32)[:, None] * inverse_freq[None, :]
    cosine, sine = jnp.cos(angles), jnp.sin(angles)
    table = jnp.concatenate([cosine, sine], axis=1)
    cosine = jnp.concatenate([cosine, cosine], axis=1)
    sine = jnp.concatenate([-sine, sine], axis=1)

    def rms(values):
        return lax.rsqrt(jnp.mean(values * values, axis=-1, keepdims=True) + EPS)

    def norm_back(grad, normed, inverse, gain):
        scaled = grad * gain
        return inverse * (scaled - normed * jnp.mean(scaled * normed, axis=-1, keepdims=True))

    gains_in = jnp.stack([attn_gain, mlp_gain]).astype(F32)
    gain_q = query_gain.astype(F32)[None]
    gain_k = key_gain.astype(F32)[None]

    q_columns, k_columns = heads * head_size, head_size
    a_weights = (query_weight, key_matrix, value_matrix)

    def halves(weights, which):
        return jnp.concatenate(
            [lax.dynamic_slice_in_dim(w, which * (w.shape[1] // 2), w.shape[1] // 2, 1) for w in weights], axis=1
        )

    if extra_bits:
        mine, theirs = split_batch(hidden_in)
        other = over_blk(theirs, b_mask)
        a_own, a_other = halves(a_weights, tensor), halves(a_weights, 1 - tensor)
        a_by_t = over_blk(a_other, t_mask)
        a_by_b = over_blk(a_own, b_mask)
        early = over_blk(jnp.concatenate([a_own, halves((down_weight,), tensor)], axis=1), x_mask)
        (mine, other, cosine, sine, start_lanes, meta) = pin((mine, other, cosine, sine, start_lanes, meta))
        if aligned:
            x_low, xa, gains_in = enter(blk, bit_order, mine, other, gains_in)
            gain_a, gain_m = gains_in[0], gains_in[1]
        else:
            gains_in = regroup(gains_in)
            gain_a, gain_m = gains_in[0], gains_in[1]
            x_low = regroup(jnp.concatenate([mine, other], axis=0))
            x_wide = x_low.astype(F32)
            xa = (x_wide * rms(x_wide) * gain_a).astype(BF16)

        plan = Plan()
        a_columns = a_own.shape[1]
        w_a = fresh_for(plan, a_weights)
        by_tb = plan.copy((plan.read(a_other), everything), (w_a, rows_at(3)), b_mask | t_mask)
        lay(plan, a_by_t, w_a, 2, onward=True)
        lay(plan, a_by_b, w_a, 1, onward=True)
        lay(plan, a_own, w_a, 0)
        lay(plan, early, w_a, 4, columns=(0, a_columns))
        here, cot_out = plan.read(cotangent), plan.fresh((2, local_rows, width), BF16)
        plan.copy(
            (here, lambda ref: ref.at[1 - bit_of(lax.axis_index("blk"), batch_bit)]),
            (cot_out, lambda ref: ref.at[1]),
            b_mask,
            point=1,
        )
        plan.local(
            (here, lambda ref: ref.at[bit_of(lax.axis_index("blk"), batch_bit)]),
            (cot_out, lambda ref: ref.at[0]),
            (local_rows, width),
        )
        w_out = fresh_for(plan, (out_weight,))
        send_over(plan, out_weight, w_out, 1, 1)
        send_over(plan, out_weight, w_out, 3, 1)
        send_over(plan, out_weight, w_out, 2, 1)
        keep_own(plan, out_weight, w_out, 0)
        w_down = fresh_for(plan, (down_weight,))
        send_over(plan, down_weight, w_down, 2, 1)
        keep_own(plan, down_weight, w_down, 0, onward=False)
        lay(plan, early, w_down, 4, columns=(a_columns, ff))
        w_gate = fresh_for(plan, (gate_weight,))
        keep_own(plan, gate_weight, w_gate, 1)
        send_on(plan, w_a, (3,), 2, after=by_tb)
        xa, (w_qkv, cot, w_out, w_down, w_gate) = spread(xa, plan, limit=56 * MIB)
        w_qkv = whole_weight(w_qkv)
        cot = cot.reshape(2 * local_rows, width)
        cot = enter(blk, bit_order, cot)[0] if aligned else regroup(cot)
        query, key_value, raw = prepare(xa, w_qkv, cosine, sine, gain_q, gain_k, heads)

        plan = Plan()
        kv_out = plan.fresh(key_value.shape, BF16)
        plan.copy((plan.read(key_value), everything), (kv_out, everything), x_mask)
        w_out = plan.through(w_out)
        send_on(plan, w_out, (1, 2, 3), 0)
        w_down = plan.through(w_down)
        send_over(plan, down_weight, w_down, 1, 0)
        send_over(plan, down_weight, w_down, 3, 0)
        send_on(plan, w_down, (2,), 1)
        w_gate = plan.through(w_gate)
        send_over(plan, gate_weight, w_gate, 2, 1)
        cot_all, (kv_x, w_out, w_down, w_gate) = spread(cot, plan)
        w_out = whole_weight(w_out)
        key_value = [key_value, kv_x]
        for b in extra_bits:
            key_value = key_value + [over_blk(c, 1 << b) for c in key_value]
        key_value = jnp.stack(key_value)
        keys = key_value[..., :head_size].reshape(parts, 2, 4, half, head_size)
        values = key_value[..., head_size:].reshape(parts, 2, 4, half, head_size)
        query = query.reshape(2, 4, half, q_columns)
        attn, attn_t, total_e = attend(meta, query, keys, values, start_lanes, scaling)
        attn = attn.reshape(tokens, q_columns)

        x_low = x_low.reshape(share)
    else:
        (
            x_low, cot, gains_group, total_e, xa, cot_all, w_qkv, w_out, w_down, w_gate, query, keys, values, raw, attn, attn_t,
        ) = first_call(
            b_mask,
            bit_order,
            scaling,
            dict(
                gain_a=attn_gain[None],
                gain_m=mlp_gain[None],
                gain_q=query_gain[None],
                gain_k=key_gain[None],
                table=table,
                start=start_lanes,
                hidden=hidden_in,
                far=over_blk(lax.dynamic_index_in_dim(hidden_in, 1 - batch, 0, keepdims=False), b_mask),
                cotangent=cotangent,
                wq=query_weight,
                wk=key_matrix,
                wv=value_matrix,
                wo=out_weight,
                wd=down_weight,
                wg=gate_weight,
            ),
            next(ids),
        )
        xa, cot_all = xa.reshape(tokens, width), cot_all.reshape(tokens, width)
        attn = attn.reshape(tokens, q_columns)

    if extra_bits:
        plan = Plan()
        w_down = plan.through(w_down)
        send_on(plan, w_down, (1, 3), 0)
        w_gate = plan.through(w_gate)
        send_over(plan, gate_weight, w_gate, 1, 0)
        send_over(plan, gate_weight, w_gate, 3, 0)
        send_on(plan, w_gate, (2,), 0)
        w_up = fresh_for(plan, (up_weight,))
        send_over(plan, up_weight, w_up, 2, 0)
        keep_own(plan, up_weight, w_up, 1)
        (middle, xm), (w_down, w_gate, w_up) = gather_sum(
            nt(attn, w_out).astype(BF16),
            plan,
            [x_low, gain_m[None]],
            [like(share, F32), like(share, BF16)],
            finish_middle,
        )
        w_down = whole_weight(w_down)

        plan = Plan()
        w_gate = plan.through(w_gate)
        w_up = plan.through(w_up)
        by_b = len(plan.jobs)
        send_over(plan, up_weight, w_up, 1, 0)
        send_on(plan, w_gate, (1, 3), 0)
        send_on(plan, w_up, (2,), 1)
        by_tb = plan.copy(
            (plan.read(up_weight), half_cut(ff, True)), (w_up, rows_at(3)), b_mask | t_mask, after=by_b, point=2
        )
        send_on(plan, w_up, (1,), 2)
        send_on(plan, w_up, (3,), 3, after=by_tb)
        xm, (w_gate, w_up, d_active) = spread(
            xm.reshape(2 * local_rows, width), plan, [fill_product(cot_all, w_down, 0)]
        )
        w_gate, w_up = whole_weight(w_gate), whole_weight(w_up)
        gate = nn(xm, w_gate)
        up = nn(xm, w_up)
        sig = jax.nn.sigmoid(gate)
        silu = gate * sig
        active = (silu * up).astype(BF16)
        d_gate = (d_active * up * sig * (1.0 + gate * (1.0 - sig))).astype(BF16)
        d_up = (d_active * silu).astype(BF16)

        keep_down, away_down = weight_sum(cot_all, active)
        got_x = over_blk(away_down, x_mask)
        (d_gate, d_up, away_down) = pin((d_gate, d_up, away_down))
        ff_cut = ff // 2
        plan, fills = Plan(), []
        if extra_bits:
            keep_gate, away_gate = weight_sum(xm, d_gate)
            keep_up, away_up = weight_sum(xm, d_up)
            source, point = plan.read(away_gate), 0
        else:
            fills = [fill_weight_grad(xm, d_gate, 0), fill_weight_grad(xm, d_up, 1)]
            source, point = ("fill", (0, 1)), 1
        gate_x = plan.fresh((4 * row_features, ff), BF16)
        fold_part(plan, source, gate_x, 0, ff_cut, point)
        (d_middle, d_mid, gain_m_grad), (gate_x, *filled) = gather_sum(
            back_through((d_gate, d_up), (w_gate, w_up)),
            plan,
            [cot.reshape(share), middle, gain_m[None]],
            [like(share, F32), like(share, BF16), like((1, width), F32)],
            finish_mlp_norm,
            fills,
        )
        if filled:
            keep_gate, away_gate, keep_up, away_up = filled
        (d_mid, got_x) = pin((d_mid, got_x))
        own_down, away_down = to_settle(keep_down, got_x)

        plan = Plan()
        settle(plan, away_down, 1)
        gate_x = plan.through(gate_x)
        fold_part(plan, plan.read(away_gate), gate_x, ff_cut, ff - ff_cut)
        up_x = plan.fresh(away_up.shape, BF16)
        fold_part(plan, plan.read(away_up), up_x, 0, ff_cut)
        d_mid_all, (got_down, gate_x, up_x, mixed_partial) = spread(
            d_mid.reshape(2 * local_rows, width), plan, [fill_back(active, w_down, 0)]
        )
        (g_down,) = settled([(own_down, got_down)], (ff,))
        own_gate, away_gate = to_settle(keep_gate, gate_x)
    else:
        (
            middle, d_middle, gain_m_grad, d_mid_all, mixed_partial, own_down, down_b, down_o, gate_b, send_gate, own_gate, keep_up, away_up,
        ) = middle_call(
            b_mask, x_low, cot.reshape(share), gains_group, attn, w_out, cot_all, w_down, w_gate, (down_weight, gate_weight, up_weight), next(ids)
        )
        d_mid_all = d_mid_all.reshape(tokens, width)
        mixed_partial = mixed_partial.reshape(tokens, width)
        up_x = None
    if extra_bits:
        d_attn = nn(d_mid_all, w_out).astype(BF16).reshape(2, 4, half, q_columns)
        d_query, d_key, d_value = attend_back(
            meta, query, d_attn, keys, values, start_lanes, attn_t, total_e, scaling
        )
        d_key = d_key.reshape(parts, tokens, head_size)
        d_value = d_value.reshape(parts, tokens, head_size)
        for b in reversed(extra_bits):
            n = d_key.shape[0] // 2
            d_key = d_key[:n] + over_blk(d_key[n:].astype(BF16), 1 << b).astype(F32)
            d_value = d_value[:n] + over_blk(d_value[n:].astype(BF16), 1 << b).astype(F32)

        plan = Plan()
        away_kv = jnp.concatenate([d_key[1], d_value[1]], axis=1).astype(BF16)
        fold(plan, plan.read(away_kv), away_kv.shape)
        settle(plan, away_gate)
        if up_x is None:
            fold(plan, plan.read(away_up), away_up.shape)
        else:
            up_x = plan.through(up_x)
            fold_part(plan, plan.read(away_up), up_x, ff_cut, ff - ff_cut)
        (mixed,), (got_kv, got_gate, up_x, *filled) = gather_sum(
            mixed_partial,
            plan,
            [middle],
            [like(share, BF16)],
            functools.partial(finish_mixed, bit_order=local_order),
            [] if extra_bits else [fill_weight_grad(d_mid_all, attn, 0)],
        )
        keep_out, away_out = filled if filled else weight_sum(d_mid_all, attn)
        (g_gate,) = settled([(own_gate, got_gate)], (ff,))
        own_up, away_up = to_settle(keep_up, up_x)
        mixed = natural(mixed)
        mixed_got = over_blk(mixed[1], b_mask)
        d_qkv, d_xa_partial, gains_qk = prepare_back(
            d_query.reshape(tokens, q_columns), d_key, d_value, got_kv, raw, cosine, sine, gain_q, gain_k, w_qkv, heads
        )
        (d_xa_partial, mixed_got) = pin((d_xa_partial, mixed_got))

        plan, fills = Plan(), []
        settle(plan, away_up)
        fold(plan, plan.read(away_out), away_out.shape)
        if extra_bits:
            keep_qkv, away_qkv = weight_sum(xa, d_qkv)
            fold(plan, plan.read(away_qkv), away_qkv.shape)
        else:
            fills = [fill_weight_grad(xa, d_qkv, 0)]
            fold(plan, ("fill", (0, 1)), (4 * row_features, a_columns), 1)
        (input_own, input_away, gain_a_grad), (got_up, out_x, got, *filled) = gather_sum(
            d_xa_partial,
            plan,
            [x_low, d_middle, gain_a[None]],
            [like((local_rows, width), F32), like((local_rows, width), BF16), like((1, width), F32)],
            functools.partial(finish_input, bit_order=local_order),
            fills,
        )
        if filled:
            keep_qkv = filled[0]
        own_out, away_out = to_settle(keep_out, out_x)
        (g_up,) = settled([(own_up, got_up)], (ff,))
        own_qkv, away_qkv = to_settle(keep_qkv, got)

        plan = Plan()
        settle(plan, away_qkv)
        settle(plan, away_out)
        input_got = plan.fresh((local_rows, width), BF16)
        plan.copy((plan.read(natural(input_away)), everything), (input_got, everything), b_mask)
        sums = jnp.concatenate([ungroup(gain_a_grad[0]), gains_qk[0], gains_qk[1], ungroup(gain_m_grad[0])])
        (sums,), (got_a, got_o, input_got) = run(
            plan, total_main(sums.reshape(-1, 128)), next(ids), [1 << i for i in range(bits)]
        )
        g_query, g_key, g_value, g_out = settled(
            [(own_qkv, got_a), (own_out, got_o)], (q_columns, k_columns, k_columns, q_columns)
        )
        mixed = in_order(batch, mixed[:1], mixed_got[None], 0)
        input_grad = in_order(batch, natural(input_own)[None], input_got.astype(F32)[None], 0)
        gains = jnp.split(sums.reshape(-1), [width, width + head_size, width + 2 * head_size])
    else:
        (
            mixed_own, mixed_got, input_own, input_got, sums, gate_o, own_up, up_b, up_o, own_qkv, a_b, a_o, own_out, out_b, out_o,
        ) = last_call(
            b_mask,
            bit_order,
            scaling,
            dict(
                low=x_low,
                middle=middle,
                d_middle=d_middle,
                gain=gains_group,
                gain_m_grad=gain_m_grad,
                gain_q=query_gain[None],
                gain_k=key_gain[None],
                start=start_lanes,
                l=total_e,
                dall=d_mid_all,
                w_out=w_out,
                attn=attn,
                q=query,
                k=keys,
                v=values,
                ot=attn_t,
                raw=raw,
                table=table,
                wa=w_qkv,
                xa=xa,
                mixed=mixed_partial.reshape(2, 2, 2, 2, local_rows, width),
                send_g=send_gate,
                keep_u=keep_up,
                away_u=away_up,
            ),
            next(ids),
        )
        mixed, input_grad, g_down, g_gate, g_up, g_query, g_key, g_value, g_out = finish_call(
            batch_bit,
            (mixed_own, mixed_got, input_own, input_got),
            [
                (own_down, down_b, down_o),
                (own_gate, gate_b, gate_o),
                (own_up, up_b, up_o),
                (own_qkv, a_b, a_o),
                (own_out, out_b, out_o),
            ],
            (ff, ff, ff, q_columns, k_columns, k_columns, q_columns),
        )
        gains = jnp.split(sums.reshape(-1), [width, width + head_size, width + 2 * head_size])
    return (
        mixed,
        input_grad,
        g_query,
        g_key,
        g_value,
        g_out,
        g_gate,
        g_up,
        g_down,
        *gains,
    )


def solution(mesh):
    rows = P(None, ("blk", "head"), None)
    weight = P("blk", "head")
    return jax.shard_map(
        local,
        mesh=mesh,
        in_specs=(rows, P(), *([weight] * 7), P(), P(), P(), P(), rows),
        out_specs=(rows, rows, *([weight] * 7), P(), P(), P(), P()),
        check_vma=False,
    )
```

```python
import functools
import math

import jax
import jax.numpy as jnp
from jax import lax
from jax.experimental import pallas as pl
from jax.experimental.pallas import tpu as pltpu
from jax.sharding import PartitionSpec as P

EPS = 1e-06
THETA = 1000000.0
LOG2E = 1.4426950408889634
F32 = jnp.float32
BF16 = jnp.bfloat16

MIB = 1024 * 1024
TINY_COST = pl.CostEstimate(flops=0, bytes_accessed=0, transcendentals=0)
VMEM_LIMIT = 32 * MIB
TENSOR_BIT = 1
SEQ_BIT = 0


def nt(a, b):
    return lax.dot_general(a, b, (((1,), (1,)), ((), ())), preferred_element_type=F32)


def tn(a, b):
    return lax.dot_general(a, b, (((0,), (0,)), ((), ())), preferred_element_type=F32)


def nn(a, b):
    return jnp.dot(a, b, preferred_element_type=F32)


def bit_of(value, bit):
    return (value >> bit) & 1


def over_blk(value, mask):
    count = lax.axis_size("blk")
    return lax.ppermute(value, "blk", [(i, i ^ mask) for i in range(count)])


def over_head(value, mask):
    count = lax.axis_size("head")
    return lax.ppermute(value, "head", [(i, i ^ mask) for i in range(count)])


def pin(values):
    return lax.optimization_barrier(values)


def in_order(flag, own, other, axis):
    return jnp.where(
        flag == 0,
        jnp.concatenate([own, other], axis=axis),
        jnp.concatenate([other, own], axis=axis),
    )


def token_offset(head_place, index, sub):
    core, upper, inner = index // (2 * sub), (index // sub) % 2, index % sub
    return (head_place ^ (upper * 2) ^ core) * sub + inner


def allowed_mask(meta_ref, start_row, q_block, k_block, rows, half, q_lanes):
    sub = half // 2
    head_place = meta_ref[0]
    k_index = lax.broadcasted_iota(jnp.int32, (2 * half, 1), 0)
    k_token = token_offset(head_place, k_index, sub) + k_block * (2 * half)
    q_index = lax.broadcasted_iota(jnp.int32, (1, q_lanes), 1) % (2 * half)
    q_token = token_offset(head_place, q_index, sub) + q_block * (2 * half)
    return (k_token <= q_token) & (k_token >= start_row)


def stacked(ref, heads, width):
    return jnp.concatenate(
        [ref[c, 0, :, h * width : (h + 1) * width] for h in range(heads) for c in range(2)], axis=0
    )


def key_rows(ref, part, block):
    return jnp.concatenate([ref[part, 0, block], ref[part, 1, block]], axis=0)


def attend_kernel(meta_ref, q_ref, k_ref, v_ref, start_ref, o_ref, ot_ref, l_ref, vt_ref, acc_ref, sum_ref, *, factor, heads):
    q_pos = pl.program_id(0)
    parts, _, blocks, half, width = k_ref.shape
    lanes = heads * 2 * half

    @pl.when(q_pos == 0)
    def _():
        for part in range(parts):
            for block in range(blocks):
                vt_ref[part * blocks + block] = key_rows(v_ref, part, block).T

    q_rows = stacked(q_ref, heads, width)
    acc_ref[...] = jnp.zeros_like(acc_ref)
    sum_ref[...] = jnp.zeros_like(sum_ref)
    start_row = start_ref[0]
    q_block = meta_ref[1 + q_pos]
    total = parts * blocks

    def add(kb, masked):
        e = jnp.exp2(nt(key_rows(k_ref, kb // blocks, kb % blocks), q_rows) * factor)
        if masked:
            k_block = meta_ref[1 + blocks + kb]
            e = jnp.where(allowed_mask(meta_ref, start_row, q_block, k_block, None, half, lanes), e, 0.0)
        sum_ref[...] += jnp.sum(e, axis=0, keepdims=True)
        acc_ref[...] += nn(vt_ref[kb], e.astype(BF16))

    def step(kb, carry):
        flag = meta_ref[1 + blocks + total + q_pos * total + kb]

        @pl.when(flag == 1)
        def _():
            add(kb, False)

        @pl.when(flag == 2)
        def _():
            add(kb, True)

        return carry

    lax.fori_loop(0, total, step, 0)
    out = acc_ref[...] / sum_ref[...]
    ot_ref[0] = out
    l_ref[0] = sum_ref[...]
    rows = out.T
    for h in range(heads):
        for c in range(2):
            at = (h * 2 + c) * half
            o_ref[c, 0, :, h * width : (h + 1) * width] = rows[at : at + half].astype(BF16)


def attend_back_kernel(
    meta_ref, q_ref, do_ref, k_ref, v_ref, start_ref, ot_ref, l_ref, dq_ref, dk_ref, dv_ref, kt_ref, acc_ref, *, factor, scaling, heads
):
    q_pos = pl.program_id(0)
    parts, _, blocks, half, width = k_ref.shape
    lanes = heads * 2 * half

    @pl.when(q_pos == 0)
    def _():
        dk_ref[...] = jnp.zeros_like(dk_ref)
        dv_ref[...] = jnp.zeros_like(dv_ref)
        for part in range(parts):
            for block in range(blocks):
                kt_ref[part * blocks + block] = key_rows(k_ref, part, block).T

    q_rows = stacked(q_ref, heads, width)
    do_rows = stacked(do_ref, heads, width)
    delta = jnp.sum(do_rows.astype(F32).T * ot_ref[0], axis=0, keepdims=True)
    inverse = 1.0 / l_ref[0]
    acc_ref[...] = jnp.zeros_like(acc_ref)
    start_row = start_ref[0]
    q_block = meta_ref[1 + q_pos]
    total = parts * blocks

    def add(kb, masked):
        part, block = kb // blocks, kb % blocks
        e = jnp.exp2(nt(key_rows(k_ref, part, block), q_rows) * factor)
        if masked:
            k_block = meta_ref[1 + blocks + kb]
            e = jnp.where(allowed_mask(meta_ref, start_row, q_block, k_block, None, half, lanes), e, 0.0)
        p = e * inverse
        dp = nt(key_rows(v_ref, part, block), do_rows)
        ds = (p * (dp - delta)).astype(BF16)
        dv = nn(p.astype(BF16), do_rows)
        dk = nn(ds, q_rows) * scaling
        for c in range(2):
            dv_ref[part, c, block] += dv[c * half : (c + 1) * half]
            dk_ref[part, c, block] += dk[c * half : (c + 1) * half]
        acc_ref[...] += nn(kt_ref[kb], ds)

    def step(kb, carry):
        flag = meta_ref[1 + blocks + total + q_pos * total + kb]

        @pl.when(flag == 1)
        def _():
            add(kb, False)

        @pl.when(flag == 2)
        def _():
            add(kb, True)

        return carry

    lax.fori_loop(0, total, step, 0)
    rows = acc_ref[...].T * scaling
    for h in range(heads):
        for c in range(2):
            at = (h * 2 + c) * half
            dq_ref[c, 0, :, h * width : (h + 1) * width] = rows[at : at + half]


def attend(meta, q, k, v, start, scaling):
    _, blocks, half, columns = q.shape
    parts, width = k.shape[0], k.shape[-1]
    heads = columns // width
    lanes = heads * 2 * half
    total = parts * blocks
    row_spec = pl.BlockSpec((2, 1, half, columns), lambda i: (0, i, 0, 0))
    key_spec = pl.BlockSpec(k.shape, lambda i: (0, 0, 0, 0, 0))
    lane_spec = pl.BlockSpec((1, 1, lanes), lambda i: (i, 0, 0))
    return pl.pallas_call(
        functools.partial(attend_kernel, factor=scaling * LOG2E, heads=heads),
        grid=(blocks,),
        in_specs=[pl.BlockSpec(memory_space=pltpu.SMEM), row_spec, key_spec, key_spec, lane_spec],
        out_specs=[row_spec, pl.BlockSpec((1, width, lanes), lambda i: (i, 0, 0)), lane_spec],
        out_shape=[
            jax.ShapeDtypeStruct(q.shape, BF16),
            jax.ShapeDtypeStruct((blocks, width, lanes), F32),
            jax.ShapeDtypeStruct((blocks, 1, lanes), F32),
        ],
        scratch_shapes=[
            pltpu.VMEM((total, width, 2 * half), BF16),
            pltpu.VMEM((width, lanes), F32),
            pltpu.VMEM((1, lanes), F32),
        ],
        compiler_params=pltpu.CompilerParams(vmem_limit_bytes=VMEM_LIMIT),
        cost_estimate=pl.CostEstimate(
            flops=2 * 2 * lanes * 2 * half * width * blocks * total,
            bytes_accessed=8 * q.size + 8 * k.size,
            transcendentals=lanes * 2 * half * blocks * total,
        ),
    )(meta, q, k, v, start)


def attend_back(meta, q, do, k, v, start, out_t, total_e, scaling):
    _, blocks, half, columns = q.shape
    parts, width = k.shape[0], k.shape[-1]
    heads = columns // width
    lanes = heads * 2 * half
    total = parts * blocks
    row_spec = pl.BlockSpec((2, 1, half, columns), lambda i: (0, i, 0, 0))
    key_spec = pl.BlockSpec(k.shape, lambda i: (0, 0, 0, 0, 0))
    lane_spec = pl.BlockSpec((1, 1, lanes), lambda i: (i, 0, 0))
    return pl.pallas_call(
        functools.partial(attend_back_kernel, factor=scaling * LOG2E, scaling=scaling, heads=heads),
        grid=(blocks,),
        in_specs=[
            pl.BlockSpec(memory_space=pltpu.SMEM),
            row_spec,
            row_spec,
            key_spec,
            key_spec,
            lane_spec,
            pl.BlockSpec((1, width, lanes), lambda i: (i, 0, 0)),
            lane_spec,
        ],
        out_specs=[row_spec, key_spec, key_spec],
        out_shape=[
            jax.ShapeDtypeStruct(q.shape, F32),
            jax.ShapeDtypeStruct(k.shape, F32),
            jax.ShapeDtypeStruct(k.shape, F32),
        ],
        scratch_shapes=[
            pltpu.VMEM((total, width, 2 * half), BF16),
            pltpu.VMEM((width, lanes), F32),
        ],
        compiler_params=pltpu.CompilerParams(vmem_limit_bytes=VMEM_LIMIT),
        cost_estimate=pl.CostEstimate(
            flops=5 * 2 * lanes * 2 * half * width * blocks * total,
            bytes_accessed=12 * q.size + 16 * k.size,
            transcendentals=lanes * 2 * half * blocks * total,
        ),
    )(meta, q, do, k, v, start, out_t, total_e)


def prepare_kernel(x_ref, w_ref, cos_ref, sin_ref, gq_ref, gk_ref, q_ref, kv_ref, raw_ref, *, heads, width):
    acc = jnp.dot(x_ref[...], w_ref[...], preferred_element_type=F32)
    raw_ref[...] = acc[:, : (heads + 1) * width]
    for h in range(heads + 1):
        part = acc[:, h * width : (h + 1) * width]
        normed = part * lax.rsqrt(jnp.mean(part * part, axis=-1, keepdims=True) + EPS)
        scaled = normed * (gq_ref if h < heads else gk_ref)[...]
        turned = (scaled * cos_ref[...] + pltpu.roll(scaled, width // 2, 1) * sin_ref[...]).astype(BF16)
        if h < heads:
            q_ref[:, h * width : (h + 1) * width] = turned
        else:
            kv_ref[:, :width] = turned
    kv_ref[:, width:] = acc[:, (heads + 1) * width :].astype(BF16)


def prepare(x, w, cos, sin, gain_q, gain_k, heads):
    tokens, depth = x.shape
    width, tile = gain_q.shape[1], 256
    row = lambda n: pl.BlockSpec((tile, n), lambda i: (i, 0))
    fixed = lambda a: pl.BlockSpec(a.shape, lambda i: (0, 0))
    return pl.pallas_call(
        functools.partial(prepare_kernel, heads=heads, width=width),
        grid=(tokens // tile,),
        in_specs=[row(depth), fixed(w), row(width), row(width), fixed(gain_q), fixed(gain_k)],
        out_specs=[row(heads * width), row(2 * width), row((heads + 1) * width)],
        out_shape=[
            jax.ShapeDtypeStruct((tokens, heads * width), BF16),
            jax.ShapeDtypeStruct((tokens, 2 * width), BF16),
            jax.ShapeDtypeStruct((tokens, (heads + 1) * width), F32),
        ],
        compiler_params=pltpu.CompilerParams(vmem_limit_bytes=VMEM_LIMIT),
        cost_estimate=TINY_COST,
    )(x, w, cos, sin, gain_q, gain_k)


def prepare_back_kernel(
    dq_ref, dk_ref, dv_ref, got_ref, raw_ref, cos_ref, sin_ref, gq_ref, gk_ref, w_ref, d_ref, p_ref, g_ref, *, heads, width
):
    @pl.when(pl.program_id(0) == 0)
    def _():
        g_ref[...] = jnp.zeros_like(g_ref)

    got = got_ref[...].astype(F32)
    for h in range(heads + 1):
        at = slice(h * width, (h + 1) * width)
        grad = dq_ref[:, at] if h < heads else dk_ref[0] + got[:, :width]
        gain = (gq_ref if h < heads else gk_ref)[...]
        raw = raw_ref[:, at]
        inverse = lax.rsqrt(jnp.mean(raw * raw, axis=-1, keepdims=True) + EPS)
        normed = raw * inverse
        turned = grad * cos_ref[...] - pltpu.roll(grad, width // 2, 1) * sin_ref[...]
        row = 0 if h < heads else 1
        g_ref[row : row + 1, :] += jnp.sum(turned * normed, axis=0, keepdims=True)
        scaled = turned * gain
        d_ref[:, at] = (inverse * (scaled - normed * jnp.mean(scaled * normed, axis=-1, keepdims=True))).astype(BF16)
    d_ref[:, (heads + 1) * width :] = (dv_ref[0] + got[:, width:]).astype(BF16)
    p_ref[...] = nt(d_ref[...], w_ref[...]).astype(BF16)


def prepare_back(dq, dk, dv, got, raw, cos, sin, gain_q, gain_k, w, heads):
    tokens, width, tile = dq.shape[0], gain_q.shape[1], 256
    row = lambda n: pl.BlockSpec((tile, n), lambda i: (i, 0))
    part = pl.BlockSpec((1, tile, width), lambda i: (0, i, 0))
    fixed = lambda a: pl.BlockSpec(a.shape, lambda i: (0, 0))
    return pl.pallas_call(
        functools.partial(prepare_back_kernel, heads=heads, width=width),
        grid=(tokens // tile,),
        in_specs=[
            row(heads * width),
            part,
            part,
            row(2 * width),
            row((heads + 1) * width),
            row(width),
            row(width),
            fixed(gain_q),
            fixed(gain_k),
            fixed(w),
        ],
        out_specs=[row(w.shape[1]), row(w.shape[0]), pl.BlockSpec((8, width), lambda i: (0, 0))],
        out_shape=[
            jax.ShapeDtypeStruct((tokens, w.shape[1]), BF16),
            jax.ShapeDtypeStruct((tokens, w.shape[0]), BF16),
            jax.ShapeDtypeStruct((8, width), F32),
        ],
        compiler_params=pltpu.CompilerParams(vmem_limit_bytes=VMEM_LIMIT),
        cost_estimate=TINY_COST,
    )(dq, dk, dv, got, raw, cos, sin, gain_q, gain_k, w)


def place_of_block(blk, bit_order, p):
    return blk ^ sum(((p >> i) & 1) << b for i, b in enumerate(bit_order))


def enter_kernel(blk_ref, *refs, bit_order, normed):
    if normed:
        mine_ref, other_ref, gain_ref, low_ref, out_ref, gains_ref = refs
    else:
        mine_ref, low_ref = refs
    rows, width = mine_ref.shape
    n = width >> len(bit_order)
    for p in range(1 << len(bit_order)):
        at = pl.ds(pl.multiple_of(place_of_block(blk_ref[0], bit_order, p) * n, n), n)
        low_ref[:rows, p * n : (p + 1) * n] = mine_ref[:, at]
        if normed:
            low_ref[rows:, p * n : (p + 1) * n] = other_ref[:, at]
            gains_ref[:, p * n : (p + 1) * n] = gain_ref[:, at]
    if normed:
        values = low_ref[...].astype(F32)
        inverse = lax.rsqrt(jnp.mean(values * values, axis=-1, keepdims=True) + EPS)
        out_ref[...] = (values * inverse * gains_ref[:1]).astype(BF16)


def enter(blk, bit_order, mine, other=None, gain=None):
    rows, width = mine.shape
    normed = gain is not None
    total = (2 * rows if normed else rows, width)
    vmem = pl.BlockSpec(memory_space=pltpu.VMEM)
    operands = [mine, other, gain] if normed else [mine]
    return pl.pallas_call(
        functools.partial(enter_kernel, bit_order=bit_order, normed=normed),
        in_specs=[pl.BlockSpec(memory_space=pltpu.SMEM), *[vmem] * len(operands)],
        out_specs=[vmem] * (3 if normed else 1),
        out_shape=[
            *[jax.ShapeDtypeStruct(total, BF16)] * (2 if normed else 1),
            *([jax.ShapeDtypeStruct(gain.shape, F32)] if normed else []),
        ],
        compiler_params=pltpu.CompilerParams(vmem_limit_bytes=VMEM_LIMIT),
        cost_estimate=TINY_COST,
    )(blk[None].astype(jnp.int32), *operands)


def assemble_kernel(place_ref, *refs, sources, widths):
    ins, outs = refs[: 2 * sources], refs[2 * sources :]
    place, k, at = place_ref[0], 0, 0
    for own_ref, got_ref in zip(ins[::2], ins[1::2]):
        f, at = own_ref.shape[0], 0
        while at < own_ref.shape[1]:
            w, cut = widths[k], slice(at, at + widths[k])
            mine = pl.ds(pl.multiple_of(place * w, w), w)
            theirs = pl.ds(pl.multiple_of((1 - place) * w, w), w)
            outs[k][:, mine] = own_ref[:, cut] + got_ref[:f, cut].astype(F32)
            outs[k][:, theirs] = got_ref[f : 2 * f, cut].astype(F32) + got_ref[2 * f :, cut].astype(F32)
            at += w
            k += 1


def assemble(place, sources, widths):
    vmem = pl.BlockSpec(memory_space=pltpu.VMEM)
    flat = [a for pair in sources for a in pair]
    return pl.pallas_call(
        functools.partial(assemble_kernel, sources=len(sources), widths=widths),
        in_specs=[pl.BlockSpec(memory_space=pltpu.SMEM), *[vmem] * len(flat)],
        out_specs=[vmem] * len(widths),
        out_shape=[jax.ShapeDtypeStruct((sources[0][0].shape[0], 2 * w), F32) for w in widths],
        compiler_params=pltpu.CompilerParams(vmem_limit_bytes=VMEM_LIMIT),
        cost_estimate=TINY_COST,
    )(place[None].astype(jnp.int32), *flat)


def back_kernel(*refs):
    *ins, out_ref = refs
    n = len(ins) // 2
    out_ref[...] = sum(nt(d[...], w[...]) for d, w in zip(ins[:n], ins[n:])).astype(BF16)


def back_through(grads, weights):
    tokens, depth, tile = grads[0].shape[0], weights[0].shape[0], 256
    return pl.pallas_call(
        back_kernel,
        grid=(depth // tile,),
        in_specs=[
            *[pl.BlockSpec(g.shape, lambda i: (0, 0)) for g in grads],
            *[pl.BlockSpec((tile, w.shape[1]), lambda i: (i, 0)) for w in weights],
        ],
        out_specs=pl.BlockSpec((tokens, tile), lambda i: (0, i)),
        out_shape=jax.ShapeDtypeStruct((tokens, depth), BF16),
        compiler_params=pltpu.CompilerParams(vmem_limit_bytes=VMEM_LIMIT),
        cost_estimate=TINY_COST,
    )(*grads, *weights)


def weight_grad_kernel(a_ref, b_ref, keep_ref, away_ref):
    product = tn(a_ref[...], b_ref[...])
    first = pl.program_id(0) < pl.num_programs(0) // 2

    @pl.when(first)
    def _():
        keep_ref[...] = product

    @pl.when(jnp.logical_not(first))
    def _():
        away_ref[...] = product.astype(BF16)


def weight_grad(a, b):
    tokens, depth = a.shape
    n, tile = b.shape[1], 256
    steps = depth // tile
    return pl.pallas_call(
        weight_grad_kernel,
        grid=(steps,),
        in_specs=[
            pl.BlockSpec((tokens, tile), lambda i: (0, i)),
            pl.BlockSpec((tokens, n), lambda i: (0, 0)),
        ],
        out_specs=[
            pl.BlockSpec((tile, n), lambda i: (jnp.minimum(i, steps // 2 - 1), 0)),
            pl.BlockSpec((tile, n), lambda i: (jnp.maximum(i - steps // 2, 0), 0)),
        ],
        out_shape=[
            jax.ShapeDtypeStruct((depth // 2, n), F32),
            jax.ShapeDtypeStruct((depth // 2, n), BF16),
        ],
        compiler_params=pltpu.CompilerParams(vmem_limit_bytes=VMEM_LIMIT),
        cost_estimate=TINY_COST,
    )(a, b)


def remote(src, dst, send, recv, target):
    copy = pltpu.make_async_remote_copy(
        src_ref=src, dst_ref=dst, send_sem=send, recv_sem=recv, device_id=target, device_id_type=pl.DeviceIdType.MESH
    )
    copy.start()
    return copy


class Plan:
    def __init__(self):
        self.inputs, self.shapes, self.aliases, self.jobs = [], [], {}, []

    def read(self, array):
        self.inputs.append(array)
        return ("in", len(self.inputs) - 1)

    def fresh(self, shape, dtype):
        self.shapes.append(jax.ShapeDtypeStruct(shape, dtype))
        return ("out", len(self.shapes) - 1)

    def through(self, array):
        self.inputs.append(array)
        self.aliases[len(self.inputs) - 1] = len(self.shapes)
        return self.fresh(array.shape, array.dtype)

    def copy(self, src, dst, mask, after=None, point=0):
        self.jobs.append((src, dst, mask, after, point, None))
        return len(self.jobs) - 1

    def local(self, src, dst, shape, point=0):
        self.jobs.append((src, dst, 0, None, point, shape))
        return len(self.jobs) - 1


class Fill:
    def __init__(self, inputs, outputs, step, point):
        self.inputs, self.outputs, self.step, self.point = inputs, outputs, step, point

    def scratch(self):
        shapes = [pltpu.VMEM(a.shape, a.dtype) for a in (*self.inputs, *self.outputs)]
        return [*shapes, pltpu.SemaphoreType.DMA((len(shapes),))]


def fill_weight_grad(a, b, point):
    depth, n, tile = a.shape[1], b.shape[1], 256
    half = depth // 2

    def step(ins, outs):
        (a_ref, b_ref), (keep_ref, away_ref) = ins, outs

        def one(i, carry):
            at = pl.ds(pl.multiple_of(i * tile, tile), tile)
            keep_ref[at, :] = tn(a_ref[:, at], b_ref[...])
            far = pl.ds(pl.multiple_of(half + i * tile, tile), tile)
            away_ref[at, :] = tn(a_ref[:, far], b_ref[...]).astype(BF16)
            return carry

        lax.fori_loop(0, half // tile, one, 0)

    outputs = [jax.ShapeDtypeStruct((half, n), F32), jax.ShapeDtypeStruct((half, n), BF16)]
    return Fill([a, b], outputs, step, point)


def fill_back(grad, weight, point):
    tokens, depth, tile = grad.shape[0], weight.shape[0], 256

    def step(ins, outs):
        (g_ref, w_ref), (out_ref,) = ins, outs

        def one(i, carry):
            at = pl.ds(pl.multiple_of(i * tile, tile), tile)
            out_ref[:, at] = nt(g_ref[...], w_ref[at, :]).astype(BF16)
            return carry

        lax.fori_loop(0, depth // tile, one, 0)

    return Fill([grad, weight], [jax.ShapeDtypeStruct((tokens, depth), BF16)], step, point)


def fill_product(left, right, point):
    tokens, n, tile = left.shape[0], right.shape[1], 256

    def step(ins, outs):
        (l_ref, r_ref), (out_ref,) = ins, outs

        def one(i, carry):
            at = pl.ds(pl.multiple_of(i * tile, tile), tile)
            out_ref[at, :] = nn(l_ref[at, :], r_ref[...])
            return carry

        lax.fori_loop(0, tokens // tile, one, 0)

    return Fill([left, right], [jax.ShapeDtypeStruct((tokens, n), F32)], step, point)


def run(plan, main, collective_id, greeted=(), fills=(), limit=None):
    inputs, in_specs, out_shapes, out_specs, scratch, body, own_limit = main
    limit = limit or own_limit + sum(math.prod(s.shape) * s.dtype.itemsize for f in fills for s in f.scratch()[:-1])
    f_in, f_out = [a for f in fills for a in f.inputs], [a for f in fills for a in f.outputs]
    n_in, n_out = len(inputs), len(out_shapes)
    m_in, m_out = len(plan.inputs), len(plan.shapes)
    jobs = plan.jobs
    local_jobs = [i for i, job in enumerate(jobs) if not job[2]]
    masks = sorted({*greeted, *[job[2] for job in jobs if job[2]]} - {1 << TENSOR_BIT})
    any_spec = pl.BlockSpec(memory_space=pltpu.HBM)

    def kernel(*refs):
        main_in, refs = refs[:n_in], refs[n_in:]
        plan_in, refs = refs[:m_in], refs[m_in:]
        fill_in, refs = refs[: len(f_in)], refs[len(f_in) :]
        main_out, refs = refs[:n_out], refs[n_out:]
        plan_out, refs = refs[:m_out], refs[m_out:]
        fill_out, refs = refs[: len(f_out)], refs[len(f_out) :]
        send, recv, *rest = refs
        bounce = dict(zip(local_jobs, rest))
        rest = rest[len(local_jobs) :]
        parts = []
        for f in fills:
            k, m = len(f.inputs), len(f.outputs)
            (*held, sems), rest = rest[: k + m + 1], rest[k + m + 1 :]
            loads = [pltpu.make_async_copy(fill_in[i], held[i], sems.at[i]) for i in range(k)]
            stores = [pltpu.make_async_copy(held[k + i], fill_out[i], sems.at[k + i]) for i in range(m)]
            fill_in, fill_out = fill_in[k:], fill_out[m:]
            for copy in loads:
                copy.start()
            parts.append((f, held[:k], held[k:], loads, stores))

        def compute(point):
            for f, ins, outs, loads, stores in parts:
                if f.point == point:
                    for copy in loads:
                        copy.wait()
                    f.step(ins, outs)
                    for copy in stores:
                        copy.start()

        blk, head = lax.axis_index("blk"), lax.axis_index("head")
        core, near, across = (blk, head ^ 1), (blk, head ^ 2), (blk ^ (1 << TENSOR_BIT), head)
        barrier = pltpu.get_barrier_semaphore()
        partners = [core, near, across, *[(blk ^ m, head) for m in masks]]
        for target in partners:
            pl.semaphore_signal(barrier, inc=1, device_id=target, device_id_type=pl.DeviceIdType.MESH)
        pl.semaphore_wait(barrier, len(partners))
        started, arrived, halfway = {}, set(), []

        def arrive(i):
            if i not in arrived:
                arrived.add(i)
                (started[i].wait_recv if jobs[i][2] else started[i].wait)()

        def part(side):
            (kind, index), cut = side
            if kind == "fill":
                return cut(parts[index[0]][2][index[1]])
            return cut((plan_in if kind == "in" else plan_out)[index])

        def issue(point):
            for i in list(halfway):
                started[i].wait()
                started[i] = pltpu.make_async_copy(bounce[i], part(jobs[i][1]), recv.at[i])
                started[i].start()
                halfway.remove(i)
            for i, (src, dst, mask, after, at, shape) in enumerate(jobs):
                if i in started or (at != point and point is not None):
                    continue
                if after is not None:
                    arrive(after)
                if mask:
                    started[i] = remote(part(src), part(dst), send.at[i], recv.at[i], (blk ^ mask, head))
                else:
                    started[i] = pltpu.make_async_copy(part(src), bounce[i], send.at[i])
                    started[i].start()
                    halfway.append(i)

        point = 0
        for _ in body((core, near, across), main_in, main_out, rest):
            issue(point)
            compute(point)
            point += 1
        issue(None)
        issue(None)
        for i in range(len(jobs)):
            arrive(i)
            if jobs[i][2]:
                started[i].wait_send()
        for *_, stores in parts:
            for copy in stores:
                copy.wait()

    results = pl.pallas_call(
        kernel,
        out_shape=[*out_shapes, *plan.shapes, *f_out],
        in_specs=[*in_specs, *[any_spec] * (m_in + len(f_in))],
        out_specs=[*out_specs, *[any_spec] * (m_out + len(f_out))],
        scratch_shapes=[
            pltpu.SemaphoreType.DMA((max(1, len(jobs)),)),
            pltpu.SemaphoreType.DMA((max(1, len(jobs)),)),
            *[pltpu.VMEM(jobs[i][5], BF16) for i in local_jobs],
            *[s for f in fills for s in f.scratch()],
            *scratch,
        ],
        input_output_aliases={n_in + i: n_out + o for i, o in plan.aliases.items()},
        compiler_params=pltpu.CompilerParams(
            collective_id=collective_id, has_side_effects=True, vmem_limit_bytes=limit
        ),
        cost_estimate=TINY_COST,
    )(*inputs, *plan.inputs, *f_in)
    return results[:n_out], results[n_out:]


def spread_main(flat, chunk):
    rows, width = flat.shape[0] // 2, flat.shape[1]
    pieces = width // chunk

    def body(partners, ins, outs, scratch):
        core, near, across = partners
        (s_ref,), (o_ref,), (hold, local_sem, send, recv) = ins, outs, scratch
        first = remote(s_ref, o_ref.at[0, :, 0, 1], send.at[0], recv.at[0], near)
        second = [
            remote(
                s_ref.at[:, :, pl.ds(i * chunk, chunk)],
                o_ref.at[0, :, 1, 0, :, pl.ds((i ^ 1) * chunk, chunk)],
                send.at[6 + i],
                recv.at[6 + i],
                across,
            )
            for i in range(pieces)
        ]
        third = remote(s_ref, o_ref.at[1, :, 0, 0], send.at[1], recv.at[1], core)
        held = pltpu.make_async_copy(s_ref, hold, local_sem.at[0])
        held.start()
        yield
        held.wait()
        own = pltpu.make_async_copy(hold, o_ref.at[0, :, 0, 0], local_sem.at[1])
        own.start()
        for copy in second:
            copy.wait_recv()
        fourth = remote(o_ref.at[0, :, 1, 0], o_ref.at[0, :, 1, 1], send.at[2], recv.at[2], near)
        fifth = remote(o_ref.at[0, :, 1, 0], o_ref.at[1, :, 1, 0], send.at[3], recv.at[3], core)
        yield
        first.wait_recv()
        sixth = remote(o_ref.at[0, :, 0, 1], o_ref.at[1, :, 0, 1], send.at[4], recv.at[4], core)
        yield
        fourth.wait_recv()
        seventh = remote(o_ref.at[0, :, 1, 1], o_ref.at[1, :, 1, 1], send.at[5], recv.at[5], core)
        yield
        own.wait()
        for copy in (first, *second, third, fourth, fifth, sixth, seventh):
            copy.wait_send()
        for copy in (third, fifth, sixth, seventh):
            copy.wait_recv()

    any_spec = pl.BlockSpec(memory_space=pltpu.HBM)
    return (
        [flat.reshape(2, rows, width)],
        [any_spec],
        [jax.ShapeDtypeStruct((2, 2, 2, 2, rows, width), flat.dtype)],
        [any_spec],
        [
            pltpu.VMEM((2, rows, width), flat.dtype),
            pltpu.SemaphoreType.DMA((2,)),
            pltpu.SemaphoreType.DMA((6 + pieces,)),
            pltpu.SemaphoreType.DMA((6 + pieces,)),
        ],
        body,
        8 * MIB,
    )


def gather_main(partial, chunk, extra, outs_like, finish):
    rows, width = partial.shape[0] // 16, partial.shape[1]
    share = (2, rows, width)
    pieces = width // chunk

    def body(partners, ins, outs, scratch):
        core, near, across = partners
        p_ref, *extra_refs = ins
        core_in, out_y, in_y, out_t, in_t, hold, send, recv = scratch
        order = ((1, 1), (0, 1), (1, 0), (0, 0))
        from_core = [
            remote(p_ref.at[1, :, t, y], core_in.at[i], send.at[i], recv.at[i], core) for i, (t, y) in enumerate(order)
        ]
        from_y = []
        for i in range(2):
            t, y = order[i]
            from_core[i].wait_recv()
            out_y[i] = (p_ref[0, :, t, y].astype(F32) + core_in[i].astype(F32)).astype(BF16)
            from_y.append(remote(out_y.at[i], in_y.at[i], send.at[4 + i], recv.at[4 + i], near))
        yield
        from_core[2].wait_recv()
        hold[...] = p_ref[0, :, 1, 0].astype(F32) + core_in[2].astype(F32)
        from_y[0].wait_recv()
        for i in range(pieces):
            a, b = slice(i * chunk, (i + 1) * chunk), slice((i ^ 1) * chunk, ((i ^ 1) + 1) * chunk)
            out_t[:, :, b] = (hold[:, :, a] + in_y[0, :, :, a].astype(F32)).astype(BF16)
        from_t = remote(out_t, in_t, send.at[6], recv.at[6], across)
        yield
        from_core[3].wait_recv()
        hold[...] = p_ref[0, :, 0, 0].astype(F32) + core_in[3].astype(F32)
        from_y[1].wait_recv()
        hold[...] += in_y[1].astype(F32)
        yield
        from_t.wait_recv()
        hold[...] += in_t[...].astype(F32)
        finish(hold, extra_refs, outs)
        for copy in (*from_core, *from_y, from_t):
            copy.wait_send()

    vmem_spec = pl.BlockSpec(memory_space=pltpu.VMEM)
    return (
        [partial.reshape(2, 2, 2, 2, rows, width), *extra],
        [vmem_spec] * (1 + len(extra)),
        outs_like,
        [vmem_spec] * len(outs_like),
        [
            pltpu.VMEM((4, *share), BF16),
            pltpu.VMEM((2, *share), BF16),
            pltpu.VMEM((2, *share), BF16),
            pltpu.VMEM(share, BF16),
            pltpu.VMEM(share, BF16),
            pltpu.VMEM(share, F32),
            pltpu.SemaphoreType.DMA((7,)),
            pltpu.SemaphoreType.DMA((7,)),
        ],
        body,
        24 * MIB,
    )


def inverse_rms(values):
    return lax.rsqrt(jnp.mean(values * values, axis=-1, keepdims=True) + EPS)


def finish_middle(total, extra, outs):
    (low_ref, gain_ref), (middle_ref, normed_ref) = extra, outs
    for m in range(2):
        middle = low_ref[m].astype(F32) + total[m]
        middle_ref[m] = middle
        normed_ref[m] = (middle * inverse_rms(middle) * gain_ref[...]).astype(BF16)


def norm_grad(total, values, gain, gain_grad_ref, m):
    inverse = inverse_rms(values)
    normal = values * inverse
    part = jnp.sum(total * normal, axis=0, keepdims=True)
    gain_grad_ref[...] = part if m == 0 else gain_grad_ref[...] + part
    scaled = total * gain
    return inverse * (scaled - normal * jnp.mean(scaled * normal, axis=-1, keepdims=True))


def finish_mlp_norm(total, extra, outs):
    (cot_ref, middle_ref, gain_ref), (grad_ref, low_ref, gain_grad_ref) = extra, outs
    for m in range(2):
        grad = cot_ref[m].astype(F32) + norm_grad(total[m], middle_ref[m], gain_ref[...], gain_grad_ref, m)
        grad_ref[m] = grad
        low_ref[m] = grad.astype(BF16)


def store_ungrouped(value, ref, blk, bit_order, lead=()):
    n = value.shape[-1] >> len(bit_order)
    for p in range(1 << len(bit_order)):
        block = value[:, p * n : (p + 1) * n]
        if bit_order and n % 128 == 0:
            at = pl.ds(pl.multiple_of(place_of_block(blk, bit_order, p) * n, n), n)
        else:
            at = pl.ds(p * n, n)
        ref[(*lead, slice(None), at)] = block.astype(ref.dtype)


def finish_mixed(total, extra, outs, *, bit_order):
    (middle_ref,), (mixed_ref,) = extra, outs
    blk = lax.axis_index("blk")
    for m in range(2):
        store_ungrouped(middle_ref[m] + total[m], mixed_ref, blk, bit_order, (m,))


def finish_input(total, extra, outs, *, bit_order):
    (low_ref, mid_ref, gain_ref), (own_ref, away_ref, gain_grad_ref) = extra, outs
    blk = lax.axis_index("blk")
    for m in range(2):
        grad = mid_ref[m] + norm_grad(total[m], low_ref[m].astype(F32), gain_ref[...], gain_grad_ref, m)
        store_ungrouped(grad, own_ref if m == 0 else away_ref, blk, bit_order)


def total_main(values):
    rows, width = values.shape
    rounds = 2 + lax.axis_size("blk").bit_length() - 1

    def body(partners, ins, outs, scratch):
        (v_ref,), (o_ref,) = ins, outs
        out_buf, in_buf, send, recv = scratch
        blk, head = lax.axis_index("blk"), lax.axis_index("head")
        o_ref[...] = v_ref[...]
        yield
        for i in range(rounds):
            target = (blk, head ^ (1 << i)) if i < 2 else (blk ^ (1 << (i - 2)), head)
            out_buf[i] = o_ref[...]
            copy = remote(out_buf.at[i], in_buf.at[i], send.at[i], recv.at[i], target)
            copy.wait_recv()
            o_ref[...] += in_buf[i]
            copy.wait_send()
        yield

    vmem_spec = pl.BlockSpec(memory_space=pltpu.VMEM)
    return (
        [values],
        [vmem_spec],
        [jax.ShapeDtypeStruct(values.shape, F32)],
        [vmem_spec],
        [
            pltpu.VMEM((rounds, rows, width), F32),
            pltpu.VMEM((rounds, rows, width), F32),
            pltpu.SemaphoreType.DMA((rounds,)),
            pltpu.SemaphoreType.DMA((rounds,)),
        ],
        body,
        8 * MIB,
    )


class Moving:
    def __init__(self, copy, away):
        self.copy, self.away, self.here, self.gone = copy, away, False, not away

    def arrive(self):
        if not self.here:
            self.here = True
            (self.copy.wait_recv if self.away else self.copy.wait)()

    def sent(self):
        if not self.gone:
            self.gone = True
            self.copy.wait_send()


class Links:
    def __init__(self, send, recv, batch_mask):
        self.send, self.recv, self.all = send, recv, []
        blk, head = lax.axis_index("blk"), lax.axis_index("head")
        self.core, self.near, self.across = (blk, head ^ 1), (blk, head ^ 2), (blk ^ (1 << TENSOR_BIT), head)
        self.seq, self.batch = (blk ^ (1 << SEQ_BIT), head), (blk ^ batch_mask, head)
        self.both = (blk ^ (batch_mask | (1 << TENSOR_BIT)), head)
        self.place = bit_of(blk, TENSOR_BIT)
        self.blk = blk

    def greet(self):
        barrier = pltpu.get_barrier_semaphore()
        partners = (self.core, self.near, self.across, self.seq, self.batch, self.both)
        for target in partners:
            pl.semaphore_signal(barrier, inc=1, device_id=target, device_id_type=pl.DeviceIdType.MESH)
        pl.semaphore_wait(barrier, len(partners))

    def to(self, target, src, dst):
        i = len(self.all)
        self.all.append(Moving(remote(src, dst, self.send.at[i], self.recv.at[i], target), True))
        return self.all[-1]

    def load(self, src, dst):
        copy = pltpu.make_async_copy(src, dst, self.recv.at[len(self.all)])
        copy.start()
        self.all.append(Moving(copy, False))
        return self.all[-1]

    def finish(self):
        for moving in self.all:
            moving.arrive()
            moving.sent()

    def half(self, ref, other):
        n = ref.shape[1] // 2
        place = 1 - self.place if other else self.place
        return ref.at[:, pl.ds(pl.multiple_of(place * n, n), n)]


def nothing(stage):
    pass


class Spread:
    def __init__(self, links, s_ref, o_ref, chunk, in_vmem=True):
        self.links, self.s_ref, self.o_ref, self.chunk, self.in_vmem = links, s_ref, o_ref, chunk, in_vmem

    def begin(self):
        links, s_ref, o_ref, chunk = self.links, self.s_ref, self.o_ref, self.chunk
        self.across = [
            links.to(
                links.across,
                s_ref.at[:, :, pl.ds(i * chunk, chunk)],
                o_ref.at[0, :, 1, 0, :, pl.ds((i ^ 1) * chunk, chunk)],
            )
            for i in range(s_ref.shape[-1] // chunk)
        ]
        self.near = links.to(links.near, s_ref, o_ref.at[0, :, 0, 1])
        self.core = [links.to(links.core, s_ref, o_ref.at[1, :, 0, 0])]
        if self.in_vmem:
            o_ref[0, :, 0, 0] = s_ref[...]
        else:
            links.load(s_ref, o_ref.at[0, :, 0, 0])

    def pass_on(self):
        links, o_ref = self.links, self.o_ref
        for copy in self.across:
            copy.arrive()
        self.onward = links.to(links.near, o_ref.at[0, :, 1, 0], o_ref.at[0, :, 1, 1])
        self.core.append(links.to(links.core, o_ref.at[0, :, 1, 0], o_ref.at[1, :, 1, 0]))
        self.near.arrive()
        self.core.append(links.to(links.core, o_ref.at[0, :, 0, 1], o_ref.at[1, :, 0, 1]))

    def end(self, between=nothing):
        links, o_ref = self.links, self.o_ref
        self.onward.arrive()
        self.core.append(links.to(links.core, o_ref.at[0, :, 1, 1], o_ref.at[1, :, 1, 1]))
        between(2)
        for copy in self.core:
            copy.arrive()
        for copy in (*self.across, self.near, self.core[0]):
            copy.sent()


def spread_in(links, s_ref, o_ref, chunk, between=nothing, in_vmem=True):
    spread = Spread(links, s_ref, o_ref, chunk, in_vmem)
    spread.begin()
    between(0)
    spread.pass_on()
    between(1)
    spread.end(between)


def sum_in(links, bufs, chunk, partial, between=nothing, far=None):
    p_ref, core_in, out_y, in_y, out_t, in_t, hold = bufs
    order = ((1, 1), (1, 0), (0, 1), (0, 0))
    if partial:
        partial(1)
        far = p_ref.at[1]
    core = [links.to(links.core, far.at[:, t, y], core_in.at[i]) for i, (t, y) in enumerate(order)]
    if partial:
        partial(0)

    def both(i):
        t, y = order[i]
        core[i].arrive()
        return p_ref[0, :, t, y].astype(F32) + core_in[i].astype(F32)

    def near(i, m):
        return links.to(links.near, out_y.at[i, m], in_y.at[i, m])

    out_y[0] = both(0).astype(BF16)
    copies = [near(0, 0)]
    hold[...] = both(1)
    out_y[1] = both(2).astype(BF16)
    between(0)
    across = []
    for m in range(2):
        copies[m].arrive()
        copies += [near(0, 1)] if m == 0 else [near(1, 0), near(1, 1)]
        for i in range(p_ref.shape[-1] // chunk):
            a, b = slice(i * chunk, (i + 1) * chunk), slice((i ^ 1) * chunk, ((i ^ 1) + 1) * chunk)
            out_t[m, :, b] = (hold[m, :, a] + in_y[0, m, :, a].astype(F32)).astype(BF16)
        across.append(links.to(links.across, out_t.at[m], in_t.at[m]))
    hold[...] = both(3)
    between(1)
    for m in range(2):
        copies[2 + m].arrive()
        hold[m] += in_y[1, m].astype(F32)
    between(2)
    for m in range(2):
        across[m].arrive()
        hold[m] += in_t[m].astype(F32)
    for copy in (*core, *copies, *across):
        copy.sent()


def loop(count, step):
    def one(i, carry):
        step(i)
        return carry

    lax.fori_loop(0, count, one, 0)


def rows_of(ref, i):
    value = ref[i // 2, i % 2]
    return value.reshape(-1, value.shape[-1])


def away_rows(a_cols, b_ref, away_ref):
    depth, tile = away_ref.shape[0], 512

    def step(i):
        product = tn(a_cols(pl.multiple_of(depth + i * tile, tile), tile), b_ref[...])
        away_ref[pl.ds(pl.multiple_of(i * tile, tile), tile), :] = product.astype(BF16)

    loop(depth // tile, step)


def keep_rows(a_cols, b_ref, fold_ref, own_ref, send_ref):
    f = own_ref.shape[0]
    own_ref[...] = tn(a_cols(0, f), b_ref[...]) + fold_ref[:f, :].astype(F32)

    def step(i):
        at = pl.multiple_of(i * f, f)
        product = tn(a_cols(pl.multiple_of(at + f, f), f), b_ref[...])
        send_ref[pl.ds(at, f), :] = (product + fold_ref[pl.ds(pl.multiple_of(at + f, f), f), :].astype(F32)).astype(BF16)

    loop(3, step)


def middle_kernel(
    gain_ref, low_in, cot_in, attn_ref, wo_ref, c_ref, wd_ref, wg_ref, down_ref, gate_ref, up_ref,
    gain_grad_ref, middle_out, dmid_out, dall_ref, mixed_ref, own_d_ref, got_d_b_ref, got_d_o_ref, got_g_b_ref, send_g_ref, own_g_ref, keep_u_ref, away_u_ref,
    low_ref, cot_ref, middle_ref, dmid_ref, attn, wo, p, core_in, out_y, in_y, out_t, in_t, hold, xm_s, xm, c, wd, wg, wu, dact, gate, act, dg, du,
    away_d, fold_d, away_g, fold_g, own_d, send_d, send_g, up_all, up_tile, send, recv, *, batch_mask, chunk,
):
    links = Links(send, recv, batch_mask)
    f, ff = own_d.shape[0], act.shape[1]
    to, load = links.to, links.load
    loads = [load(attn_ref, attn), load(wo_ref, wo)]
    links.greet()

    def rows(ref, q):
        return ref.at[pl.ds(q * f, f), :]

    down = [to(links.seq, rows(wd_ref, q), rows(wd, q + 4)) for q in (1, 3)]
    gate_z = [to(links.batch, links.half(gate_ref, 0), rows(wg, 1)), to(links.both, links.half(gate_ref, 1), rows(wg, 3))]
    gates = [to(links.seq, rows(wg_ref, 2), rows(wg, 6))]
    up_t = to(links.across, links.half(up_ref, 1), rows(wu, 2))
    ups = []
    for copy in loads:
        copy.arrive()
    down += [load(rows(wd_ref, q), rows(wd, q)) for q in (1, 2, 3, 4, 6)]
    gates += [load(rows(wg_ref, q), rows(wg, q)) for q in (2, 4)]
    down.append(load(links.half(down_ref, 0), rows(wd, 0)))
    gates.append(load(links.half(gate_ref, 0), rows(wg, 0)))
    c_load = load(c_ref, c)
    low_load, cot_load = load(low_in, low_ref), load(cot_in, cot_ref)
    up_own = load(links.half(up_ref, 0), rows(wu, 0))
    bufs = (p, core_in, out_y, in_y, out_t, in_t, hold)

    def out_partial(k):
        for m in range(2):
            at = (k * 2 + m) * attn.shape[0] // 4
            p[k, m] = nt(attn[at : at + attn.shape[0] // 4], wo[...]).astype(BF16).reshape(p.shape[2:])

    def while_out(stage):
        if stage == 0:
            ups.append(to(links.seq, links.half(up_ref, 0), rows(wu, 4)))
        if stage == 1:
            up_t.arrive()
            ups.append(to(links.seq, rows(wu, 2), rows(wu, 6)))
            up_z.append(to(links.batch, links.half(up_ref, 0), rows(wu, 1)))

    up_z = []
    sum_in(links, bufs, chunk, out_partial, while_out)
    low_load.arrive()
    for m in range(2):
        middle = low_ref[m].astype(F32) + hold[m]
        middle_ref[m] = middle
        xm_s[m] = (middle * inverse_rms(middle) * gain_ref[1:2, :]).astype(BF16)
    load(middle_ref, middle_out)

    def while_xm(stage):
        if stage == 0:
            up_z.append(to(links.both, links.half(up_ref, 1), rows(wu, 3)))
            for copy in (*down, c_load):
                copy.arrive()

            def step(i):
                at = pl.ds(pl.multiple_of(i * 512, 512), 512)
                dact[at, :] = nn(c[at, :], wd[...])

            loop(c.shape[0] // 512, step)
            for copy in gate_z:
                copy.arrive()
            gates.extend(to(links.seq, rows(wg, q), rows(wg, q + 4)) for q in (1, 3))
        if stage == 1:
            up_z[0].arrive()
            ups.append(to(links.seq, rows(wu, 1), rows(wu, 5)))
        if stage == 2:
            up_z[1].arrive()
            ups.append(to(links.seq, rows(wu, 3), rows(wu, 7)))

    spread_in(links, xm_s, xm, chunk, while_xm)
    for copy in gates:
        copy.arrive()

    def gate_step(i):
        at = pl.ds(pl.multiple_of(i * 256, 256), 256)
        gate[at, :] = nn(rows_of(xm, i), wg[...])

    loop(4, gate_step)
    up_own.arrive()
    for copy in ups[:-1]:
        copy.arrive()
    most = 7 * f

    def most_step(i):
        at = pl.ds(pl.multiple_of(i * 256, 256), 256)
        up_all[at, :] = nn(rows_of(xm, i)[:, :most], wu[:most, :])

    loop(4, most_step)
    ups[-1].arrive()

    def up_step(i):
        base = pl.multiple_of(i * 256, 256)
        up_tile[...] = up_all[pl.ds(base, 256), :] + nn(rows_of(xm, i)[:, most:], wu[most:, :])

        def part(j):
            at, here = pl.ds(pl.multiple_of(base + j * 32, 32), 32), pl.ds(pl.multiple_of(j * 32, 32), 32)
            g, u, d = gate[at, :], up_tile[here, :], dact[at, :]
            sig = 1.0 / (1.0 + jnp.exp(-g))
            silu = g * sig
            act[at, :] = (silu * u).astype(BF16)
            dg[at, :] = (d * u * sig * (1.0 + g * (1.0 - sig))).astype(BF16)
            du[at, :] = (d * silu).astype(BF16)

        loop(8, part)

    loop(4, up_step)

    def c_cols(at, n):
        return c[:, pl.ds(at, n)]

    def xm_cols(at, n):
        return xm[:, :, :, :, :, pl.ds(at, n)].reshape(-1, n)

    def fold(away, into, *places):
        return {i: to(links.seq, rows(away, i), rows(into, i)) for i in places}

    def compute_away(a_cols, b_ref, away, *places):
        for i in places:
            away[pl.ds(i * f, f), :] = tn(a_cols((i + 4) * f, f), b_ref[...]).astype(BF16)

    def total(a_cols, b_ref, into, i):
        return tn(a_cols(i * f, f), b_ref[...]) + into[pl.ds(i * f, f), :].astype(F32)

    compute_away(c_cols, act, away_d, 1)
    folds_d = fold(away_d, fold_d, 1)
    folds_g = {}
    compute_away(c_cols, act, away_d, 3)

    def back_partial(k):
        def step(m):
            at = pl.ds(pl.multiple_of((k * 2 + m) * 256, 256), 256)
            value = nt(dg[at, :], wg[...]) + nt(du[at, :], wu[...])
            p[k, m] = value.astype(BF16).reshape(p.shape[2:])

        loop(2, step)
        if k == 1:
            folds_d.update(fold(away_d, fold_d, 3))

    def settle_d(i, target, dst):
        folds_d[i].arrive()
        send_d[pl.ds((i - 1) * f, f), :] = total(c_cols, act, fold_d, i).astype(BF16)
        to(target, rows(send_d, i - 1), dst)

    def while_back(stage):
        if stage == 0:
            compute_away(c_cols, act, away_d, 0, 2)
        if stage == 1:
            settle_d(1, links.batch, got_d_b_ref)
            folds_d.update(fold(away_d, fold_d, 2, 0))
            settle_d(3, links.both, rows(got_d_o_ref, 1))
            compute_away(xm_cols, dg, away_g, 1, 3)
            folds_g.update(fold(away_g, fold_g, 1))
        if stage == 2:
            folds_g.update(fold(away_g, fold_g, 3))
            compute_away(xm_cols, dg, away_g, 0, 2)

    sum_in(links, bufs, chunk, back_partial, while_back)
    cot_load.arrive()
    for m in range(2):
        middle = middle_ref[m]
        grad = cot_ref[m].astype(F32) + norm_grad(hold[m], middle, gain_ref[1:2, :], gain_grad_ref, m)
        dmid_ref[m] = grad
        xm_s[m] = grad.astype(BF16)
    load(dmid_ref, dmid_out)
    later = []

    def while_mid(stage):
        if stage == 0:
            folds_d[0].arrive()
            own_d[...] = total(c_cols, act, fold_d, 0)
            own_load = load(own_d, own_d_ref)
            later.append(own_load)
        if stage == 1:
            settle_d(2, links.across, rows(got_d_o_ref, 0))
            folds_g[1].arrive()
            send_g[pl.ds(0, f), :] = total(xm_cols, dg, fold_g, 1).astype(BF16)
            to(links.batch, rows(send_g, 0), got_g_b_ref)
            folds_g.update(fold(away_g, fold_g, 2, 0))

            def step(i):
                at = pl.ds(pl.multiple_of(i * 512, 512), 512)
                dact[at, :] = tn(xm_cols(pl.multiple_of(i * 512, 512), 512), du[...])

            loop(2, step)
            load(dact, keep_u_ref)
            for copy in folds_d.values():
                copy.sent()
            compute_away(xm_cols, du, away_d, 0, 1, 2, 3)
            load(away_d, away_u_ref)

            def step(i):
                at = pl.ds(pl.multiple_of(i * 256, 256), 256)
                p[i // 2, i % 2] = nt(act[at, :], wd[...]).astype(BF16).reshape(p.shape[2:])

            loop(4, step)
            load(p, mixed_ref)
        if stage == 2:
            folds_g[3].arrive()
            send_g[pl.ds(2 * f, f), :] = total(xm_cols, dg, fold_g, 3).astype(BF16)

    spread_in(links, xm_s, dall_ref, chunk, while_mid, in_vmem=False)
    folds_g[2].arrive()
    send_g[pl.ds(f, f), :] = total(xm_cols, dg, fold_g, 2).astype(BF16)
    load(send_g.at[pl.ds(f, 2 * f), :], send_g_ref)
    folds_g[0].arrive()
    later[0].arrive()
    own_d[...] = total(xm_cols, dg, fold_g, 0)
    load(own_d, own_g_ref)
    links.finish()


def middle_call(batch_mask, low, cot, gain, attn, w_out, cot_all, w_down, w_gate, params, collective_id):
    _, rows, width = low.shape
    tokens, columns = attn.shape
    ff = w_down.shape[1]
    f = w_down.shape[0] // 8
    share, full = (2, rows, width), (2, 2, 2, 2, rows, width)
    vmem, hbm = pl.BlockSpec(memory_space=pltpu.VMEM), pl.BlockSpec(memory_space=pltpu.HBM)
    like = jax.ShapeDtypeStruct
    return pl.pallas_call(
        functools.partial(middle_kernel, batch_mask=batch_mask, chunk=2 * width // 8),
        in_specs=[vmem] + [hbm] * 10,
        out_specs=[vmem] + [hbm] * 12,
        out_shape=[
            like((1, width), F32),
            like(share, F32),
            like(share, F32),
            like(full, BF16),
            like(full, BF16),
            like((f, ff), F32),
            like((f, ff), BF16),
            like((2 * f, ff), BF16),
            like((f, ff), BF16),
            like((2 * f, ff), BF16),
            like((f, ff), F32),
            like((4 * f, ff), F32),
            like((4 * f, ff), BF16),
        ],
        scratch_shapes=[
            pltpu.VMEM(share, BF16),
            pltpu.VMEM(share, BF16),
            pltpu.VMEM(share, F32),
            pltpu.VMEM(share, F32),
            pltpu.VMEM((tokens, columns), BF16),
            pltpu.VMEM((width, columns), BF16),
            pltpu.VMEM(full, BF16),
            pltpu.VMEM((4, *share), BF16),
            pltpu.VMEM((2, *share), BF16),
            pltpu.VMEM((2, *share), BF16),
            pltpu.VMEM(share, BF16),
            pltpu.VMEM(share, BF16),
            pltpu.VMEM(share, F32),
            pltpu.VMEM(share, BF16),
            pltpu.VMEM(full, BF16),
            pltpu.VMEM((tokens, width), BF16),
            *[pltpu.VMEM((width, ff), BF16)] * 3,
            *[pltpu.VMEM((tokens, ff), F32)] * 2,
            *[pltpu.VMEM((tokens, ff), BF16)] * 3,
            *[pltpu.VMEM((4 * f, ff), BF16)] * 4,
            pltpu.VMEM((f, ff), F32),
            pltpu.VMEM((3 * f, ff), BF16),
            pltpu.VMEM((3 * f, ff), BF16),
            pltpu.VMEM((tokens, ff), F32),
            pltpu.VMEM((256, ff), F32),
            pltpu.SemaphoreType.DMA((96,)),
            pltpu.SemaphoreType.DMA((96,)),
        ],
        compiler_params=pltpu.CompilerParams(
            collective_id=collective_id, has_side_effects=True, vmem_limit_bytes=60 * MIB
        ),
        cost_estimate=TINY_COST,
    )(gain, low, cot, attn, w_out, cot_all, w_down, w_gate, *params)


def block_of(n, batch_mask):
    blk = lax.axis_index("blk")
    return blk ^ ((n // 2) * batch_mask) ^ ((n % 2) << TENSOR_BIT)


def key_tokens(block, half):
    head = lax.axis_index("head")
    index = lax.broadcasted_iota(jnp.int32, (2 * half, 1), 0)
    return token_offset(head, index, half // 2) + block * (2 * half)


def query_tokens(block, half, lanes):
    head = lax.axis_index("head")
    index = lax.broadcasted_iota(jnp.int32, (1, lanes), 1) % (2 * half)
    return token_offset(head, index, half // 2) + block * (2 * half)


def head_rows(ref, i, heads, width):
    both = [ref[c, i] for c in range(2)]
    return jnp.concatenate([b[:, h * width : (h + 1) * width] for h in range(heads) for b in both], axis=0)


def attention_back(q, do, k, v, start, ot, l, dq, dk, dv, kt, acc, batch_mask, scaling):
    parts, _, blocks, half, width = k.shape
    heads = q.shape[-1] // width
    lanes = heads * 2 * half
    dk[...] = jnp.zeros_like(dk)
    dv[...] = jnp.zeros_like(dv)

    def turn(kb):
        kt[kb] = key_rows(k, kb // blocks, kb % blocks).T

    loop(parts * blocks, turn)

    def per_query(i):
        q_rows, do_rows = head_rows(q, i, heads, width), head_rows(do, i, heads, width)
        delta = jnp.sum(do_rows.astype(F32).T * ot[i], axis=0, keepdims=True)
        inverse, first = 1.0 / l[i], start[i]
        acc[...] = jnp.zeros_like(acc)
        q_block = block_of(i, batch_mask)

        def per_key(kb):
            part, block = kb // blocks, kb % blocks
            k_block = block_of(block, batch_mask) ^ (part << SEQ_BIT)

            def add(diagonal):
                tokens = key_tokens(k_block, half)
                allowed = tokens >= first
                if diagonal:
                    allowed = allowed & (tokens <= query_tokens(q_block, half, lanes))
                score = nt(key_rows(k, part, block), q_rows) * (scaling * LOG2E)
                prob = jnp.where(allowed, jnp.exp2(score), 0.0) * inverse
                d_prob = nt(key_rows(v, part, block), do_rows)
                d_score = (prob * (d_prob - delta)).astype(BF16)
                d_v, d_k = nn(prob.astype(BF16), do_rows), nn(d_score, q_rows) * scaling
                for c in range(2):
                    dv[part, c, block] += d_v[c * half : (c + 1) * half]
                    dk[part, c, block] += d_k[c * half : (c + 1) * half]
                acc[...] += nn(kt[kb], d_score)

            @pl.when(k_block < q_block)
            def _():
                add(False)

            @pl.when(k_block == q_block)
            def _():
                add(True)

        loop(parts * blocks, per_key)
        rows = acc[...].T * scaling
        for h in range(heads):
            for c in range(2):
                at = (h * 2 + c) * half
                dq[c, i, :, h * width : (h + 1) * width] = rows[at : at + half]

    loop(blocks, per_query)


def last_kernel(
    gain_ref, gain_m_grad_ref, gain_q_ref, gain_k_ref, start_ref, l_ref, low_in, middle_in, dmid_in,
    dall_ref, wo_ref, attn_ref, q_ref, k_ref, v_ref, ot_ref, raw_ref, table_ref, wa_ref, xa_ref, mixed_ref,
    send_g_ref, keep_u_ref, away_u_ref,
    mixed_own_ref, mixed_got_ref, input_own_ref, input_got_ref, sums_ref,
    got_g_o_ref, own_u_ref, got_u_b_ref, got_u_o_ref, own_a_ref, got_a_b_ref, got_a_o_ref, own_o_ref, got_o_b_ref, got_o_o_ref,
    low_ref, middle_ref, dmid_ref, dall, wo, attn, q, do, k, v, ot, raw, table, wa, xa, dq, dk, dv, kt, acc, kv_out, kv_in, d_qkv,
    p, core_in, out_y, in_y, out_t, in_t, hold, m_near, m_core_in, m_out_y, m_in_y, m_out_t, m_in_t, m_hold,
    swap_m, swap_i, keep_u, fold_u, own_u, send_u, away_o, fold_o, own_o, send_o, away_a, fold_a, own_a, send_a,
    gains_qk, gain_a_grad, ring_out, ring_in, send, recv, *, batch_mask, bit_order, scaling, chunk,
):
    links = Links(send, recv, batch_mask)
    to, load = links.to, links.load
    f = own_u.shape[0]
    heads = q.shape[-1] // k.shape[-1]
    width = k.shape[-1]

    def rows(ref, i):
        return ref.at[pl.ds(i * f, f), :]

    first = [load(dall_ref, dall), load(wo_ref, wo), load(attn_ref, attn)]
    second = [load(a, b) for a, b in ((q_ref, q), (k_ref, k), (v_ref, v), (ot_ref, ot))]
    third = [load(a, b) for a, b in ((raw_ref, raw), (table_ref, table), (wa_ref, wa), (xa_ref, xa))]
    third += [load(a, b) for a, b in ((low_in, low_ref), (middle_in, middle_ref), (dmid_in, dmid_ref))]
    mixed_near, keep_load = load(mixed_ref.at[0], m_near.at[0]), load(keep_u_ref, keep_u)
    links.greet()

    def settle(src, dst_b, dst_o):
        to(links.batch, rows(src, 0), dst_b)
        to(links.both, rows(src, 2), rows(dst_o, 1))
        to(links.across, rows(src, 1), rows(dst_o, 0))

    to(links.both, rows(send_g_ref, 1), rows(got_g_o_ref, 1))
    to(links.across, rows(send_g_ref, 0), rows(got_g_o_ref, 0))
    folds_u = {i: to(links.seq, rows(away_u_ref, i), rows(fold_u, i)) for i in (1, 3)}
    for copy in (*first, *second):
        copy.arrive()

    def total_u(i):
        return keep_u[pl.ds(i * f, f), :] + fold_u[pl.ds(i * f, f), :].astype(F32)

    def settle_u(i, target, dst):
        folds_u[i].arrive()
        send_u[pl.ds((i - 1) * f, f), :] = total_u(i).astype(BF16)
        to(target, rows(send_u, i - 1), dst)

    def d_attn(i):
        at = pl.ds(pl.multiple_of(i * 256, 256), 256)
        value = nn(dall[at, :], wo[...]).astype(BF16)
        do[i // 2, pl.ds((i % 2) * 2, 2)] = value.reshape(2, 128, value.shape[1])

    def dall_cols(at, n):
        return dall[:, pl.ds(at, n)]

    def xa_cols(at, n):
        return xa[:, pl.ds(at, n)]

    def input_partial(c):
        def step(m):
            at = pl.ds(pl.multiple_of((c * 2 + m) * 256, 256), 256)
            pair = pl.ds(m * 2, 2)
            got = kv_in[at, :].astype(F32)
            cos, sin = table[at, : width // 2], table[at, width // 2 :]
            cos, sin = jnp.concatenate([cos, cos], axis=1), jnp.concatenate([-sin, sin], axis=1)
            for h in range(heads + 1):
                cut = slice(h * width, (h + 1) * width)
                if h < heads:
                    grad = dq[c, pair, :, cut].reshape(256, width)
                else:
                    grad = dk[0, c, pair].reshape(256, width) + got[:, :width]
                gain = (gain_q_ref if h < heads else gain_k_ref)[...].astype(F32)
                values = raw[at, cut]
                inverse = inverse_rms(values)
                normed = values * inverse
                turned = grad * cos - pltpu.roll(grad, width // 2, 1) * sin
                row = 0 if h < heads else 1
                gains_qk[row : row + 1, :] += jnp.sum(turned * normed, axis=0, keepdims=True)
                scaled = turned * gain
                mean = jnp.mean(scaled * normed, axis=-1, keepdims=True)
                d_qkv[at, cut] = (inverse * (scaled - normed * mean)).astype(BF16)
            d_qkv[at, (heads + 1) * width :] = (dv[0, c, pair].reshape(256, width) + got[:, width:]).astype(BF16)
            p[c, m] = nt(d_qkv[at, :], wa[...]).astype(BF16).reshape(p.shape[2:])

        loop(2, step)

    def while_input(stage):
        if stage == 0:
            away_rows(xa_cols, d_qkv, away_a)
            folds.extend(to(links.seq, rows(away_a, i), rows(fold_a, i)) for i in (1, 3, 0, 2))
        if stage == 1:
            folds[0].arrive()
            keep_rows(dall_cols, attn, fold_o, own_o, send_o)
            settle(send_o, got_o_b_ref, got_o_o_ref)
            load(own_o, own_o_ref)
            folds_u.update({i: to(links.seq, rows(away_u_ref, i), rows(fold_u, i)) for i in (2, 0)})

    folds = []

    def while_mixed(stage):
        if stage == 0:
            loop(4, d_attn)
            attention_back(q, do, k, v, start_ref, ot, l_ref, dq, dk, dv, kt, acc, batch_mask, scaling)
            kv_out[:, :width] = dk[1].reshape(-1, width).astype(BF16)
            kv_out[:, width:] = dv[1].reshape(-1, width).astype(BF16)
            folds.extend(
                to(links.seq, kv_out.at[pl.ds(i, 128), :], kv_in.at[pl.ds(i, 128), :])
                for i in range(0, kv_out.shape[0], 128)
            )
            keep_load.arrive()
            settle_u(1, links.batch, got_u_b_ref)
            settle_u(3, links.both, rows(got_u_o_ref, 1))
        if stage == 1:
            away_rows(dall_cols, attn, away_o)
            out_fold = to(links.seq, away_o, fold_o)
            for copy in (*folds, *third):
                copy.arrive()
            folds[:] = [out_fold]
            gains_qk[...] = jnp.zeros_like(gains_qk)
            sum_in(links, (p, core_in, out_y, in_y, out_t, in_t, hold), chunk, input_partial, while_input)
            for m in range(2):
                grad = dmid_ref[m] + norm_grad(hold[m], low_ref[m].astype(F32), gain_ref[0:1, :], gain_a_grad, m)
                store_ungrouped(grad, input_own_ref if m == 0 else swap_i, blk, bit_order)
            to(links.batch, swap_i, input_got_ref)
            for copy in folds:
                copy.arrive()
            keep_rows(xa_cols, d_qkv, fold_a, own_a, send_a)
            settle(send_a, got_a_b_ref, got_a_o_ref)
            load(own_a, own_a_ref)

    mixed_near.arrive()
    blk = lax.axis_index("blk")
    sum_in(links, (m_near, m_core_in, m_out_y, m_in_y, m_out_t, m_in_t, m_hold), chunk, None, while_mixed, mixed_ref.at[1])
    store_ungrouped(middle_ref[0] + m_hold[0], mixed_own_ref, blk, bit_order)
    store_ungrouped(middle_ref[1] + m_hold[1], swap_m, blk, bit_order)
    to(links.batch, swap_m, mixed_got_ref)
    settle_u(2, links.across, rows(got_u_o_ref, 0))
    folds_u[0].arrive()
    own_u[...] = total_u(0)
    load(own_u, own_u_ref)
    n = gain_a_grad.shape[1]
    store_ungrouped(gain_a_grad[...], sums_ref.at[:, pl.ds(0, n)], blk, bit_order)
    sums_ref[:, n : n + width] = gains_qk[0:1, :]
    sums_ref[:, n + width : n + 2 * width] = gains_qk[1:2, :]
    store_ungrouped(gain_m_grad_ref[...], sums_ref.at[:, pl.ds(n + 2 * width, n)], blk, bit_order)
    for i, target in enumerate((links.core, links.near, links.seq, links.across, links.batch)):
        ring_out[i] = sums_ref[...]
        to(target, ring_out.at[i], ring_in.at[i]).arrive()
        sums_ref[...] += ring_in[i]
    links.finish()


def last_call(batch_mask, bit_order, scaling, arrays, collective_id):
    low, dall, attn, q, k, raw, wa, away_u = (arrays[n] for n in ("low", "dall", "attn", "q", "k", "raw", "wa", "away_u"))
    _, rows, width = low.shape
    tokens, columns = attn.shape
    head_size = k.shape[-1]
    ff, f = away_u.shape[1], away_u.shape[0] // 4
    n_a = wa.shape[1]
    share, full, half_full = (2, rows, width), (2, 2, 2, 2, rows, width), (1, 2, 2, 2, rows, width)
    vmem, hbm = pl.BlockSpec(memory_space=pltpu.VMEM), pl.BlockSpec(memory_space=pltpu.HBM)
    like, held = jax.ShapeDtypeStruct, pltpu.VMEM
    in_vmem = ("gain", "gain_m_grad", "gain_q", "gain_k", "start", "l")
    in_hbm = (
        "low", "middle", "d_middle", "dall", "w_out", "attn", "q", "k", "v", "ot", "raw", "table", "wa", "xa", "mixed", "send_g", "keep_u", "away_u",
    )
    total = 2 * width + 2 * head_size
    lanes = 2 * 2 * 128
    sums = (1, total)
    own_and_send = lambda n: [held((f, n), F32), held((3 * f, n), BF16)]
    sum_bufs = [
        held((4, *share), BF16), held((2, *share), BF16), held((2, *share), BF16), held(share, BF16), held(share, BF16),
    ]
    return pl.pallas_call(
        functools.partial(last_kernel, batch_mask=batch_mask, bit_order=bit_order, scaling=scaling, chunk=2 * width // 8),
        in_specs=[vmem] * len(in_vmem) + [hbm] * len(in_hbm),
        out_specs=[vmem, hbm, vmem, hbm, vmem] + [hbm] * 10,
        out_shape=[
            like((rows, width), BF16),
            like((rows, width), BF16),
            like((rows, width), F32),
            like((rows, width), BF16),
            like(sums, F32),
            like((2 * f, ff), BF16),
            *[
                like((m * f, n), dtype)
                for n in (ff, n_a, columns)
                for m, dtype in ((1, F32), (1, BF16), (2, BF16))
            ],
        ],
        scratch_shapes=[
            held(share, BF16),
            held(share, F32),
            held(share, F32),
            held((tokens, width), BF16),
            held((width, columns), BF16),
            held((tokens, columns), BF16),
            held(q.shape, BF16),
            held(q.shape, BF16),
            held(k.shape, BF16),
            held(k.shape, BF16),
            held((4, head_size, lanes), F32),
            held(raw.shape, F32),
            held((tokens, head_size), F32),
            held(wa.shape, BF16),
            held((tokens, width), BF16),
            held(q.shape, F32),
            held(k.shape, F32),
            held(k.shape, F32),
            held((8, head_size, 256), BF16),
            held((head_size, lanes), F32),
            held((tokens, 2 * head_size), BF16),
            held((tokens, 2 * head_size), BF16),
            held((tokens, n_a), BF16),
            held(full, BF16),
            *sum_bufs,
            held(share, F32),
            held(half_full, BF16),
            *sum_bufs,
            held(share, F32),
            held((rows, width), BF16),
            held((rows, width), BF16),
            held((4 * f, ff), F32),
            held((4 * f, ff), BF16),
            *own_and_send(ff),
            held((4 * f, columns), BF16),
            held((4 * f, columns), BF16),
            *own_and_send(columns),
            held((4 * f, n_a), BF16),
            held((4 * f, n_a), BF16),
            *own_and_send(n_a),
            held((8, head_size), F32),
            held((1, width), F32),
            held((5, *sums), F32),
            held((5, *sums), F32),
            pltpu.SemaphoreType.DMA((96,)),
            pltpu.SemaphoreType.DMA((96,)),
        ],
        compiler_params=pltpu.CompilerParams(
            collective_id=collective_id, has_side_effects=True, vmem_limit_bytes=60 * MIB
        ),
        cost_estimate=TINY_COST,
    )(*[arrays[n] for n in (*in_vmem, *in_hbm)])


def attention(q, k, v, start, out, ot, total_ref, vt, acc, total, batch_mask, scaling):
    parts, _, blocks, half, width = k.shape
    heads = q.shape[-1] // width
    lanes = heads * 2 * half

    def turn(kb):
        vt[kb] = key_rows(v, kb // blocks, kb % blocks).T

    loop(parts * blocks, turn)

    def per_query(i):
        q_rows = head_rows(q, i, heads, width)
        first = start[i]
        acc[...] = jnp.zeros_like(acc)
        total[...] = jnp.zeros_like(total)
        q_block = block_of(i, batch_mask)

        def per_key(kb):
            part, block = kb // blocks, kb % blocks
            k_block = block_of(block, batch_mask) ^ (part << SEQ_BIT)

            def add(diagonal):
                tokens = key_tokens(k_block, half)
                allowed = tokens >= first
                if diagonal:
                    allowed = allowed & (tokens <= query_tokens(q_block, half, lanes))
                score = nt(key_rows(k, part, block), q_rows) * (scaling * LOG2E)
                e = jnp.where(allowed, jnp.exp2(score), 0.0)
                total[...] += jnp.sum(e, axis=0, keepdims=True)
                acc[...] += nn(vt[kb], e.astype(BF16))

            @pl.when(k_block < q_block)
            def _():
                add(False)

            @pl.when(k_block == q_block)
            def _():
                add(True)

        loop(parts * blocks, per_key)
        value = acc[...] / total[...]
        ot[i] = value
        total_ref[i] = total[...]
        rows = value.T
        for h in range(heads):
            for c in range(2):
                at = (h * 2 + c) * half
                out[c, i, :, h * width : (h + 1) * width] = rows[at : at + half].astype(BF16)

    loop(blocks, per_query)


def first_kernel(
    gain_a_ref, gain_m_ref, gain_q_ref, gain_k_ref, table_ref, start_ref,
    hid_ref, far_ref, cot_ref, wq_ref, wk_ref, wv_ref, wo_ref, wd_ref, wg_ref,
    low_ref, cot_low_ref, gains_out_ref, l_ref,
    xa_ref, call_ref, wa_out, wo_out, wd_out, wg_out, q_ref, k_ref, v_ref, raw_ref, attn_ref, ot_ref,
    x_in, c_in, xa_s, xa, wa, wb, q, k, v, raw, out, ot, vt, acc, total, send, recv, *, batch_mask, bit_order, scaling, chunk,
):
    links = Links(send, recv, batch_mask)
    to, load = links.to, links.load
    blk = lax.axis_index("blk")
    batch = bit_of(blk, bit_order[0])
    width = k.shape[-1]
    heads = q.shape[-1] // width
    f = wa.shape[0] // 8
    a_params, at = [], 0
    for ref in (wq_ref, wk_ref, wv_ref):
        n = ref.shape[1] // 2
        a_params.append((ref, at, n))
        at += n

    def rows(ref, i):
        return ref.at[pl.ds(i * f, f), :]

    x_own, x_far = load(hid_ref.at[batch], x_in.at[0]), load(far_ref, x_in.at[1])
    c_own = load(cot_ref.at[batch], c_in.at[0])
    a_own = [load(links.half(ref, 0), wa.at[pl.ds(0, f), pl.ds(start, n)]) for ref, start, n in a_params]
    a_other = [load(links.half(ref, 1), wb.at[:, pl.ds(start, n)]) for ref, start, n in a_params]
    links.greet()
    for copy in (*a_own, *a_other):
        copy.arrive()
    a_t = to(links.across, wb, rows(wa, 2))
    a_rest = [to(links.seq, rows(wa, 0), rows(wa, 4))]
    to(links.seq, links.half(wo_ref, 0), rows(wo_out, 4))
    load(links.half(wo_ref, 0), rows(wo_out, 0))
    to(links.seq, links.half(wd_ref, 0), rows(wd_out, 4))
    to(links.seq, links.half(wg_ref, 0), rows(wg_out, 4))
    n_blocks = 1 << len(bit_order)
    n = x_in.shape[-1] // n_blocks

    def regroup(src, dst, lead):
        for p in range(n_blocks):
            cut = pl.ds(pl.multiple_of(place_of_block(blk, bit_order, p) * n, n), n)
            dst[(*lead, pl.ds(p * n, n))] = src[(*lead, cut)]

    all_rows = (slice(None), slice(None))
    for p in range(n_blocks):
        cut = pl.ds(pl.multiple_of(place_of_block(blk, bit_order, p) * n, n), n)
        gains_out_ref[0:1, p * n : (p + 1) * n] = gain_a_ref[:, cut].astype(F32)
        gains_out_ref[1:2, p * n : (p + 1) * n] = gain_m_ref[:, cut].astype(F32)
    x_own.arrive()
    x_far.arrive()
    a_far = {1: to(links.batch, rows(wa, 0), rows(wa, 1)), 3: to(links.both, wb, rows(wa, 3))}
    c_far = to(links.batch, cot_ref.at[1 - batch], c_in.at[1])
    regroup(x_in, low_ref, all_rows)
    for m in range(2):
        value = low_ref[m].astype(F32)
        xa_s[m] = (value * inverse_rms(value) * gains_out_ref[0:1, :]).astype(BF16)

    by_rows = Spread(links, xa_s, xa, chunk)
    by_rows.begin()
    a_t.arrive()
    a_rest.append(to(links.seq, rows(wa, 2), rows(wa, 6)))
    by_rows.pass_on()
    down_t = to(links.across, links.half(wd_ref, 1), rows(wd_out, 2))
    out_rows = [to(links.across, links.half(wo_ref, 1), rows(wo_out, 2))]
    for i, copy in a_far.items():
        copy.arrive()
        a_rest.append(to(links.seq, rows(wa, i), rows(wa, i + 4)))
    c_own.arrive()
    c_far.arrive()
    regroup(c_in, cot_low_ref, all_rows)
    by_cot = Spread(links, cot_low_ref, call_ref, chunk, in_vmem=False)
    by_cot.begin()
    out_rows.append(to(links.batch, links.half(wo_ref, 0), rows(wo_out, 1)))
    out_rows.append(to(links.both, links.half(wo_ref, 1), rows(wo_out, 3)))
    to(links.both, links.half(wd_ref, 1), rows(wd_out, 3))
    by_rows.end()
    load(xa, xa_ref)

    def prepare_rows(i):
        c, m = i // 2, i % 2
        pair = pl.ds(m * 2, 2)
        at = pl.ds(pl.multiple_of(i * 256, 256), 256)
        acc_rows = nn(rows_of(xa, i), wa[...])
        raw[at, :] = acc_rows[:, : (heads + 1) * width]
        cos, sin = table_ref[at, : width // 2], table_ref[at, width // 2 :]
        cos, sin = jnp.concatenate([cos, cos], axis=1), jnp.concatenate([-sin, sin], axis=1)
        for h in range(heads + 1):
            part = acc_rows[:, h * width : (h + 1) * width]
            scaled = part * inverse_rms(part) * (gain_q_ref if h < heads else gain_k_ref)[...].astype(F32)
            turned = (scaled * cos + pltpu.roll(scaled, width // 2, 1) * sin).astype(BF16).reshape(2, 128, width)
            if h < heads:
                q[c, pair, :, h * width : (h + 1) * width] = turned
            else:
                k[0, c, pair] = turned
        v[0, c, pair] = acc_rows[:, (heads + 1) * width :].astype(BF16).reshape(2, 128, width)

    for copy in a_rest:
        copy.arrive()
    loop(4, prepare_rows)
    kv = [to(links.seq, ref.at[0, c, i], ref.at[1, c, i]) for ref in (k, v) for c in range(2) for i in range(4)]
    to(links.batch, links.half(wd_ref, 0), rows(wd_out, 1))
    load(wa, wa_out)
    load(raw, raw_ref)
    load(q, q_ref)
    down_t.arrive()
    to(links.seq, rows(wd_out, 2), rows(wd_out, 6))
    by_cot.pass_on()
    to(links.across, links.half(wg_ref, 1), rows(wg_out, 2))
    for i, copy in zip((2, 1, 3), out_rows):
        copy.arrive()
        to(links.seq, rows(wo_out, i), rows(wo_out, i + 4))
    for copy in kv:
        copy.arrive()
    load(k, k_ref)
    load(v, v_ref)
    attention(q, k, v, start_ref, out, ot, l_ref, vt, acc, total, batch_mask, scaling)
    load(out, attn_ref)
    load(ot, ot_ref)
    by_cot.end()
    links.finish()


def first_call(batch_mask, bit_order, scaling, arrays, collective_id):
    hid, wq, wk, wv, wo, wd, wg = (arrays[n] for n in ("hidden", "wq", "wk", "wv", "wo", "wd", "wg"))
    _, rows, width = hid.shape
    tokens, head_size = 16 * rows, arrays["gain_q"].shape[1]
    columns, n_a = wq.shape[1] // 2, (wq.shape[1] + wk.shape[1] + wv.shape[1]) // 2
    heads = columns // head_size
    half, lanes = tokens // 8, heads * tokens // 4
    share, full = (2, rows, width), (2, 2, 2, 2, rows, width)
    vmem, hbm = pl.BlockSpec(memory_space=pltpu.VMEM), pl.BlockSpec(memory_space=pltpu.HBM)
    like, held = jax.ShapeDtypeStruct, pltpu.VMEM
    in_vmem = ("gain_a", "gain_m", "gain_q", "gain_k", "table", "start")
    in_hbm = ("hidden", "far", "cotangent", "wq", "wk", "wv", "wo", "wd", "wg")
    q_shape, k_shape = (2, 4, half, columns), (2, 2, 4, half, head_size)
    ot_shape, raw_shape = (4, head_size, lanes), (tokens, (heads + 1) * head_size)
    return pl.pallas_call(
        functools.partial(first_kernel, batch_mask=batch_mask, bit_order=bit_order, scaling=scaling, chunk=2 * width // 8),
        in_specs=[vmem] * len(in_vmem) + [hbm] * len(in_hbm),
        out_specs=[vmem] * 4 + [hbm] * 12,
        out_shape=[
            like(share, BF16),
            like(share, BF16),
            like((2, width), F32),
            like((4, 1, lanes), F32),
            like(full, BF16),
            like(full, BF16),
            like((width, n_a), BF16),
            like((width, columns), BF16),
            like((width, wd.shape[1] // 2), BF16),
            like((width, wg.shape[1] // 2), BF16),
            like(q_shape, BF16),
            like(k_shape, BF16),
            like(k_shape, BF16),
            like(raw_shape, F32),
            like(q_shape, BF16),
            like(ot_shape, F32),
        ],
        scratch_shapes=[
            held(share, BF16),
            held(share, BF16),
            held(share, BF16),
            held(full, BF16),
            held((width, n_a), BF16),
            held((width // 8, n_a), BF16),
            held(q_shape, BF16),
            held(k_shape, BF16),
            held(k_shape, BF16),
            held(raw_shape, F32),
            held(q_shape, BF16),
            held(ot_shape, F32),
            held((8, head_size, 2 * half), BF16),
            held((head_size, lanes), F32),
            held((1, lanes), F32),
            pltpu.SemaphoreType.DMA((96,)),
            pltpu.SemaphoreType.DMA((96,)),
        ],
        compiler_params=pltpu.CompilerParams(
            collective_id=collective_id, has_side_effects=True, vmem_limit_bytes=56 * MIB
        ),
        cost_estimate=TINY_COST,
    )(*[arrays[n] for n in (*in_vmem, *in_hbm)])


def finish_kernel(sums, mixed_own, mixed_got, input_own, input_got, *refs, sources, widths, gains, batch_bit):
    ins, outs = refs[: 3 * sources], refs[3 * sources :]
    gain_refs, (mixed_ref, input_ref, *outs) = outs[: len(gains)], outs[len(gains) :]
    at = 0
    for ref, n in zip(gain_refs, gains):
        ref[...] = sums[0, at : at + n]
        at += n
    blk = lax.axis_index("blk")
    place, batch, k = bit_of(blk, TENSOR_BIT), bit_of(blk, batch_bit), 0
    mixed_ref[batch] = mixed_own[...]
    mixed_ref[1 - batch] = mixed_got[...]
    input_ref[batch] = input_own[...]
    input_ref[1 - batch] = input_got[...].astype(F32)
    for own, by_batch, by_other in zip(ins[::3], ins[1::3], ins[2::3]):
        at = 0
        while at < own.shape[1]:
            w, cut = widths[k], slice(at, at + widths[k])
            mine = pl.ds(pl.multiple_of(place * w, w), w)
            theirs = pl.ds(pl.multiple_of((1 - place) * w, w), w)
            outs[k][:, mine] = own[:, cut] + by_batch[:, cut].astype(F32)
            outs[k][:, theirs] = by_other[0, :, cut].astype(F32) + by_other[1, :, cut].astype(F32)
            at += w
            k += 1


def finish_call(batch_bit, sums, gains, rows, sources, widths):
    steps = 4
    f, (n_rows, width) = sources[0][0].shape[0], rows[0].shape
    tile, row_tile = f // steps, n_rows // steps
    by_rows = lambda t, n: pl.BlockSpec((t, n), lambda i: (i, 0))
    by_pairs = lambda t, n: pl.BlockSpec((2, t, n), lambda i: (0, i, 0))
    flat, specs = [], []
    for own, by_batch, by_other in sources:
        n = own.shape[1]
        flat += [own, by_batch, by_other.reshape(2, f, n)]
        specs += [by_rows(tile, n), by_rows(tile, n), by_pairs(tile, n)]
    like = jax.ShapeDtypeStruct
    return pl.pallas_call(
        functools.partial(finish_kernel, sources=len(sources), widths=widths, gains=gains, batch_bit=batch_bit),
        grid=(steps,),
        in_specs=[pl.BlockSpec(sums.shape, lambda i: (0, 0)), *[by_rows(row_tile, width)] * 4, *specs],
        out_specs=[*[pl.BlockSpec((n,), lambda i: (0,)) for n in gains], *[by_pairs(row_tile, width)] * 2, *[by_rows(tile, 2 * w) for w in widths]],
        out_shape=[
            *[like((n,), F32) for n in gains],
            like((2, n_rows, width), BF16),
            like((2, n_rows, width), F32),
            *[like((f, 2 * w), F32) for w in widths],
        ],
        compiler_params=pltpu.CompilerParams(vmem_limit_bytes=60 * MIB),
        cost_estimate=TINY_COST,
    )(sums, *rows, *flat)


def local(
    hidden_in,
    lengths,
    query_weight,
    key_matrix,
    value_matrix,
    out_weight,
    gate_weight,
    up_weight,
    down_weight,
    attn_gain,
    query_gain,
    key_gain,
    mlp_gain,
    cotangent,
):
    ring = lax.axis_size("blk")
    bits = ring.bit_length() - 1
    batch_bit = bits - 1
    extra_bits = [i for i in range(bits) if i not in (TENSOR_BIT, SEQ_BIT, batch_bit)]
    seq_bits = [SEQ_BIT, *extra_bits]
    parts = 1 << len(seq_bits)
    bit_order = [batch_bit, TENSOR_BIT, SEQ_BIT, *extra_bits]
    b_mask, t_mask, x_mask = 1 << batch_bit, 1 << TENSOR_BIT, 1 << SEQ_BIT
    blk, head = lax.axis_index("blk"), lax.axis_index("head")
    batch, tensor = bit_of(blk, batch_bit), bit_of(blk, TENSOR_BIT)

    local_rows, width = hidden_in.shape[1:]
    block_rows = local_rows * lax.axis_size("head")
    half = block_rows // 2
    row_features = width // ring
    head_size = query_gain.shape[0]
    scaling = head_size ** (-0.5)
    tokens = 16 * local_rows
    heads = query_weight.shape[1] // (2 * head_size)
    ff = gate_weight.shape[1] // 2

    def moved(values, place_of):
        axis = values.ndim - 1
        return jnp.concatenate(
            [
                lax.dynamic_slice_in_dim(values, place_of(i) * row_features, row_features, axis)
                for i in range(ring)
            ],
            axis=axis,
        )

    def regroup(values):
        return moved(values, lambda p: blk ^ sum(((p >> i) & 1) << b for i, b in enumerate(bit_order)))

    def ungroup(values):
        return moved(values, lambda n: sum(bit_of(blk ^ n, b) << i for i, b in enumerate(bit_order)))

    def everything(ref):
        return ref

    def mask_of(p):
        return sum(((p >> i) & 1) << b for i, b in enumerate(bit_order))

    def rows_at(p):
        return lambda ref: ref.at[pl.ds(p * row_features, row_features), :]

    def half_cut(n, other):
        def cut(ref):
            place = bit_of(lax.axis_index("blk"), TENSOR_BIT)
            place = 1 - place if other else place
            return ref.at[:, pl.ds(pl.multiple_of(place * n, n), n)]

        return cut

    def send_over(plan, weight, buffer, p, point):
        mask, n = mask_of(p), weight.shape[1] // 2
        plan.copy((plan.read(weight), half_cut(n, mask & t_mask)), (buffer, rows_at(p)), mask, point=point)

    def keep_own(plan, weight, buffer, point, onward=True):
        here, n = plan.read(weight), weight.shape[1] // 2
        if onward:
            plan.copy((here, half_cut(n, 0)), (buffer, rows_at(4)), x_mask, point=point)
        plan.local((here, half_cut(n, 0)), (buffer, rows_at(0)), (row_features, n), point=point)

    def send_on(plan, buffer, places, point, after=None):
        for p in places:
            plan.copy((buffer, rows_at(p)), (buffer, rows_at(p + 4)), x_mask, after=after, point=point)

    def lay(plan, array, buffer, p, point=0, columns=None, onward=False):
        here = plan.read(array)
        cut = (lambda ref: ref.at[:, pl.ds(*columns)]) if columns else everything
        if onward:
            plan.copy((here, cut), (buffer, rows_at(p + 4)), x_mask, point=point)
        plan.local((here, cut), (buffer, rows_at(p)), (row_features, columns[1] if columns else array.shape[1]), point)

    def fresh_for(plan, weights):
        return plan.fresh(buffer_shape(weights), BF16)

    def buffer_shape(weights):
        return (8 * row_features, sum(w.shape[1] for w in weights) // 2)

    def whole_weight(buffer):
        pieces = [buffer]
        for b in extra_bits:
            pieces = pieces + [over_blk(c, 1 << b) for c in pieces]
        return jnp.concatenate(pieces, axis=0) if extra_bits else buffer

    def split_grad(grad):
        for b in reversed(extra_bits):
            n = grad.shape[0] // 2
            grad = grad[:n] + over_blk(grad[n:].astype(BF16), 1 << b).astype(F32)
        n = grad.shape[0] // 2
        return grad[:n], grad[n:].astype(BF16)

    def weight_sum(a, b):
        return split_grad(tn(a, b)) if extra_bits else weight_grad(a, b)

    def fold(plan, source, shape, point=0):
        plan.copy((source, everything), (plan.fresh(shape, BF16), everything), x_mask, point=point)

    def fold_part(plan, source, buffer, start, n, point=0):
        def part(ref):
            return ref.at[:, pl.ds(start, n)]

        plan.copy((source, part), (buffer, part), x_mask, point=point)

    def to_settle(keep, got):
        total = keep + got.astype(F32)
        return total[:row_features], total[row_features:].astype(BF16)

    def settle(plan, away, t_point=0):
        out, here = plan.fresh(away.shape, away.dtype), plan.read(away)
        for i, mask in ((0, b_mask), (2, b_mask | t_mask), (1, t_mask)):
            plan.copy((here, rows_at(i)), (out, rows_at(i)), mask, point=t_point if mask == t_mask else 0)

    def settled(sources, column_widths):
        if all(w % 128 == 0 for w in column_widths):
            return assemble(tensor, sources, column_widths)
        f, results = row_features, []
        widths = iter(column_widths)
        for own, got in sources:
            own = own + got[:f].astype(F32)
            other = got[f : 2 * f].astype(F32) + got[2 * f :].astype(F32)
            at = 0
            while at < own.shape[1]:
                w = next(widths)
                results.append(in_order(tensor, own[:, at : at + w], other[:, at : at + w], 1))
                at += w
        return results

    chunk = 2 * row_features
    ids = iter(range(100))

    def spread(flat, plan, fills=(), limit=None):
        (out,), rest = run(plan, spread_main(flat, chunk), next(ids), fills=fills, limit=limit)
        return out.reshape(tokens, width), rest

    share = (2, local_rows, width)

    def gather_sum(partial, plan, extra, outs_like, finish, fills=()):
        return run(plan, gather_main(partial, chunk, extra, outs_like, finish), next(ids), fills=fills)

    def like(shape, dtype):
        return jax.ShapeDtypeStruct(shape, dtype)

    aligned = row_features % 128 == 0
    local_order = bit_order if aligned else []

    def split_batch(rows):
        mine = lax.dynamic_index_in_dim(rows, batch, 0, keepdims=False)
        theirs = lax.dynamic_index_in_dim(rows, 1 - batch, 0, keepdims=False)
        return mine, theirs

    def natural(rows):
        return rows if aligned else ungroup(rows)

    length_row = lax.dynamic_index_in_dim(lengths, batch, 0, keepdims=False)
    doc_ends = jnp.cumsum(length_row)
    batch_flip = jnp.arange(2, dtype=jnp.int32)[:, None] << batch_bit
    tensor_flip = jnp.arange(2, dtype=jnp.int32)[None, :] << TENSOR_BIT
    q_blocks = (blk ^ batch_flip ^ tensor_flip).reshape(4)
    index = jnp.arange(2 * half, dtype=jnp.int32)
    in_block = token_offset(head, index, local_rows).reshape(2, 1, half)
    token_index = q_blocks[None, :, None] * block_rows + in_block
    passed = doc_ends <= token_index[..., None]
    doc_start = jnp.max(jnp.where(passed, doc_ends, 0), axis=-1).astype(jnp.int32)
    position = (token_index - doc_start).reshape(tokens)
    start_lanes = jnp.tile(jnp.transpose(doc_start, (1, 0, 2)).reshape(4, 1, 2 * half), (1, 1, heads))
    k_blocks = q_blocks
    for b in seq_bits:
        k_blocks = jnp.concatenate([k_blocks, k_blocks ^ (1 << b)])
    least_start = jnp.min(doc_start, axis=(0, 2))[:, None]
    last_start = jnp.max(doc_start, axis=(0, 2))[:, None]
    k_first = (k_blocks * block_rows)[None, :]
    none = (k_blocks[None, :] > q_blocks[:, None]) | (k_first + block_rows <= least_start)
    whole = (k_blocks[None, :] < q_blocks[:, None]) & (k_first >= last_start)
    flags = jnp.where(none, 0, jnp.where(whole, 1, 2))
    meta = jnp.concatenate([head[None], q_blocks, k_blocks, flags.reshape(-1)]).astype(jnp.int32)

    inverse_freq = THETA ** (-jnp.arange(head_size // 2, dtype=F32) / (head_size // 2))
    angles = position.astype(F32)[:, None] * inverse_freq[None, :]
    cosine, sine = jnp.cos(angles), jnp.sin(angles)
    table = jnp.concatenate([cosine, sine], axis=1)
    cosine = jnp.concatenate([cosine, cosine], axis=1)
    sine = jnp.concatenate([-sine, sine], axis=1)

    def rms(values):
        return lax.rsqrt(jnp.mean(values * values, axis=-1, keepdims=True) + EPS)

    def norm_back(grad, normed, inverse, gain):
        scaled = grad * gain
        return inverse * (scaled - normed * jnp.mean(scaled * normed, axis=-1, keepdims=True))

    gains_in = jnp.stack([attn_gain, mlp_gain]).astype(F32)
    gain_q = query_gain.astype(F32)[None]
    gain_k = key_gain.astype(F32)[None]

    q_columns, k_columns = heads * head_size, head_size
    a_weights = (query_weight, key_matrix, value_matrix)

    def halves(weights, which):
        return jnp.concatenate(
            [lax.dynamic_slice_in_dim(w, which * (w.shape[1] // 2), w.shape[1] // 2, 1) for w in weights], axis=1
        )

    if extra_bits:
        mine, theirs = split_batch(hidden_in)
        other = over_blk(theirs, b_mask)
        a_own, a_other = halves(a_weights, tensor), halves(a_weights, 1 - tensor)
        a_by_t = over_blk(a_other, t_mask)
        a_by_b = over_blk(a_own, b_mask)
        early = over_blk(jnp.concatenate([a_own, halves((down_weight,), tensor)], axis=1), x_mask)
        (mine, other, cosine, sine, start_lanes, meta) = pin((mine, other, cosine, sine, start_lanes, meta))
        if aligned:
            x_low, xa, gains_in = enter(blk, bit_order, mine, other, gains_in)
            gain_a, gain_m = gains_in[0], gains_in[1]
        else:
            gains_in = regroup(gains_in)
            gain_a, gain_m = gains_in[0], gains_in[1]
            x_low = regroup(jnp.concatenate([mine, other], axis=0))
            x_wide = x_low.astype(F32)
            xa = (x_wide * rms(x_wide) * gain_a).astype(BF16)

        plan = Plan()
        a_columns = a_own.shape[1]
        w_a = fresh_for(plan, a_weights)
        by_tb = plan.copy((plan.read(a_other), everything), (w_a, rows_at(3)), b_mask | t_mask)
        lay(plan, a_by_t, w_a, 2, onward=True)
        lay(plan, a_by_b, w_a, 1, onward=True)
        lay(plan, a_own, w_a, 0)
        lay(plan, early, w_a, 4, columns=(0, a_columns))
        here, cot_out = plan.read(cotangent), plan.fresh((2, local_rows, width), BF16)
        plan.copy(
            (here, lambda ref: ref.at[1 - bit_of(lax.axis_index("blk"), batch_bit)]),
            (cot_out, lambda ref: ref.at[1]),
            b_mask,
            point=1,
        )
        plan.local(
            (here, lambda ref: ref.at[bit_of(lax.axis_index("blk"), batch_bit)]),
            (cot_out, lambda ref: ref.at[0]),
            (local_rows, width),
        )
        w_out = fresh_for(plan, (out_weight,))
        send_over(plan, out_weight, w_out, 1, 1)
        send_over(plan, out_weight, w_out, 3, 1)
        send_over(plan, out_weight, w_out, 2, 1)
        keep_own(plan, out_weight, w_out, 0)
        w_down = fresh_for(plan, (down_weight,))
        send_over(plan, down_weight, w_down, 2, 1)
        keep_own(plan, down_weight, w_down, 0, onward=False)
        lay(plan, early, w_down, 4, columns=(a_columns, ff))
        w_gate = fresh_for(plan, (gate_weight,))
        keep_own(plan, gate_weight, w_gate, 1)
        send_on(plan, w_a, (3,), 2, after=by_tb)
        xa, (w_qkv, cot, w_out, w_down, w_gate) = spread(xa, plan, limit=56 * MIB)
        w_qkv = whole_weight(w_qkv)
        cot = cot.reshape(2 * local_rows, width)
        cot = enter(blk, bit_order, cot)[0] if aligned else regroup(cot)
        query, key_value, raw = prepare(xa, w_qkv, cosine, sine, gain_q, gain_k, heads)

        plan = Plan()
        kv_out = plan.fresh(key_value.shape, BF16)
        plan.copy((plan.read(key_value), everything), (kv_out, everything), x_mask)
        w_out = plan.through(w_out)
        send_on(plan, w_out, (1, 2, 3), 0)
        w_down = plan.through(w_down)
        send_over(plan, down_weight, w_down, 1, 0)
        send_over(plan, down_weight, w_down, 3, 0)
        send_on(plan, w_down, (2,), 1)
        w_gate = plan.through(w_gate)
        send_over(plan, gate_weight, w_gate, 2, 1)
        cot_all, (kv_x, w_out, w_down, w_gate) = spread(cot, plan)
        w_out = whole_weight(w_out)
        key_value = [key_value, kv_x]
        for b in extra_bits:
            key_value = key_value + [over_blk(c, 1 << b) for c in key_value]
        key_value = jnp.stack(key_value)
        keys = key_value[..., :head_size].reshape(parts, 2, 4, half, head_size)
        values = key_value[..., head_size:].reshape(parts, 2, 4, half, head_size)
        query = query.reshape(2, 4, half, q_columns)
        attn, attn_t, total_e = attend(meta, query, keys, values, start_lanes, scaling)
        attn = attn.reshape(tokens, q_columns)

        x_low = x_low.reshape(share)
    else:
        (
            x_low, cot, gains_group, total_e, xa, cot_all, w_qkv, w_out, w_down, w_gate, query, keys, values, raw, attn, attn_t,
        ) = first_call(
            b_mask,
            bit_order,
            scaling,
            dict(
                gain_a=attn_gain[None],
                gain_m=mlp_gain[None],
                gain_q=query_gain[None],
                gain_k=key_gain[None],
                table=table,
                start=start_lanes,
                hidden=hidden_in,
                far=over_blk(lax.dynamic_index_in_dim(hidden_in, 1 - batch, 0, keepdims=False), b_mask),
                cotangent=cotangent,
                wq=query_weight,
                wk=key_matrix,
                wv=value_matrix,
                wo=out_weight,
                wd=down_weight,
                wg=gate_weight,
            ),
            next(ids),
        )
        xa, cot_all = xa.reshape(tokens, width), cot_all.reshape(tokens, width)
        attn = attn.reshape(tokens, q_columns)

    if extra_bits:
        plan = Plan()
        w_down = plan.through(w_down)
        send_on(plan, w_down, (1, 3), 0)
        w_gate = plan.through(w_gate)
        send_over(plan, gate_weight, w_gate, 1, 0)
        send_over(plan, gate_weight, w_gate, 3, 0)
        send_on(plan, w_gate, (2,), 0)
        w_up = fresh_for(plan, (up_weight,))
        send_over(plan, up_weight, w_up, 2, 0)
        keep_own(plan, up_weight, w_up, 1)
        (middle, xm), (w_down, w_gate, w_up) = gather_sum(
            nt(attn, w_out).astype(BF16),
            plan,
            [x_low, gain_m[None]],
            [like(share, F32), like(share, BF16)],
            finish_middle,
        )
        w_down = whole_weight(w_down)

        plan = Plan()
        w_gate = plan.through(w_gate)
        w_up = plan.through(w_up)
        by_b = len(plan.jobs)
        send_over(plan, up_weight, w_up, 1, 0)
        send_on(plan, w_gate, (1, 3), 0)
        send_on(plan, w_up, (2,), 1)
        by_tb = plan.copy(
            (plan.read(up_weight), half_cut(ff, True)), (w_up, rows_at(3)), b_mask | t_mask, after=by_b, point=2
        )
        send_on(plan, w_up, (1,), 2)
        send_on(plan, w_up, (3,), 3, after=by_tb)
        xm, (w_gate, w_up, d_active) = spread(
            xm.reshape(2 * local_rows, width), plan, [fill_product(cot_all, w_down, 0)]
        )
        w_gate, w_up = whole_weight(w_gate), whole_weight(w_up)
        gate = nn(xm, w_gate)
        up = nn(xm, w_up)
        sig = jax.nn.sigmoid(gate)
        silu = gate * sig
        active = (silu * up).astype(BF16)
        d_gate = (d_active * up * sig * (1.0 + gate * (1.0 - sig))).astype(BF16)
        d_up = (d_active * silu).astype(BF16)

        keep_down, away_down = weight_sum(cot_all, active)
        got_x = over_blk(away_down, x_mask)
        (d_gate, d_up, away_down) = pin((d_gate, d_up, away_down))
        ff_cut = ff // 2
        plan, fills = Plan(), []
        if extra_bits:
            keep_gate, away_gate = weight_sum(xm, d_gate)
            keep_up, away_up = weight_sum(xm, d_up)
            source, point = plan.read(away_gate), 0
        else:
            fills = [fill_weight_grad(xm, d_gate, 0), fill_weight_grad(xm, d_up, 1)]
            source, point = ("fill", (0, 1)), 1
        gate_x = plan.fresh((4 * row_features, ff), BF16)
        fold_part(plan, source, gate_x, 0, ff_cut, point)
        (d_middle, d_mid, gain_m_grad), (gate_x, *filled) = gather_sum(
            back_through((d_gate, d_up), (w_gate, w_up)),
            plan,
            [cot.reshape(share), middle, gain_m[None]],
            [like(share, F32), like(share, BF16), like((1, width), F32)],
            finish_mlp_norm,
            fills,
        )
        if filled:
            keep_gate, away_gate, keep_up, away_up = filled
        (d_mid, got_x) = pin((d_mid, got_x))
        own_down, away_down = to_settle(keep_down, got_x)

        plan = Plan()
        settle(plan, away_down, 1)
        gate_x = plan.through(gate_x)
        fold_part(plan, plan.read(away_gate), gate_x, ff_cut, ff - ff_cut)
        up_x = plan.fresh(away_up.shape, BF16)
        fold_part(plan, plan.read(away_up), up_x, 0, ff_cut)
        d_mid_all, (got_down, gate_x, up_x, mixed_partial) = spread(
            d_mid.reshape(2 * local_rows, width), plan, [fill_back(active, w_down, 0)]
        )
        (g_down,) = settled([(own_down, got_down)], (ff,))
        own_gate, away_gate = to_settle(keep_gate, gate_x)
    else:
        (
            gain_m_grad, middle, d_middle, d_mid_all, mixed_partial, own_down, down_b, down_o, gate_b, send_gate, own_gate, keep_up, away_up,
        ) = middle_call(
            b_mask, x_low, cot.reshape(share), gains_group, attn, w_out, cot_all, w_down, w_gate, (down_weight, gate_weight, up_weight), next(ids)
        )
        d_mid_all = d_mid_all.reshape(tokens, width)
        mixed_partial = mixed_partial.reshape(tokens, width)
        up_x = None
    if extra_bits:
        d_attn = nn(d_mid_all, w_out).astype(BF16).reshape(2, 4, half, q_columns)
        d_query, d_key, d_value = attend_back(
            meta, query, d_attn, keys, values, start_lanes, attn_t, total_e, scaling
        )
        d_key = d_key.reshape(parts, tokens, head_size)
        d_value = d_value.reshape(parts, tokens, head_size)
        for b in reversed(extra_bits):
            n = d_key.shape[0] // 2
            d_key = d_key[:n] + over_blk(d_key[n:].astype(BF16), 1 << b).astype(F32)
            d_value = d_value[:n] + over_blk(d_value[n:].astype(BF16), 1 << b).astype(F32)

        plan = Plan()
        away_kv = jnp.concatenate([d_key[1], d_value[1]], axis=1).astype(BF16)
        fold(plan, plan.read(away_kv), away_kv.shape)
        settle(plan, away_gate)
        if up_x is None:
            fold(plan, plan.read(away_up), away_up.shape)
        else:
            up_x = plan.through(up_x)
            fold_part(plan, plan.read(away_up), up_x, ff_cut, ff - ff_cut)
        (mixed,), (got_kv, got_gate, up_x, *filled) = gather_sum(
            mixed_partial,
            plan,
            [middle],
            [like(share, BF16)],
            functools.partial(finish_mixed, bit_order=local_order),
            [] if extra_bits else [fill_weight_grad(d_mid_all, attn, 0)],
        )
        keep_out, away_out = filled if filled else weight_sum(d_mid_all, attn)
        (g_gate,) = settled([(own_gate, got_gate)], (ff,))
        own_up, away_up = to_settle(keep_up, up_x)
        mixed = natural(mixed)
        mixed_got = over_blk(mixed[1], b_mask)
        d_qkv, d_xa_partial, gains_qk = prepare_back(
            d_query.reshape(tokens, q_columns), d_key, d_value, got_kv, raw, cosine, sine, gain_q, gain_k, w_qkv, heads
        )
        (d_xa_partial, mixed_got) = pin((d_xa_partial, mixed_got))

        plan, fills = Plan(), []
        settle(plan, away_up)
        fold(plan, plan.read(away_out), away_out.shape)
        if extra_bits:
            keep_qkv, away_qkv = weight_sum(xa, d_qkv)
            fold(plan, plan.read(away_qkv), away_qkv.shape)
        else:
            fills = [fill_weight_grad(xa, d_qkv, 0)]
            fold(plan, ("fill", (0, 1)), (4 * row_features, a_columns), 1)
        (input_own, input_away, gain_a_grad), (got_up, out_x, got, *filled) = gather_sum(
            d_xa_partial,
            plan,
            [x_low, d_middle, gain_a[None]],
            [like((local_rows, width), F32), like((local_rows, width), BF16), like((1, width), F32)],
            functools.partial(finish_input, bit_order=local_order),
            fills,
        )
        if filled:
            keep_qkv = filled[0]
        own_out, away_out = to_settle(keep_out, out_x)
        (g_up,) = settled([(own_up, got_up)], (ff,))
        own_qkv, away_qkv = to_settle(keep_qkv, got)

        plan = Plan()
        settle(plan, away_qkv)
        settle(plan, away_out)
        input_got = plan.fresh((local_rows, width), BF16)
        plan.copy((plan.read(natural(input_away)), everything), (input_got, everything), b_mask)
        sums = jnp.concatenate([ungroup(gain_a_grad[0]), gains_qk[0], gains_qk[1], ungroup(gain_m_grad[0])])
        (sums,), (got_a, got_o, input_got) = run(
            plan, total_main(sums.reshape(-1, 128)), next(ids), [1 << i for i in range(bits)]
        )
        g_query, g_key, g_value, g_out = settled(
            [(own_qkv, got_a), (own_out, got_o)], (q_columns, k_columns, k_columns, q_columns)
        )
        mixed = in_order(batch, mixed[:1], mixed_got[None], 0)
        input_grad = in_order(batch, natural(input_own)[None], input_got.astype(F32)[None], 0)
        gains = jnp.split(sums.reshape(-1), [width, width + head_size, width + 2 * head_size])
    else:
        (
            mixed_own, mixed_got, input_own, input_got, sums, gate_o, own_up, up_b, up_o, own_qkv, a_b, a_o, own_out, out_b, out_o,
        ) = last_call(
            b_mask,
            bit_order,
            scaling,
            dict(
                low=x_low,
                middle=middle,
                d_middle=d_middle,
                gain=gains_group,
                gain_m_grad=gain_m_grad,
                gain_q=query_gain[None],
                gain_k=key_gain[None],
                start=start_lanes,
                l=total_e,
                dall=d_mid_all,
                w_out=w_out,
                attn=attn,
                q=query,
                k=keys,
                v=values,
                ot=attn_t,
                raw=raw,
                table=table,
                wa=w_qkv,
                xa=xa,
                mixed=mixed_partial.reshape(2, 2, 2, 2, local_rows, width),
                send_g=send_gate,
                keep_u=keep_up,
                away_u=away_up,
            ),
            next(ids),
        )
        *gains, mixed, input_grad, g_down, g_gate, g_up, g_query, g_key, g_value, g_out = finish_call(
            batch_bit,
            sums,
            (width, head_size, head_size, width),
            (mixed_own, mixed_got, input_own, input_got),
            [
                (own_down, down_b, down_o),
                (own_gate, gate_b, gate_o),
                (own_up, up_b, up_o),
                (own_qkv, a_b, a_o),
                (own_out, out_b, out_o),
            ],
            (ff, ff, ff, q_columns, k_columns, k_columns, q_columns),
        )
    return (
        mixed,
        input_grad,
        g_query,
        g_key,
        g_value,
        g_out,
        g_gate,
        g_up,
        g_down,
        *gains,
    )


def solution(mesh):
    rows = P(None, ("blk", "head"), None)
    weight = P("blk", "head")
    return jax.shard_map(
        local,
        mesh=mesh,
        in_specs=(rows, P(), *([weight] * 7), P(), P(), P(), P(), rows),
        out_specs=(rows, rows, *([weight] * 7), P(), P(), P(), P()),
        check_vma=False,
    )
```
